32 devices in a mesh: dp: 2 (over y), seq: 16 (over z, x, core).
Axes of the slice: x: 2, y: 2, z: 4, core: 2. Of those that a mesh axis runs over, the one named last changes fastest.
Arguments:
- tokens: bfloat16 [4, 2048, 1024], P('dp', 'seq'), may hold values from -24 to 24
- doc_ids: int32 [4, 2048], P('dp'), may hold values from 0 to 3, as said below
- norm_attn: bfloat16 [1024], P(('dp', 'seq')), may hold values from 0.5 to 1.5
- norm_mlp: bfloat16 [1024], P(('dp', 'seq')), may hold values from 0.5 to 1.5
- w_qkv: bfloat16 [1024, 3072], P(('dp', 'seq')), may hold values from -0.1875 to 0.1875
- w_out: bfloat16 [1024, 1024], P(('dp', 'seq')), may hold values from -0.5 to 0.5
- w_in: bfloat16 [1024, 5248], P(('dp', 'seq')), may hold values from -0.1875 to 0.1875
- w_down: bfloat16 [1024, 2624], P(('dp', 'seq')), may hold values from -0.125 to 0.125
- cotangent: bfloat16 [4, 2048, 1024], P('dp', 'seq'), may hold values from -6 to 6
Outputs:
- layer_out: bfloat16 [4, 2048, 1024], P('dp', 'seq')
- input_grad: float32 [4, 2048, 1024], P('dp', 'seq')
- grad_norm_attn: float32 [1024], P(('dp', 'seq'))
- grad_norm_mlp: float32 [1024], P(('dp', 'seq'))
- grad_w_qkv: float32 [1024, 3072], P(('dp', 'seq'))
- grad_w_out: float32 [1024, 1024], P(('dp', 'seq'))
- grad_w_in: float32 [1024, 5248], P(('dp', 'seq'))
- grad_w_down: float32 [1024, 2624], P(('dp', 'seq'))
The draws below stay inside these ranges and needn't reach their ends.
Inputs may be any that keep to these rules, and one draw needn't show every extreme that they name: `doc_ids`: along each stream the ids start at 0, never fall, and rise by at most one from one token to the next.
All inputs are finite; a program needn't handle non-finite values.
Results may differ from the reference program's by a relative error of at most 0.014.
Values may be sent and summed in bfloat16 or wider, within the bound.
No kernel may reach another device: no remote copies, remote signals or barrier semaphores. Data moves between devices by JAX's collectives and lax.ppermute only.
A program may use at most 192 MiB of HBM per device.

```python
import math
from functools import partial
import jax
import jax.numpy as jnp
from jax import lax

D = 1024
HD = 64
FF = 2624
HALF = 64
BLOCK = 128
STREAMS_DEV = 2
STREAMS = 4
STREAM = 2048


def draw_tokens(key, part):
    key = jax.random.fold_in(key, 11)
    key_cols, key_rows, key_main = jax.random.split(key, 3)
    column_scale = jnp.exp(jax.random.uniform(key_cols, (D,), jnp.float32, math.log(0.3), math.log(3.0)))
    row_scale = jnp.exp(jax.random.uniform(key_rows, (STREAMS, STREAM, 1), jnp.float32, math.log(0.5), math.log(2.0)))
    base_values = jnp.clip(jax.random.normal(key_main, (STREAMS, STREAM, D), jnp.float32), -4.0, 4.0)
    return (base_values * row_scale * column_scale).astype(jnp.bfloat16)


def draw_doc_ids(key, part):
    key = jax.random.fold_in(key, 5)
    key_long, key_first, key_last, key_cuts = jax.random.split(key, 4)
    group_count = STREAMS // STREAMS_DEV
    chosen = jax.random.randint(key_long, (group_count,), 0, STREAMS_DEV)
    is_long = jnp.arange(STREAMS) % STREAMS_DEV == jnp.repeat(chosen, STREAMS_DEV)
    first_cut = jax.random.randint(key_first, (STREAMS, 1), 1, BLOCK // 2)
    last_cut = STREAM - jax.random.randint(key_last, (STREAMS, 1), 1, BLOCK // 2)
    orders = jax.vmap(lambda one_key: jax.random.permutation(one_key, STREAM - 1))(jax.random.split(key_cuts, STREAMS)) + 1
    positions = jnp.arange(STREAM)[None, :]
    random_marks = jnp.any(orders[:, :3, None] == positions[:, None, :], axis=1)
    long_marks = (positions == first_cut) | (positions == last_cut)
    cut_marks = jnp.where(is_long[:, None], long_marks, random_marks)
    return jnp.cumsum(cut_marks.astype(jnp.int32), axis=1).astype(jnp.int32)


def raised(result, key, source, target, parts, factor):
    owner, partner = [(jnp.arange(result.shape[position]) // (result.shape[position] // parts)).reshape([-1 if axis == position else 1 for axis in range(result.ndim)]) for position in (source, target)]
    chosen = jax.random.permutation(key, parts)[partner]
    strong = (owner == chosen) | (owner == (partner + parts // 2) % parts)
    return jnp.where(strong, factor * result, result)


def levels(key, shape, cuts, low, largest):
    level = 1.0
    for dim, shards_of in cuts:
        draws = jax.random.uniform(jax.random.fold_in(jax.random.fold_in(key, 6), dim), (shards_of,), jnp.float32, low / len(cuts), largest / len(cuts))
        level = level * jnp.repeat(jnp.exp(draws), shape[dim] // shards_of).reshape((-1,) + (1,) * (len(shape) - 1 - dim))
    return level


def gaussian(own_key, dims, width, most, cuts=(), kind=jnp.bfloat16):
    values = width * jax.random.normal(own_key, dims, jnp.float32)
    if cuts:
        values = values * levels(own_key, dims, cuts, -0.22, 0.18)
    return jnp.clip(values, -most, most).astype(kind)


def noise_with(key, dims, scale, most, cuts, heavy, kind=jnp.bfloat16):
    drawn = scale * jax.random.normal(key, dims, jnp.float32)
    if cuts:
        drawn = drawn * levels(key, dims, cuts, -0.22, 0.18)
    return jnp.clip(raised(drawn, jax.random.fold_in(key, 3), *heavy), -most, most).astype(kind)


def setup_inputs(seed: int = 0) -> dict:
    streams_of = jax.random.split(jax.random.key(seed), 10)
    return {
        "tokens": draw_tokens(jax.random.fold_in(streams_of[9], 71), 0),
        "doc_ids": draw_doc_ids(jax.random.fold_in(streams_of[9], 71), 0),
        "norm_attn": jnp.clip(1.0 + 0.1 * jax.random.normal(streams_of[2], (D,), jnp.float32), 0.5, 1.5).astype(jnp.bfloat16),
        "norm_mlp": jnp.clip(1.0 + 0.1 * jax.random.normal(streams_of[3], (D,), jnp.float32), 0.5, 1.5).astype(jnp.bfloat16),
        "w_qkv": gaussian(streams_of[4], (D, 3 * D), D ** -0.5, 0.1875, ((0, 32),)),
        "w_out": gaussian(streams_of[5], (D, D), (D * HALF // 512) ** -0.5, 0.5, ((0, 32),)),
        "w_in": gaussian(streams_of[6], (D, 2 * FF), D ** -0.5, 0.1875, ((0, 32),)),
        "w_down": gaussian(streams_of[7], (D, FF), FF ** -0.5, 0.125, ((0, 32),)),
        "cotangent": noise_with(streams_of[8], (STREAMS, STREAM, D), 1.0, 6.0, ((0, 2), (1, 16)), (1, 2, 16, 2.0)),
    }


NORM_EPSILON = 1e-05
ROPE_BASE = 10000.0

@jax.custom_vjp
def low(v):
    return lax.optimization_barrier(v.astype(jnp.bfloat16)).astype(jnp.float32)

@jax.custom_vjp
def low_back(v):
    return v

def low_keep(v):
    return (low(v), None)

def low_pass(kept, grad):
    return (grad,)

def back_keep(v):
    return (v, None)

def back_low(kept, grad):
    return (low(grad),)
low.defvjp(low_keep, low_pass)
low_back.defvjp(back_keep, back_low)

def matmul(left, right):
    return jnp.dot(left, right, precision=lax.Precision.HIGHEST, preferred_element_type=jnp.float32)

def layer_norm(values, gain_vec):
    row_mean = lax.optimization_barrier(jnp.mean(values, -1, keepdims=True))
    centred = values - row_mean
    variance = lax.optimization_barrier(jnp.mean(centred * centred, -1, keepdims=True))
    return centred * lax.rsqrt(variance + NORM_EPSILON) * gain_vec

def rotate(values, cosine, sine_table):
    half_width = values.shape[-1] // 2
    turned = jnp.concatenate([-values[..., half_width:], values[..., :half_width]], -1)
    return values * cosine + turned * sine_table

def rope_tables(positions):
    frequency = ROPE_BASE ** (-(jnp.arange(HD // 2, dtype=jnp.float32) * 2.0 / HD))
    angles = positions[:, None] * frequency[None, :]
    angles = jnp.concatenate([angles, angles], -1)
    return (jnp.cos(angles)[:, None, :], jnp.sin(angles)[:, None, :])

def gated_gelu(expanded):
    hidden_units = expanded.shape[-1] // 2
    return jax.nn.gelu(expanded[:, :hidden_units], approximate=False) * expanded[:, hidden_units:]

def attend_block(query_rot, key_padded, value_padded, ids_padded, block_index, query_rows):
    first_row = (block_index * query_rows).astype(jnp.int32)
    window_len = query_rows + 2 * HALF
    query_part = lax.dynamic_slice_in_dim(query_rot, first_row, query_rows, 0)
    key_part = lax.dynamic_slice_in_dim(key_padded, first_row, window_len, 0)
    value_part = lax.dynamic_slice_in_dim(value_padded, first_row, window_len, 0)
    query_ids = lax.dynamic_slice_in_dim(ids_padded, (first_row + HALF).astype(jnp.int32), query_rows, 0)
    key_ids = lax.dynamic_slice_in_dim(ids_padded, first_row, window_len, 0)
    offsets = jnp.arange(window_len)[None, :] - jnp.arange(query_rows)[:, None]
    allowed = (offsets >= 0) & (offsets <= 2 * HALF) & (query_ids[:, None] == key_ids[None, :])
    raw_scores = jnp.einsum('qhd,khd->hqk', query_part, key_part, precision=lax.Precision.HIGHEST) * HD ** (-0.5)
    scores = jnp.where(allowed[None], low_back(raw_scores), -1e+30)
    row_peak = lax.optimization_barrier(jnp.max(scores, -1, keepdims=True))
    log_total = row_peak + jnp.log(lax.optimization_barrier(jnp.sum(jnp.exp(scores - row_peak), -1, keepdims=True)))
    probabilities = low(jnp.exp(scores - log_total))
    return jnp.einsum('hqk,khd->qhd', probabilities, value_part, precision=lax.Precision.HIGHEST)

def attend(query_rot, key_rot, value_rot, doc_row):
    length = query_rot.shape[0]
    query_rows = math.gcd(length, 512)
    padding = ((HALF, HALF), (0, 0), (0, 0))
    key_padded = jnp.pad(key_rot, padding)
    value_padded = jnp.pad(value_rot, padding)
    ids_padded = jnp.pad(doc_row, (HALF, HALF), constant_values=-1)
    block_fn = jax.checkpoint(partial(attend_block, query_rows=query_rows))
    outputs = lax.map(lambda block_index: block_fn(query_rot, key_padded, value_padded, ids_padded, block_index), jnp.arange(length // query_rows, dtype=jnp.int32))
    return outputs.reshape(length, query_rot.shape[1], query_rot.shape[2])

def stream_layer(values, doc_row, gain_attn, gain_mlp, m_qkv, m_out, m_in, m_down):
    length, model_width = values.shape
    head_count = model_width // HD
    normed = low(layer_norm(values, gain_attn))
    joined = low_back(matmul(normed, m_qkv))
    cosine, sine_table = rope_tables(jnp.arange(length, dtype=jnp.float32))
    query_proj = joined[:, :model_width].reshape(length, head_count, HD)
    key_proj = joined[:, model_width:2 * model_width].reshape(length, head_count, HD)
    value_proj = joined[:, 2 * model_width:].reshape(length, head_count, HD)
    query_rot = low(rotate(query_proj, cosine, sine_table))
    key_rot = low(rotate(key_proj, cosine, sine_table))
    value_rot = low(value_proj)
    attended = attend(query_rot, key_rot, value_rot, doc_row).reshape(length, model_width)
    attended = low(low_back(attended))
    branch = low_back(matmul(attended, m_out))
    hidden = values + branch
    normed_mlp = low(layer_norm(hidden, gain_mlp))
    expanded = low_back(matmul(normed_mlp, m_in))
    mixed_low = low(gated_gelu(expanded))
    return hidden + matmul(mixed_low, m_down.T)

def reference(tokens, doc_ids, norm_attn, norm_mlp, w_qkv, w_out, w_in, w_down, cotangent):

    def forward(values, gain_attn, gain_mlp, m_qkv, m_out, m_in, m_down):

        def step_fn(carry, pieces):
            return (carry, stream_layer(pieces[0], pieces[1], gain_attn, gain_mlp, m_qkv, m_out, m_in, m_down))
        unused, outputs = lax.scan(step_fn, jnp.zeros((), jnp.float32), (values, doc_ids))
        return outputs
    layer_out, pullback = jax.vjp(forward, tokens.astype(jnp.float32), norm_attn.astype(jnp.float32), norm_mlp.astype(jnp.float32), w_qkv.astype(jnp.float32), w_out.astype(jnp.float32), w_in.astype(jnp.float32), w_down.astype(jnp.float32))
    grads = pullback(cotangent.astype(jnp.float32))
    return (layer_out.astype(jnp.bfloat16), grads[0], grads[1], grads[2], grads[3], grads[4], grads[5], grads[6])
```

```python
import functools

import jax
import jax.numpy as jnp
from jax import lax
from jax.experimental import pallas as pl
from jax.experimental.pallas import tpu as pltpu
from jax.sharding import Mesh, PartitionSpec as P

HD = 64
HALF = 64
LANES = 128
NORM_EPSILON = 1e-05
ROPE_BASE = 10000.0
CHIPS = ("dp", "outer", "inner")
F32 = jnp.float32
BF16 = jnp.bfloat16


def contract_cols(left, right):
    return lax.dot_general(left, right, (((1,), (1,)), ((), ())), preferred_element_type=F32)


def contract_rows(left, right):
    return lax.dot_general(left, right, (((0,), (0,)), ((), ())), preferred_element_type=F32)


def matmul(left, right):
    return jnp.dot(left, right, preferred_element_type=F32)


def swap(value):
    return lax.ppermute(value, "core", [(0, 1), (1, 0)])


def ordered(mine, other, axis):
    first = lax.axis_index("core") == 0
    return jnp.concatenate(
        [jnp.where(first, mine, other), jnp.where(first, other, mine)], axis=axis
    )


def normalise(values):
    centred = values - jnp.mean(values, -1, keepdims=True)
    scale = lax.rsqrt(jnp.mean(centred * centred, -1, keepdims=True) + NORM_EPSILON)
    return centred * scale, scale


def norm_back(unit, scale, gain, incoming):
    grad = incoming * gain
    return scale * (
        grad
        - jnp.mean(grad, -1, keepdims=True)
        - unit * jnp.mean(grad * unit, -1, keepdims=True)
    )


def turned(values):
    width = values.shape[-1]
    lane = lax.broadcasted_iota(jnp.int32, values.shape, values.ndim - 1)
    ahead = pltpu.roll(values, width - HD // 2, values.ndim - 1)
    behind = pltpu.roll(values, HD // 2, values.ndim - 1)
    return jnp.where(lane % HD < HD // 2, ahead, behind)


def project_kernel(rotated_tiles, normed_ref, weight_ref, cos_ref, sin_ref, out_ref):
    values = matmul(normed_ref[...], weight_ref[...])
    rotated = values * cos_ref[...] + turned(values) * sin_ref[...]
    keep = pl.program_id(0) >= rotated_tiles
    out_ref[...] = jnp.where(keep, values, rotated).astype(BF16)


def project(normed, weight, cosine, sine, columns):
    rows, depth = normed.shape
    tile = cosine.shape[1]
    return pl.pallas_call(
        functools.partial(project_kernel, 2 * columns // 3 // tile),
        grid=(columns // tile,),
        in_specs=[
            pl.BlockSpec((rows, depth), lambda j: (0, 0)),
            pl.BlockSpec((depth, tile), lambda j: (0, j)),
            pl.BlockSpec((rows, tile), lambda j: (0, 0)),
            pl.BlockSpec((rows, tile), lambda j: (0, 0)),
        ],
        out_specs=pl.BlockSpec((rows, tile), lambda j: (0, j)),
        out_shape=jax.ShapeDtypeStruct((rows, columns), BF16),
        compiler_params=pltpu.CompilerParams(vmem_limit_bytes=24 * 2**20),
        cost_estimate=pl.CostEstimate(
            flops=2 * rows * depth * columns,
            bytes_accessed=2 * (rows * depth + depth * columns + rows * columns),
            transcendentals=0,
        ),
    )(normed, weight, cosine, sine)


def head_masks():
    lane = lax.broadcasted_iota(jnp.int32, (1, LANES), 1)
    return [(lane // HD == head).astype(F32).astype(BF16) for head in range(LANES // HD)]


def block_mask(query_ids, key_ids):
    rows, width = query_ids.shape[0], key_ids.shape[1]
    offset = lax.broadcasted_iota(jnp.int32, (rows, width), 1) - lax.broadcasted_iota(
        jnp.int32, (rows, width), 0
    )
    return (offset >= 0) & (offset <= 2 * HALF) & (query_ids == key_ids)


def block_probs(query, keys, allowed):
    scores = jnp.where(allowed, contract_cols(query, keys) * HD**-0.5, -1e30)
    grown = jnp.exp(scores - jnp.max(scores, -1, keepdims=True))
    return grown / jnp.sum(grown, -1, keepdims=True)


def attend_kernel(block, q_ref, k_ref, v_ref, kl_ref, vl_ref, kh_ref, vh_ref, qid_ref, kid_ref, out_ref):
    keys = jnp.concatenate([kl_ref[0], k_ref[0], kh_ref[0]], 0)
    values = jnp.concatenate([vl_ref[0], v_ref[0], vh_ref[0]], 0)
    masks = head_masks()
    for start in range(0, q_ref.shape[1], block):
        span = slice(start, start + block + 2 * HALF)
        allowed = block_mask(qid_ref[0, start : start + block], kid_ref[0, :, span])
        query = q_ref[0, start : start + block]
        total = None
        for mask in masks:
            probs = block_probs(query * mask, keys[span], allowed)
            part = matmul(probs.astype(BF16), values[span]) * mask.astype(F32)
            total = part if total is None else total + part
        out_ref[0, start : start + block] = total.astype(BF16)


def attend_back_kernel(
    block, q_ref, k_ref, v_ref, kl_ref, vl_ref, kh_ref, vh_ref, qid_ref, kid_ref,
    grad_ref, cos_ref, sin_ref, dq_ref, mid_ref, low_ref, high_ref,
):
    keys = jnp.concatenate([kl_ref[0], k_ref[0], kh_ref[0]], 0)
    values = jnp.concatenate([vl_ref[0], v_ref[0], vh_ref[0]], 0)
    masks = head_masks()
    length = q_ref.shape[1]
    window = jnp.zeros((length + 2 * HALF, LANES), F32)
    grad_keys, grad_values = window, window
    for start in range(0, length, block):
        span = slice(start, start + block + 2 * HALF)
        allowed = block_mask(qid_ref[0, start : start + block], kid_ref[0, :, span])
        query_all = q_ref[0, start : start + block]
        grad_all = grad_ref[0, start : start + block]
        grad_query, part_keys, part_values = 0.0, 0.0, 0.0
        for mask in masks:
            query, grad = query_all * mask, grad_all * mask
            probs = block_probs(query, keys[span], allowed)
            grad_probs = contract_cols(grad, values[span])
            delta = jnp.sum(probs * grad_probs, -1, keepdims=True)
            grad_scores = (probs * (grad_probs - delta)).astype(BF16)
            grad_query += matmul(grad_scores, keys[span]) * mask.astype(F32)
            part_keys += contract_rows(grad_scores, query)
            part_values += contract_rows(probs.astype(BF16), grad)
        grad_query = grad_query * HD**-0.5
        rows = slice(start, start + block)
        dq_ref[0, rows] = (
            grad_query * cos_ref[rows] - turned(grad_query) * sin_ref[rows]
        ).astype(BF16)
        before, after = start, length - start - block

        def placed(part):
            pieces = [part]
            if before:
                pieces.insert(0, jnp.zeros((before, LANES), F32))
            if after:
                pieces.append(jnp.zeros((after, LANES), F32))
            return jnp.concatenate(pieces, 0)

        grad_keys += placed(part_keys)
        grad_values += placed(part_values)
    for index, total in enumerate((grad_keys * HD**-0.5, grad_values)):
        low_ref[0, index] = total[:HALF].astype(BF16)
        mid_ref[0, index] = total[HALF : HALF + length]
        high_ref[0, index] = total[HALF + length :].astype(BF16)


def attention_specs(length, groups):
    def at(rows, shift):
        return pl.BlockSpec((1, rows, LANES), lambda s, h: (s, 0, h + shift))

    return [
        at(length, 0),
        at(length, groups),
        at(length, 2 * groups),
        at(HALF, 0),
        at(HALF, groups),
        at(HALF, 0),
        at(HALF, groups),
        pl.BlockSpec((1, length, 1), lambda s, h: (s, 0, 0)),
        pl.BlockSpec((1, 1, length + 2 * HALF), lambda s, h: (s, 0, 0)),
    ]


def attend(block, joined, low, high, query_ids, key_ids):
    streams, length, columns = joined.shape
    groups = columns // 3 // LANES
    work = streams * groups * 2 * length * (block + 2 * HALF)
    return pl.pallas_call(
        functools.partial(attend_kernel, block),
        grid=(streams, groups),
        in_specs=attention_specs(length, groups),
        out_specs=pl.BlockSpec((1, length, LANES), lambda s, h: (s, 0, h)),
        out_shape=jax.ShapeDtypeStruct((streams, length, columns // 3), BF16),
        compiler_params=pltpu.CompilerParams(vmem_limit_bytes=24 * 2**20),
        cost_estimate=pl.CostEstimate(
            flops=4 * work * LANES, bytes_accessed=4 * joined.size, transcendentals=work
        ),
    )(joined, joined, joined, low, low, high, high, query_ids, key_ids)


def attend_back(block, joined, low, high, query_ids, key_ids, grad, cosine, sine):
    streams, length, columns = joined.shape
    groups = columns // 3 // LANES
    work = streams * groups * 2 * length * (block + 2 * HALF)

    def pair(rows):
        return pl.BlockSpec((1, 2, rows, LANES), lambda s, h: (s, 0, 0, h))

    def shape(rows, kind):
        return jax.ShapeDtypeStruct((streams, 2, rows, columns // 3), kind)

    return pl.pallas_call(
        functools.partial(attend_back_kernel, block),
        grid=(streams, groups),
        in_specs=attention_specs(length, groups)
        + [pl.BlockSpec((1, length, LANES), lambda s, h: (s, 0, h))]
        + [pl.BlockSpec((length, LANES), lambda s, h: (0, 0))] * 2,
        out_specs=[
            pl.BlockSpec((1, length, LANES), lambda s, h: (s, 0, h)),
            pair(length),
            pair(HALF),
            pair(HALF),
        ],
        out_shape=[
            jax.ShapeDtypeStruct((streams, length, columns // 3), BF16),
            shape(length, F32),
            shape(HALF, BF16),
            shape(HALF, BF16),
        ],
        compiler_params=pltpu.CompilerParams(vmem_limit_bytes=24 * 2**20),
        cost_estimate=pl.CostEstimate(
            flops=10 * work * LANES, bytes_accessed=8 * joined.size, transcendentals=work
        ),
    )(joined, joined, joined, low, low, high, high, query_ids, key_ids, grad, cosine, sine)


def join_kernel(dq_ref, mid_ref, low_ref, high_ref, cos_ref, sin_ref, out_ref):
    length, width = dq_ref.shape[1:]
    out_ref[0, :, :width] = dq_ref[0]
    cosine, sine = cos_ref[...], sin_ref[...]
    for index in range(2):
        for start in range(0, width, LANES):
            lanes = slice(start, start + LANES)
            total = mid_ref[0, index, :, lanes]
            total = total + jnp.concatenate(
                [
                    low_ref[0, index, :, lanes].astype(F32),
                    jnp.zeros((length - 2 * HALF, LANES), F32),
                    high_ref[0, index, :, lanes].astype(F32),
                ],
                0,
            )
            if index == 0:
                total = total * cosine - turned(total) * sine
            to = (1 + index) * width + start
            out_ref[0, :, to : to + LANES] = total.astype(BF16)


def join_grads(grad_query, mid, from_lower, from_upper, cosine, sine):
    streams, length, width = grad_query.shape
    return pl.pallas_call(
        join_kernel,
        grid=(streams,),
        in_specs=[
            pl.BlockSpec((1, length, width), lambda s: (s, 0, 0)),
            pl.BlockSpec((1, 2, length, width), lambda s: (s, 0, 0, 0)),
            pl.BlockSpec((1, 2, HALF, width), lambda s: (s, 0, 0, 0)),
            pl.BlockSpec((1, 2, HALF, width), lambda s: (s, 0, 0, 0)),
            pl.BlockSpec((length, LANES), lambda s: (0, 0)),
            pl.BlockSpec((length, LANES), lambda s: (0, 0)),
        ],
        out_specs=pl.BlockSpec((1, length, 3 * width), lambda s: (s, 0, 0)),
        out_shape=jax.ShapeDtypeStruct((streams, length, 3 * width), BF16),
        compiler_params=pltpu.CompilerParams(vmem_limit_bytes=24 * 2**20),
        cost_estimate=pl.CostEstimate(
            flops=8 * mid.size, bytes_accessed=8 * mid.size, transcendentals=0
        ),
    )(grad_query, mid, from_lower, from_upper, cosine, sine)


def chunk_kernel(pairs, picks_ref, *refs):
    lefts, rights, rest = refs[:pairs], refs[pairs : 2 * pairs], refs[2 * pairs :]
    adds, out_ref = rest[:-1], rest[-1]
    start = 0
    for left, right in zip(lefts, rights):
        columns = slice(start, start + right.shape[1])
        total = matmul(left[0, 0, 0], right[...])
        for add in adds:
            total = total + add[0, :, columns].astype(F32)
        out_ref[0, :, columns] = total.astype(BF16)
        start = columns.stop


def grad_chunks(lefts, rights, picks, adds):
    rows, depth = lefts[0].shape[3:]
    columns = sum(right.shape[1] for right in rights)
    fields = 3 + len(adds)
    table = [
        jnp.asarray(entry, jnp.int32)
        for index, pick in enumerate(picks)
        for entry in list(pick) + [where[index] for _, where in adds]
    ]
    count = len(picks)

    def left_at(i, table):
        return (table[i * fields], table[i * fields + 1], table[i * fields + 2], 0, 0)

    def add_at(position):
        return lambda i, table: (table[i * fields + 3 + position], 0, 0)

    return pl.pallas_call(
        functools.partial(chunk_kernel, len(lefts)),
        grid_spec=pltpu.PrefetchScalarGridSpec(
            num_scalar_prefetch=1,
            grid=(count,),
            in_specs=[pl.BlockSpec((1, 1, 1, rows, depth), left_at) for _ in lefts]
            + [pl.BlockSpec(right.shape, lambda i, table: (0, 0)) for right in rights]
            + [pl.BlockSpec((1, rows, columns), add_at(n)) for n in range(len(adds))],
            out_specs=pl.BlockSpec((1, rows, columns), lambda i, table: (i, 0, 0)),
        ),
        out_shape=jax.ShapeDtypeStruct((count, rows, columns), BF16),
        compiler_params=pltpu.CompilerParams(vmem_limit_bytes=40 * 2**20),
        cost_estimate=pl.CostEstimate(
            flops=2 * count * rows * depth * columns,
            bytes_accessed=2 * (depth * columns + (1 + len(adds)) * count * rows * columns),
            transcendentals=0,
        ),
    )(jnp.stack(table), *lefts, *rights, *[array for array, _ in adds])


def ring(axis, chunk):
    count, me = lax.axis_size(axis), lax.axis_index(axis)
    arrived = None
    for step in range(1, count):
        arrived = lax.ppermute(
            chunk((me + count - step) % count, arrived),
            axis,
            [(i, (i + 1) % count) for i in range(count)],
        )
    return arrived


def with_adds(*adds):
    return [add for add in adds if add[0] is not None]


def scatter_grads(lefts, rights):
    inner, outer, dp = (lax.axis_size(name) for name in ("inner", "outer", "dp"))
    x, z, y = (lax.axis_index(name) for name in ("inner", "outer", "dp"))
    chunks = functools.partial(grad_chunks, lefts, rights)
    all_x, all_y = list(range(inner)), list(range(dp))
    a_one = ring(
        "inner",
        lambda t, got: chunks([(t, i, 0) for i in all_y], with_adds((got, all_y))),
    )
    b_one = ring(
        "dp",
        lambda t, got: chunks([(i, t, 1) for i in all_x], with_adds((got, all_x))),
    )
    a_two = ring(
        "dp", lambda t, got: chunks([(x, t, 0)], with_adds((a_one, [t]), (got, [0])))
    )
    b_two = ring(
        "inner", lambda t, got: chunks([(t, y, 1)], with_adds((b_one, [t]), (got, [0])))
    )
    mine = [
        chunks([(x, y, 0)], with_adds((a_one, [y]), (a_two, [0]))),
        chunks([(x, y, 1)], with_adds((b_one, [x]), (b_two, [0]))),
    ]
    mine = [part.reshape(outer, -1, part.shape[-1]) for part in mine]

    def part(target):
        return jnp.stack(
            [lax.dynamic_index_in_dim(half, target, 0, keepdims=False) for half in mine]
        ).astype(F32)

    up = down = jnp.zeros((), F32)
    for step in range(1, outer):
        up = lax.ppermute(
            (part(jnp.clip(z + outer - step, 0, outer - 1)) + up).astype(BF16),
            "outer",
            [(i, i + 1) for i in range(step)],
        ).astype(F32)
        down = lax.ppermute(
            (part(jnp.clip(z - outer + step, 0, outer - 1)) + down).astype(BF16),
            "outer",
            [(outer - 1 - i, outer - 2 - i) for i in range(step)],
        ).astype(F32)
    return part(z) + up + down


def both_halves(total):
    core = lax.axis_index("core")
    mine = lax.dynamic_index_in_dim(total, core, 0, keepdims=False)
    other = swap(lax.dynamic_index_in_dim(total, 1 - core, 0, keepdims=False))
    return (
        jnp.where(core == 0, mine, other),
        jnp.where(core == 0, other, mine),
    )


def shards(tokens, doc_ids, norm_attn, norm_mlp, w_qkv, w_out, w_in, w_down, cotangent):
    streams, block, width = tokens.shape
    shard_rows = w_qkv.shape[0]
    inner, outer, dp = (lax.axis_size(name) for name in ("inner", "outer", "dp"))
    core = lax.axis_index("core")
    length = 2 * block
    rows = streams * length
    side = width // 2
    units = w_down.shape[1] // 2
    padded = -(-units // LANES) * LANES

    def halves(weight, parts, pad):
        size = weight.shape[1] // (2 * parts)
        cut = [weight[:, i * size : (i + 1) * size] for i in range(2 * parts)]
        if pad != size:
            cut = [jnp.pad(piece, ((0, 0), (0, pad - size))) for piece in cut]
        return cut[0::2], cut[1::2]

    def spread(pieces):
        low = jnp.concatenate([piece for one, _ in pieces for piece in one], 1)
        high = jnp.concatenate([piece for _, two in pieces for piece in two], 1)
        mine = jnp.where(core == 0, low, high)
        other = swap(jnp.where(core == 0, high, low))
        return lax.all_gather(ordered(mine, other, 0), CHIPS, axis=0, tiled=True)

    gains = jnp.pad(jnp.stack([norm_attn, norm_mlp], 1), ((0, 0), (0, LANES - 2)))
    first = spread([halves(w_qkv, 3, side), ([gains], [gains])])
    second = spread(
        [halves(w_out, 1, side), halves(w_in, 2, padded), halves(w_down, 1, padded)]
    )

    def both_blocks(value):
        return ordered(value, swap(value), 1).reshape(rows, width)

    tokens_low = both_blocks(tokens)
    grad_output = both_blocks(cotangent)

    gain_attn, gain_mlp = (first[:, 3 * side + i].astype(F32) for i in range(2))

    chip = lax.axis_index(("outer", "inner"))
    chips = outer * inner
    start = chip * length
    positions = (start + jnp.arange(length, dtype=jnp.int32)).astype(F32)
    frequency = ROPE_BASE ** (-(jnp.arange(HD // 2, dtype=F32) * 2.0 / HD))
    angles = positions[:, None] * frequency[None, :]
    cosine, sine = jnp.cos(angles), jnp.sin(angles)
    cosine = jnp.tile(cosine, (1, LANES // (HD // 2)))
    sine = jnp.tile(jnp.concatenate([-sine, sine], 1), (1, LANES // HD))
    wide_cosine, wide_sine = (jnp.tile(table, (streams, 2)) for table in (cosine, sine))

    values = tokens_low.astype(F32)
    unit_attn, scale_attn = normalise(values)
    normed_low = (unit_attn * gain_attn).astype(BF16)
    joined = project(normed_low, first, wide_cosine, wide_sine, 3 * side)
    joined = joined.reshape(streams, length, 3 * side)
    onward = [(i, i + 1) for i in range(chips - 1)]
    back = [(i + 1, i) for i in range(chips - 1)]
    low = lax.ppermute(joined[:, length - HALF :, side:], ("outer", "inner"), onward)
    high = lax.ppermute(joined[:, :HALF, side:], ("outer", "inner"), back)
    ids_padded = jnp.pad(doc_ids, ((0, 0), (HALF, HALF)), constant_values=-1)
    key_ids = lax.dynamic_slice_in_dim(ids_padded, start, length + 2 * HALF, 1)[:, None, :]
    query_ids = lax.dynamic_slice_in_dim(doc_ids, start, length, 1)[:, :, None]
    attended_half = attend(block, joined, low, high, query_ids, key_ids).reshape(rows, side)
    attended_low = ordered(attended_half, swap(attended_half), 1)
    out_half = second[:, :side]
    full_out = ordered(out_half, swap(out_half), 1)
    hidden = values + matmul(attended_low, full_out)
    unit_mlp, scale_mlp = normalise(hidden)
    normed_mlp_low = (unit_mlp * gain_mlp).astype(BF16)
    in_half = second[:, side : side + 2 * padded]
    down_half = second[:, side + 2 * padded :]
    expanded = matmul(normed_mlp_low, in_half)
    gate, up = expanded[:, :padded], expanded[:, padded:]
    below = 0.5 * (1.0 + lax.erf(gate * 0.5**0.5))
    active = gate * below
    mixed_low = (active * up).astype(BF16)

    grad_mixed = matmul(grad_output, down_half)
    density = jnp.exp(-0.5 * gate * gate) * (2.0 * jnp.pi) ** -0.5
    grad_expanded_low = jnp.concatenate(
        [
            (grad_mixed * up * (below + gate * density)).astype(BF16),
            (grad_mixed * active).astype(BF16),
        ],
        1,
    )

    def own_rows(value):
        value = value.reshape(streams, 2, block, width)
        mine = lax.dynamic_index_in_dim(value, core, 1, keepdims=False)
        other = lax.dynamic_index_in_dim(value, 1 - core, 1, keepdims=False)
        return mine, other

    def summed_rows(partial):
        mine, other = own_rows(partial)
        return mine + swap(other.astype(BF16)).astype(F32)

    output = (own_rows(hidden)[0] + summed_rows(contract_cols(mixed_low, down_half))).astype(BF16)

    def by_chunk(activations):
        cut = activations.reshape(rows, dp, outer, inner, 2, shard_rows)
        return cut.transpose(3, 1, 4, 2, 5, 0).reshape(inner, dp, 2, outer * shard_rows, rows)

    mlp_total = scatter_grads(
        [by_chunk(grad_output), by_chunk(normed_mlp_low)], [mixed_low, grad_expanded_low]
    )

    grad_normed_mlp = contract_cols(grad_expanded_low, in_half)
    grad_normed_mlp = grad_normed_mlp + swap(grad_normed_mlp.astype(BF16)).astype(F32)
    grad_hidden = grad_output.astype(F32) + norm_back(
        unit_mlp, scale_mlp, gain_mlp, grad_normed_mlp
    )
    grad_hidden_low = grad_hidden.astype(BF16)

    out_rows = lax.dynamic_slice_in_dim(full_out, core * side, side, 0)
    grad_attended = contract_cols(grad_hidden_low, out_rows).astype(BF16)
    grad_query, mid, to_lower, to_upper = attend_back(
        block, joined, low, high, query_ids, key_ids,
        grad_attended.reshape(streams, length, side), cosine, sine,
    )
    from_lower = lax.ppermute(to_upper, ("outer", "inner"), onward)
    from_upper = lax.ppermute(to_lower, ("outer", "inner"), back)
    grad_joined = join_grads(grad_query, mid, from_lower, from_upper, cosine, sine)
    grad_joined = grad_joined.reshape(rows, 3 * side)
    hidden_side = lax.dynamic_slice_in_dim(grad_hidden_low, core * side, side, 1)
    attn_total = scatter_grads(
        [by_chunk(normed_low), by_chunk(attended_low)], [grad_joined, hidden_side]
    )
    grad_normed = summed_rows(contract_cols(grad_joined, first[:, : 3 * side]))
    unit_mine, scale_mine = normalise(tokens.astype(F32))
    grad_tokens = own_rows(grad_hidden)[0] + norm_back(
        unit_mine, scale_mine, gain_attn, grad_normed
    )

    def interleaved(pair, start, parts, stride, size):
        cuts = []
        for i in range(parts):
            first_column = start + i * stride
            cuts += [half[:, first_column : first_column + size] for half in pair]
        return jnp.concatenate(cuts, 1)

    pair = both_halves(mlp_total)
    grad_down = interleaved(pair, 0, 1, padded, units)
    grad_in = interleaved(pair, padded, 2, padded, units)
    pair = both_halves(attn_total)
    grad_qkv = interleaved(pair, 0, 3, side, side)
    grad_out = interleaved(pair, 3 * side, 1, side, side)

    def gain_grad(weight, grad, gain):
        return jnp.sum(weight.astype(F32) * grad, -1) / gain.astype(F32)

    return (
        output,
        grad_tokens,
        gain_grad(w_qkv, grad_qkv, norm_attn),
        gain_grad(w_in, grad_in, norm_mlp),
        grad_qkv,
        grad_out,
        grad_in,
        grad_down,
    )


def solution(mesh):
    dp, seq = mesh.shape["dp"], mesh.shape["seq"]
    chips = seq // 2
    outer = 4 if chips % 4 == 0 else 1
    fine = Mesh(
        mesh.devices.reshape(dp, outer, chips // outer, 2), ("dp", "outer", "inner", "core")
    )
    line = ("outer", "inner", "core")
    every = ("dp",) + line
    token = P("dp", line, None)
    vector = P(every)
    matrix = P(every, None)
    return jax.shard_map(
        shards,
        mesh=fine,
        in_specs=(token, P("dp", None), vector, vector, matrix, matrix, matrix, matrix, token),
        out_specs=(token, token, vector, vector, matrix, matrix, matrix, matrix),
        check_vma=False,
    )
```

```python
import functools

import jax
import jax.numpy as jnp
from jax import lax
from jax.experimental import pallas as pl
from jax.experimental.pallas import tpu as pltpu
from jax.sharding import Mesh, PartitionSpec as P

HD = 64
HALF = 64
LANES = 128
NORM_EPSILON = 1e-05
ROPE_BASE = 10000.0
F32 = jnp.float32
BF16 = jnp.bfloat16
LIGHT = pl.CostEstimate(flops=1024, bytes_accessed=1024, transcendentals=0)


def contract_cols(left, right):
    return lax.dot_general(left, right, (((1,), (1,)), ((), ())), preferred_element_type=F32)


def contract_rows(left, right):
    return lax.dot_general(left, right, (((0,), (0,)), ((), ())), preferred_element_type=F32)


def matmul(left, right):
    return jnp.dot(left, right, preferred_element_type=F32)


def swap(value):
    return lax.ppermute(value, "core", [(0, 1), (1, 0)])


def ordered(mine, other, axis):
    first = lax.axis_index("core") == 0
    return jnp.concatenate(
        [jnp.where(first, mine, other), jnp.where(first, other, mine)], axis=axis
    )


def normalise(values):
    centred = values - jnp.mean(values, -1, keepdims=True)
    scale = lax.rsqrt(jnp.mean(centred * centred, -1, keepdims=True) + NORM_EPSILON)
    return centred * scale, scale


def norm_back(unit, scale, gain, incoming):
    grad = incoming * gain
    return scale * (
        grad
        - jnp.mean(grad, -1, keepdims=True)
        - unit * jnp.mean(grad * unit, -1, keepdims=True)
    )


def turned(values):
    width = values.shape[-1]
    lane = lax.broadcasted_iota(jnp.int32, values.shape, values.ndim - 1)
    ahead = pltpu.roll(values, width - HD // 2, values.ndim - 1)
    behind = pltpu.roll(values, HD // 2, values.ndim - 1)
    return jnp.where(lane % HD < HD // 2, ahead, behind)


def project_kernel(rotated_tiles, normed_ref, weight_ref, cos_ref, sin_ref, out_ref):
    values = matmul(normed_ref[...], weight_ref[...])
    rotated = values * cos_ref[...] + turned(values) * sin_ref[...]
    keep = pl.program_id(0) >= rotated_tiles
    out_ref[...] = jnp.where(keep, values, rotated).astype(BF16)


def project(normed, weight, cosine, sine, columns):
    rows, depth = normed.shape
    tile = cosine.shape[1]
    return pl.pallas_call(
        functools.partial(project_kernel, 2 * columns // 3 // tile),
        grid=(columns // tile,),
        in_specs=[
            pl.BlockSpec((rows, depth), lambda j: (0, 0)),
            pl.BlockSpec((depth, tile), lambda j: (0, j)),
            pl.BlockSpec((rows, tile), lambda j: (0, 0)),
            pl.BlockSpec((rows, tile), lambda j: (0, 0)),
        ],
        out_specs=pl.BlockSpec((rows, tile), lambda j: (0, j)),
        out_shape=jax.ShapeDtypeStruct((rows, columns), BF16),
        compiler_params=pltpu.CompilerParams(vmem_limit_bytes=24 * 2**20),
        cost_estimate=LIGHT,
    )(normed, weight, cosine, sine)


def head_masks():
    lane = lax.broadcasted_iota(jnp.int32, (1, LANES), 1)
    return [(lane // HD == head).astype(F32).astype(BF16) for head in range(LANES // HD)]


def block_mask(query_ids, key_ids):
    rows, width = query_ids.shape[0], key_ids.shape[1]
    offset = lax.broadcasted_iota(jnp.int32, (rows, width), 1) - lax.broadcasted_iota(
        jnp.int32, (rows, width), 0
    )
    return (offset >= 0) & (offset <= 2 * HALF) & (query_ids == key_ids)


def block_probs(query, keys, allowed):
    scores = jnp.where(allowed, contract_cols(query, keys) * HD**-0.5, -1e30)
    grown = jnp.exp(scores - jnp.max(scores, -1, keepdims=True))
    return grown / jnp.sum(grown, -1, keepdims=True)


def attend_kernel(block, q_ref, k_ref, v_ref, kl_ref, vl_ref, kh_ref, vh_ref, qid_ref, kid_ref, out_ref):
    keys = jnp.concatenate([kl_ref[0], k_ref[0], kh_ref[0]], 0)
    values = jnp.concatenate([vl_ref[0], v_ref[0], vh_ref[0]], 0)
    masks = head_masks()
    for start in range(0, q_ref.shape[1], block):
        span = slice(start, start + block + 2 * HALF)
        allowed = block_mask(qid_ref[0, start : start + block], kid_ref[0, :, span])
        query = q_ref[0, start : start + block]
        total = None
        for mask in masks:
            probs = block_probs(query * mask, keys[span], allowed)
            part = matmul(probs.astype(BF16), values[span]) * mask.astype(F32)
            total = part if total is None else total + part
        out_ref[0, start : start + block] = total.astype(BF16)


def attend_back_kernel(
    block, q_ref, k_ref, v_ref, kl_ref, vl_ref, kh_ref, vh_ref, qid_ref, kid_ref,
    grad_ref, cos_ref, sin_ref, dq_ref, mid_ref, low_ref, high_ref,
):
    keys = jnp.concatenate([kl_ref[0], k_ref[0], kh_ref[0]], 0)
    values = jnp.concatenate([vl_ref[0], v_ref[0], vh_ref[0]], 0)
    masks = head_masks()
    length = q_ref.shape[1]
    window = jnp.zeros((length + 2 * HALF, LANES), F32)
    grad_keys, grad_values = window, window
    for start in range(0, length, block):
        span = slice(start, start + block + 2 * HALF)
        allowed = block_mask(qid_ref[0, start : start + block], kid_ref[0, :, span])
        query_all = q_ref[0, start : start + block]
        grad_all = grad_ref[0, start : start + block]
        grad_query, part_keys, part_values = 0.0, 0.0, 0.0
        for mask in masks:
            query, grad = query_all * mask, grad_all * mask
            probs = block_probs(query, keys[span], allowed)
            grad_probs = contract_cols(grad, values[span])
            delta = jnp.sum(probs * grad_probs, -1, keepdims=True)
            grad_scores = (probs * (grad_probs - delta)).astype(BF16)
            grad_query += matmul(grad_scores, keys[span]) * mask.astype(F32)
            part_keys += contract_rows(grad_scores, query)
            part_values += contract_rows(probs.astype(BF16), grad)
        grad_query = grad_query * HD**-0.5
        rows = slice(start, start + block)
        dq_ref[0, rows] = (
            grad_query * cos_ref[rows] - turned(grad_query) * sin_ref[rows]
        ).astype(BF16)
        before, after = start, length - start - block

        def placed(part):
            pieces = [part]
            if before:
                pieces.insert(0, jnp.zeros((before, LANES), F32))
            if after:
                pieces.append(jnp.zeros((after, LANES), F32))
            return jnp.concatenate(pieces, 0)

        grad_keys += placed(part_keys)
        grad_values += placed(part_values)
    for index, total in enumerate((grad_keys * HD**-0.5, grad_values)):
        low_ref[0, index] = total[:HALF].astype(BF16)
        mid_ref[0, index] = total[HALF : HALF + length]
        high_ref[0, index] = total[HALF + length :].astype(BF16)


def attention_specs(length, groups):
    def at(rows, shift):
        return pl.BlockSpec((1, rows, LANES), lambda s, h: (s, 0, h + shift))

    return [
        at(length, 0),
        at(length, groups),
        at(length, 2 * groups),
        at(HALF, 0),
        at(HALF, groups),
        at(HALF, 0),
        at(HALF, groups),
        pl.BlockSpec((1, length, 1), lambda s, h: (s, 0, 0)),
        pl.BlockSpec((1, 1, length + 2 * HALF), lambda s, h: (s, 0, 0)),
    ]


def attend(block, joined, low, high, query_ids, key_ids):
    streams, length, columns = joined.shape
    groups = columns // 3 // LANES
    return pl.pallas_call(
        functools.partial(attend_kernel, block),
        grid=(streams, groups),
        in_specs=attention_specs(length, groups),
        out_specs=pl.BlockSpec((1, length, LANES), lambda s, h: (s, 0, h)),
        out_shape=jax.ShapeDtypeStruct((streams, length, columns // 3), BF16),
        compiler_params=pltpu.CompilerParams(vmem_limit_bytes=24 * 2**20),
        cost_estimate=LIGHT,
    )(joined, joined, joined, low, low, high, high, query_ids, key_ids)


def attend_back(block, joined, low, high, query_ids, key_ids, grad, cosine, sine):
    streams, length, columns = joined.shape
    groups = columns // 3 // LANES

    def pair(rows):
        return pl.BlockSpec((1, 2, rows, LANES), lambda s, h: (s, 0, 0, h))

    def shape(rows, kind):
        return jax.ShapeDtypeStruct((streams, 2, rows, columns // 3), kind)

    return pl.pallas_call(
        functools.partial(attend_back_kernel, block),
        grid=(streams, groups),
        in_specs=attention_specs(length, groups)
        + [pl.BlockSpec((1, length, LANES), lambda s, h: (s, 0, h))]
        + [pl.BlockSpec((length, LANES), lambda s, h: (0, 0))] * 2,
        out_specs=[
            pl.BlockSpec((1, length, LANES), lambda s, h: (s, 0, h)),
            pair(length),
            pair(HALF),
            pair(HALF),
        ],
        out_shape=[
            jax.ShapeDtypeStruct((streams, length, columns // 3), BF16),
            shape(length, F32),
            shape(HALF, BF16),
            shape(HALF, BF16),
        ],
        compiler_params=pltpu.CompilerParams(vmem_limit_bytes=24 * 2**20),
        cost_estimate=LIGHT,
    )(joined, joined, joined, low, low, high, high, query_ids, key_ids, grad, cosine, sine)


def join_kernel(dq_ref, mid_ref, low_ref, high_ref, cos_ref, sin_ref, out_ref):
    length, width = dq_ref.shape[1:]
    out_ref[0, :, :width] = dq_ref[0]
    cosine, sine = cos_ref[...], sin_ref[...]
    for index in range(2):
        for start in range(0, width, LANES):
            lanes = slice(start, start + LANES)
            total = mid_ref[0, index, :, lanes]
            total = total + jnp.concatenate(
                [
                    low_ref[0, index, :, lanes].astype(F32),
                    jnp.zeros((length - 2 * HALF, LANES), F32),
                    high_ref[0, index, :, lanes].astype(F32),
                ],
                0,
            )
            if index == 0:
                total = total * cosine - turned(total) * sine
            to = (1 + index) * width + start
            out_ref[0, :, to : to + LANES] = total.astype(BF16)


def join_grads(grad_query, mid, from_lower, from_upper, cosine, sine):
    streams, length, width = grad_query.shape
    return pl.pallas_call(
        join_kernel,
        grid=(streams,),
        in_specs=[
            pl.BlockSpec((1, length, width), lambda s: (s, 0, 0)),
            pl.BlockSpec((1, 2, length, width), lambda s: (s, 0, 0, 0)),
            pl.BlockSpec((1, 2, HALF, width), lambda s: (s, 0, 0, 0)),
            pl.BlockSpec((1, 2, HALF, width), lambda s: (s, 0, 0, 0)),
            pl.BlockSpec((length, LANES), lambda s: (0, 0)),
            pl.BlockSpec((length, LANES), lambda s: (0, 0)),
        ],
        out_specs=pl.BlockSpec((1, length, 3 * width), lambda s: (s, 0, 0)),
        out_shape=jax.ShapeDtypeStruct((streams, length, 3 * width), BF16),
        compiler_params=pltpu.CompilerParams(vmem_limit_bytes=24 * 2**20),
        cost_estimate=LIGHT,
    )(grad_query, mid, from_lower, from_upper, cosine, sine)


def arrival_order(width, shard_rows):
    inner, outer, dp = (lax.axis_size(name) for name in ("inner", "outer", "dp"))
    x, z, y = (lax.axis_index(name) for name in ("inner", "outer", "dp"))
    place = jnp.arange(width, dtype=jnp.int32)
    part, rest = place // (width // 2), place % (width // 2)
    chunk, rest = rest // (outer * shard_rows), rest % (outer * shard_rows)
    along_x = jnp.where(part == 0, chunk // dp, chunk % inner)
    along_y = jnp.where(part == 0, chunk % dp, chunk // inner)
    along_z, row = rest // shard_rows, rest % shard_rows
    at_x = (x - along_x + inner) % inner
    at_y = (y - along_y + dp) % dp
    at_z = (z - along_z + outer) % outer
    source = (((at_y * outer + at_z) * inner + at_x) * 2 + part) * shard_rows + row
    return (place[:, None] == source[None, :]).astype(BF16)


def forward(axis, distance=1):
    count = lax.axis_size(axis)
    return [(i, (i + distance) % count) for i in range(count)]


def ring_gather(axis, piece):
    pieces = [piece]
    for _ in range(1, lax.axis_size(axis)):
        pieces.append(lax.ppermute(pieces[-1], axis, forward(axis)))
    return jnp.concatenate(pieces, 0)


def direct_gather(pair):
    arrived = [pair] + [
        lax.ppermute(pair, "outer", forward("outer", distance))
        for distance in range(1, lax.axis_size("outer"))
    ]
    return [jnp.concatenate([piece[part] for piece in arrived], 0) for part in range(2)]


def gather_rest(parts):
    one = ring_gather("inner", ring_gather("dp", parts[0]))
    two = ring_gather("dp", ring_gather("inner", parts[1]))
    return jnp.concatenate([one, two], 0)


def chunk_kernel(pairs, *refs):
    lefts, rights, rest = refs[:pairs], refs[pairs : 2 * pairs], refs[2 * pairs :]
    adds, out_ref = rest[:-1], rest[-1]
    start = 0
    for left, right in zip(lefts, rights):
        columns = slice(start, start + right.shape[1])
        total = contract_rows(left[...], right[...])
        for add in adds:
            total = total + add[:, columns].astype(F32)
        out_ref[:, columns] = total.astype(BF16)
        start = columns.stop


def grad_chunk(lefts, rights, start, rows, adds):
    depth = lefts[0].shape[0]
    columns = sum(right.shape[1] for right in rights)
    index = start // rows
    if rows % LANES:
        lefts = [left[:, start : start + rows] for left in lefts]
        index = 0

    def whole(shape):
        return pl.BlockSpec(shape, lambda i: (0, 0))

    def block_at(shape, block):
        return pl.BlockSpec(shape, lambda i: block)

    return pl.pallas_call(
        functools.partial(chunk_kernel, len(lefts)),
        grid=(1,),
        in_specs=[block_at((depth, rows), (0, index)) for _ in lefts]
        + [whole(right.shape) for right in rights]
        + [block_at((rows, columns), (at, 0)) for _, at in adds],
        out_specs=whole((rows, columns)),
        out_shape=jax.ShapeDtypeStruct((rows, columns), BF16),
        compiler_params=pltpu.CompilerParams(vmem_limit_bytes=40 * 2**20),
        cost_estimate=LIGHT,
    )(*lefts, *rights, *[array for array, _ in adds])


def ring(axis, chunk):
    arrived = None
    for step in range(1, lax.axis_size(axis)):
        arrived = lax.ppermute(chunk(step, arrived), axis, forward(axis))
    return arrived


def with_adds(*adds):
    return [add for add in adds if add[0] is not None]


def scatter_grads(lefts, rights, shard_rows):
    inner, outer, dp = (lax.axis_size(name) for name in ("inner", "outer", "dp"))
    rows = outer * shard_rows
    half = inner * dp * rows
    chunk = functools.partial(grad_chunk, lefts, rights)
    a_one = ring(
        "inner", lambda d, got: chunk(d * dp * rows, dp * rows, with_adds((got, 0)))
    )
    b_one = ring(
        "dp",
        lambda d, got: chunk(half + d * inner * rows, inner * rows, with_adds((got, 0))),
    )
    a_two = ring(
        "dp", lambda d, got: chunk(d * rows, rows, with_adds((a_one, d), (got, 0)))
    )
    b_two = ring(
        "inner", lambda d, got: chunk(half + d * rows, rows, with_adds((b_one, d), (got, 0)))
    )
    mine = [
        chunk(0, rows, with_adds((a_one, 0), (a_two, 0))),
        chunk(half, rows, with_adds((b_one, 0), (b_two, 0))),
    ]

    def part(distance):
        cut = slice(distance * shard_rows, (distance + 1) * shard_rows)
        return jnp.stack([piece[cut] for piece in mine])

    arrived = [
        lax.ppermute(part(distance), "outer", forward("outer", outer - distance))
        for distance in range(1, outer)
    ]
    return sum([piece.astype(F32) for piece in arrived], part(0).astype(F32))


def both_halves(total):
    core = lax.axis_index("core")
    mine = lax.dynamic_index_in_dim(total, core, 0, keepdims=False)
    other = swap(lax.dynamic_index_in_dim(total, 1 - core, 0, keepdims=False))
    return (
        jnp.where(core == 0, mine, other),
        jnp.where(core == 0, other, mine),
    )


def shards(tokens, doc_ids, norm_attn, norm_mlp, w_qkv, w_out, w_in, w_down, cotangent):
    streams, block, width = tokens.shape
    shard_rows = w_qkv.shape[0]
    inner, outer, dp = (lax.axis_size(name) for name in ("inner", "outer", "dp"))
    core = lax.axis_index("core")
    length = 2 * block
    rows = streams * length
    side = width // 2
    units = w_down.shape[1] // 2
    padded = -(-units // LANES) * LANES

    def halves(weight, parts, pad):
        size = weight.shape[1] // (2 * parts)
        cut = [weight[:, i * size : (i + 1) * size] for i in range(2 * parts)]
        if pad != size:
            cut = [jnp.pad(piece, ((0, 0), (0, pad - size))) for piece in cut]
        return cut[0::2], cut[1::2]

    def paired(pieces):
        low = jnp.concatenate([piece for one, _ in pieces for piece in one], 1)
        high = jnp.concatenate([piece for _, two in pieces for piece in two], 1)
        mine = jnp.where(core == 0, low, high)
        other = swap(jnp.where(core == 0, high, low))
        return ordered(mine[None], other[None], 0)

    gains = jnp.pad(jnp.stack([norm_attn, norm_mlp], 1), ((0, 0), (0, LANES - 2)))
    one = direct_gather(paired([halves(w_qkv, 3, side), ([gains], [gains])]))
    pair_two = paired([halves(w_out, 1, side), halves(w_in, 2, padded)])
    pair_three = paired([halves(w_down, 1, padded)])
    pair_two, one = lax.optimization_barrier((pair_two, one))
    two = direct_gather(pair_two)
    first = gather_rest(one)
    pair_three, two, first = lax.optimization_barrier((pair_three, two, first))
    three = direct_gather(pair_three)
    second = gather_rest(two)
    three, second = lax.optimization_barrier((three, second))
    down_half = gather_rest(three)
    order = arrival_order(width, shard_rows)

    def in_order(value):
        return matmul(value, order).astype(BF16)

    def out_of_order(value):
        return contract_cols(value, order).astype(BF16)

    def both_blocks(value):
        return in_order(ordered(value, swap(value), 1).reshape(rows, width))

    tokens_low = both_blocks(tokens)
    grad_output = both_blocks(cotangent)

    gain_attn, gain_mlp = (first[:, 3 * side + i].astype(F32) for i in range(2))

    chip = lax.axis_index(("outer", "inner"))
    chips = outer * inner
    start = chip * length
    positions = (start + jnp.arange(length, dtype=jnp.int32)).astype(F32)
    frequency = ROPE_BASE ** (-(jnp.arange(HD // 2, dtype=F32) * 2.0 / HD))
    angles = positions[:, None] * frequency[None, :]
    cosine, sine = jnp.cos(angles), jnp.sin(angles)
    cosine = jnp.tile(cosine, (1, LANES // (HD // 2)))
    sine = jnp.tile(jnp.concatenate([-sine, sine], 1), (1, LANES // HD))
    wide_cosine, wide_sine = (jnp.tile(table, (streams, 2)) for table in (cosine, sine))

    values = tokens_low.astype(F32)
    unit_attn, scale_attn = normalise(values)
    normed_low = (unit_attn * gain_attn).astype(BF16)
    joined = project(normed_low, first, wide_cosine, wide_sine, 3 * side)
    joined = joined.reshape(streams, length, 3 * side)
    onward = [(i, i + 1) for i in range(chips - 1)]
    back = [(i + 1, i) for i in range(chips - 1)]
    low = lax.ppermute(joined[:, length - HALF :, side:], ("outer", "inner"), onward)
    high = lax.ppermute(joined[:, :HALF, side:], ("outer", "inner"), back)
    ids_padded = jnp.pad(doc_ids, ((0, 0), (HALF, HALF)), constant_values=-1)
    key_ids = lax.dynamic_slice_in_dim(ids_padded, start, length + 2 * HALF, 1)[:, None, :]
    query_ids = lax.dynamic_slice_in_dim(doc_ids, start, length, 1)[:, :, None]
    attended_half = attend(block, joined, low, high, query_ids, key_ids).reshape(rows, side)
    attended_low = ordered(attended_half, swap(attended_half), 1)
    out_half = second[:, :side]
    full_out = ordered(out_half, swap(out_half), 1)
    full_out = matmul(order, in_order(full_out)).astype(BF16)
    hidden = values + matmul(attended_low, full_out)
    unit_mlp, scale_mlp = normalise(hidden)
    normed_mlp_low = (unit_mlp * gain_mlp).astype(BF16)
    in_half = second[:, side:]
    expanded = matmul(normed_mlp_low, in_half)
    gate, up = expanded[:, :padded], expanded[:, padded:]
    below = 0.5 * (1.0 + lax.erf(gate * 0.5**0.5))
    active = gate * below
    mixed_low = (active * up).astype(BF16)

    grad_mixed = matmul(grad_output, down_half)
    density = jnp.exp(-0.5 * gate * gate) * (2.0 * jnp.pi) ** -0.5
    grad_expanded_low = jnp.concatenate(
        [
            (grad_mixed * up * (below + gate * density)).astype(BF16),
            (grad_mixed * active).astype(BF16),
        ],
        1,
    )

    def own_rows(value):
        value = value.reshape(streams, 2, block, width)
        mine = lax.dynamic_index_in_dim(value, core, 1, keepdims=False)
        other = lax.dynamic_index_in_dim(value, 1 - core, 1, keepdims=False)
        return mine, other

    def summed_rows(partial):
        mine, other = own_rows(partial)
        return mine + swap(other.astype(BF16)).astype(F32)

    output = own_rows(hidden)[0] + summed_rows(contract_cols(mixed_low, down_half))
    output = out_of_order(output.astype(BF16).reshape(-1, width)).reshape(tokens.shape)

    mlp_total = scatter_grads(
        [grad_output, normed_mlp_low], [mixed_low, grad_expanded_low], shard_rows
    )

    grad_normed_mlp = contract_cols(grad_expanded_low, in_half)
    grad_normed_mlp = grad_normed_mlp + swap(grad_normed_mlp.astype(BF16)).astype(F32)
    grad_hidden = grad_output.astype(F32) + norm_back(
        unit_mlp, scale_mlp, gain_mlp, grad_normed_mlp
    )
    grad_hidden_low = grad_hidden.astype(BF16)

    out_rows = lax.dynamic_slice_in_dim(full_out, core * side, side, 0)
    grad_attended = contract_cols(grad_hidden_low, out_rows).astype(BF16)
    grad_query, mid, to_lower, to_upper = attend_back(
        block, joined, low, high, query_ids, key_ids,
        grad_attended.reshape(streams, length, side), cosine, sine,
    )
    from_lower = lax.ppermute(to_upper, ("outer", "inner"), onward)
    from_upper = lax.ppermute(to_lower, ("outer", "inner"), back)
    grad_joined = join_grads(grad_query, mid, from_lower, from_upper, cosine, sine)
    grad_joined = grad_joined.reshape(rows, 3 * side)
    hidden_side = lax.dynamic_slice_in_dim(out_of_order(grad_hidden_low), core * side, side, 1)
    attn_total = scatter_grads(
        [normed_low, in_order(attended_low)], [grad_joined, hidden_side], shard_rows
    )
    grad_normed = summed_rows(contract_cols(grad_joined, first[:, : 3 * side]))
    unit_mine, scale_mine = normalise(own_rows(values)[0])
    grad_tokens = own_rows(grad_hidden)[0] + norm_back(
        unit_mine, scale_mine, gain_attn, grad_normed
    )
    grad_tokens = lax.dot_general(
        grad_tokens.reshape(-1, width),
        order.astype(F32),
        (((1,), (1,)), ((), ())),
        precision=lax.Precision.HIGHEST,
        preferred_element_type=F32,
    ).reshape(tokens.shape)

    def interleaved(pair, start, parts, stride, size):
        cuts = []
        for i in range(parts):
            first_column = start + i * stride
            cuts += [half[:, first_column : first_column + size] for half in pair]
        return jnp.concatenate(cuts, 1)

    pair = both_halves(mlp_total)
    grad_down = interleaved(pair, 0, 1, padded, units)
    grad_in = interleaved(pair, padded, 2, padded, units)
    pair = both_halves(attn_total)
    grad_qkv = interleaved(pair, 0, 3, side, side)
    grad_out = interleaved(pair, 3 * side, 1, side, side)

    def gain_grad(weight, grad, gain):
        return jnp.sum(weight.astype(F32) * grad, -1) / gain.astype(F32)

    return (
        output,
        grad_tokens,
        gain_grad(w_qkv, grad_qkv, norm_attn),
        gain_grad(w_in, grad_in, norm_mlp),
        grad_qkv,
        grad_out,
        grad_in,
        grad_down,
    )


def solution(mesh):
    dp, seq = mesh.shape["dp"], mesh.shape["seq"]
    chips = seq // 2
    outer = 4 if chips % 4 == 0 else 1
    fine = Mesh(
        mesh.devices.reshape(dp, outer, chips // outer, 2), ("dp", "outer", "inner", "core")
    )
    line = ("outer", "inner", "core")
    every = ("dp",) + line
    token = P("dp", line, None)
    vector = P(every)
    matrix = P(every, None)
    return jax.shard_map(
        shards,
        mesh=fine,
        in_specs=(token, P("dp", None), vector, vector, matrix, matrix, matrix, matrix, token),
        out_specs=(token, token, vector, vector, matrix, matrix, matrix, matrix),
        check_vma=False,
    )
```

```python
import functools

import jax
import jax.numpy as jnp
from jax import lax
from jax.experimental import pallas as pl
from jax.experimental.pallas import tpu as pltpu
from jax.sharding import Mesh, PartitionSpec as P

HD = 64
HALF = 64
LANES = 128
NORM_EPSILON = 1e-05
ROPE_BASE = 10000.0
F32 = jnp.float32
BF16 = jnp.bfloat16
LIGHT = pl.CostEstimate(flops=1024, bytes_accessed=1024, transcendentals=0)


def contract_cols(left, right):
    return lax.dot_general(left, right, (((1,), (1,)), ((), ())), preferred_element_type=F32)


def contract_rows(left, right):
    return lax.dot_general(left, right, (((0,), (0,)), ((), ())), preferred_element_type=F32)


def matmul(left, right):
    return jnp.dot(left, right, preferred_element_type=F32)


def tied(*values):
    return lax.optimization_barrier(values)


def swap(value):
    return lax.ppermute(value, "core", [(0, 1), (1, 0)])


def ordered(mine, other, axis):
    first = lax.axis_index("core") == 0
    return jnp.concatenate(
        [jnp.where(first, mine, other), jnp.where(first, other, mine)], axis=axis
    )


def normalise(values):
    centred = values - jnp.mean(values, -1, keepdims=True)
    scale = lax.rsqrt(jnp.mean(centred * centred, -1, keepdims=True) + NORM_EPSILON)
    return centred * scale, scale


def norm_back(unit, scale, gain, incoming):
    grad = incoming * gain
    return scale * (
        grad
        - jnp.mean(grad, -1, keepdims=True)
        - unit * jnp.mean(grad * unit, -1, keepdims=True)
    )


def turned(values):
    width = values.shape[-1]
    lane = lax.broadcasted_iota(jnp.int32, values.shape, values.ndim - 1)
    ahead = pltpu.roll(values, width - HD // 2, values.ndim - 1)
    behind = pltpu.roll(values, HD // 2, values.ndim - 1)
    return jnp.where(lane % HD < HD // 2, ahead, behind)


def project_kernel(rotated_tiles, normed_ref, weight_ref, cos_ref, sin_ref, out_ref):
    values = matmul(normed_ref[...], weight_ref[...])
    rotated = values * cos_ref[...] + turned(values) * sin_ref[...]
    keep = pl.program_id(0) >= rotated_tiles
    out_ref[...] = jnp.where(keep, values, rotated).astype(BF16)


def project(normed, weight, cosine, sine, columns):
    rows, depth = normed.shape
    tile = cosine.shape[1]
    return pl.pallas_call(
        functools.partial(project_kernel, 2 * columns // 3 // tile),
        grid=(columns // tile,),
        in_specs=[
            pl.BlockSpec((rows, depth), lambda j: (0, 0)),
            pl.BlockSpec((depth, tile), lambda j: (0, j)),
            pl.BlockSpec((rows, tile), lambda j: (0, 0)),
            pl.BlockSpec((rows, tile), lambda j: (0, 0)),
        ],
        out_specs=pl.BlockSpec((rows, tile), lambda j: (0, j)),
        out_shape=jax.ShapeDtypeStruct((rows, columns), BF16),
        compiler_params=pltpu.CompilerParams(vmem_limit_bytes=24 * 2**20),
        cost_estimate=LIGHT,
    )(normed, weight, cosine, sine)


def head_masks():
    lane = lax.broadcasted_iota(jnp.int32, (1, LANES), 1)
    return [(lane // HD == head).astype(F32).astype(BF16) for head in range(LANES // HD)]


def block_mask(query_ids, key_ids):
    rows, width = query_ids.shape[0], key_ids.shape[1]
    offset = lax.broadcasted_iota(jnp.int32, (rows, width), 1) - lax.broadcasted_iota(
        jnp.int32, (rows, width), 0
    )
    return (offset >= 0) & (offset <= 2 * HALF) & (query_ids == key_ids)


def block_probs(query, keys, allowed):
    scores = jnp.where(allowed, contract_cols(query, keys) * HD**-0.5, -1e30)
    grown = jnp.exp(scores - jnp.max(scores, -1, keepdims=True))
    return grown / jnp.sum(grown, -1, keepdims=True)


def attend_kernel(block, q_ref, k_ref, v_ref, kl_ref, vl_ref, kh_ref, vh_ref, qid_ref, kid_ref, out_ref):
    keys = jnp.concatenate([kl_ref[0], k_ref[0], kh_ref[0]], 0)
    values = jnp.concatenate([vl_ref[0], v_ref[0], vh_ref[0]], 0)
    masks = head_masks()
    for start in range(0, q_ref.shape[1], block):
        span = slice(start, start + block + 2 * HALF)
        allowed = block_mask(qid_ref[0, start : start + block], kid_ref[0, :, span])
        query = q_ref[0, start : start + block]
        total = None
        for mask in masks:
            probs = block_probs(query * mask, keys[span], allowed)
            part = matmul(probs.astype(BF16), values[span]) * mask.astype(F32)
            total = part if total is None else total + part
        out_ref[0, start : start + block] = total.astype(BF16)


def attend_back_kernel(
    block, q_ref, k_ref, v_ref, kl_ref, vl_ref, kh_ref, vh_ref, qid_ref, kid_ref,
    grad_ref, cos_ref, sin_ref, dq_ref, mid_ref, low_ref, high_ref,
):
    keys = jnp.concatenate([kl_ref[0], k_ref[0], kh_ref[0]], 0)
    values = jnp.concatenate([vl_ref[0], v_ref[0], vh_ref[0]], 0)
    masks = head_masks()
    length = q_ref.shape[1]
    window = jnp.zeros((length + 2 * HALF, LANES), F32)
    grad_keys, grad_values = window, window
    for start in range(0, length, block):
        span = slice(start, start + block + 2 * HALF)
        allowed = block_mask(qid_ref[0, start : start + block], kid_ref[0, :, span])
        query_all = q_ref[0, start : start + block]
        grad_all = grad_ref[0, start : start + block]
        grad_query, part_keys, part_values = 0.0, 0.0, 0.0
        for mask in masks:
            query, grad = query_all * mask, grad_all * mask
            probs = block_probs(query, keys[span], allowed)
            grad_probs = contract_cols(grad, values[span])
            delta = jnp.sum(probs * grad_probs, -1, keepdims=True)
            grad_scores = (probs * (grad_probs - delta)).astype(BF16)
            grad_query += matmul(grad_scores, keys[span]) * mask.astype(F32)
            part_keys += contract_rows(grad_scores, query)
            part_values += contract_rows(probs.astype(BF16), grad)
        grad_query = grad_query * HD**-0.5
        rows = slice(start, start + block)
        dq_ref[0, rows] = (
            grad_query * cos_ref[rows] - turned(grad_query) * sin_ref[rows]
        ).astype(BF16)
        before, after = start, length - start - block

        def placed(part):
            pieces = [part]
            if before:
                pieces.insert(0, jnp.zeros((before, LANES), F32))
            if after:
                pieces.append(jnp.zeros((after, LANES), F32))
            return jnp.concatenate(pieces, 0)

        grad_keys += placed(part_keys)
        grad_values += placed(part_values)
    for index, total in enumerate((grad_keys * HD**-0.5, grad_values)):
        low_ref[0, index] = total[:HALF].astype(BF16)
        mid_ref[0, index] = total[HALF : HALF + length]
        high_ref[0, index] = total[HALF + length :].astype(BF16)


def attention_specs(length, groups):
    def at(rows, shift):
        return pl.BlockSpec((1, rows, LANES), lambda s, h: (s, 0, h + shift))

    return [
        at(length, 0),
        at(length, groups),
        at(length, 2 * groups),
        at(HALF, 0),
        at(HALF, groups),
        at(HALF, 0),
        at(HALF, groups),
        pl.BlockSpec((1, length, 1), lambda s, h: (s, 0, 0)),
        pl.BlockSpec((1, 1, length + 2 * HALF), lambda s, h: (s, 0, 0)),
    ]


def attend(block, joined, low, high, query_ids, key_ids):
    streams, length, columns = joined.shape
    groups = columns // 3 // LANES
    return pl.pallas_call(
        functools.partial(attend_kernel, block),
        grid=(streams, groups),
        in_specs=attention_specs(length, groups),
        out_specs=pl.BlockSpec((1, length, LANES), lambda s, h: (s, 0, h)),
        out_shape=jax.ShapeDtypeStruct((streams, length, columns // 3), BF16),
        compiler_params=pltpu.CompilerParams(vmem_limit_bytes=24 * 2**20),
        cost_estimate=LIGHT,
    )(joined, joined, joined, low, low, high, high, query_ids, key_ids)


def attend_back(block, joined, low, high, query_ids, key_ids, grad, cosine, sine):
    streams, length, columns = joined.shape
    groups = columns // 3 // LANES

    def pair(rows):
        return pl.BlockSpec((1, 2, rows, LANES), lambda s, h: (s, 0, 0, h))

    def shape(rows, kind):
        return jax.ShapeDtypeStruct((streams, 2, rows, columns // 3), kind)

    return pl.pallas_call(
        functools.partial(attend_back_kernel, block),
        grid=(streams, groups),
        in_specs=attention_specs(length, groups)
        + [pl.BlockSpec((1, length, LANES), lambda s, h: (s, 0, h))]
        + [pl.BlockSpec((length, LANES), lambda s, h: (0, 0))] * 2,
        out_specs=[
            pl.BlockSpec((1, length, LANES), lambda s, h: (s, 0, h)),
            pair(length),
            pair(HALF),
            pair(HALF),
        ],
        out_shape=[
            jax.ShapeDtypeStruct((streams, length, columns // 3), BF16),
            shape(length, F32),
            shape(HALF, BF16),
            shape(HALF, BF16),
        ],
        compiler_params=pltpu.CompilerParams(vmem_limit_bytes=24 * 2**20),
        cost_estimate=LIGHT,
    )(joined, joined, joined, low, low, high, high, query_ids, key_ids, grad, cosine, sine)


def join_kernel(dq_ref, mid_ref, low_ref, high_ref, cos_ref, sin_ref, out_ref):
    length, width = dq_ref.shape[1:]
    out_ref[0, :, :width] = dq_ref[0]
    cosine, sine = cos_ref[...], sin_ref[...]
    for index in range(2):
        for start in range(0, width, LANES):
            lanes = slice(start, start + LANES)
            total = mid_ref[0, index, :, lanes]
            total = total + jnp.concatenate(
                [
                    low_ref[0, index, :, lanes].astype(F32),
                    jnp.zeros((length - 2 * HALF, LANES), F32),
                    high_ref[0, index, :, lanes].astype(F32),
                ],
                0,
            )
            if index == 0:
                total = total * cosine - turned(total) * sine
            to = (1 + index) * width + start
            out_ref[0, :, to : to + LANES] = total.astype(BF16)


def join_grads(grad_query, mid, from_lower, from_upper, cosine, sine):
    streams, length, width = grad_query.shape
    return pl.pallas_call(
        join_kernel,
        grid=(streams,),
        in_specs=[
            pl.BlockSpec((1, length, width), lambda s: (s, 0, 0)),
            pl.BlockSpec((1, 2, length, width), lambda s: (s, 0, 0, 0)),
            pl.BlockSpec((1, 2, HALF, width), lambda s: (s, 0, 0, 0)),
            pl.BlockSpec((1, 2, HALF, width), lambda s: (s, 0, 0, 0)),
            pl.BlockSpec((length, LANES), lambda s: (0, 0)),
            pl.BlockSpec((length, LANES), lambda s: (0, 0)),
        ],
        out_specs=pl.BlockSpec((1, length, 3 * width), lambda s: (s, 0, 0)),
        out_shape=jax.ShapeDtypeStruct((streams, length, 3 * width), BF16),
        compiler_params=pltpu.CompilerParams(vmem_limit_bytes=24 * 2**20),
        cost_estimate=LIGHT,
    )(grad_query, mid, from_lower, from_upper, cosine, sine)


def arrival_order(width, shard_rows):
    inner, outer, dp = (lax.axis_size(name) for name in ("inner", "outer", "dp"))
    x, z, y = (lax.axis_index(name) for name in ("inner", "outer", "dp"))
    place = jnp.arange(width, dtype=jnp.int32)
    part, rest = place // (width // 2), place % (width // 2)
    chunk, rest = rest // (outer * shard_rows), rest % (outer * shard_rows)
    along_x = jnp.where(part == 0, chunk // dp, chunk % inner)
    along_y = jnp.where(part == 0, chunk % dp, chunk // inner)
    along_z, row = rest // shard_rows, rest % shard_rows
    at_x = (x - along_x + inner) % inner
    at_y = (y - along_y + dp) % dp
    at_z = (z - along_z + outer) % outer
    source = (((at_y * outer + at_z) * inner + at_x) * 2 + part) * shard_rows + row
    return (place[:, None] == source[None, :]).astype(BF16)


def forward(axis, distance=1):
    count = lax.axis_size(axis)
    return [(i, (i + distance) % count) for i in range(count)]


def ring_gather(axis, piece):
    pieces = [piece]
    for _ in range(1, lax.axis_size(axis)):
        pieces.append(lax.ppermute(pieces[-1], axis, forward(axis)))
    return pieces


def direct_sends(pair):
    return [pair] + [
        lax.ppermute(pair, "outer", forward("outer", distance))
        for distance in range(1, lax.axis_size("outer"))
    ]


def by_part(arrived):
    return [jnp.concatenate([piece[part] for piece in arrived], 0) for part in range(2)]


def gather_near(parts):
    both = tied(ring_gather("dp", parts[0]), ring_gather("inner", parts[1]))
    return [jnp.concatenate(pieces, 0) for pieces in both]


def gather_far(parts):
    one, two = tied(ring_gather("inner", parts[0]), ring_gather("dp", parts[1]))
    return jnp.concatenate(one + two, 0)


def chunk_kernel(pairs, *refs):
    lefts, rights, rest = refs[:pairs], refs[pairs : 2 * pairs], refs[2 * pairs :]
    adds, out_ref = rest[:-1], rest[-1]
    start = 0
    for left, right in zip(lefts, rights):
        columns = slice(start, start + right.shape[1])
        total = contract_rows(left[...], right[...])
        for add in adds:
            total = total + add[:, columns].astype(F32)
        out_ref[:, columns] = total.astype(BF16)
        start = columns.stop


def grad_chunk(lefts, rights, start, rows, adds):
    depth = lefts[0].shape[0]
    columns = sum(right.shape[1] for right in rights)
    index = start // rows
    if rows % LANES:
        lefts = [left[:, start : start + rows] for left in lefts]
        index = 0

    def whole(shape):
        return pl.BlockSpec(shape, lambda i: (0, 0))

    def block_at(shape, block):
        return pl.BlockSpec(shape, lambda i: block)

    return pl.pallas_call(
        functools.partial(chunk_kernel, len(lefts)),
        grid=(1,),
        in_specs=[block_at((depth, rows), (0, index)) for _ in lefts]
        + [whole(right.shape) for right in rights]
        + [block_at((rows, columns), (at, 0)) for _, at in adds],
        out_specs=whole((rows, columns)),
        out_shape=jax.ShapeDtypeStruct((rows, columns), BF16),
        compiler_params=pltpu.CompilerParams(vmem_limit_bytes=40 * 2**20),
        cost_estimate=LIGHT,
    )(*lefts, *rights, *[array for array, _ in adds])


def ring(axis, chunk, first):
    arrived = None
    for step in range(1, lax.axis_size(axis)):
        sent = first if step == 1 else chunk(step, arrived)
        arrived = lax.ppermute(sent, axis, forward(axis))
    return arrived


def with_adds(*adds):
    return [add for add in adds if add[0] is not None]


class GradSum:
    def __init__(self, lefts, rights, shard_rows):
        self.inner, self.outer, self.dp = (
            lax.axis_size(name) for name in ("inner", "outer", "dp")
        )
        self.shard_rows = shard_rows
        self.rows = self.outer * shard_rows
        self.half = self.inner * self.dp * self.rows
        self.chunk = functools.partial(grad_chunk, lefts, rights)

    def near_chunk(self, part, distance, arrived):
        rows = (self.inner if part else self.dp) * self.rows
        return self.chunk(part * self.half + distance * rows, rows, with_adds((arrived, 0)))

    def near(self):
        return [self.near_chunk(part, 1, None) for part in range(2)]

    def send_near(self, firsts):
        return tied(
            *[
                ring(axis, functools.partial(self.near_chunk, part), firsts[part])
                for part, axis in enumerate(("inner", "dp"))
            ]
        )

    def far_chunk(self, part, distance, arrived):
        start = part * self.half + distance * self.rows
        return self.chunk(
            start, self.rows, with_adds((self.ones[part], distance), (arrived, 0))
        )

    def far(self, ones):
        self.ones = ones
        return [self.far_chunk(part, 1, None) for part in range(2)]

    def send_far(self, firsts):
        return tied(
            *[
                ring(axis, functools.partial(self.far_chunk, part), firsts[part])
                for part, axis in enumerate(("dp", "inner"))
            ]
        )

    def finish(self, twos):
        mine = [self.far_chunk(part, 0, twos[part]) for part in range(2)]

        def cut(distance):
            span = slice(distance * self.shard_rows, (distance + 1) * self.shard_rows)
            return jnp.stack([piece[span] for piece in mine])

        arrived = [
            lax.ppermute(cut(distance), "outer", forward("outer", self.outer - distance))
            for distance in range(1, self.outer)
        ]
        return sum([piece.astype(F32) for piece in arrived], cut(0).astype(F32))


def both_halves(total):
    core = lax.axis_index("core")
    mine = lax.dynamic_index_in_dim(total, core, 0, keepdims=False)
    other = swap(lax.dynamic_index_in_dim(total, 1 - core, 0, keepdims=False))
    return (
        jnp.where(core == 0, mine, other),
        jnp.where(core == 0, other, mine),
    )


def shards(tokens, doc_ids, norm_attn, norm_mlp, w_qkv, w_out, w_in, w_down, cotangent):
    streams, block, width = tokens.shape
    shard_rows = w_qkv.shape[0]
    inner, outer, dp = (lax.axis_size(name) for name in ("inner", "outer", "dp"))
    core = lax.axis_index("core")
    length = 2 * block
    rows = streams * length
    side = width // 2
    units = w_down.shape[1] // 2
    padded = -(-units // LANES) * LANES

    def halves(weight, parts, pad):
        size = weight.shape[1] // (2 * parts)
        cut = [weight[:, i * size : (i + 1) * size] for i in range(2 * parts)]
        if pad != size:
            cut = [jnp.pad(piece, ((0, 0), (0, pad - size))) for piece in cut]
        return cut[0::2], cut[1::2]

    def paired(pieces):
        low = jnp.concatenate([piece for one, _ in pieces for piece in one], 1)
        high = jnp.concatenate([piece for _, two in pieces for piece in two], 1)
        mine = jnp.where(core == 0, low, high)
        other = swap(jnp.where(core == 0, high, low))
        return ordered(mine[None], other[None], 0)

    gains = jnp.pad(jnp.stack([norm_attn, norm_mlp], 1), ((0, 0), (0, LANES - 2)))
    pair_one = paired([halves(w_qkv, 3, side), ([gains], [gains]), halves(w_out, 1, side)])
    later_in, later_down, pair_one = tied(w_in, w_down, pair_one)
    one = direct_sends(pair_one)
    pair_two = paired([halves(later_in, 2, padded)])
    pair_three = paired([halves(later_down, 1, padded)])
    pair_two, one = tied(pair_two, one)
    two = direct_sends(pair_two)
    first = gather_far(gather_near(by_part(one)))
    pair_three, two, first = tied(pair_three, two, first)
    three = direct_sends(pair_three)
    two = gather_near(by_part(two))
    in_half = gather_far(two)
    order = arrival_order(width, shard_rows)

    def in_order(value):
        return matmul(value, order).astype(BF16)

    def out_of_order(value):
        return contract_cols(value, order).astype(BF16)

    def both_blocks(value):
        return in_order(ordered(value, swap(value), 1).reshape(rows, width))

    tokens_low = both_blocks(tokens)
    grad_output = both_blocks(cotangent)

    gain_attn, gain_mlp = (first[:, 3 * side + i].astype(F32) for i in range(2))

    chip = lax.axis_index(("outer", "inner"))
    chips = outer * inner
    start = chip * length
    positions = (start + jnp.arange(length, dtype=jnp.int32)).astype(F32)
    frequency = ROPE_BASE ** (-(jnp.arange(HD // 2, dtype=F32) * 2.0 / HD))
    angles = positions[:, None] * frequency[None, :]
    cosine, sine = jnp.cos(angles), jnp.sin(angles)
    cosine = jnp.tile(cosine, (1, LANES // (HD // 2)))
    sine = jnp.tile(jnp.concatenate([-sine, sine], 1), (1, LANES // HD))
    wide_cosine, wide_sine = (jnp.tile(table, (streams, 2)) for table in (cosine, sine))

    values = tokens_low.astype(F32)
    unit_attn, scale_attn = normalise(values)
    normed_low = (unit_attn * gain_attn).astype(BF16)
    joined = project(normed_low, first, wide_cosine, wide_sine, 3 * side)
    joined = joined.reshape(streams, length, 3 * side)
    onward = [(i, i + 1) for i in range(chips - 1)]
    back = [(i + 1, i) for i in range(chips - 1)]
    low = lax.ppermute(joined[:, length - HALF :, side:], ("outer", "inner"), onward)
    high = lax.ppermute(joined[:, :HALF, side:], ("outer", "inner"), back)
    ids_padded = jnp.pad(doc_ids, ((0, 0), (HALF, HALF)), constant_values=-1)
    key_ids = lax.dynamic_slice_in_dim(ids_padded, start, length + 2 * HALF, 1)[:, None, :]
    query_ids = lax.dynamic_slice_in_dim(doc_ids, start, length, 1)[:, :, None]
    low, high, two = tied(low, high, two)
    attended_half = attend(block, joined, low, high, query_ids, key_ids).reshape(rows, side)
    three, in_half, attended_half = tied(three, in_half, attended_half)
    three = gather_near(by_part(three))
    attended_low = ordered(attended_half, swap(attended_half), 1)
    out_half = first[:, 3 * side + LANES :]
    full_out = ordered(out_half, swap(out_half), 1)
    full_out = matmul(order, in_order(full_out)).astype(BF16)
    hidden = values + matmul(attended_low, full_out)
    three, hidden = tied(three, hidden)
    down_half = gather_far(three)
    unit_mlp, scale_mlp = normalise(hidden)
    normed_mlp_low = (unit_mlp * gain_mlp).astype(BF16)
    expanded = matmul(normed_mlp_low, in_half)
    gate, up = expanded[:, :padded], expanded[:, padded:]
    below = 0.5 * (1.0 + lax.erf(gate * 0.5**0.5))
    active = gate * below
    mixed_low = (active * up).astype(BF16)

    mixed_low, down_half = tied(mixed_low, down_half)
    sum_down = GradSum([grad_output], [mixed_low], shard_rows)
    down_ones = sum_down.send_near(sum_down.near())
    grad_mixed = matmul(grad_output, down_half)
    density = jnp.exp(-0.5 * gate * gate) * (2.0 * jnp.pi) ** -0.5
    grad_expanded_low = jnp.concatenate(
        [
            (grad_mixed * up * (below + gate * density)).astype(BF16),
            (grad_mixed * active).astype(BF16),
        ],
        1,
    )

    def own_rows(value):
        value = value.reshape(streams, 2, block, width)
        mine = lax.dynamic_index_in_dim(value, core, 1, keepdims=False)
        other = lax.dynamic_index_in_dim(value, 1 - core, 1, keepdims=False)
        return mine, other

    def summed_rows(partial):
        mine, other = own_rows(partial)
        return mine + swap(other.astype(BF16)).astype(F32)

    output = own_rows(hidden)[0] + summed_rows(contract_cols(mixed_low, down_half))
    output = out_of_order(output.astype(BF16).reshape(-1, width)).reshape(tokens.shape)

    grad_expanded_low, down_ones = tied(grad_expanded_low, down_ones)
    down_sent = sum_down.far(down_ones)
    sum_in = GradSum([normed_mlp_low], [grad_expanded_low], shard_rows)
    in_sent, down_sent, grad_expanded_low = tied(sum_in.near(), down_sent, grad_expanded_low)
    down_twos = sum_down.send_far(down_sent)
    in_ones = sum_in.send_near(in_sent)
    grad_normed_mlp = contract_cols(grad_expanded_low, in_half)
    grad_normed_mlp, down_twos = tied(grad_normed_mlp, down_twos)
    down_total = sum_down.finish(down_twos)
    grad_normed_mlp = grad_normed_mlp + swap(grad_normed_mlp.astype(BF16)).astype(F32)
    grad_hidden = grad_output.astype(F32) + norm_back(
        unit_mlp, scale_mlp, gain_mlp, grad_normed_mlp
    )
    grad_hidden_low = grad_hidden.astype(BF16)

    out_rows = lax.dynamic_slice_in_dim(full_out, core * side, side, 0)
    grad_attended = contract_cols(grad_hidden_low, out_rows).astype(BF16)
    grad_query, mid, to_lower, to_upper = attend_back(
        block, joined, low, high, query_ids, key_ids,
        grad_attended.reshape(streams, length, side), cosine, sine,
    )
    from_lower = lax.ppermute(to_upper, ("outer", "inner"), onward)
    from_upper = lax.ppermute(to_lower, ("outer", "inner"), back)
    from_lower, from_upper, in_ones = tied(from_lower, from_upper, in_ones)
    in_sent = sum_in.far(in_ones)
    from_lower, in_sent = tied(from_lower, in_sent)
    in_twos = sum_in.send_far(in_sent)
    grad_joined = join_grads(grad_query, mid, from_lower, from_upper, cosine, sine)
    grad_joined = grad_joined.reshape(rows, 3 * side)
    hidden_side = lax.dynamic_slice_in_dim(out_of_order(grad_hidden_low), core * side, side, 1)
    sum_attn = GradSum(
        [normed_low, in_order(attended_low)], [grad_joined, hidden_side], shard_rows
    )
    attn_sent, in_twos, grad_joined = tied(sum_attn.near(), in_twos, grad_joined)
    in_total = sum_in.finish(in_twos)
    attn_ones = sum_attn.send_near(attn_sent)
    grad_normed = summed_rows(contract_cols(grad_joined, first[:, : 3 * side]))
    unit_mine, scale_mine = normalise(own_rows(values)[0])
    grad_tokens = own_rows(grad_hidden)[0] + norm_back(
        unit_mine, scale_mine, gain_attn, grad_normed
    )
    grad_tokens = lax.dot_general(
        grad_tokens.reshape(-1, width),
        order.astype(F32),
        (((1,), (1,)), ((), ())),
        precision=lax.Precision.HIGHEST,
        preferred_element_type=F32,
    ).reshape(tokens.shape)

    attn_twos = sum_attn.send_far(sum_attn.far(attn_ones))
    attn_total = sum_attn.finish(attn_twos)

    def interleaved(pair, start, parts, stride, size):
        cuts = []
        for i in range(parts):
            first_column = start + i * stride
            cuts += [half[:, first_column : first_column + size] for half in pair]
        return jnp.concatenate(cuts, 1)

    grad_down = interleaved(both_halves(down_total), 0, 1, padded, units)
    grad_in = interleaved(both_halves(in_total), 0, 2, padded, units)
    pair = both_halves(attn_total)
    grad_qkv = interleaved(pair, 0, 3, side, side)
    grad_out = interleaved(pair, 3 * side, 1, side, side)

    def gain_grad(weight, grad, gain):
        return jnp.sum(weight.astype(F32) * grad, -1) / gain.astype(F32)

    return (
        output,
        grad_tokens,
        gain_grad(w_qkv, grad_qkv, norm_attn),
        gain_grad(w_in, grad_in, norm_mlp),
        grad_qkv,
        grad_out,
        grad_in,
        grad_down,
    )


def solution(mesh):
    dp, seq = mesh.shape["dp"], mesh.shape["seq"]
    chips = seq // 2
    outer = 4 if chips % 4 == 0 else 1
    fine = Mesh(
        mesh.devices.reshape(dp, outer, chips // outer, 2), ("dp", "outer", "inner", "core")
    )
    line = ("outer", "inner", "core")
    every = ("dp",) + line
    token = P("dp", line, None)
    vector = P(every)
    matrix = P(every, None)
    return jax.shard_map(
        shards,
        mesh=fine,
        in_specs=(token, P("dp", None), vector, vector, matrix, matrix, matrix, matrix, token),
        out_specs=(token, token, vector, vector, matrix, matrix, matrix, matrix),
        check_vma=False,
    )
```

```python
import functools

import jax
import jax.numpy as jnp
import numpy as np
from jax import lax
from jax.experimental import pallas as pl
from jax.experimental.pallas import tpu as pltpu
from jax.sharding import Mesh, PartitionSpec as P

HD = 64
HALF = 64
LANES = 128
NORM_EPSILON = 1e-05
ROPE_BASE = 10000.0
F32 = jnp.float32
BF16 = jnp.bfloat16


def contract_cols(left, right):
    return lax.dot_general(left, right, (((1,), (1,)), ((), ())), preferred_element_type=F32)


def contract_rows(left, right):
    return lax.dot_general(left, right, (((0,), (0,)), ((), ())), preferred_element_type=F32)


def matmul(left, right):
    return jnp.dot(left, right, preferred_element_type=F32)


def tied(*values):
    return lax.optimization_barrier(values)


def call(kernel, grid, ins, outs, scratch=(), limit=40):
    out = pl.pallas_call(
        kernel,
        grid=grid,
        in_specs=[pl.BlockSpec(block, index) for _, block, index in ins],
        out_specs=[pl.BlockSpec(block, index) for _, _, block, index in outs],
        out_shape=[jax.ShapeDtypeStruct(shape, kind) for shape, kind, _, _ in outs],
        scratch_shapes=list(scratch),
        compiler_params=pltpu.CompilerParams(vmem_limit_bytes=limit * 2**20),
        cost_estimate=pl.CostEstimate(flops=1024, bytes_accessed=1024, transcendentals=0),
    )(*[array for array, _, _ in ins])
    return out


def whole(array):
    return (array, array.shape, lambda *_: (0,) * array.ndim)


def swap(value):
    return lax.ppermute(value, "core", [(0, 1), (1, 0)])


def ordered(mine, other, axis):
    first = lax.axis_index("core") == 0
    return jnp.concatenate(
        [jnp.where(first, mine, other), jnp.where(first, other, mine)], axis=axis
    )


def forward(axis, distance=1):
    count = lax.axis_size(axis)
    return [(i, (i + distance) % count) for i in range(count)]


def ring_gather(axis, piece):
    pieces = [piece]
    for _ in range(1, lax.axis_size(axis)):
        pieces.append(lax.ppermute(pieces[-1], axis, forward(axis)))
    return pieces[1:]


def direct_sends(rows):
    return [rows] + [
        lax.ppermute(rows, "outer", forward("outer", distance))
        for distance in range(1, lax.axis_size("outer"))
    ]


def joined_rows(pieces):
    return jnp.concatenate(pieces, 0) if len(pieces) > 1 else pieces[0]


def gather_near(arrived):
    own = joined_rows(arrived)
    return (own,) + tied(ring_gather("inner", own), ring_gather("dp", own))


def gather_far(own, along_x, along_y):
    half = own.shape[0] // 2
    one = ring_gather("inner", joined_rows([piece[:half] for piece in along_y]))
    two = ring_gather("dp", joined_rows([piece[half:] for piece in along_x]))
    return tied(one, two)


def in_pieces(own, along_x, along_y, one, two):
    pieces = [own, *along_x, *along_y, *one, *two]
    if any(piece.shape[0] % LANES for piece in pieces):
        pieces = [joined_rows(pieces)]
    return pieces


def arrival_order(width, shard_rows):
    inner, outer, dp = (lax.axis_size(name) for name in ("inner", "outer", "dp"))
    x, z, y = (lax.axis_index(name) for name in ("inner", "outer", "dp"))
    half = outer * shard_rows
    blocks = [(0, 0, 0, 2)]
    blocks += [(d, 0, 0, 2) for d in range(1, inner)] + [(0, d, 0, 2) for d in range(1, dp)]
    blocks += [(d, e, 0, 1) for d in range(1, inner) for e in range(1, dp)]
    blocks += [(d, e, 1, 2) for e in range(1, dp) for d in range(1, inner)]
    place = np.concatenate([np.arange(low * half, high * half) for _, _, low, high in blocks])
    sizes = [(high - low) * half for _, _, low, high in blocks]
    along_x = np.repeat([block[0] for block in blocks], sizes)
    along_y = np.repeat([block[1] for block in blocks], sizes)
    along_z, row = place // (2 * shard_rows), place % (2 * shard_rows)
    at_x = (x - jnp.asarray(along_x, jnp.int32) + inner) % inner
    at_y = (y - jnp.asarray(along_y, jnp.int32) + dp) % dp
    at_z = (z - jnp.asarray(along_z, jnp.int32) + outer) % outer
    source = ((at_y * outer + at_z) * inner + at_x) * 2 * shard_rows + row
    return (jnp.arange(width, dtype=jnp.int32)[:, None] == source[None, :]).astype(BF16)


def rows_kernel(pairs, places, *refs):
    lefts, rights, rest = refs[:pairs], refs[pairs : 2 * pairs], refs[2 * pairs :]
    adds, out_ref = rest[:-1], rest[-1]
    start = 0
    for left, right in zip(lefts, rights):
        columns = slice(start, start + right.shape[1])
        total = contract_rows(left[...], right[...])
        full = [add for add in adds if add.shape[0] == total.shape[0]]
        for add in full:
            total = total + add[:, columns].astype(F32)
        out_ref[:, columns] = total.astype(BF16)
        for add, at in zip(adds, places):
            if add.shape[0] != total.shape[0]:
                span = slice(at, at + add.shape[0])
                part = total[span] + add[:, columns].astype(F32)
                out_ref[span, columns] = part.astype(BF16)
        start = columns.stop


class GradSum:
    def __init__(self, lefts, rights, shard_rows):
        self.lefts, self.rights = lefts, rights
        self.inner, self.outer, self.dp = (
            lax.axis_size(name) for name in ("inner", "outer", "dp")
        )
        self.shard = 2 * shard_rows
        self.half = self.outer * shard_rows
        self.at_x = 2 * self.half
        self.at_y = self.at_x + (self.inner - 1) * 2 * self.half
        self.at_one = self.at_y + (self.dp - 1) * 2 * self.half
        self.at_two = self.at_one + (self.inner - 1) * (self.dp - 1) * self.half

    def rows(self, start, count, adds):
        adds = [(rows, place) for rows, place in adds if rows is not None]
        lefts, index = self.lefts, start // max(count, 1)
        if count % LANES or start % count:
            lefts, index = [left[:, start : start + count] for left in lefts], 0
        depth = lefts[0].shape[0]
        columns = sum(right.shape[1] for right in self.rights)
        return call(
            functools.partial(rows_kernel, len(lefts), [place for _, place in adds]),
            (1,),
            [(left, (depth, count), lambda i: (0, index)) for left in lefts]
            + [whole(right) for right in self.rights]
            + [whole(rows) for rows, _ in adds],
            [((count, columns), BF16, (count, columns), lambda i: (0, 0))],
        )[0]

    def ring(self, axis, chunk, first):
        arrived = None
        for step in range(1, lax.axis_size(axis)):
            sent = first if step == 1 else chunk(step, arrived)
            arrived = lax.ppermute(sent, axis, forward(axis))
        return arrived

    def one(self, distance, arrived):
        count = (self.dp - 1) * self.half
        return self.rows(self.at_one + (distance - 1) * count, count, [(arrived, 0)])

    def two(self, distance, arrived):
        count = (self.inner - 1) * self.half
        return self.rows(self.at_two + (distance - 1) * count, count, [(arrived, 0)])

    def far(self):
        if self.dp == 1 or self.inner == 1:
            return (None, None)
        return self.one(1, None), self.two(1, None)

    def send_far(self, firsts):
        if firsts[0] is None:
            return firsts
        return tied(
            self.ring("inner", self.one, firsts[0]), self.ring("dp", self.two, firsts[1])
        )

    def along(self, start, distance, arrived, extra, place):
        count = 2 * self.half
        if extra is not None:
            extra = extra[(distance - 1) * self.half : distance * self.half]
        at = start + (distance - 1) * count
        return self.rows(at, count, [(arrived, 0), (extra, place)])

    def along_x(self, distance, arrived):
        return self.along(self.at_x, distance, arrived, self.sums[1], self.half)

    def along_y(self, distance, arrived):
        return self.along(self.at_y, distance, arrived, self.sums[0], 0)

    def near(self, sums):
        self.sums = sums
        return (
            self.along_x(1, None) if self.inner > 1 else None,
            self.along_y(1, None) if self.dp > 1 else None,
        )

    def send_near(self, firsts):
        return tied(
            self.ring("inner", self.along_x, firsts[0]),
            self.ring("dp", self.along_y, firsts[1]),
        )

    def own(self, nears):
        return self.rows(0, 2 * self.half, [(near, 0) for near in nears])

    def finish(self, own):
        def cut(distance):
            return own[distance * self.shard : (distance + 1) * self.shard]

        arrived = [
            lax.ppermute(cut(distance), "outer", forward("outer", self.outer - distance))
            for distance in range(1, self.outer)
        ]
        total = sum([piece.astype(F32) for piece in arrived], cut(0).astype(F32))
        return total.reshape(2, self.shard // 2, -1)


def both_halves(total):
    core = lax.axis_index("core")
    mine = lax.dynamic_index_in_dim(total, core, 0, keepdims=False)
    other = swap(lax.dynamic_index_in_dim(total, 1 - core, 0, keepdims=False))
    return (
        jnp.where(core == 0, mine, other),
        jnp.where(core == 0, other, mine),
    )


def normalise(values):
    centred = values - jnp.mean(values, -1, keepdims=True)
    scale = lax.rsqrt(jnp.mean(centred * centred, -1, keepdims=True) + NORM_EPSILON)
    return centred * scale, scale


def norm_back(unit, scale, gain, incoming):
    grad = incoming * gain
    return scale * (
        grad
        - jnp.mean(grad, -1, keepdims=True)
        - unit * jnp.mean(grad * unit, -1, keepdims=True)
    )


def piece_matmul(left, pieces):
    total, start = None, 0
    for piece in pieces:
        part = matmul(left[:, start : start + piece.shape[0]], piece[...])
        total = part if total is None else total + part
        start += piece.shape[0]
    return total


def back_kernel(starts, count, *refs):
    grads, pieces, out_refs = refs[: len(starts)], refs[len(starts) : count], refs[count:]
    at = 0
    for piece in pieces:
        total = None
        for grad, start in zip(grads, starts):
            part = contract_cols(grad[...], piece[:, start : start + grad.shape[1]])
            total = part if total is None else total + part
        for out_ref in out_refs:
            out_ref[:, at : at + piece.shape[0]] = total.astype(out_ref.dtype)
        at += piece.shape[0]


def back_project(grads, pieces, kinds):
    rows = grads[0].shape[0]
    block = rows // 2
    starts, end = [], 0
    for grad in grads:
        starts.append(end)
        end += grad.shape[1]
    width = sum(piece.shape[0] for piece in pieces)
    return call(
        functools.partial(back_kernel, starts, len(grads) + len(pieces)),
        (2,),
        [(grad, (block, grad.shape[1]), lambda i: (i, 0)) for grad in grads]
        + [(piece, (piece.shape[0], end), lambda i: (0, 0)) for piece in pieces],
        [((rows, width), kind, (block, width), lambda i: (i, 0)) for kind in kinds],
    )


def turned(values):
    width = values.shape[-1]
    lane = lax.broadcasted_iota(jnp.int32, values.shape, values.ndim - 1)
    ahead = pltpu.roll(values, width - HD // 2, values.ndim - 1)
    behind = pltpu.roll(values, HD // 2, values.ndim - 1)
    return jnp.where(lane % HD < HD // 2, ahead, behind)


def project_kernel(count, x_ref, cos_ref, sin_ref, *refs):
    gains, weights = refs[:count], refs[count : 2 * count]
    out_ref, norm_ref, gain_ref = refs[2 * count :]

    @pl.when(pl.program_id(0) == 0)
    def _():
        pick = lax.broadcasted_iota(jnp.int32, (8, LANES), 0) == lax.broadcasted_iota(
            jnp.int32, (8, LANES), 1
        )
        pick = pick.astype(F32).astype(BF16)
        start = 0
        for piece in gains:
            gain_ref[:, start : start + piece.shape[0]] = contract_cols(pick, piece[...])
            start += piece.shape[0]
        unit, _ = normalise(x_ref[...].astype(F32))
        norm_ref[...] = (unit * gain_ref[0:1, :]).astype(BF16)

    values = piece_matmul(norm_ref, weights)
    keep = pl.program_id(0) == 2
    length = cos_ref.shape[0]
    for top in range(0, values.shape[0], length):
        for left in range(0, values.shape[1], LANES):
            part = values[top : top + length, left : left + LANES]
            rotated = part * cos_ref[...] + turned(part) * sin_ref[...]
            out_ref[top : top + length, left : left + LANES] = jnp.where(
                keep, part, rotated
            ).astype(BF16)


def project(tokens, pieces, cosine, sine, side):
    rows, width = tokens.shape
    gain_block = 3 * side // LANES
    return call(
        functools.partial(project_kernel, len(pieces)),
        (3,),
        [whole(tokens), whole(cosine), whole(sine)]
        + [(piece, (piece.shape[0], LANES), lambda j: (0, gain_block)) for piece in pieces]
        + [(piece, (piece.shape[0], side), lambda j: (0, j)) for piece in pieces],
        [
            ((rows, 3 * side), BF16, (rows, side), lambda j: (0, j)),
            ((rows, width), BF16, (rows, width), lambda j: (0, 0)),
            ((8, width), F32, (8, width), lambda j: (0, 0)),
        ],
    )


def head_masks():
    lane = lax.broadcasted_iota(jnp.int32, (1, LANES), 1)
    return [(lane // HD == head).astype(F32).astype(BF16) for head in range(LANES // HD)]


def block_mask(query_ids, key_ids):
    rows, width = query_ids.shape[0], key_ids.shape[1]
    offset = lax.broadcasted_iota(jnp.int32, (rows, width), 1) - lax.broadcasted_iota(
        jnp.int32, (rows, width), 0
    )
    return (offset >= 0) & (offset <= 2 * HALF) & (query_ids == key_ids)


def block_probs(query, keys, allowed):
    scores = jnp.where(allowed, contract_cols(query, keys) * HD**-0.5, -1e30)
    grown = jnp.exp(scores - jnp.max(scores, -1, keepdims=True))
    return grown / jnp.sum(grown, -1, keepdims=True)


def attend_kernel(block, q_ref, k_ref, v_ref, qid_ref, kid_ref, out_ref):
    masks = head_masks()
    for start in range(0, out_ref.shape[1], block):
        span = slice(start, start + block + 2 * HALF)
        allowed = block_mask(qid_ref[0, start : start + block], kid_ref[0, :, span])
        query = q_ref[0, HALF + start : HALF + start + block]
        total = None
        for mask in masks:
            probs = block_probs(query * mask, k_ref[0, span], allowed)
            part = matmul(probs.astype(BF16), v_ref[0, span]) * mask.astype(F32)
            total = part if total is None else total + part
        out_ref[0, start : start + block] = total.astype(BF16)


def attend_back_kernel(
    block, q_ref, k_ref, v_ref, qid_ref, kid_ref, grad_ref, cos_ref, sin_ref,
    dq_ref, mid_ref, low_ref, high_ref,
):
    masks = head_masks()
    length = dq_ref.shape[1]
    grad_keys = grad_values = jnp.zeros((length + 2 * HALF, LANES), F32)
    for start in range(0, length, block):
        span = slice(start, start + block + 2 * HALF)
        mid = slice(HALF + start, HALF + start + block)
        rows = slice(start, start + block)
        allowed = block_mask(qid_ref[0, rows], kid_ref[0, :, span])
        query_all, grad_all = q_ref[0, mid], grad_ref[0, rows]
        keys, values = k_ref[0, span], v_ref[0, span]
        grad_query, part_keys, part_values = 0.0, 0.0, 0.0
        for mask in masks:
            query, grad = query_all * mask, grad_all * mask
            probs = block_probs(query, keys, allowed)
            grad_probs = contract_cols(grad, values)
            delta = jnp.sum(probs * grad_probs, -1, keepdims=True)
            grad_scores = (probs * (grad_probs - delta)).astype(BF16)
            grad_query += matmul(grad_scores, keys) * mask.astype(F32)
            part_keys += contract_rows(grad_scores, query)
            part_values += contract_rows(probs.astype(BF16), grad)
        grad_query = grad_query * HD**-0.5
        dq_ref[0, rows] = (
            grad_query * cos_ref[mid] - turned(grad_query) * sin_ref[mid]
        ).astype(BF16)
        before, after = start, length - start - block

        def placed(part):
            pieces = [part]
            if before:
                pieces.insert(0, jnp.zeros((before, LANES), F32))
            if after:
                pieces.append(jnp.zeros((after, LANES), F32))
            return jnp.concatenate(pieces, 0)

        grad_keys += placed(part_keys)
        grad_values += placed(part_values)
    for index, total in enumerate((grad_keys * HD**-0.5, grad_values)):
        low_ref[0, index] = total[:HALF].astype(BF16)
        mid_ref[0, index] = total[HALF : HALF + length]
        high_ref[0, index] = total[HALF + length :].astype(BF16)


def attention_inputs(joined, query_ids, key_ids):
    window, groups = joined.shape[1], joined.shape[2] // 3 // LANES
    inputs = [
        (joined, (1, window, LANES), lambda s, h, shift=shift: (s, 0, h + shift))
        for shift in (0, groups, 2 * groups)
    ]
    inputs += [
        (ids, (1,) + ids.shape[1:], lambda s, h: (s, 0, 0)) for ids in (query_ids, key_ids)
    ]
    return inputs


def attend(block, joined, query_ids, key_ids):
    streams, window, columns = joined.shape
    length, side = window - 2 * HALF, columns // 3
    return call(
        functools.partial(attend_kernel, block),
        (streams, side // LANES),
        attention_inputs(joined, query_ids, key_ids),
        [((streams, length, side), BF16, (1, length, LANES), lambda s, h: (s, 0, h))],
        limit=24,
    )[0]


def attend_back(block, joined, query_ids, key_ids, grad, cosine, sine):
    streams, length, side = grad.shape

    def pair(rows, kind):
        return (
            (streams, 2, rows, side), kind, (1, 2, rows, LANES), lambda s, h: (s, 0, 0, h)
        )

    return call(
        functools.partial(attend_back_kernel, block),
        (streams, side // LANES),
        attention_inputs(joined, query_ids, key_ids)
        + [(grad, (1, length, LANES), lambda s, h: (s, 0, h)), whole(cosine), whole(sine)],
        [
            ((streams, length, side), BF16, (1, length, LANES), lambda s, h: (s, 0, h)),
            pair(length, F32),
            pair(HALF, BF16),
            pair(HALF, BF16),
        ],
        limit=24,
    )


def join_kernel(dq_ref, mid_ref, low_ref, high_ref, cos_ref, sin_ref, out_ref):
    length, width = dq_ref.shape[1:]
    out_ref[0, :, :width] = dq_ref[0]
    cosine, sine = cos_ref[HALF : HALF + length], sin_ref[HALF : HALF + length]
    for index in range(2):
        for start in range(0, width, LANES):
            lanes = slice(start, start + LANES)
            total = mid_ref[0, index, :, lanes]
            total = total + jnp.concatenate(
                [
                    low_ref[0, index, :, lanes].astype(F32),
                    jnp.zeros((length - 2 * HALF, LANES), F32),
                    high_ref[0, index, :, lanes].astype(F32),
                ],
                0,
            )
            if index == 0:
                total = total * cosine - turned(total) * sine
            to = (1 + index) * width + start
            out_ref[0, :, to : to + LANES] = total.astype(BF16)


def join_grads(grad_query, mid, from_lower, from_upper, cosine, sine):
    streams, length, width = grad_query.shape

    def of_stream(array):
        block = (1,) + array.shape[1:]
        return (array, block, lambda s: (s,) + (0,) * (array.ndim - 1))

    return call(
        join_kernel,
        (streams,),
        [of_stream(array) for array in (grad_query, mid, from_lower, from_upper)]
        + [whole(cosine), whole(sine)],
        [((streams, length, 3 * width), BF16, (1, length, 3 * width), lambda s: (s, 0, 0))],
        limit=24,
    )[0]


def by_rows(array, block):
    return (array, (block, array.shape[1]), lambda i: (i, 0))


def out_kernel(att_ref, weight_ref, x_ref, gain_ref, hidden_ref, norm_ref):
    hidden = x_ref[...].astype(F32) + matmul(att_ref[...], weight_ref[...])
    hidden_ref[...] = hidden
    norm_ref[...] = (normalise(hidden)[0] * gain_ref[1:2, :]).astype(BF16)


def out_project(attended, weight, tokens, gains):
    rows, width = tokens.shape
    block = rows // 4
    return call(
        out_kernel,
        (4,),
        [by_rows(attended, block), whole(weight), by_rows(tokens, block), whole(gains)],
        [
            ((rows, width), kind, (block, width), lambda i: (i, 0)) for kind in (F32, BF16)
        ],
        limit=24,
    )


def hidden_back_kernel(
    part_ref, other_ref, hidden_ref, g_ref, gain_ref, weight_ref, grad_ref, low_ref, att_ref
):
    unit, scale = normalise(hidden_ref[...])
    incoming = part_ref[...] + other_ref[...].astype(F32)
    grad = g_ref[...].astype(F32) + norm_back(unit, scale, gain_ref[1:2, :], incoming)
    low = grad.astype(BF16)
    grad_ref[...] = grad
    low_ref[...] = low
    att_ref[...] = contract_cols(low, weight_ref[...]).astype(BF16)


def hidden_back(part, other, hidden, grad_output, gains, weight):
    rows, width = hidden.shape
    block, side = rows // 4, weight.shape[0]
    return call(
        hidden_back_kernel,
        (4,),
        [by_rows(array, block) for array in (part, other, hidden, grad_output)]
        + [whole(gains), whole(weight)],
        [
            ((rows, size), kind, (block, size), lambda i: (i, 0))
            for size, kind in ((width, F32), (width, BF16), (side, BF16))
        ],
        limit=24,
    )


def feed_kernel(count, norm_ref, *refs):
    gates, ups = refs[:count], refs[count : 2 * count]
    mixed_ref, factor_ref, active_ref = refs[2 * count :]
    gate, up = piece_matmul(norm_ref, gates), piece_matmul(norm_ref, ups)
    below = 0.5 * (1.0 + lax.erf(gate * 0.5**0.5))
    active = gate * below
    mixed_ref[...] = (active * up).astype(BF16)
    active_ref[...] = active
    density = jnp.exp(-0.5 * gate * gate) * (2.0 * np.pi) ** -0.5
    factor_ref[...] = up * (below + gate * density)


def feed(normed, pieces, units):
    rows = normed.shape[0]
    tiles = units // LANES
    return call(
        functools.partial(feed_kernel, len(pieces)),
        (tiles,),
        [whole(normed)]
        + [(piece, (piece.shape[0], LANES), lambda j: (0, j)) for piece in pieces]
        + [(piece, (piece.shape[0], LANES), lambda j: (0, j + tiles)) for piece in pieces],
        [
            ((rows, units), kind, (rows, LANES), lambda j: (0, j))
            for kind in (BF16, F32, F32)
        ],
        limit=24,
    )


def feed_back_kernel(count, g_ref, factor_ref, active_ref, *refs):
    grad = piece_matmul(g_ref, refs[:count])
    gate_ref, up_ref = refs[count:]
    gate_ref[...] = (grad * factor_ref[...]).astype(BF16)
    up_ref[...] = (grad * active_ref[...]).astype(BF16)


def feed_back(grad_output, factor, active, pieces):
    rows, units = factor.shape

    def tile(array):
        return (array, (array.shape[0], LANES), lambda j: (0, j))

    return call(
        functools.partial(feed_back_kernel, len(pieces)),
        (units // LANES,),
        [whole(grad_output), tile(factor), tile(active)] + [tile(piece) for piece in pieces],
        [((rows, units), BF16, (rows, LANES), lambda j: (0, j)) for _ in range(2)],
        limit=24,
    )


def shards(tokens, doc_ids, norm_attn, norm_mlp, w_qkv, w_out, w_in, w_down, cotangent):
    streams, block, width = tokens.shape
    shard_rows = w_qkv.shape[0]
    inner, outer = lax.axis_size("inner"), lax.axis_size("outer")
    core = lax.axis_index("core")
    length = 2 * block
    window = length + 2 * HALF
    rows = streams * length
    side = width // 2
    units = w_down.shape[1] // 2
    padded = -(-units // LANES) * LANES
    chips = outer * inner
    onward = [(i, i + 1) for i in range(chips - 1)]
    back = [(i + 1, i) for i in range(chips - 1)]

    def halves(weight, parts, pad):
        size = weight.shape[1] // (2 * parts)
        cut = [weight[:, i * size : (i + 1) * size] for i in range(2 * parts)]
        if pad != size:
            cut = [jnp.pad(piece, ((0, 0), (0, pad - size))) for piece in cut]
        return cut[0::2], cut[1::2]

    def paired(pieces):
        low = jnp.concatenate([piece for one, _ in pieces for piece in one], 1)
        high = jnp.concatenate([piece for _, two in pieces for piece in two], 1)
        mine = jnp.where(core == 0, low, high)
        return ordered(mine, swap(jnp.where(core == 0, high, low)), 0)

    pair_tokens = ordered(tokens, swap(tokens), 1)

    gains = jnp.pad(jnp.stack([norm_attn, norm_mlp], 1), ((0, 0), (0, LANES - 2)))
    pair_one = paired([halves(w_qkv, 3, side), ([gains], [gains]), halves(w_out, 1, side)])
    later_in, later_down, pair_one, pair_tokens = tied(w_in, w_down, pair_one, pair_tokens)
    low = lax.ppermute(pair_tokens[:, length - HALF :], ("outer", "inner"), onward)
    high = lax.ppermute(pair_tokens[:, :HALF], ("outer", "inner"), back)
    one = direct_sends(pair_one)
    pair_two = paired([halves(later_in, 2, padded)])
    pair_three = paired([halves(later_down, 1, padded)])
    pair_two, one, low, high, pair_tokens = tied(pair_two, one, low, high, pair_tokens)
    two = direct_sends(pair_two)
    near = gather_near(one)
    far = gather_far(*near)
    pair_three, two, near, far = tied(pair_three, two, near, far)
    three = direct_sends(pair_three)
    first = in_pieces(*near, *far)
    two_near = gather_near(two)

    order = arrival_order(width, shard_rows)

    def in_order(value):
        return matmul(value, order).astype(BF16)

    def out_of_order(value):
        return contract_cols(value, order).astype(BF16)

    window_tokens = jnp.concatenate([low, pair_tokens, high], 1).reshape(-1, width)
    window_tokens = in_order(window_tokens)
    own_tokens = window_tokens.reshape(streams, window, width)[:, HALF : HALF + length]
    own_tokens = own_tokens.reshape(rows, width)
    grad_output = in_order(ordered(cotangent, swap(cotangent), 1).reshape(rows, width))

    start = lax.axis_index(("outer", "inner")) * length
    positions = (start - HALF + jnp.arange(window, dtype=jnp.int32)).astype(F32)
    frequency = ROPE_BASE ** (-(jnp.arange(HD // 2, dtype=F32) * 2.0 / HD))
    angles = positions[:, None] * frequency[None, :]
    cosine, sine = jnp.cos(angles), jnp.sin(angles)
    cosine = jnp.tile(cosine, (1, LANES // (HD // 2)))
    sine = jnp.tile(jnp.concatenate([-sine, sine], 1), (1, LANES // HD))
    ids_padded = jnp.pad(doc_ids, ((0, 0), (HALF, HALF)), constant_values=-1)
    key_ids = lax.dynamic_slice_in_dim(ids_padded, start, window, 1)[:, None, :]
    query_ids = lax.dynamic_slice_in_dim(doc_ids, start, length, 1)[:, :, None]

    joined, window_norm, gain_rows = project(window_tokens, first, cosine, sine, side)
    joined, two_near = tied(joined, two_near)
    two_far = gather_far(*two_near)
    joined = joined.reshape(streams, window, 3 * side)
    attended_half = attend(block, joined, query_ids, key_ids).reshape(rows, side)
    out_half = joined_rows([piece[:, 3 * side + LANES :] for piece in first])
    full_out = ordered(out_half, swap(out_half), 1)
    full_out = matmul(order, in_order(full_out)).astype(BF16)
    attended_half, full_out, two_near, two_far, three = tied(
        attended_half, full_out, two_near, two_far, three
    )
    in_half = in_pieces(*two_near, *two_far)
    three_near = gather_near(three)
    attended_low = ordered(attended_half, swap(attended_half), 1)
    hidden, normed_mlp_low = out_project(attended_low, full_out, own_tokens, gain_rows)
    hidden, normed_mlp_low, three_near = tied(hidden, normed_mlp_low, three_near)
    three_far = gather_far(*three_near)
    mixed_low, factor, active = feed(normed_mlp_low, in_half, padded)
    mixed_low, factor, active, three_near, three_far = tied(
        mixed_low, factor, active, three_near, three_far
    )
    down_half = in_pieces(*three_near, *three_far)

    sum_down = GradSum([grad_output], [mixed_low], shard_rows)
    down_far = sum_down.send_far(sum_down.far())
    grad_gate, grad_up = feed_back(grad_output, factor, active, down_half)
    grad_gate, grad_up, down_far = tied(grad_gate, grad_up, down_far)
    sum_in = GradSum([normed_mlp_low], [jnp.concatenate([grad_gate, grad_up], 1)], shard_rows)
    sent_down, sent_in = sum_down.near(down_far), sum_in.far()
    grad_gate, grad_up, sent_down, sent_in = tied(grad_gate, grad_up, sent_down, sent_in)
    down_near = sum_down.send_near(sent_down)
    in_far = sum_in.send_far(sent_in)
    part, part_low = back_project([grad_gate, grad_up], in_half, [F32, BF16])
    out_rows = lax.dynamic_slice_in_dim(full_out, core * side, side, 0)
    grad_hidden, grad_hidden_low, grad_attended = hidden_back(
        part, swap(part_low), hidden, grad_output, gain_rows, out_rows
    )
    grad_attended, down_near, in_far = tied(grad_attended, down_near, in_far)
    down_total = sum_down.finish(sum_down.own(down_near))

    grad_query, mid, to_lower, to_upper = attend_back(
        block, joined, query_ids, key_ids, grad_attended.reshape(streams, length, side),
        cosine, sine,
    )
    sent_in = sum_in.near(in_far)
    to_lower, to_upper, sent_in = tied(to_lower, to_upper, sent_in)
    from_lower = lax.ppermute(to_upper, ("outer", "inner"), onward)
    from_upper = lax.ppermute(to_lower, ("outer", "inner"), back)
    in_near = sum_in.send_near(sent_in)
    grad_joined = join_grads(grad_query, mid, from_lower, from_upper, cosine, sine)
    grad_joined = grad_joined.reshape(rows, 3 * side)
    hidden_side = lax.dynamic_slice_in_dim(out_of_order(grad_hidden_low), core * side, side, 1)
    normed_low = window_norm.reshape(streams, window, width)[:, HALF : HALF + length]
    sum_attn = GradSum(
        [normed_low.reshape(rows, width), in_order(attended_low)],
        [grad_joined, hidden_side],
        shard_rows,
    )
    sent_attn = sum_attn.far()
    sent_attn, in_near, grad_joined = tied(sent_attn, in_near, grad_joined)
    in_own = sum_in.own(in_near)
    attn_far = sum_attn.send_far(sent_attn)
    in_total = sum_in.finish(in_own)

    def own_rows(value):
        value = value.reshape(streams, 2, block, width)
        mine = lax.dynamic_index_in_dim(value, core, 1, keepdims=False)
        other = lax.dynamic_index_in_dim(value, 1 - core, 1, keepdims=False)
        return mine, other

    def summed_rows(partial):
        mine, other = own_rows(partial)
        return mine + swap(other.astype(BF16)).astype(F32)

    (out_part,) = back_project([mixed_low], down_half, [F32])
    output = own_rows(hidden)[0] + summed_rows(out_part)
    output = out_of_order(output.astype(BF16).reshape(-1, width)).reshape(tokens.shape)

    (norm_part,) = back_project([grad_joined], first, [F32])
    grad_normed = summed_rows(norm_part)
    unit, scale = normalise(own_rows(own_tokens)[0].astype(F32))
    grad_tokens = own_rows(grad_hidden)[0] + norm_back(unit, scale, gain_rows[0], grad_normed)
    grad_tokens = lax.dot_general(
        grad_tokens.reshape(-1, width),
        order.astype(F32),
        (((1,), (1,)), ((), ())),
        precision=lax.Precision.HIGHEST,
        preferred_element_type=F32,
    ).reshape(tokens.shape)

    attn_near = sum_attn.send_near(sum_attn.near(attn_far))
    attn_total = sum_attn.finish(sum_attn.own(attn_near))

    def interleaved(pair, start, parts, stride, size):
        cuts = []
        for i in range(parts):
            first_column = start + i * stride
            cuts += [half[:, first_column : first_column + size] for half in pair]
        return jnp.concatenate(cuts, 1)

    grad_down = interleaved(both_halves(down_total), 0, 1, padded, units)
    grad_in = interleaved(both_halves(in_total), 0, 2, padded, units)
    pair = both_halves(attn_total)
    grad_qkv = interleaved(pair, 0, 3, side, side)
    grad_out = interleaved(pair, 3 * side, 1, side, side)

    def gain_grad(weight, grad, gain):
        return jnp.sum(weight.astype(F32) * grad, -1) / gain.astype(F32)

    return (
        output,
        grad_tokens,
        gain_grad(w_qkv, grad_qkv, norm_attn),
        gain_grad(w_in, grad_in, norm_mlp),
        grad_qkv,
        grad_out,
        grad_in,
        grad_down,
    )


def solution(mesh):
    dp, seq = mesh.shape["dp"], mesh.shape["seq"]
    chips = seq // 2
    outer = 4 if chips % 4 == 0 else 1
    fine = Mesh(
        mesh.devices.reshape(dp, outer, chips // outer, 2), ("dp", "outer", "inner", "core")
    )
    line = ("outer", "inner", "core")
    every = ("dp",) + line
    token = P("dp", line, None)
    vector = P(every)
    matrix = P(every, None)
    return jax.shard_map(
        shards,
        mesh=fine,
        in_specs=(token, P("dp", None), vector, vector, matrix, matrix, matrix, matrix, token),
        out_specs=(token, token, vector, vector, matrix, matrix, matrix, matrix),
        check_vma=False,
    )
```

```python
import functools

import jax
import jax.numpy as jnp
import numpy as np
from jax import lax
from jax.experimental import pallas as pl
from jax.experimental.pallas import tpu as pltpu
from jax.sharding import Mesh, PartitionSpec as P

HD = 64
HALF = 64
LANES = 128
NORM_EPSILON = 1e-05
ROPE_BASE = 10000.0
F32 = jnp.float32
BF16 = jnp.bfloat16


def contract_cols(left, right):
    return lax.dot_general(left, right, (((1,), (1,)), ((), ())), preferred_element_type=F32)


def contract_rows(left, right):
    return lax.dot_general(left, right, (((0,), (0,)), ((), ())), preferred_element_type=F32)


def matmul(left, right):
    return jnp.dot(left, right, preferred_element_type=F32)


def tied(*values):
    return lax.optimization_barrier(values)


def call(kernel, grid, ins, outs, scratch=(), limit=40):
    out = pl.pallas_call(
        kernel,
        grid=grid,
        in_specs=[pl.BlockSpec(block, index) for _, block, index in ins],
        out_specs=[pl.BlockSpec(block, index) for _, _, block, index in outs],
        out_shape=[jax.ShapeDtypeStruct(shape, kind) for shape, kind, _, _ in outs],
        scratch_shapes=list(scratch),
        compiler_params=pltpu.CompilerParams(vmem_limit_bytes=limit * 2**20),
        cost_estimate=pl.CostEstimate(flops=1024, bytes_accessed=1024, transcendentals=0),
    )(*[array for array, _, _ in ins])
    return out


def whole(array):
    return (array, array.shape, lambda *_: (0,) * array.ndim)


def swap(value):
    return lax.ppermute(value, "core", [(0, 1), (1, 0)])


def ordered(mine, other, axis):
    first = lax.axis_index("core") == 0
    return jnp.concatenate(
        [jnp.where(first, mine, other), jnp.where(first, other, mine)], axis=axis
    )


def forward(axis, distance=1):
    count = lax.axis_size(axis)
    return [(i, (i + distance) % count) for i in range(count)]


def ring_gather(axis, piece):
    pieces = [piece]
    for _ in range(1, lax.axis_size(axis)):
        pieces.append(lax.ppermute(pieces[-1], axis, forward(axis)))
    return pieces[1:]


def direct_sends(rows):
    return [rows] + [
        lax.ppermute(rows, "outer", forward("outer", distance))
        for distance in range(1, lax.axis_size("outer"))
    ]


def joined_rows(pieces):
    return jnp.concatenate(pieces, 0) if len(pieces) > 1 else pieces[0]


def gather_near(arrived):
    own = joined_rows(arrived)
    return own, ring_gather("inner", own), ring_gather("dp", own)


def gather_far(own, along_x, along_y):
    half = own.shape[0] // 2
    one = ring_gather("inner", joined_rows([piece[:half] for piece in along_y]))
    two = ring_gather("dp", joined_rows([piece[half:] for piece in along_x]))
    return one, two


def in_pieces(own, along_x, along_y, one, two):
    pieces = [own, *along_x, *along_y, *one, *two]
    if any(piece.shape[0] % LANES for piece in pieces):
        pieces = [joined_rows(pieces)]
    return pieces


def arrival_order(width, shard_rows):
    inner, outer, dp = (lax.axis_size(name) for name in ("inner", "outer", "dp"))
    x, z, y = (lax.axis_index(name) for name in ("inner", "outer", "dp"))
    half = outer * shard_rows
    blocks = [(0, 0, 0, 2)]
    blocks += [(d, 0, 0, 2) for d in range(1, inner)] + [(0, d, 0, 2) for d in range(1, dp)]
    blocks += [(d, e, 0, 1) for d in range(1, inner) for e in range(1, dp)]
    blocks += [(d, e, 1, 2) for e in range(1, dp) for d in range(1, inner)]
    place = np.concatenate([np.arange(low * half, high * half) for _, _, low, high in blocks])
    sizes = [(high - low) * half for _, _, low, high in blocks]
    along_x = np.repeat([block[0] for block in blocks], sizes)
    along_y = np.repeat([block[1] for block in blocks], sizes)
    along_z, row = place // (2 * shard_rows), place % (2 * shard_rows)
    at_x = (x - jnp.asarray(along_x, jnp.int32) + inner) % inner
    at_y = (y - jnp.asarray(along_y, jnp.int32) + dp) % dp
    at_z = (z - jnp.asarray(along_z, jnp.int32) + outer) % outer
    source = ((at_y * outer + at_z) * inner + at_x) * 2 * shard_rows + row
    return (jnp.arange(width, dtype=jnp.int32)[:, None] == source[None, :]).astype(BF16)


def rows_kernel(pairs, layout, *refs):
    rights, refs = refs[:pairs], refs[pairs:]
    inputs, outs = refs[: -len(layout)], refs[-len(layout) :]
    for places, out_ref in zip(layout, outs):
        lefts, adds = inputs[:pairs], inputs[pairs : pairs + len(places)]
        inputs = inputs[pairs + len(places) :]
        start = 0
        for left, right in zip(lefts, rights):
            columns = slice(start, start + right.shape[1])
            start = columns.stop
            total = contract_rows(left[...], right[...])
            for add in adds:
                if add.shape[0] == total.shape[0]:
                    total = total + add[:, columns].astype(F32)
            out_ref[:, columns] = total.astype(BF16)
            for add, at in zip(adds, places):
                if add.shape[0] != total.shape[0]:
                    span = slice(at, at + add.shape[0])
                    part = total[span] + add[:, columns].astype(F32)
                    out_ref[span, columns] = part.astype(BF16)


class GradSum:
    def __init__(self, lefts, rights, shard_rows):
        self.lefts, self.rights = lefts, rights
        self.inner, self.outer, self.dp = (
            lax.axis_size(name) for name in ("inner", "outer", "dp")
        )
        self.shard = 2 * shard_rows
        self.half = self.outer * shard_rows
        self.at_x = 2 * self.half
        self.at_y = self.at_x + (self.inner - 1) * 2 * self.half
        self.at_one = self.at_y + (self.dp - 1) * 2 * self.half
        self.at_two = self.at_one + (self.inner - 1) * (self.dp - 1) * self.half

    def rows(self, *parts):
        depth = self.lefts[0].shape[0]
        columns = sum(right.shape[1] for right in self.rights)
        ins, outs, layout = [whole(right) for right in self.rights], [], []
        for start, count, adds in parts:
            adds = [(rows, place) for rows, place in adds if rows is not None]
            lefts, index = self.lefts, start // count
            if count % LANES or start % count:
                lefts, index = [left[:, start : start + count] for left in lefts], 0
            ins += [
                (left, (depth, count), lambda i, index=index: (0, index)) for left in lefts
            ]
            ins += [whole(rows) for rows, _ in adds]
            outs.append(((count, columns), BF16, (count, columns), lambda i: (0, 0)))
            layout.append([place for _, place in adds])
        return call(
            functools.partial(rows_kernel, len(self.rights), layout), (1,), ins, outs
        )

    def ring(self, axis, part, first):
        arrived = None
        for step in range(1, lax.axis_size(axis)):
            sent = first if step == 1 else self.rows(part(step, arrived))[0]
            arrived = lax.ppermute(sent, axis, forward(axis))
        return arrived

    def one(self, distance, arrived):
        count = (self.dp - 1) * self.half
        return (self.at_one + (distance - 1) * count, count, [(arrived, 0)])

    def two(self, distance, arrived):
        count = (self.inner - 1) * self.half
        return (self.at_two + (distance - 1) * count, count, [(arrived, 0)])

    def far(self):
        return self.rows(self.one(1, None), self.two(1, None))

    def send_far(self, firsts):
        return (
            self.ring("inner", self.one, firsts[0]), self.ring("dp", self.two, firsts[1])
        )

    def along(self, start, distance, arrived, extra, place):
        count = 2 * self.half
        extra = extra[(distance - 1) * self.half : distance * self.half]
        return (start + (distance - 1) * count, count, [(arrived, 0), (extra, place)])

    def along_x(self, distance, arrived):
        return self.along(self.at_x, distance, arrived, self.sums[1], self.half)

    def along_y(self, distance, arrived):
        return self.along(self.at_y, distance, arrived, self.sums[0], 0)

    def near(self, sums):
        self.sums = sums
        return self.rows(self.along_x(1, None), self.along_y(1, None))

    def send_near(self, firsts):
        return (
            self.ring("inner", self.along_x, firsts[0]),
            self.ring("dp", self.along_y, firsts[1]),
        )

    def own(self, nears):
        return self.rows((0, 2 * self.half, [(near, 0) for near in nears]))[0]

    def cut(self, own, distance):
        return own[distance * self.shard : (distance + 1) * self.shard]

    def send_direct(self, own):
        return [
            lax.ppermute(
                self.cut(own, distance), "outer", forward("outer", self.outer - distance)
            )
            for distance in range(1, self.outer)
        ]

    def total(self, own, arrived):
        total = sum([piece.astype(F32) for piece in arrived], self.cut(own, 0).astype(F32))
        return total.reshape(2, self.shard // 2, -1)


def both_halves(total):
    core = lax.axis_index("core")
    mine = lax.dynamic_index_in_dim(total, core, 0, keepdims=False)
    other = swap(lax.dynamic_index_in_dim(total, 1 - core, 0, keepdims=False))
    return (
        jnp.where(core == 0, mine, other),
        jnp.where(core == 0, other, mine),
    )


def normalise(values):
    centred = values - jnp.mean(values, -1, keepdims=True)
    scale = lax.rsqrt(jnp.mean(centred * centred, -1, keepdims=True) + NORM_EPSILON)
    return centred * scale, scale


def norm_back(unit, scale, gain, incoming):
    grad = incoming * gain
    return scale * (
        grad
        - jnp.mean(grad, -1, keepdims=True)
        - unit * jnp.mean(grad * unit, -1, keepdims=True)
    )


def piece_matmul(left, pieces):
    total, start = None, 0
    for piece in pieces:
        part = matmul(left[:, start : start + piece.shape[0]], piece[...])
        total = part if total is None else total + part
        start += piece.shape[0]
    return total


def back_kernel(starts, count, *refs):
    grads, pieces, out_refs = refs[: len(starts)], refs[len(starts) : count], refs[count:]
    at = 0
    for piece in pieces:
        total = None
        for grad, start in zip(grads, starts):
            part = contract_cols(grad[...], piece[:, start : start + grad.shape[1]])
            total = part if total is None else total + part
        for out_ref in out_refs:
            out_ref[:, at : at + piece.shape[0]] = total.astype(out_ref.dtype)
        at += piece.shape[0]


def back_project(grads, pieces, kinds):
    rows = grads[0].shape[0]
    block = rows // 2
    starts, end = [], 0
    for grad in grads:
        starts.append(end)
        end += grad.shape[1]
    width = sum(piece.shape[0] for piece in pieces)
    return call(
        functools.partial(back_kernel, starts, len(grads) + len(pieces)),
        (2,),
        [(grad, (block, grad.shape[1]), lambda i: (i, 0)) for grad in grads]
        + [(piece, (piece.shape[0], end), lambda i: (0, 0)) for piece in pieces],
        [((rows, width), kind, (block, width), lambda i: (i, 0)) for kind in kinds],
    )


def turned(values):
    width = values.shape[-1]
    lane = lax.broadcasted_iota(jnp.int32, values.shape, values.ndim - 1)
    ahead = pltpu.roll(values, width - HD // 2, values.ndim - 1)
    behind = pltpu.roll(values, HD // 2, values.ndim - 1)
    return jnp.where(lane % HD < HD // 2, ahead, behind)


def project_kernel(count, x_ref, cos_ref, sin_ref, *refs):
    gains, weights = refs[:count], refs[count : 2 * count]
    out_ref, norm_ref, gain_ref = refs[2 * count :]

    @pl.when(pl.program_id(0) == 0)
    def _():
        pick = lax.broadcasted_iota(jnp.int32, (8, LANES), 0) == lax.broadcasted_iota(
            jnp.int32, (8, LANES), 1
        )
        pick = pick.astype(F32).astype(BF16)
        start = 0
        for piece in gains:
            gain_ref[:, start : start + piece.shape[0]] = contract_cols(pick, piece[...])
            start += piece.shape[0]
        unit, _ = normalise(x_ref[...].astype(F32))
        norm_ref[...] = (unit * gain_ref[0:1, :]).astype(BF16)

    values = piece_matmul(norm_ref, weights)
    keep = pl.program_id(0) == 2
    length = cos_ref.shape[0]
    for top in range(0, values.shape[0], length):
        for left in range(0, values.shape[1], LANES):
            part = values[top : top + length, left : left + LANES]
            rotated = part * cos_ref[...] + turned(part) * sin_ref[...]
            out_ref[top : top + length, left : left + LANES] = jnp.where(
                keep, part, rotated
            ).astype(BF16)


def project(tokens, pieces, cosine, sine, side):
    rows, width = tokens.shape
    gain_block = 3 * side // LANES
    return call(
        functools.partial(project_kernel, len(pieces)),
        (3,),
        [whole(tokens), whole(cosine), whole(sine)]
        + [(piece, (piece.shape[0], LANES), lambda j: (0, gain_block)) for piece in pieces]
        + [(piece, (piece.shape[0], side), lambda j: (0, j)) for piece in pieces],
        [
            ((rows, 3 * side), BF16, (rows, side), lambda j: (0, j)),
            ((rows, width), BF16, (rows, width), lambda j: (0, 0)),
            ((8, width), F32, (8, width), lambda j: (0, 0)),
        ],
    )


def head_masks():
    lane = lax.broadcasted_iota(jnp.int32, (1, LANES), 1)
    return [(lane // HD == head).astype(F32).astype(BF16) for head in range(LANES // HD)]


def block_mask(query_ids, key_ids):
    rows, width = query_ids.shape[0], key_ids.shape[1]
    offset = lax.broadcasted_iota(jnp.int32, (rows, width), 1) - lax.broadcasted_iota(
        jnp.int32, (rows, width), 0
    )
    return (offset >= 0) & (offset <= 2 * HALF) & (query_ids == key_ids)


def block_probs(query, keys, allowed):
    scores = jnp.where(allowed, contract_cols(query, keys) * HD**-0.5, -1e30)
    grown = jnp.exp(scores - jnp.max(scores, -1, keepdims=True))
    return grown / jnp.sum(grown, -1, keepdims=True)


def attend_kernel(block, q_ref, k_ref, v_ref, qid_ref, kid_ref, out_ref):
    masks = head_masks()
    for start in range(0, out_ref.shape[1], block):
        span = slice(start, start + block + 2 * HALF)
        allowed = block_mask(qid_ref[0, start : start + block], kid_ref[0, :, span])
        query = q_ref[0, HALF + start : HALF + start + block]
        total = None
        for mask in masks:
            probs = block_probs(query * mask, k_ref[0, span], allowed)
            part = matmul(probs.astype(BF16), v_ref[0, span]) * mask.astype(F32)
            total = part if total is None else total + part
        out_ref[0, start : start + block] = total.astype(BF16)


def attend_back_kernel(
    block, q_ref, k_ref, v_ref, qid_ref, kid_ref, grad_ref, cos_ref, sin_ref,
    dq_ref, mid_ref, low_ref, high_ref,
):
    masks = head_masks()
    length = dq_ref.shape[1]
    grad_keys = grad_values = jnp.zeros((length + 2 * HALF, LANES), F32)
    for start in range(0, length, block):
        span = slice(start, start + block + 2 * HALF)
        mid = slice(HALF + start, HALF + start + block)
        rows = slice(start, start + block)
        allowed = block_mask(qid_ref[0, rows], kid_ref[0, :, span])
        query_all, grad_all = q_ref[0, mid], grad_ref[0, rows]
        keys, values = k_ref[0, span], v_ref[0, span]
        grad_query, part_keys, part_values = 0.0, 0.0, 0.0
        for mask in masks:
            query, grad = query_all * mask, grad_all * mask
            probs = block_probs(query, keys, allowed)
            grad_probs = contract_cols(grad, values)
            delta = jnp.sum(probs * grad_probs, -1, keepdims=True)
            grad_scores = (probs * (grad_probs - delta)).astype(BF16)
            grad_query += matmul(grad_scores, keys) * mask.astype(F32)
            part_keys += contract_rows(grad_scores, query)
            part_values += contract_rows(probs.astype(BF16), grad)
        grad_query = grad_query * HD**-0.5
        dq_ref[0, rows] = (
            grad_query * cos_ref[mid] - turned(grad_query) * sin_ref[mid]
        ).astype(BF16)
        before, after = start, length - start - block

        def placed(part):
            pieces = [part]
            if before:
                pieces.insert(0, jnp.zeros((before, LANES), F32))
            if after:
                pieces.append(jnp.zeros((after, LANES), F32))
            return jnp.concatenate(pieces, 0)

        grad_keys += placed(part_keys)
        grad_values += placed(part_values)
    for index, total in enumerate((grad_keys * HD**-0.5, grad_values)):
        low_ref[0, index] = total[:HALF].astype(BF16)
        mid_ref[0, index] = total[HALF : HALF + length]
        high_ref[0, index] = total[HALF + length :].astype(BF16)


def attention_inputs(joined, query_ids, key_ids):
    window, groups = joined.shape[1], joined.shape[2] // 3 // LANES
    inputs = [
        (joined, (1, window, LANES), lambda s, h, shift=shift: (s, 0, h + shift))
        for shift in (0, groups, 2 * groups)
    ]
    inputs += [
        (ids, (1,) + ids.shape[1:], lambda s, h: (s, 0, 0)) for ids in (query_ids, key_ids)
    ]
    return inputs


def attend(block, joined, query_ids, key_ids):
    streams, window, columns = joined.shape
    length, side = window - 2 * HALF, columns // 3
    return call(
        functools.partial(attend_kernel, block),
        (streams, side // LANES),
        attention_inputs(joined, query_ids, key_ids),
        [((streams, length, side), BF16, (1, length, LANES), lambda s, h: (s, 0, h))],
        limit=24,
    )[0]


def attend_back(block, joined, query_ids, key_ids, grad, cosine, sine):
    streams, length, side = grad.shape

    def pair(rows, kind):
        return (
            (streams, 2, rows, side), kind, (1, 2, rows, LANES), lambda s, h: (s, 0, 0, h)
        )

    return call(
        functools.partial(attend_back_kernel, block),
        (streams, side // LANES),
        attention_inputs(joined, query_ids, key_ids)
        + [(grad, (1, length, LANES), lambda s, h: (s, 0, h)), whole(cosine), whole(sine)],
        [
            ((streams, length, side), BF16, (1, length, LANES), lambda s, h: (s, 0, h)),
            pair(length, F32),
            pair(HALF, BF16),
            pair(HALF, BF16),
        ],
        limit=24,
    )


def join_kernel(dq_ref, mid_ref, low_ref, high_ref, cos_ref, sin_ref, out_ref):
    length, width = dq_ref.shape[1:]
    out_ref[0, :, :width] = dq_ref[0]
    cosine, sine = cos_ref[HALF : HALF + length], sin_ref[HALF : HALF + length]
    for index in range(2):
        for start in range(0, width, LANES):
            lanes = slice(start, start + LANES)
            total = mid_ref[0, index, :, lanes]
            total = total + jnp.concatenate(
                [
                    low_ref[0, index, :, lanes].astype(F32),
                    jnp.zeros((length - 2 * HALF, LANES), F32),
                    high_ref[0, index, :, lanes].astype(F32),
                ],
                0,
            )
            if index == 0:
                total = total * cosine - turned(total) * sine
            to = (1 + index) * width + start
            out_ref[0, :, to : to + LANES] = total.astype(BF16)


def join_grads(grad_query, mid, from_lower, from_upper, cosine, sine):
    streams, length, width = grad_query.shape

    def of_stream(array):
        block = (1,) + array.shape[1:]
        return (array, block, lambda s: (s,) + (0,) * (array.ndim - 1))

    return call(
        join_kernel,
        (streams,),
        [of_stream(array) for array in (grad_query, mid, from_lower, from_upper)]
        + [whole(cosine), whole(sine)],
        [((streams, length, 3 * width), BF16, (1, length, 3 * width), lambda s: (s, 0, 0))],
        limit=24,
    )[0]


def by_rows(array, block):
    return (array, (block, array.shape[1]), lambda i: (i, 0))


def weight_kernel(count, other_ref, own_order_ref, other_order_ref, *refs):
    start = 0
    out_ref = refs[count]
    for piece in refs[:count]:
        span = slice(start, start + piece.shape[0])
        total = matmul(piece[...], own_order_ref[...])
        total = total + matmul(other_ref[span, :], other_order_ref[...])
        out_ref[span, :] = total.astype(BF16)
        start = span.stop


def out_weight(pieces, own, other, own_order, other_order):
    side, width = own_order.shape
    if len(pieces) == 1:
        own_pieces = [(own, own.shape, lambda i: (0, 0))]
    else:
        own_pieces, start = [], 0
        for piece in pieces:
            count = piece.shape[0]
            own_pieces.append(
                (own, (count, side), lambda i, index=start // count: (index, 0))
            )
            start += count
    return call(
        functools.partial(weight_kernel, len(own_pieces)),
        (1,),
        [whole(other), whole(own_order), whole(other_order)] + own_pieces,
        [((width, width), BF16, (width, width), lambda i: (0, 0))],
    )[0]


def out_kernel(
    own_ref, other_ref, own_order_ref, other_order_ref, weight_ref, x_ref, gain_ref,
    att_ref, hidden_ref, norm_ref,
):
    attended = matmul(own_ref[...], own_order_ref[...])
    attended = (attended + matmul(other_ref[...], other_order_ref[...])).astype(BF16)
    att_ref[...] = attended
    hidden = x_ref[...].astype(F32) + matmul(attended, weight_ref[...])
    hidden_ref[...] = hidden
    norm_ref[...] = (normalise(hidden)[0] * gain_ref[1:2, :]).astype(BF16)


def out_project(own, other, own_order, other_order, weight, tokens, gains):
    rows, width = tokens.shape
    block = rows // 2
    return call(
        out_kernel,
        (2,),
        [by_rows(own, block), by_rows(other, block), whole(own_order), whole(other_order)]
        + [whole(weight), by_rows(tokens, block), whole(gains)],
        [
            ((rows, width), kind, (block, width), lambda i: (i, 0))
            for kind in (BF16, F32, BF16)
        ],
    )


def hidden_back_kernel(
    part_ref, other_ref, hidden_ref, g_ref, gain_ref, weight_ref, order_ref,
    grad_ref, side_ref, att_ref,
):
    unit, scale = normalise(hidden_ref[...])
    incoming = part_ref[...] + other_ref[...].astype(F32)
    grad = g_ref[...].astype(F32) + norm_back(unit, scale, gain_ref[1:2, :], incoming)
    low = grad.astype(BF16)
    grad_ref[...] = grad
    side_ref[...] = contract_cols(low, order_ref[...]).astype(BF16)
    attended = contract_cols(low, weight_ref[...]).astype(BF16)
    att_ref[...] = contract_cols(attended, order_ref[...]).astype(BF16)


def hidden_back(part, other, hidden, grad_output, gains, weight, own_order):
    rows, width = hidden.shape
    block, side = rows // 2, own_order.shape[0]
    return call(
        hidden_back_kernel,
        (2,),
        [by_rows(array, block) for array in (part, other, hidden, grad_output)]
        + [whole(gains), whole(weight), whole(own_order)],
        [
            ((rows, size), kind, (block, size), lambda i: (i, 0))
            for size, kind in ((width, F32), (side, BF16), (side, BF16))
        ],
    )


def column_spans(width):
    return [slice(at, min(at + 2 * LANES, width)) for at in range(0, width, 2 * LANES)]


def tile_matmul(left, pieces, columns):
    total, start = None, 0
    for piece in pieces:
        part = matmul(left[:, start : start + piece.shape[0]], piece[:, columns])
        total = part if total is None else total + part
        start += piece.shape[0]
    return total


def feed_kernel(norm_ref, *refs):
    pieces, (mixed_ref, factor_ref, active_ref) = refs[:-3], refs[-3:]
    units = mixed_ref.shape[1]
    for span in column_spans(units):
        gate = tile_matmul(norm_ref, pieces, span)
        up = tile_matmul(norm_ref, pieces, slice(units + span.start, units + span.stop))
        below = 0.5 * (1.0 + lax.erf(gate * 0.5**0.5))
        active = gate * below
        mixed_ref[:, span] = (active * up).astype(BF16)
        active_ref[:, span] = active
        density = jnp.exp(-0.5 * gate * gate) * (2.0 * np.pi) ** -0.5
        factor_ref[:, span] = up * (below + gate * density)


def feed(normed, pieces, units):
    rows = normed.shape[0]
    block = rows // 2
    return call(
        feed_kernel,
        (2,),
        [by_rows(normed, block)] + [whole(piece) for piece in pieces],
        [
            ((rows, units), kind, (block, units), lambda i: (i, 0))
            for kind in (BF16, F32, F32)
        ],
    )


def feed_back_kernel(g_ref, factor_ref, active_ref, *refs):
    pieces, (gate_ref, up_ref) = refs[:-2], refs[-2:]
    for span in column_spans(factor_ref.shape[1]):
        grad = tile_matmul(g_ref, pieces, span)
        gate_ref[:, span] = (grad * factor_ref[:, span]).astype(BF16)
        up_ref[:, span] = (grad * active_ref[:, span]).astype(BF16)


def feed_back(grad_output, factor, active, pieces):
    rows, units = factor.shape
    block = rows // 2
    return call(
        feed_back_kernel,
        (2,),
        [by_rows(array, block) for array in (grad_output, factor, active)]
        + [whole(piece) for piece in pieces],
        [((rows, units), BF16, (block, units), lambda i: (i, 0)) for _ in range(2)],
    )


def shards(tokens, doc_ids, norm_attn, norm_mlp, w_qkv, w_out, w_in, w_down, cotangent):
    streams, block, width = tokens.shape
    shard_rows = w_qkv.shape[0]
    inner, outer = lax.axis_size("inner"), lax.axis_size("outer")
    core = lax.axis_index("core")
    length = 2 * block
    window = length + 2 * HALF
    rows = streams * length
    side = width // 2
    units = w_down.shape[1] // 2
    padded = -(-units // LANES) * LANES
    chips = outer * inner
    onward = [(i, i + 1) for i in range(chips - 1)]
    back = [(i + 1, i) for i in range(chips - 1)]

    def halves(weight, parts, pad):
        size = weight.shape[1] // (2 * parts)
        cut = [weight[:, i * size : (i + 1) * size] for i in range(2 * parts)]
        if pad != size:
            cut = [jnp.pad(piece, ((0, 0), (0, pad - size))) for piece in cut]
        return cut[0::2], cut[1::2]

    def paired(pieces):
        low = jnp.concatenate([piece for one, _ in pieces for piece in one], 1)
        high = jnp.concatenate([piece for _, two in pieces for piece in two], 1)
        mine = jnp.where(core == 0, low, high)
        return ordered(mine, swap(jnp.where(core == 0, high, low)), 0)

    pair_tokens = ordered(tokens, swap(tokens), 1)

    gains = jnp.pad(jnp.stack([norm_attn, norm_mlp], 1), ((0, 0), (0, LANES - 2)))
    pair_one = paired([halves(w_qkv, 3, side), ([gains], [gains]), halves(w_out, 1, side)])
    later_in, later_down, pair_one, pair_tokens = tied(w_in, w_down, pair_one, pair_tokens)
    low = lax.ppermute(pair_tokens[:, length - HALF :], ("outer", "inner"), onward)
    high = lax.ppermute(pair_tokens[:, :HALF], ("outer", "inner"), back)
    one = direct_sends(pair_one)
    pair_two = paired([halves(later_in, 2, padded)])
    pair_three = paired([halves(later_down, 1, padded)])
    pair_two, one, low, high, pair_tokens = tied(pair_two, one, low, high, pair_tokens)
    two = direct_sends(pair_two)
    near = gather_near(one)
    order = arrival_order(width, shard_rows)

    def in_order(value):
        return matmul(value, order).astype(BF16)

    window_tokens = jnp.concatenate([low, pair_tokens, high], 1).reshape(-1, width)
    window_tokens = in_order(window_tokens)
    own_tokens = window_tokens.reshape(streams, window, width)[:, HALF : HALF + length]
    own_tokens = own_tokens.reshape(rows, width)
    grad_output = in_order(ordered(cotangent, swap(cotangent), 1).reshape(rows, width))

    start = lax.axis_index(("outer", "inner")) * length
    positions = (start - HALF + jnp.arange(window, dtype=jnp.int32)).astype(F32)
    frequency = ROPE_BASE ** (-(jnp.arange(HD // 2, dtype=F32) * 2.0 / HD))
    angles = positions[:, None] * frequency[None, :]
    cosine, sine = jnp.cos(angles), jnp.sin(angles)
    cosine = jnp.tile(cosine, (1, LANES // (HD // 2)))
    sine = jnp.tile(jnp.concatenate([-sine, sine], 1), (1, LANES // HD))
    ids_padded = jnp.pad(doc_ids, ((0, 0), (HALF, HALF)), constant_values=-1)
    key_ids = lax.dynamic_slice_in_dim(ids_padded, start, window, 1)[:, None, :]
    query_ids = lax.dynamic_slice_in_dim(doc_ids, start, length, 1)[:, :, None]

    own_order = lax.dynamic_slice_in_dim(order, core * side, side, 0)
    other_order = lax.dynamic_slice_in_dim(order, (1 - core) * side, side, 0)
    prepared = (window_tokens, own_tokens, grad_output, order, own_order, other_order)
    prepared += (cosine, sine, key_ids, query_ids, pair_three)
    prepared, two, near = tied(prepared, two, near)
    window_tokens, own_tokens, grad_output, order, own_order, other_order = prepared[:6]
    cosine, sine, key_ids, query_ids, pair_three = prepared[6:]

    far = gather_far(*near)
    two_near = gather_near(two)
    three = direct_sends(pair_three)
    first = in_pieces(*near, *far)
    joined, window_norm, gain_rows = project(window_tokens, first, cosine, sine, side)
    out_half = joined_rows([piece[:, 3 * side + LANES :] for piece in first])
    weight = out_weight(first, out_half, swap(out_half), own_order, other_order)
    joined, weight, first, two_near, three = tied(joined, weight, first, two_near, three)

    two_far = gather_far(*two_near)
    joined = joined.reshape(streams, window, 3 * side)
    attended = attend(block, joined, query_ids, key_ids).reshape(rows, side)
    attended_other = swap(attended)
    attended, attended_other, two_near, two_far = tied(
        attended, attended_other, two_near, two_far
    )
    in_half = in_pieces(*two_near, *two_far)

    three_near = gather_near(three)
    attended_low, hidden, normed_mlp_low = out_project(
        attended, attended_other, own_order, other_order, weight, own_tokens, gain_rows
    )
    hidden, normed_mlp_low, three_near = tied(hidden, normed_mlp_low, three_near)

    three_far = gather_far(*three_near)
    mixed_low, factor, active = feed(normed_mlp_low, in_half, padded)
    mixed_low, factor, active, three_near, three_far = tied(
        mixed_low, factor, active, three_near, three_far
    )
    down_half = in_pieces(*three_near, *three_far)

    sum_down = GradSum([grad_output], [mixed_low], shard_rows)
    down_far = sum_down.send_far(sum_down.far())
    grad_gate, grad_up = feed_back(grad_output, factor, active, down_half)
    grad_gate, grad_up, down_far = tied(grad_gate, grad_up, down_far)

    sum_in = GradSum([normed_mlp_low] * 2, [grad_gate, grad_up], shard_rows)
    down_near = sum_down.send_near(sum_down.near(down_far))
    sent_in = sum_in.far()
    part, part_low = back_project([grad_gate, grad_up], in_half, [F32, BF16])
    part, part_low, down_near, sent_in = tied(part, part_low, down_near, sent_in)

    in_far = sum_in.send_far(sent_in)
    down_own = sum_down.own(down_near)
    down_arrived = sum_down.send_direct(down_own)
    grad_hidden, hidden_side, grad_attended = hidden_back(
        part, swap(part_low), hidden, grad_output, gain_rows, weight, own_order
    )
    grad_attended, in_far, down_arrived = tied(grad_attended, in_far, down_arrived)

    in_near = sum_in.send_near(sum_in.near(in_far))
    grad_query, mid, to_lower, to_upper = attend_back(
        block, joined, query_ids, key_ids, grad_attended.reshape(streams, length, side),
        cosine, sine,
    )
    from_lower = lax.ppermute(to_upper, ("outer", "inner"), onward)
    from_upper = lax.ppermute(to_lower, ("outer", "inner"), back)
    from_lower, from_upper, in_near = tied(from_lower, from_upper, in_near)

    grad_joined = join_grads(grad_query, mid, from_lower, from_upper, cosine, sine)
    grad_joined = grad_joined.reshape(rows, 3 * side)
    normed_low = window_norm.reshape(streams, window, width)[:, HALF : HALF + length]
    sum_attn = GradSum(
        [normed_low.reshape(rows, width), attended_low], [grad_joined, hidden_side], shard_rows
    )
    sent_attn, in_own = sum_attn.far(), sum_in.own(in_near)
    sent_attn, in_own, grad_joined = tied(sent_attn, in_own, grad_joined)

    attn_far = sum_attn.send_far(sent_attn)
    attn_far, grad_joined, mixed_low, grad_hidden, hidden = tied(
        attn_far, grad_joined, mixed_low, grad_hidden, hidden
    )
    in_arrived = sum_in.send_direct(in_own)
    attn_near = sum_attn.send_near(sum_attn.near(attn_far))

    def own_rows(value):
        value = value.reshape(streams, 2, block, width)
        mine = lax.dynamic_index_in_dim(value, core, 1, keepdims=False)
        other = lax.dynamic_index_in_dim(value, 1 - core, 1, keepdims=False)
        return mine, other

    def summed_rows(partial):
        mine, other = own_rows(partial)
        return mine + swap(other.astype(BF16)).astype(F32)

    (out_part,) = back_project([mixed_low], down_half, [F32])
    output = own_rows(hidden)[0] + summed_rows(out_part)
    output = contract_cols(output.astype(BF16).reshape(-1, width), order)
    output = output.astype(BF16).reshape(tokens.shape)

    (norm_part,) = back_project([grad_joined], first, [F32])
    grad_normed = summed_rows(norm_part)
    unit, scale = normalise(own_rows(own_tokens)[0].astype(F32))
    grad_tokens = own_rows(grad_hidden)[0] + norm_back(unit, scale, gain_rows[0], grad_normed)
    grad_tokens = lax.dot_general(
        grad_tokens.reshape(-1, width),
        order.astype(F32),
        (((1,), (1,)), ((), ())),
        precision=lax.Precision.HIGHEST,
        preferred_element_type=F32,
    ).reshape(tokens.shape)

    attn_near, in_arrived = tied(attn_near, in_arrived)
    attn_own = sum_attn.own(attn_near)
    attn_total = sum_attn.total(attn_own, sum_attn.send_direct(attn_own))
    down_total = sum_down.total(down_own, down_arrived)
    in_total = sum_in.total(in_own, in_arrived)

    def interleaved(pair, start, parts, stride, size):
        cuts = []
        for i in range(parts):
            first_column = start + i * stride
            cuts += [half[:, first_column : first_column + size] for half in pair]
        return jnp.concatenate(cuts, 1)

    grad_down = interleaved(both_halves(down_total), 0, 1, padded, units)
    grad_in = interleaved(both_halves(in_total), 0, 2, padded, units)
    pair = both_halves(attn_total)
    grad_qkv = interleaved(pair, 0, 3, side, side)
    grad_out = interleaved(pair, 3 * side, 1, side, side)

    def gain_grad(weight, grad, gain):
        return jnp.sum(weight.astype(F32) * grad, -1) / gain.astype(F32)

    return (
        output,
        grad_tokens,
        gain_grad(w_qkv, grad_qkv, norm_attn),
        gain_grad(w_in, grad_in, norm_mlp),
        grad_qkv,
        grad_out,
        grad_in,
        grad_down,
    )


def solution(mesh):
    dp, seq = mesh.shape["dp"], mesh.shape["seq"]
    chips = seq // 2
    outer = 4 if chips % 4 == 0 else 1
    fine = Mesh(
        mesh.devices.reshape(dp, outer, chips // outer, 2), ("dp", "outer", "inner", "core")
    )
    line = ("outer", "inner", "core")
    every = ("dp",) + line
    token = P("dp", line, None)
    vector = P(every)
    matrix = P(every, None)
    return jax.shard_map(
        shards,
        mesh=fine,
        in_specs=(token, P("dp", None), vector, vector, matrix, matrix, matrix, matrix, token),
        out_specs=(token, token, vector, vector, matrix, matrix, matrix, matrix),
        check_vma=False,
    )
```

```python
import functools

import jax
import jax.numpy as jnp
import numpy as np
from jax import lax
from jax.experimental import pallas as pl
from jax.experimental.pallas import tpu as pltpu
from jax.sharding import Mesh, PartitionSpec as P

HD = 64
HALF = 64
LANES = 128
NORM_EPSILON = 1e-05
ROPE_BASE = 10000.0
F32 = jnp.float32
BF16 = jnp.bfloat16


def contract_cols(left, right):
    return lax.dot_general(left, right, (((1,), (1,)), ((), ())), preferred_element_type=F32)


def contract_rows(left, right):
    return lax.dot_general(left, right, (((0,), (0,)), ((), ())), preferred_element_type=F32)


def matmul(left, right):
    return jnp.dot(left, right, preferred_element_type=F32)


def tied(*values):
    return lax.optimization_barrier(values)


def call(kernel, grid, ins, outs, scratch=(), limit=40):
    out = pl.pallas_call(
        kernel,
        grid=grid,
        in_specs=[
            pl.BlockSpec(memory_space=pltpu.SMEM) if block is None else pl.BlockSpec(block, index)
            for _, block, index in ins
        ],
        out_specs=[pl.BlockSpec(block, index) for _, _, block, index in outs],
        out_shape=[jax.ShapeDtypeStruct(shape, kind) for shape, kind, _, _ in outs],
        scratch_shapes=list(scratch),
        compiler_params=pltpu.CompilerParams(vmem_limit_bytes=limit * 2**20),
        cost_estimate=pl.CostEstimate(flops=1024, bytes_accessed=1024, transcendentals=0),
    )(*[array for array, _, _ in ins])
    return out


def whole(array):
    return (array, array.shape, lambda *_: (0,) * array.ndim)


def swap(value):
    return lax.ppermute(value, "core", [(0, 1), (1, 0)])


def ordered(mine, other, axis):
    first = lax.axis_index("core") == 0
    return jnp.concatenate(
        [jnp.where(first, mine, other), jnp.where(first, other, mine)], axis=axis
    )


def forward(axis, distance=1):
    count = lax.axis_size(axis)
    return [(i, (i + distance) % count) for i in range(count)]


def ring_gather(axis, piece):
    pieces = [piece]
    for _ in range(1, lax.axis_size(axis)):
        pieces.append(lax.ppermute(pieces[-1], axis, forward(axis)))
    return pieces[1:]


def direct_sends(rows):
    return [rows] + [
        lax.ppermute(rows, "outer", forward("outer", distance))
        for distance in range(1, lax.axis_size("outer"))
    ]


def joined_rows(pieces):
    return jnp.concatenate(pieces, 0) if len(pieces) > 1 else pieces[0]


def gather_near(arrived):
    own = joined_rows(arrived)
    return own, ring_gather("inner", own), ring_gather("dp", own)


def gather_far(own, along_x, along_y):
    half = own.shape[0] // 2
    one = ring_gather("inner", joined_rows([piece[:half] for piece in along_y]))
    two = ring_gather("dp", joined_rows([piece[half:] for piece in along_x]))
    return one, two


def in_pieces(own, along_x, along_y, one, two):
    pieces = [own, *along_x, *along_y, *one, *two]
    if any(piece.shape[0] % LANES for piece in pieces):
        pieces = [joined_rows(pieces)]
    return pieces


def arrival_order(width, shard_rows):
    inner, outer, dp = (lax.axis_size(name) for name in ("inner", "outer", "dp"))
    x, z, y = (lax.axis_index(name) for name in ("inner", "outer", "dp"))
    half = outer * shard_rows
    blocks = [(0, 0, 0, 2)]
    blocks += [(d, 0, 0, 2) for d in range(1, inner)] + [(0, d, 0, 2) for d in range(1, dp)]
    blocks += [(d, e, 0, 1) for d in range(1, inner) for e in range(1, dp)]
    blocks += [(d, e, 1, 2) for e in range(1, dp) for d in range(1, inner)]
    place = np.concatenate([np.arange(low * half, high * half) for _, _, low, high in blocks])
    sizes = [(high - low) * half for _, _, low, high in blocks]
    along_x = np.repeat([block[0] for block in blocks], sizes)
    along_y = np.repeat([block[1] for block in blocks], sizes)
    along_z, row = place // (2 * shard_rows), place % (2 * shard_rows)
    at_x = (x - jnp.asarray(along_x, jnp.int32) + inner) % inner
    at_y = (y - jnp.asarray(along_y, jnp.int32) + dp) % dp
    at_z = (z - jnp.asarray(along_z, jnp.int32) + outer) % outer
    source = ((at_y * outer + at_z) * inner + at_x) * 2 * shard_rows + row
    return (jnp.arange(width, dtype=jnp.int32)[:, None] == source[None, :]).astype(BF16)


def rows_kernel(pairs, layout, *refs):
    rights, refs = refs[:pairs], refs[pairs:]
    inputs, outs = refs[: -len(layout)], refs[-len(layout) :]
    for places, out_ref in zip(layout, outs):
        lefts, adds = inputs[:pairs], inputs[pairs : pairs + len(places)]
        inputs = inputs[pairs + len(places) :]
        start = 0
        for left, right in zip(lefts, rights):
            columns = slice(start, start + right.shape[1])
            start = columns.stop
            total = contract_rows(left[...], right[...])
            for add in adds:
                if add.shape[0] == total.shape[0]:
                    total = total + add[:, columns].astype(F32)
            out_ref[:, columns] = total.astype(BF16)
            for add, at in zip(adds, places):
                if add.shape[0] != total.shape[0]:
                    span = slice(at, at + add.shape[0])
                    part = total[span] + add[:, columns].astype(F32)
                    out_ref[span, columns] = part.astype(BF16)


class GradSum:
    def __init__(self, lefts, rights, shard_rows):
        self.lefts, self.rights = lefts, rights
        self.inner, self.outer, self.dp = (
            lax.axis_size(name) for name in ("inner", "outer", "dp")
        )
        self.shard = 2 * shard_rows
        self.half = self.outer * shard_rows
        self.at_x = 2 * self.half
        self.at_y = self.at_x + (self.inner - 1) * 2 * self.half
        self.at_one = self.at_y + (self.dp - 1) * 2 * self.half
        self.at_two = self.at_one + (self.inner - 1) * (self.dp - 1) * self.half

    def rows(self, *parts):
        depth = self.lefts[0].shape[0]
        columns = sum(right.shape[1] for right in self.rights)
        ins, outs, layout = [whole(right) for right in self.rights], [], []
        for start, count, adds in parts:
            adds = [(rows, place) for rows, place in adds if rows is not None]
            lefts, index = self.lefts, start // count
            if count % LANES or start % count:
                lefts, index = [left[:, start : start + count] for left in lefts], 0
            ins += [
                (left, (depth, count), lambda i, index=index: (0, index)) for left in lefts
            ]
            ins += [whole(rows) for rows, _ in adds]
            outs.append(((count, columns), BF16, (count, columns), lambda i: (0, 0)))
            layout.append([place for _, place in adds])
        return call(
            functools.partial(rows_kernel, len(self.rights), layout), (1,), ins, outs
        )

    def ring(self, axis, part, first):
        arrived = None
        for step in range(1, lax.axis_size(axis)):
            sent = first if step == 1 else self.rows(part(step, arrived))[0]
            arrived = lax.ppermute(sent, axis, forward(axis))
        return arrived

    def one(self, distance, arrived):
        count = (self.dp - 1) * self.half
        return (self.at_one + (distance - 1) * count, count, [(arrived, 0)])

    def two(self, distance, arrived):
        count = (self.inner - 1) * self.half
        return (self.at_two + (distance - 1) * count, count, [(arrived, 0)])

    def far(self):
        return self.rows(self.one(1, None), self.two(1, None))

    def send_far(self, firsts):
        return (
            self.ring("inner", self.one, firsts[0]), self.ring("dp", self.two, firsts[1])
        )

    def along(self, start, distance, arrived, extra, place):
        count = 2 * self.half
        extra = extra[(distance - 1) * self.half : distance * self.half]
        return (start + (distance - 1) * count, count, [(arrived, 0), (extra, place)])

    def along_x(self, distance, arrived):
        return self.along(self.at_x, distance, arrived, self.sums[1], self.half)

    def along_y(self, distance, arrived):
        return self.along(self.at_y, distance, arrived, self.sums[0], 0)

    def near(self, sums):
        self.sums = sums
        return self.rows(self.along_x(1, None), self.along_y(1, None))

    def send_near(self, firsts):
        return (
            self.ring("inner", self.along_x, firsts[0]),
            self.ring("dp", self.along_y, firsts[1]),
        )

    def own(self, nears):
        return self.rows((0, 2 * self.half, [(near, 0) for near in nears]))[0]

    def cut(self, own, distance):
        return own[distance * self.shard : (distance + 1) * self.shard]

    def send_direct(self, own):
        return [
            lax.ppermute(
                self.cut(own, distance), "outer", forward("outer", self.outer - distance)
            )
            for distance in range(1, self.outer)
        ]

    def total(self, core, own, arrived):
        columns = own.shape[1]
        half = self.shard // 2
        return call(
            total_kernel,
            (1,),
            [(core, None, None), (own, (self.shard, columns), lambda i: (0, 0))]
            + [whole(rows) for rows in arrived],
            [((half, columns), F32, (half, columns), lambda i: (0, 0)) for _ in range(2)],
        )


def own_half(core_ref, value):
    half = value.shape[0] // 2
    return jnp.where(core_ref[0] == 0, value[:half], value[half:])


def total_kernel(core_ref, *refs):
    total = None
    for ref in refs[:-2]:
        rows = ref[...].astype(F32)
        total = rows if total is None else total + rows
    half = total.shape[0] // 2
    first = core_ref[0] == 0
    refs[-2][...] = jnp.where(first, total[:half], total[half:])
    refs[-1][...] = jnp.where(first, total[half:], total[:half])


def assemble_kernel(layout, core_ref, mine_ref, other_ref, *refs):
    first = core_ref[0] == 0
    count = len(layout)
    pair = (
        jnp.where(first, mine_ref[...], other_ref[...]),
        jnp.where(first, other_ref[...], mine_ref[...]),
    )
    outs = refs[-count:] if len(refs) == count else refs[2:-1]
    for out_ref, (start, parts, stride, size) in zip(outs, layout):
        cuts = []
        for i in range(parts):
            at = start + i * stride
            cuts += [half[:, at : at + size] for half in pair]
        out_ref[...] = jnp.concatenate(cuts, 1)
    if len(refs) > count:
        weight_ref, gain_ref = refs[:2]
        product = weight_ref[...].astype(F32) * outs[0][...]
        refs[-1][...] = jnp.sum(product, -1, keepdims=True) / gain_ref[...].astype(F32)


def assemble(core, mine, other, layout, weight=None, gain=None):
    rows = mine.shape[0]
    ins = [(core, None, None), whole(mine), whole(other)]
    sizes = [2 * parts * size for _, parts, _, size in layout]
    if weight is not None:
        ins += [whole(weight), whole(gain.reshape(rows, 1))]
        sizes.append(1)
    return call(
        functools.partial(assemble_kernel, layout),
        (1,),
        ins,
        [((rows, size), F32, (rows, size), lambda i: (0, 0)) for size in sizes],
    )


def normalise(values):
    centred = values - jnp.mean(values, -1, keepdims=True)
    scale = lax.rsqrt(jnp.mean(centred * centred, -1, keepdims=True) + NORM_EPSILON)
    return centred * scale, scale


def norm_back(unit, scale, gain, incoming):
    grad = incoming * gain
    return scale * (
        grad
        - jnp.mean(grad, -1, keepdims=True)
        - unit * jnp.mean(grad * unit, -1, keepdims=True)
    )


def piece_matmul(left, pieces):
    total, start = None, 0
    for piece in pieces:
        part = matmul(left[:, start : start + piece.shape[0]], piece[...])
        total = part if total is None else total + part
        start += piece.shape[0]
    return total


def back_kernel(starts, count, *refs):
    grads, pieces, out_refs = refs[: len(starts)], refs[len(starts) : count], refs[count:]
    at = 0
    for piece in pieces:
        total = None
        for grad, start in zip(grads, starts):
            part = contract_cols(grad[...], piece[:, start : start + grad.shape[1]])
            total = part if total is None else total + part
        for out_ref in out_refs:
            out_ref[:, at : at + piece.shape[0]] = total.astype(out_ref.dtype)
        at += piece.shape[0]


def back_project(grads, pieces, kinds):
    rows = grads[0].shape[0]
    block = rows // 2
    starts, end = [], 0
    for grad in grads:
        starts.append(end)
        end += grad.shape[1]
    width = sum(piece.shape[0] for piece in pieces)
    return call(
        functools.partial(back_kernel, starts, len(grads) + len(pieces)),
        (2,),
        [(grad, (block, grad.shape[1]), lambda i: (i, 0)) for grad in grads]
        + [(piece, (piece.shape[0], end), lambda i: (0, 0)) for piece in pieces],
        [((rows, width), kind, (block, width), lambda i: (i, 0)) for kind in kinds],
    )


def split_kernel(core_ref, grad_ref, *refs):
    pieces, (mine_ref, other_ref) = refs[:-2], refs[-2:]
    width = grad_ref.shape[1]
    half = grad_ref.shape[0] // 2
    at = 0
    for piece in pieces:
        total = contract_cols(grad_ref[...], piece[:, :width])
        first = core_ref[0] == 0
        span = slice(at, at + piece.shape[0])
        mine_ref[:, span] = jnp.where(first, total[:half], total[half:])
        other_ref[:, span] = jnp.where(first, total[half:], total[:half]).astype(BF16)
        at = span.stop


def back_split(core, grad, pieces, streams):
    rows, columns = grad.shape
    block = rows // streams
    width = sum(piece.shape[0] for piece in pieces)
    return call(
        split_kernel,
        (streams,),
        [(core, None, None), (grad, (block, columns), lambda i: (i, 0))]
        + [(piece, (piece.shape[0], columns), lambda i: (0, 0)) for piece in pieces],
        [
            ((rows // 2, width), kind, (block // 2, width), lambda i: (i, 0))
            for kind in (F32, BF16)
        ],
    )


def output_kernel(core_ref, mine_ref, other_ref, hidden_ref, order_ref, out_ref):
    total = own_half(core_ref, hidden_ref[...]) + mine_ref[...] + other_ref[...].astype(F32)
    out_ref[...] = contract_cols(total.astype(BF16), order_ref[...]).astype(BF16)


def input_grad_kernel(
    core_ref, mine_ref, other_ref, hidden_ref, x_ref, gain_ref, order_ref, out_ref
):
    unit, scale = normalise(own_half(core_ref, x_ref[...].astype(F32)))
    incoming = mine_ref[...] + other_ref[...].astype(F32)
    total = own_half(core_ref, hidden_ref[...])
    total = total + norm_back(unit, scale, gain_ref[0:1, :], incoming)
    result = None
    for _ in range(3):
        part = total.astype(BF16)
        total = total - part.astype(F32)
        part = contract_cols(part, order_ref[...])
        result = part if result is None else result + part
    out_ref[...] = result


def end_rows(kernel, core, halves, fulls, wholes, kind, streams):
    rows, width = halves[0].shape
    block = rows // streams
    return call(
        kernel,
        (streams,),
        [(core, None, None)]
        + [(array, (block, width), lambda i: (i, 0)) for array in halves]
        + [(array, (2 * block, width), lambda i: (i, 0)) for array in fulls]
        + [whole(array) for array in wholes],
        [((rows, width), kind, (block, width), lambda i: (i, 0))],
    )[0]


def turned(values):
    width = values.shape[-1]
    lane = lax.broadcasted_iota(jnp.int32, values.shape, values.ndim - 1)
    ahead = pltpu.roll(values, width - HD // 2, values.ndim - 1)
    behind = pltpu.roll(values, HD // 2, values.ndim - 1)
    return jnp.where(lane % HD < HD // 2, ahead, behind)


def project_kernel(count, low_ref, x_ref, high_ref, cos_ref, sin_ref, *refs):
    gains, weights = refs[:count], refs[count : 2 * count]
    out_ref, norm_ref, gain_ref = refs[2 * count :]

    @pl.when(pl.program_id(0) == 0)
    def _():
        pick = lax.broadcasted_iota(jnp.int32, (8, LANES), 0) == lax.broadcasted_iota(
            jnp.int32, (8, LANES), 1
        )
        pick = pick.astype(F32).astype(BF16)
        start = 0
        for piece in gains:
            gain_ref[:, start : start + piece.shape[0]] = contract_cols(pick, piece[...])
            start += piece.shape[0]
        for stream in range(x_ref.shape[0]):
            at = stream * cos_ref.shape[0]
            for ref in (low_ref, x_ref, high_ref):
                unit, _ = normalise(ref[stream].astype(F32))
                span = slice(at, at + ref.shape[1])
                norm_ref[span, :] = (unit * gain_ref[0:1, :]).astype(BF16)
                at = span.stop

    values = piece_matmul(norm_ref, weights)
    keep = pl.program_id(0) == 2
    length = cos_ref.shape[0]
    for top in range(0, values.shape[0], length):
        for left in range(0, values.shape[1], LANES):
            part = values[top : top + length, left : left + LANES]
            rotated = part * cos_ref[...] + turned(part) * sin_ref[...]
            out_ref[top : top + length, left : left + LANES] = jnp.where(
                keep, part, rotated
            ).astype(BF16)


def project(low, tokens, high, pieces, cosine, sine, side):
    width = tokens.shape[2]
    rows = tokens.shape[0] * cosine.shape[0]
    gain_block = 3 * side // LANES
    return call(
        functools.partial(project_kernel, len(pieces)),
        (3,),
        [whole(low), whole(tokens), whole(high), whole(cosine), whole(sine)]
        + [(piece, (piece.shape[0], LANES), lambda j: (0, gain_block)) for piece in pieces]
        + [(piece, (piece.shape[0], side), lambda j: (0, j)) for piece in pieces],
        [
            ((rows, 3 * side), BF16, (rows, side), lambda j: (0, j)),
            ((rows, width), BF16, (rows, width), lambda j: (0, 0)),
            ((8, width), F32, (8, width), lambda j: (0, 0)),
        ],
    )


def head_masks():
    lane = lax.broadcasted_iota(jnp.int32, (1, LANES), 1)
    return [(lane // HD == head).astype(F32).astype(BF16) for head in range(LANES // HD)]


def block_mask(query_ids, key_ids):
    rows, width = query_ids.shape[0], key_ids.shape[1]
    offset = lax.broadcasted_iota(jnp.int32, (rows, width), 1) - lax.broadcasted_iota(
        jnp.int32, (rows, width), 0
    )
    return (offset >= 0) & (offset <= 2 * HALF) & (query_ids == key_ids)


def block_probs(query, keys, allowed):
    scores = jnp.where(allowed, contract_cols(query, keys) * HD**-0.5, -1e30)
    grown = jnp.exp(scores - jnp.max(scores, -1, keepdims=True))
    return grown / jnp.sum(grown, -1, keepdims=True)


def attend_kernel(block, q_ref, k_ref, v_ref, qid_ref, kid_ref, out_ref):
    masks = head_masks()
    for start in range(0, out_ref.shape[1], block):
        span = slice(start, start + block + 2 * HALF)
        allowed = block_mask(qid_ref[0, start : start + block], kid_ref[0, :, span])
        query = q_ref[0, HALF + start : HALF + start + block]
        total = None
        for mask in masks:
            probs = block_probs(query * mask, k_ref[0, span], allowed)
            part = matmul(probs.astype(BF16), v_ref[0, span]) * mask.astype(F32)
            total = part if total is None else total + part
        out_ref[0, start : start + block] = total.astype(BF16)


def attend_back_kernel(
    block, q_ref, k_ref, v_ref, qid_ref, kid_ref, grad_ref, cos_ref, sin_ref,
    dq_ref, mid_ref, low_ref, high_ref,
):
    masks = head_masks()
    length = dq_ref.shape[1]
    grad_keys = grad_values = jnp.zeros((length + 2 * HALF, LANES), F32)
    for start in range(0, length, block):
        span = slice(start, start + block + 2 * HALF)
        mid = slice(HALF + start, HALF + start + block)
        rows = slice(start, start + block)
        allowed = block_mask(qid_ref[0, rows], kid_ref[0, :, span])
        query_all, grad_all = q_ref[0, mid], grad_ref[0, rows]
        keys, values = k_ref[0, span], v_ref[0, span]
        grad_query, part_keys, part_values = 0.0, 0.0, 0.0
        for mask in masks:
            query, grad = query_all * mask, grad_all * mask
            probs = block_probs(query, keys, allowed)
            grad_probs = contract_cols(grad, values)
            delta = jnp.sum(probs * grad_probs, -1, keepdims=True)
            grad_scores = (probs * (grad_probs - delta)).astype(BF16)
            grad_query += matmul(grad_scores, keys) * mask.astype(F32)
            part_keys += contract_rows(grad_scores, query)
            part_values += contract_rows(probs.astype(BF16), grad)
        grad_query = grad_query * HD**-0.5
        dq_ref[0, rows] = (
            grad_query * cos_ref[mid] - turned(grad_query) * sin_ref[mid]
        ).astype(BF16)
        before, after = start, length - start - block

        def placed(part):
            pieces = [part]
            if before:
                pieces.insert(0, jnp.zeros((before, LANES), F32))
            if after:
                pieces.append(jnp.zeros((after, LANES), F32))
            return jnp.concatenate(pieces, 0)

        grad_keys += placed(part_keys)
        grad_values += placed(part_values)
    for index, total in enumerate((grad_keys * HD**-0.5, grad_values)):
        low_ref[0, index] = total[:HALF].astype(BF16)
        mid_ref[0, index] = total[HALF : HALF + length]
        high_ref[0, index] = total[HALF + length :].astype(BF16)


def attention_inputs(joined, query_ids, key_ids):
    window, groups = joined.shape[1], joined.shape[2] // 3 // LANES
    inputs = [
        (joined, (1, window, LANES), lambda s, h, shift=shift: (s, 0, h + shift))
        for shift in (0, groups, 2 * groups)
    ]
    inputs += [
        (ids, (1,) + ids.shape[1:], lambda s, h: (s, 0, 0)) for ids in (query_ids, key_ids)
    ]
    return inputs


def attend(block, joined, query_ids, key_ids):
    streams, window, columns = joined.shape
    length, side = window - 2 * HALF, columns // 3
    return call(
        functools.partial(attend_kernel, block),
        (streams, side // LANES),
        attention_inputs(joined, query_ids, key_ids),
        [((streams, length, side), BF16, (1, length, LANES), lambda s, h: (s, 0, h))],
        limit=24,
    )[0]


def attend_back(block, joined, query_ids, key_ids, grad, cosine, sine):
    streams, length, side = grad.shape

    def pair(rows, kind):
        return (
            (streams, 2, rows, side), kind, (1, 2, rows, LANES), lambda s, h: (s, 0, 0, h)
        )

    return call(
        functools.partial(attend_back_kernel, block),
        (streams, side // LANES),
        attention_inputs(joined, query_ids, key_ids)
        + [(grad, (1, length, LANES), lambda s, h: (s, 0, h)), whole(cosine), whole(sine)],
        [
            ((streams, length, side), BF16, (1, length, LANES), lambda s, h: (s, 0, h)),
            pair(length, F32),
            pair(HALF, BF16),
            pair(HALF, BF16),
        ],
        limit=24,
    )


def join_kernel(dq_ref, mid_ref, low_ref, high_ref, cos_ref, sin_ref, out_ref):
    length, width = dq_ref.shape[1:]
    out_ref[0, :, :width] = dq_ref[0]
    cosine, sine = cos_ref[HALF : HALF + length], sin_ref[HALF : HALF + length]
    for index in range(2):
        for start in range(0, width, LANES):
            lanes = slice(start, start + LANES)
            total = mid_ref[0, index, :, lanes]
            total = total + jnp.concatenate(
                [
                    low_ref[0, index, :, lanes].astype(F32),
                    jnp.zeros((length - 2 * HALF, LANES), F32),
                    high_ref[0, index, :, lanes].astype(F32),
                ],
                0,
            )
            if index == 0:
                total = total * cosine - turned(total) * sine
            to = (1 + index) * width + start
            out_ref[0, :, to : to + LANES] = total.astype(BF16)


def join_grads(grad_query, mid, from_lower, from_upper, cosine, sine):
    streams, length, width = grad_query.shape

    def of_stream(array):
        block = (1,) + array.shape[1:]
        return (array, block, lambda s: (s,) + (0,) * (array.ndim - 1))

    return call(
        join_kernel,
        (streams,),
        [of_stream(array) for array in (grad_query, mid, from_lower, from_upper)]
        + [whole(cosine), whole(sine)],
        [((streams, length, 3 * width), BF16, (1, length, 3 * width), lambda s: (s, 0, 0))],
        limit=24,
    )[0]


def by_rows(array, block):
    return (array, (block, array.shape[1]), lambda i: (i, 0))


def weight_kernel(count, other_ref, own_order_ref, other_order_ref, *refs):
    start = 0
    out_ref = refs[count]
    for piece in refs[:count]:
        span = slice(start, start + piece.shape[0])
        total = matmul(piece[...], own_order_ref[...])
        total = total + matmul(other_ref[span, :], other_order_ref[...])
        out_ref[span, :] = total.astype(BF16)
        start = span.stop


def out_weight(pieces, own, other, own_order, other_order):
    side, width = own_order.shape
    if len(pieces) == 1:
        own_pieces = [(own, own.shape, lambda i: (0, 0))]
    else:
        own_pieces, start = [], 0
        for piece in pieces:
            count = piece.shape[0]
            own_pieces.append(
                (own, (count, side), lambda i, index=start // count: (index, 0))
            )
            start += count
    return call(
        functools.partial(weight_kernel, len(own_pieces)),
        (1,),
        [whole(other), whole(own_order), whole(other_order)] + own_pieces,
        [((width, width), BF16, (width, width), lambda i: (0, 0))],
    )[0]


def out_kernel(
    own_ref, other_ref, own_order_ref, other_order_ref, weight_ref, x_ref, gain_ref,
    att_ref, hidden_ref, norm_ref,
):
    attended = matmul(own_ref[...], own_order_ref[...])
    attended = (attended + matmul(other_ref[...], other_order_ref[...])).astype(BF16)
    att_ref[...] = attended
    hidden = x_ref[...].astype(F32) + matmul(attended, weight_ref[...])
    hidden_ref[...] = hidden
    norm_ref[...] = (normalise(hidden)[0] * gain_ref[1:2, :]).astype(BF16)


def out_project(own, other, own_order, other_order, weight, tokens, gains):
    rows, width = tokens.shape
    block = rows // 2
    return call(
        out_kernel,
        (2,),
        [by_rows(own, block), by_rows(other, block), whole(own_order), whole(other_order)]
        + [whole(weight), by_rows(tokens, block), whole(gains)],
        [
            ((rows, width), kind, (block, width), lambda i: (i, 0))
            for kind in (BF16, F32, BF16)
        ],
    )


def hidden_back_kernel(
    part_ref, other_ref, hidden_ref, g_ref, gain_ref, weight_ref, order_ref,
    grad_ref, side_ref, att_ref,
):
    unit, scale = normalise(hidden_ref[...])
    incoming = part_ref[...] + other_ref[...].astype(F32)
    grad = g_ref[...].astype(F32) + norm_back(unit, scale, gain_ref[1:2, :], incoming)
    low = grad.astype(BF16)
    grad_ref[...] = grad
    side_ref[...] = contract_cols(low, order_ref[...]).astype(BF16)
    attended = contract_cols(low, weight_ref[...]).astype(BF16)
    att_ref[...] = contract_cols(attended, order_ref[...]).astype(BF16)


def hidden_back(part, other, hidden, grad_output, gains, weight, own_order):
    rows, width = hidden.shape
    block, side = rows // 2, own_order.shape[0]
    return call(
        hidden_back_kernel,
        (2,),
        [by_rows(array, block) for array in (part, other, hidden, grad_output)]
        + [whole(gains), whole(weight), whole(own_order)],
        [
            ((rows, size), kind, (block, size), lambda i: (i, 0))
            for size, kind in ((width, F32), (side, BF16), (side, BF16))
        ],
    )


def column_spans(width):
    return [slice(at, min(at + 2 * LANES, width)) for at in range(0, width, 2 * LANES)]


def tile_matmul(left, pieces, columns):
    total, start = None, 0
    for piece in pieces:
        part = matmul(left[:, start : start + piece.shape[0]], piece[:, columns])
        total = part if total is None else total + part
        start += piece.shape[0]
    return total


def feed_kernel(norm_ref, *refs):
    pieces, (mixed_ref, factor_ref, active_ref) = refs[:-3], refs[-3:]
    units = mixed_ref.shape[1]
    for span in column_spans(units):
        gate = tile_matmul(norm_ref, pieces, span)
        up = tile_matmul(norm_ref, pieces, slice(units + span.start, units + span.stop))
        below = 0.5 * (1.0 + lax.erf(gate * 0.5**0.5))
        active = gate * below
        mixed_ref[:, span] = (active * up).astype(BF16)
        active_ref[:, span] = active
        density = jnp.exp(-0.5 * gate * gate) * (2.0 * np.pi) ** -0.5
        factor_ref[:, span] = up * (below + gate * density)


def feed(normed, pieces, units):
    rows = normed.shape[0]
    block = rows // 2
    return call(
        feed_kernel,
        (2,),
        [by_rows(normed, block)] + [whole(piece) for piece in pieces],
        [
            ((rows, units), kind, (block, units), lambda i: (i, 0))
            for kind in (BF16, F32, F32)
        ],
    )


def feed_back_kernel(g_ref, factor_ref, active_ref, *refs):
    pieces, (gate_ref, up_ref) = refs[:-2], refs[-2:]
    for span in column_spans(factor_ref.shape[1]):
        grad = tile_matmul(g_ref, pieces, span)
        gate_ref[:, span] = (grad * factor_ref[:, span]).astype(BF16)
        up_ref[:, span] = (grad * active_ref[:, span]).astype(BF16)


def feed_back(grad_output, factor, active, pieces):
    rows, units = factor.shape
    block = rows // 2
    return call(
        feed_back_kernel,
        (2,),
        [by_rows(array, block) for array in (grad_output, factor, active)]
        + [whole(piece) for piece in pieces],
        [((rows, units), BF16, (block, units), lambda i: (i, 0)) for _ in range(2)],
    )


def shards(tokens, doc_ids, norm_attn, norm_mlp, w_qkv, w_out, w_in, w_down, cotangent):
    streams, block, width = tokens.shape
    shard_rows = w_qkv.shape[0]
    inner, outer = lax.axis_size("inner"), lax.axis_size("outer")
    core = lax.axis_index("core")
    length = 2 * block
    window = length + 2 * HALF
    rows = streams * length
    side = width // 2
    units = w_down.shape[1] // 2
    padded = -(-units // LANES) * LANES
    chips = outer * inner
    onward = [(i, i + 1) for i in range(chips - 1)]
    back = [(i + 1, i) for i in range(chips - 1)]

    def halves(weight, parts, pad):
        size = weight.shape[1] // (2 * parts)
        cut = [weight[:, i * size : (i + 1) * size] for i in range(2 * parts)]
        if pad != size:
            cut = [jnp.pad(piece, ((0, 0), (0, pad - size))) for piece in cut]
        return cut[0::2], cut[1::2]

    def paired(pieces):
        low = jnp.concatenate([piece for one, _ in pieces for piece in one], 1)
        high = jnp.concatenate([piece for _, two in pieces for piece in two], 1)
        mine = jnp.where(core == 0, low, high)
        return ordered(mine, swap(jnp.where(core == 0, high, low)), 0)

    pair_tokens = ordered(tokens, swap(tokens), 1)

    gains = jnp.pad(jnp.stack([norm_attn, norm_mlp], 1), ((0, 0), (0, LANES - 2)))
    pair_one = paired([halves(w_qkv, 3, side), ([gains], [gains]), halves(w_out, 1, side)])
    later_in, later_down, pair_one, pair_tokens = tied(w_in, w_down, pair_one, pair_tokens)
    low = lax.ppermute(pair_tokens[:, length - HALF :], ("outer", "inner"), onward)
    high = lax.ppermute(pair_tokens[:, :HALF], ("outer", "inner"), back)
    one = direct_sends(pair_one)
    pair_two = paired([halves(later_in, 2, padded)])
    pair_three = paired([halves(later_down, 1, padded)])
    order = arrival_order(width, shard_rows)
    own_order = lax.dynamic_slice_in_dim(order, core * side, side, 0)
    other_order = lax.dynamic_slice_in_dim(order, (1 - core) * side, side, 0)

    def in_order(value):
        return matmul(value.reshape(-1, width), order).astype(BF16)

    own_tokens = in_order(pair_tokens)
    grad_output = in_order(ordered(cotangent, swap(cotangent), 1))

    start = lax.axis_index(("outer", "inner")) * length
    positions = (start - HALF + jnp.arange(window, dtype=jnp.int32)).astype(F32)
    frequency = ROPE_BASE ** (-(jnp.arange(HD // 2, dtype=F32) * 2.0 / HD))
    angles = positions[:, None] * frequency[None, :]
    cosine, sine = jnp.cos(angles), jnp.sin(angles)
    cosine = jnp.tile(cosine, (1, LANES // (HD // 2)))
    sine = jnp.tile(jnp.concatenate([-sine, sine], 1), (1, LANES // HD))
    ids_padded = jnp.pad(doc_ids, ((0, 0), (HALF, HALF)), constant_values=-1)
    key_ids = lax.dynamic_slice_in_dim(ids_padded, start, window, 1)[:, None, :]
    query_ids = lax.dynamic_slice_in_dim(doc_ids, start, length, 1)[:, :, None]

    prepared = (own_tokens, grad_output, order, own_order, other_order)
    prepared += (cosine, sine, key_ids, query_ids)
    prepared, pair_two, pair_three, one, low, high = tied(
        prepared, pair_two, pair_three, one, low, high
    )
    own_tokens, grad_output, order, own_order, other_order = prepared[:5]
    cosine, sine, key_ids, query_ids = prepared[5:]
    two = direct_sends(pair_two)
    near = gather_near(one)
    low, high = (in_order(end).reshape(end.shape) for end in (low, high))
    low, high, two, near = tied(low, high, two, near)

    far = gather_far(*near)
    two_own = joined_rows(two)
    near, far, two_own = tied(near, far, two_own)

    three = direct_sends(pair_three)
    two_near = gather_near([two_own])
    first = in_pieces(*near, *far)
    joined, window_norm, gain_rows = project(
        low, own_tokens.reshape(streams, length, width), high, first, cosine, sine, side
    )
    out_half = joined_rows([piece[:, 3 * side + LANES :] for piece in first])
    weight = out_weight(first, out_half, swap(out_half), own_order, other_order)
    joined, weight, first, two_near, three = tied(joined, weight, first, two_near, three)

    two_far = gather_far(*two_near)
    joined = joined.reshape(streams, window, 3 * side)
    attended = attend(block, joined, query_ids, key_ids).reshape(rows, side)
    attended_other = swap(attended)
    three_own = joined_rows(three)
    attended, attended_other, two_near, two_far, three_own = tied(
        attended, attended_other, two_near, two_far, three_own
    )
    in_half = in_pieces(*two_near, *two_far)

    three_near = gather_near([three_own])
    attended_low, hidden, normed_mlp_low = out_project(
        attended, attended_other, own_order, other_order, weight, own_tokens, gain_rows
    )
    mixed_low, factor, active = feed(normed_mlp_low, in_half, padded)
    mixed_low, factor, active, three_near = tied(mixed_low, factor, active, three_near)

    three_far = gather_far(*three_near)
    sum_down = GradSum([grad_output], [mixed_low], shard_rows)
    sent_down = sum_down.far()
    sent_down, three_near, three_far = tied(sent_down, three_near, three_far)
    down_half = in_pieces(*three_near, *three_far)

    down_far = sum_down.send_far(sent_down)
    grad_gate, grad_up = feed_back(grad_output, factor, active, down_half)
    grad_gate, grad_up, down_far = tied(grad_gate, grad_up, down_far)

    sum_in = GradSum([normed_mlp_low] * 2, [grad_gate, grad_up], shard_rows)
    down_near = sum_down.send_near(sum_down.near(down_far))
    sent_in = sum_in.far()
    part, part_low = back_project([grad_gate, grad_up], in_half, [F32, BF16])
    part, part_low, down_near, sent_in = tied(part, part_low, down_near, sent_in)

    in_far = sum_in.send_far(sent_in)
    down_own = sum_down.own(down_near)
    down_arrived = sum_down.send_direct(down_own)
    grad_hidden, hidden_side, grad_attended = hidden_back(
        part, swap(part_low), hidden, grad_output, gain_rows, weight, own_order
    )
    grad_attended, in_far = tied(grad_attended, in_far)

    in_near = sum_in.send_near(sum_in.near(in_far))
    grad_query, mid, to_lower, to_upper = attend_back(
        block, joined, query_ids, key_ids, grad_attended.reshape(streams, length, side),
        cosine, sine,
    )
    from_lower = lax.ppermute(to_upper, ("outer", "inner"), onward)
    from_upper = lax.ppermute(to_lower, ("outer", "inner"), back)
    from_lower, from_upper, in_near, down_arrived = tied(
        from_lower, from_upper, in_near, down_arrived
    )

    grad_joined = join_grads(grad_query, mid, from_lower, from_upper, cosine, sine)
    grad_joined = grad_joined.reshape(rows, 3 * side)
    normed_low = window_norm.reshape(streams, window, width)[:, HALF : HALF + length]
    sum_attn = GradSum(
        [normed_low.reshape(rows, width), attended_low], [grad_joined, hidden_side], shard_rows
    )
    sent_attn, in_own = sum_attn.far(), sum_in.own(in_near)
    sent_attn, in_own, grad_joined = tied(sent_attn, in_own, grad_joined)

    attn_far = sum_attn.send_far(sent_attn)
    in_arrived = sum_in.send_direct(in_own)
    attn_far, in_arrived[0], grad_joined, mixed_low = tied(
        attn_far, in_arrived[0], grad_joined, mixed_low
    )

    attn_near = sum_attn.send_near(sum_attn.near(attn_far))
    cores = core.astype(jnp.int32).reshape(1)
    down_mine, down_other = sum_down.total(cores, down_own, down_arrived)
    (grad_down,) = assemble(cores, down_mine, swap(down_other), [(0, 1, padded, units)])
    out_mine, out_other = back_split(cores, mixed_low, down_half, streams)
    in_mine, in_other = back_split(cores, grad_joined, first, streams)
    attn_near, in_arrived, out_mine, out_other, in_mine, in_other, grad_down = tied(
        attn_near, in_arrived, out_mine, out_other, in_mine, in_other, grad_down
    )

    attn_own = sum_attn.own(attn_near)
    attn_arrived = sum_attn.send_direct(attn_own)
    output = end_rows(
        output_kernel, cores, [out_mine, swap(out_other)], [hidden], [order], BF16, streams
    ).reshape(tokens.shape)
    grad_tokens = end_rows(
        input_grad_kernel, cores, [in_mine, swap(in_other)], [grad_hidden, own_tokens],
        [gain_rows, order], F32, streams,
    ).reshape(tokens.shape)
    total_mine, total_other = sum_in.total(cores, in_own, in_arrived)
    grad_in, gain_grad_mlp = assemble(
        cores, total_mine, swap(total_other), [(0, 2, padded, units)], w_in, norm_mlp
    )
    attn_arrived, output, grad_tokens, grad_in, gain_grad_mlp = tied(
        attn_arrived, output, grad_tokens, grad_in, gain_grad_mlp
    )
    total_mine, total_other = sum_attn.total(cores, attn_own, attn_arrived)
    grad_qkv, grad_out, gain_grad_attn = assemble(
        cores, total_mine, swap(total_other),
        [(0, 3, side, side), (3 * side, 1, side, side)], w_qkv, norm_attn,
    )
    return (
        output,
        grad_tokens,
        gain_grad_attn.reshape(-1),
        gain_grad_mlp.reshape(-1),
        grad_qkv,
        grad_out,
        grad_in,
        grad_down,
    )


def solution(mesh):
    dp, seq = mesh.shape["dp"], mesh.shape["seq"]
    chips = seq // 2
    outer = 4 if chips % 4 == 0 else 1
    fine = Mesh(
        mesh.devices.reshape(dp, outer, chips // outer, 2), ("dp", "outer", "inner", "core")
    )
    line = ("outer", "inner", "core")
    every = ("dp",) + line
    token = P("dp", line, None)
    vector = P(every)
    matrix = P(every, None)
    return jax.shard_map(
        shards,
        mesh=fine,
        in_specs=(token, P("dp", None), vector, vector, matrix, matrix, matrix, matrix, token),
        out_specs=(token, token, vector, vector, matrix, matrix, matrix, matrix),
        check_vma=False,
    )
```

```python
import functools

import jax
import jax.numpy as jnp
import numpy as np
from jax import lax
from jax.experimental import pallas as pl
from jax.experimental.pallas import tpu as pltpu
from jax.sharding import Mesh, PartitionSpec as P

HD = 64
HALF = 64
LANES = 128
NORM_EPSILON = 1e-05
ROPE_BASE = 10000.0
F32 = jnp.float32
BF16 = jnp.bfloat16


def contract_cols(left, right):
    return lax.dot_general(left, right, (((1,), (1,)), ((), ())), preferred_element_type=F32)


def contract_rows(left, right):
    return lax.dot_general(left, right, (((0,), (0,)), ((), ())), preferred_element_type=F32)


def matmul(left, right):
    return jnp.dot(left, right, preferred_element_type=F32)


def tied(*values):
    return lax.optimization_barrier(values)


def call(kernel, grid, ins, outs, scratch=(), limit=40):
    out = pl.pallas_call(
        kernel,
        grid=grid,
        in_specs=[
            pl.BlockSpec(memory_space=pltpu.SMEM) if block is None else pl.BlockSpec(block, index)
            for _, block, index in ins
        ],
        out_specs=[pl.BlockSpec(block, index) for _, _, block, index in outs],
        out_shape=[jax.ShapeDtypeStruct(shape, kind) for shape, kind, _, _ in outs],
        scratch_shapes=list(scratch),
        compiler_params=pltpu.CompilerParams(vmem_limit_bytes=limit * 2**20),
        cost_estimate=pl.CostEstimate(flops=1024, bytes_accessed=1024, transcendentals=0),
    )(*[array for array, _, _ in ins])
    return out


def whole(array):
    return (array, array.shape, lambda *_: (0,) * array.ndim)


def swap(value):
    return lax.ppermute(value, "core", [(0, 1), (1, 0)])


def ordered(mine, other, axis):
    first = lax.axis_index("core") == 0
    return jnp.concatenate(
        [jnp.where(first, mine, other), jnp.where(first, other, mine)], axis=axis
    )


def forward(axis, distance=1):
    count = lax.axis_size(axis)
    return [(i, (i + distance) % count) for i in range(count)]


def ring_gather(axis, piece):
    pieces = [piece]
    for _ in range(1, lax.axis_size(axis)):
        pieces.append(lax.ppermute(pieces[-1], axis, forward(axis)))
    return pieces[1:]


def direct_sends(rows):
    return [rows] + [
        lax.ppermute(rows, "outer", forward("outer", distance))
        for distance in range(1, lax.axis_size("outer"))
    ]


def joined_rows(pieces):
    return jnp.concatenate(pieces, 0) if len(pieces) > 1 else pieces[0]


def gather_near(arrived):
    own = joined_rows(arrived)
    return own, ring_gather("inner", own), ring_gather("dp", own)


def copy_kernel(*refs):
    count = len(refs) // 2
    for source, target in zip(refs[:count], refs[count:]):
        target[...] = source[...]


def far_halves(along_x, along_y, half):
    if len(along_x) > 1 or len(along_y) > 1 or half % 32:
        return (
            joined_rows([piece[:half] for piece in along_y]),
            joined_rows([piece[half:] for piece in along_x]),
        )
    columns = along_x[0].shape[1]
    return call(
        copy_kernel,
        (1,),
        [(along_y[0], (half, columns), lambda i: (0, 0))]
        + [(along_x[0], (half, columns), lambda i: (1, 0))],
        [((half, columns), BF16, (half, columns), lambda i: (0, 0)) for _ in range(2)],
    )


def gather_far(own, along_x, along_y):
    one, two = far_halves(along_x, along_y, own.shape[0] // 2)
    return ring_gather("inner", one), ring_gather("dp", two)


def in_pieces(own, along_x, along_y, one, two):
    pieces = [own, *along_x, *along_y, *one, *two]
    if any(piece.shape[0] % LANES for piece in pieces):
        pieces = [joined_rows(pieces)]
    return pieces


def order_blocks(inner, dp):
    blocks = [(0, 0, 0, 2)]
    blocks += [(d, 0, 0, 2) for d in range(1, inner)] + [(0, d, 0, 2) for d in range(1, dp)]
    blocks += [(d, e, 0, 1) for d in range(1, inner) for e in range(1, dp)]
    return blocks + [(d, e, 1, 2) for e in range(1, dp) for d in range(1, inner)]


def late_segments(shard_rows):
    inner, outer, dp = (lax.axis_size(name) for name in ("inner", "outer", "dp"))
    start, at = 0, {}
    for d, e, low, high in order_blocks(inner, dp):
        for part in range(low, high):
            at[d, e, part] = start
            start += shard_rows
    segments = []
    for d, e, low, high in order_blocks(inner, dp):
        for distance in range(low * outer // 2, high * outer // 2):
            first, second = at[d, e, 0], at[d, e, 1]
            if second == first + shard_rows:
                segments.append((distance, first, 2 * shard_rows))
            else:
                segments += [(distance, first, shard_rows), (distance, second, shard_rows)]
    return segments


def join_kernel_rows(segments, *refs):
    pieces, out_ref = refs[:-1], refs[-1]
    at = 0
    for distance, start, count in segments:
        out_ref[at : at + count, :] = pieces[distance][start : start + count, :]
        at += count


def join_late(pieces, shard_rows):
    segments = late_segments(shard_rows)
    columns = pieces[0].shape[1]
    rows = sum(count for _, _, count in segments)
    if shard_rows % 32:
        return jnp.concatenate([pieces[d][at : at + n] for d, at, n in segments], 0)
    return call(
        functools.partial(join_kernel_rows, segments),
        (1,),
        [whole(piece) for piece in pieces],
        [((rows, columns), BF16, (rows, columns), lambda i: (0, 0))],
    )[0]


def split_kernel_rows(segments, left_ref, right_ref, *outs):
    place, at = [], 0
    for distance, start, count in segments:
        place.append((at, distance, start, count))
        at += count
    for top in range(0, at, LANES):
        rows = contract_rows(left_ref[:, top : top + LANES], right_ref[...]).astype(BF16)
        for begin, distance, start, count in place:
            if top <= begin < top + LANES:
                outs[distance][start : start + count, :] = rows[begin - top : begin - top + count]


def split_late(left, right, shard_rows):
    segments = late_segments(shard_rows)
    outer = lax.axis_size("outer")
    rows, columns = left.shape[1] // outer, right.shape[1]
    if shard_rows % 32:
        total, at, cuts = contract_rows(left, right).astype(BF16), 0, {}
        for distance, start, count in segments:
            cuts[distance, start] = total[at : at + count]
            at += count
        return [
            jnp.concatenate([cuts[key] for key in sorted(cuts) if key[0] == distance], 0)
            for distance in range(outer)
        ]
    return call(
        functools.partial(split_kernel_rows, segments),
        (1,),
        [whole(left), whole(right)],
        [((rows, columns), BF16, (rows, columns), lambda i: (0, 0)) for _ in range(outer)],
    )


def arrival_order(x, z, y, width, shard_rows):
    inner, outer, dp = (lax.axis_size(name) for name in ("inner", "outer", "dp"))
    half = outer * shard_rows
    blocks = order_blocks(inner, dp)
    place = np.concatenate([np.arange(low * half, high * half) for _, _, low, high in blocks])
    sizes = [(high - low) * half for _, _, low, high in blocks]
    along_x = np.repeat([block[0] for block in blocks], sizes)
    along_y = np.repeat([block[1] for block in blocks], sizes)
    along_z, row = place // (2 * shard_rows), place % (2 * shard_rows)
    at_x = (x - jnp.asarray(along_x, jnp.int32) + inner) % inner
    at_y = (y - jnp.asarray(along_y, jnp.int32) + dp) % dp
    at_z = (z - jnp.asarray(along_z, jnp.int32) + outer) % outer
    source = ((at_y * outer + at_z) * inner + at_x) * 2 * shard_rows + row
    return (jnp.arange(width, dtype=jnp.int32)[:, None] == source[None, :]).astype(BF16)


def rows_kernel(pairs, layout, *refs):
    rights, refs = refs[:pairs], refs[pairs:]
    inputs, outs = refs[: -len(layout)], refs[-len(layout) :]
    for places, out_ref in zip(layout, outs):
        lefts, adds = inputs[:pairs], inputs[pairs : pairs + len(places)]
        inputs = inputs[pairs + len(places) :]
        start = 0
        for left, right in zip(lefts, rights):
            columns = slice(start, start + right.shape[1])
            start = columns.stop
            total = contract_rows(left[...], right[...])
            for add in adds:
                if add.shape[0] == total.shape[0]:
                    total = total + add[:, columns].astype(F32)
            out_ref[:, columns] = total.astype(BF16)
            for add, at in zip(adds, places):
                if add.shape[0] != total.shape[0]:
                    span = slice(at, at + add.shape[0])
                    part = total[span] + add[:, columns].astype(F32)
                    out_ref[span, columns] = part.astype(BF16)


class GradSum:
    def __init__(self, lefts, rights, shard_rows):
        self.lefts, self.rights = lefts, rights
        self.inner, self.outer, self.dp = (
            lax.axis_size(name) for name in ("inner", "outer", "dp")
        )
        self.shard = 2 * shard_rows
        self.half = self.outer * shard_rows
        self.at_x = 2 * self.half
        self.at_y = self.at_x + (self.inner - 1) * 2 * self.half
        self.at_one = self.at_y + (self.dp - 1) * 2 * self.half
        self.at_two = self.at_one + (self.inner - 1) * (self.dp - 1) * self.half

    def rows(self, *parts):
        depth = self.lefts[0].shape[0]
        columns = sum(right.shape[1] for right in self.rights)
        ins, outs, layout = [whole(right) for right in self.rights], [], []
        for start, count, adds in parts:
            adds = [(rows, place) for rows, place in adds if rows is not None]
            lefts, index = self.lefts, start // count
            if count % LANES or start % count:
                lefts, index = [left[:, start : start + count] for left in lefts], 0
            ins += [
                (left, (depth, count), lambda i, index=index: (0, index)) for left in lefts
            ]
            ins += [whole(rows) for rows, _ in adds]
            outs.append(((count, columns), BF16, (count, columns), lambda i: (0, 0)))
            layout.append([place for _, place in adds])
        return call(
            functools.partial(rows_kernel, len(self.rights), layout), (1,), ins, outs
        )

    def ring(self, axis, part, first):
        arrived = None
        for step in range(1, lax.axis_size(axis)):
            sent = first if step == 1 else self.rows(part(step, arrived))[0]
            arrived = lax.ppermute(sent, axis, forward(axis))
        return arrived

    def one(self, distance, arrived):
        count = (self.dp - 1) * self.half
        return (self.at_one + (distance - 1) * count, count, [(arrived, 0)])

    def two(self, distance, arrived):
        count = (self.inner - 1) * self.half
        return (self.at_two + (distance - 1) * count, count, [(arrived, 0)])

    def far(self):
        return self.rows(self.one(1, None), self.two(1, None))

    def send_far(self, firsts):
        return (
            self.ring("inner", self.one, firsts[0]), self.ring("dp", self.two, firsts[1])
        )

    def along(self, start, distance, arrived, extra, place):
        count = 2 * self.half
        extra = extra[(distance - 1) * self.half : distance * self.half]
        return (start + (distance - 1) * count, count, [(arrived, 0), (extra, place)])

    def along_x(self, distance, arrived):
        return self.along(self.at_x, distance, arrived, self.sums[1], self.half)

    def along_y(self, distance, arrived):
        return self.along(self.at_y, distance, arrived, self.sums[0], 0)

    def near(self, sums):
        self.sums = sums
        return self.rows(self.along_x(1, None), self.along_y(1, None))

    def send_near(self, firsts):
        return (
            self.ring("inner", self.along_x, firsts[0]),
            self.ring("dp", self.along_y, firsts[1]),
        )

    def own(self, nears):
        return self.rows((0, 2 * self.half, [(near, 0) for near in nears]))[0]

    def cut(self, own, distance):
        return own[distance * self.shard : (distance + 1) * self.shard]

    def send_direct(self, own):
        return [
            lax.ppermute(
                self.cut(own, distance), "outer", forward("outer", self.outer - distance)
            )
            for distance in range(1, self.outer)
        ]

    def total(self, core, own, arrived):
        columns = own.shape[1]
        half = self.shard // 2
        return call(
            total_kernel,
            (1,),
            [(core, None, None), (own, (self.shard, columns), lambda i: (0, 0))]
            + [whole(rows) for rows in arrived],
            [((half, columns), F32, (half, columns), lambda i: (0, 0)) for _ in range(2)],
        )


def late_kernel(count, layout, *refs):
    blocks, refs = refs[:count], refs[count:]
    adds, outs = refs[: -len(layout)], refs[-len(layout) :]
    for (start, rows, places), out_ref in zip(layout, outs):
        mine, adds = adds[: len(places)], adds[len(places) :]
        total = None
        for block in blocks:
            part = block[start : start + rows, :].astype(F32)
            total = part if total is None else total + part
        for add in mine:
            if add.shape[0] == rows:
                total = total + add[...].astype(F32)
        out_ref[...] = total.astype(BF16)
        for add, at in zip(mine, places):
            if add.shape[0] != rows:
                span = slice(at, at + add.shape[0])
                out_ref[span, :] = (total[span] + add[...].astype(F32)).astype(BF16)


class LateSum(GradSum):
    def __init__(self, blocks, shard_rows):
        GradSum.__init__(self, [], [], shard_rows)
        self.blocks, self.half = blocks, shard_rows
        self.at_x = 2 * self.half
        self.at_y = self.at_x + (self.inner - 1) * 2 * self.half
        self.at_one = self.at_y + (self.dp - 1) * 2 * self.half
        self.at_two = self.at_one + (self.inner - 1) * (self.dp - 1) * self.half

    def rows(self, *parts):
        columns = self.blocks[0].shape[1]
        parts = [
            (start, count, [add for add in adds if add[0] is not None])
            for start, count, adds in parts
        ]
        if self.half % 32:
            results = []
            for start, count, adds in parts:
                total = sum(block[start : start + count].astype(F32) for block in self.blocks)
                for rows, place in adds:
                    span = slice(place, place + rows.shape[0])
                    total = total.at[span].add(rows.astype(F32))
                results.append(total.astype(BF16))
            return results
        return call(
            functools.partial(
                late_kernel,
                len(self.blocks),
                [(start, count, [at for _, at in adds]) for start, count, adds in parts],
            ),
            (1,),
            [whole(block) for block in self.blocks]
            + [whole(rows) for _, _, adds in parts for rows, _ in adds],
            [
                ((count, columns), BF16, (count, columns), lambda i: (0, 0))
                for _, count, _ in parts
            ],
        )


def own_half(core_ref, value):
    half = value.shape[0] // 2
    return jnp.where(core_ref[0] == 0, value[:half], value[half:])


def total_kernel(core_ref, *refs):
    total = None
    for ref in refs[:-2]:
        rows = ref[...].astype(F32)
        total = rows if total is None else total + rows
    half = total.shape[0] // 2
    first = core_ref[0] == 0
    refs[-2][...] = jnp.where(first, total[:half], total[half:])
    refs[-1][...] = jnp.where(first, total[half:], total[:half])


def assemble_kernel(layout, core_ref, mine_ref, other_ref, *refs):
    first = core_ref[0] == 0
    count = len(layout)
    pair = (
        jnp.where(first, mine_ref[...], other_ref[...]),
        jnp.where(first, other_ref[...], mine_ref[...]),
    )
    outs = refs[-count:] if len(refs) == count else refs[2:-1]
    for out_ref, (start, parts, stride, size) in zip(outs, layout):
        cuts = []
        for i in range(parts):
            at = start + i * stride
            cuts += [half[:, at : at + size] for half in pair]
        out_ref[...] = jnp.concatenate(cuts, 1)
    if len(refs) > count:
        weight_ref, gain_ref = refs[:2]
        product = weight_ref[...].astype(F32) * outs[0][...]
        refs[-1][...] = jnp.sum(product, -1, keepdims=True) / gain_ref[...].astype(F32)


def assemble(core, mine, other, layout, weight=None, gain=None):
    rows = mine.shape[0]
    ins = [(core, None, None), whole(mine), whole(other)]
    sizes = [2 * parts * size for _, parts, _, size in layout]
    if weight is not None:
        ins += [whole(weight), whole(gain.reshape(rows, 1))]
        sizes.append(1)
    return call(
        functools.partial(assemble_kernel, layout),
        (1,),
        ins,
        [((rows, size), F32, (rows, size), lambda i: (0, 0)) for size in sizes],
    )


def pack_kernel(side, core_ref, qkv_ref, gain_ref, out_ref, mine_ref, other_ref):
    def fill(target, half):
        for part in range(3):
            start = (2 * part + half) * side
            target[:, part * side : (part + 1) * side] = qkv_ref[:, start : start + side]
        target[:, 3 * side : 3 * side + LANES] = gain_ref[...]
        target[:, 3 * side + LANES :] = out_ref[:, half * side : (half + 1) * side]

    for half in range(2):

        @pl.when(core_ref[0] == half)
        def _():
            fill(mine_ref, half)
            fill(other_ref, 1 - half)


def pack_first(core, w_qkv, gains, w_out):
    rows, side = w_out.shape[0], w_out.shape[1] // 2
    columns = 4 * side + LANES
    return call(
        functools.partial(pack_kernel, side),
        (1,),
        [(core, None, None), whole(w_qkv), whole(gains), whole(w_out)],
        [((rows, columns), BF16, (rows, columns), lambda i: (0, 0)) for _ in range(2)],
    )


def normalise(values):
    centred = values - jnp.mean(values, -1, keepdims=True)
    scale = lax.rsqrt(jnp.mean(centred * centred, -1, keepdims=True) + NORM_EPSILON)
    return centred * scale, scale


def norm_back(unit, scale, gain, incoming):
    grad = incoming * gain
    return scale * (
        grad
        - jnp.mean(grad, -1, keepdims=True)
        - unit * jnp.mean(grad * unit, -1, keepdims=True)
    )


def piece_matmul(left, pieces):
    total, start = None, 0
    for piece in pieces:
        part = matmul(left[:, start : start + piece.shape[0]], piece[...])
        total = part if total is None else total + part
        start += piece.shape[0]
    return total


def back_kernel(starts, count, *refs):
    grads, pieces, out_refs = refs[: len(starts)], refs[len(starts) : count], refs[count:]
    at = 0
    for piece in pieces:
        total = None
        for grad, start in zip(grads, starts):
            part = contract_cols(grad[...], piece[:, start : start + grad.shape[1]])
            total = part if total is None else total + part
        for out_ref in out_refs:
            out_ref[:, at : at + piece.shape[0]] = total.astype(out_ref.dtype)
        at += piece.shape[0]


def back_project(grads, pieces, kinds):
    rows = grads[0].shape[0]
    block = rows // 2
    starts, end = [], 0
    for grad in grads:
        starts.append(end)
        end += grad.shape[1]
    width = sum(piece.shape[0] for piece in pieces)
    return call(
        functools.partial(back_kernel, starts, len(grads) + len(pieces)),
        (2,),
        [(grad, (block, grad.shape[1]), lambda i: (i, 0)) for grad in grads]
        + [(piece, (piece.shape[0], end), lambda i: (0, 0)) for piece in pieces],
        [((rows, width), kind, (block, width), lambda i: (i, 0)) for kind in kinds],
    )


def split_kernel(core_ref, grad_ref, *refs):
    pieces, (mine_ref, other_ref) = refs[:-2], refs[-2:]
    width = grad_ref.shape[1]
    half = grad_ref.shape[0] // 2
    at = 0
    for piece in pieces:
        total = contract_cols(grad_ref[...], piece[:, :width])
        first = core_ref[0] == 0
        span = slice(at, at + piece.shape[0])
        mine_ref[:, span] = jnp.where(first, total[:half], total[half:])
        other_ref[:, span] = jnp.where(first, total[half:], total[:half]).astype(BF16)
        at = span.stop


def back_split(core, grad, pieces, streams):
    rows, columns = grad.shape
    block = rows // streams
    width = sum(piece.shape[0] for piece in pieces)
    return call(
        split_kernel,
        (streams,),
        [(core, None, None), (grad, (block, columns), lambda i: (i, 0))]
        + [(piece, (piece.shape[0], columns), lambda i: (0, 0)) for piece in pieces],
        [
            ((rows // 2, width), kind, (block // 2, width), lambda i: (i, 0))
            for kind in (F32, BF16)
        ],
    )


def output_kernel(core_ref, mine_ref, other_ref, hidden_ref, order_ref, out_ref):
    total = own_half(core_ref, hidden_ref[...]) + mine_ref[...] + other_ref[...].astype(F32)
    out_ref[...] = contract_cols(total.astype(BF16), order_ref[...]).astype(BF16)


def input_grad_kernel(
    core_ref, mine_ref, other_ref, hidden_ref, x_ref, gain_ref, order_ref, out_ref
):
    unit, scale = normalise(own_half(core_ref, x_ref[...].astype(F32)))
    incoming = mine_ref[...] + other_ref[...].astype(F32)
    total = own_half(core_ref, hidden_ref[...])
    total = total + norm_back(unit, scale, gain_ref[0:1, :], incoming)
    result = None
    for _ in range(3):
        part = total.astype(BF16)
        total = total - part.astype(F32)
        part = contract_cols(part, order_ref[...])
        result = part if result is None else result + part
    out_ref[...] = result


def end_rows(kernel, core, halves, fulls, wholes, kind, streams):
    rows, width = halves[0].shape
    block = rows // streams
    return call(
        kernel,
        (streams,),
        [(core, None, None)]
        + [(array, (block, width), lambda i: (i, 0)) for array in halves]
        + [(array, (2 * block, width), lambda i: (i, 0)) for array in fulls]
        + [whole(array) for array in wholes],
        [((rows, width), kind, (block, width), lambda i: (i, 0))],
    )[0]


def turned(values):
    width = values.shape[-1]
    lane = lax.broadcasted_iota(jnp.int32, values.shape, values.ndim - 1)
    ahead = pltpu.roll(values, width - HD // 2, values.ndim - 1)
    behind = pltpu.roll(values, HD // 2, values.ndim - 1)
    return jnp.where(lane % HD < HD // 2, ahead, behind)


def project_kernel(count, low_ref, x_ref, high_ref, cos_ref, sin_ref, *refs):
    gains, weights = refs[:count], refs[count : 2 * count]
    out_ref, norm_ref, gain_ref = refs[2 * count :]

    @pl.when(pl.program_id(0) == 0)
    def _():
        pick = lax.broadcasted_iota(jnp.int32, (8, LANES), 0) == lax.broadcasted_iota(
            jnp.int32, (8, LANES), 1
        )
        pick = pick.astype(F32).astype(BF16)
        start = 0
        for piece in gains:
            gain_ref[:, start : start + piece.shape[0]] = contract_cols(pick, piece[...])
            start += piece.shape[0]
        for stream in range(x_ref.shape[0]):
            at = stream * cos_ref.shape[0]
            for ref in (low_ref, x_ref, high_ref):
                unit, _ = normalise(ref[stream].astype(F32))
                span = slice(at, at + ref.shape[1])
                norm_ref[span, :] = (unit * gain_ref[0:1, :]).astype(BF16)
                at = span.stop

    values = piece_matmul(norm_ref, weights)
    keep = pl.program_id(0) == 2
    length = cos_ref.shape[0]
    for top in range(0, values.shape[0], length):
        for left in range(0, values.shape[1], LANES):
            part = values[top : top + length, left : left + LANES]
            rotated = part * cos_ref[...] + turned(part) * sin_ref[...]
            out_ref[top : top + length, left : left + LANES] = jnp.where(
                keep, part, rotated
            ).astype(BF16)


def project(low, tokens, high, pieces, cosine, sine, side):
    width = tokens.shape[2]
    rows = tokens.shape[0] * cosine.shape[0]
    gain_block = 3 * side // LANES
    return call(
        functools.partial(project_kernel, len(pieces)),
        (3,),
        [whole(low), whole(tokens), whole(high), whole(cosine), whole(sine)]
        + [(piece, (piece.shape[0], LANES), lambda j: (0, gain_block)) for piece in pieces]
        + [(piece, (piece.shape[0], side), lambda j: (0, j)) for piece in pieces],
        [
            ((rows, 3 * side), BF16, (rows, side), lambda j: (0, j)),
            ((rows, width), BF16, (rows, width), lambda j: (0, 0)),
            ((8, width), F32, (8, width), lambda j: (0, 0)),
        ],
    )


def head_masks():
    lane = lax.broadcasted_iota(jnp.int32, (1, LANES), 1)
    return [(lane // HD == head).astype(F32).astype(BF16) for head in range(LANES // HD)]


def block_mask(query_ids, key_ids):
    rows, width = query_ids.shape[0], key_ids.shape[1]
    offset = lax.broadcasted_iota(jnp.int32, (rows, width), 1) - lax.broadcasted_iota(
        jnp.int32, (rows, width), 0
    )
    return (offset >= 0) & (offset <= 2 * HALF) & (query_ids == key_ids)


def block_probs(query, keys, allowed):
    scores = jnp.where(allowed, contract_cols(query, keys) * HD**-0.5, -1e30)
    grown = jnp.exp(scores - jnp.max(scores, -1, keepdims=True))
    return grown / jnp.sum(grown, -1, keepdims=True)


def attend_kernel(block, q_ref, k_ref, v_ref, qid_ref, kid_ref, out_ref):
    masks = head_masks()
    for start in range(0, out_ref.shape[1], block):
        span = slice(start, start + block + 2 * HALF)
        allowed = block_mask(qid_ref[0, start : start + block], kid_ref[0, :, span])
        query = q_ref[0, HALF + start : HALF + start + block]
        total = None
        for mask in masks:
            probs = block_probs(query * mask, k_ref[0, span], allowed)
            part = matmul(probs.astype(BF16), v_ref[0, span]) * mask.astype(F32)
            total = part if total is None else total + part
        out_ref[0, start : start + block] = total.astype(BF16)


def attend_back_kernel(
    block, q_ref, k_ref, v_ref, qid_ref, kid_ref, grad_ref, cos_ref, sin_ref,
    dq_ref, mid_ref, low_ref, high_ref,
):
    masks = head_masks()
    length = dq_ref.shape[1]
    grad_keys = grad_values = jnp.zeros((length + 2 * HALF, LANES), F32)
    for start in range(0, length, block):
        span = slice(start, start + block + 2 * HALF)
        mid = slice(HALF + start, HALF + start + block)
        rows = slice(start, start + block)
        allowed = block_mask(qid_ref[0, rows], kid_ref[0, :, span])
        query_all, grad_all = q_ref[0, mid], grad_ref[0, rows]
        keys, values = k_ref[0, span], v_ref[0, span]
        grad_query, part_keys, part_values = 0.0, 0.0, 0.0
        for mask in masks:
            query, grad = query_all * mask, grad_all * mask
            probs = block_probs(query, keys, allowed)
            grad_probs = contract_cols(grad, values)
            delta = jnp.sum(probs * grad_probs, -1, keepdims=True)
            grad_scores = (probs * (grad_probs - delta)).astype(BF16)
            grad_query += matmul(grad_scores, keys) * mask.astype(F32)
            part_keys += contract_rows(grad_scores, query)
            part_values += contract_rows(probs.astype(BF16), grad)
        grad_query = grad_query * HD**-0.5
        dq_ref[0, rows] = (
            grad_query * cos_ref[mid] - turned(grad_query) * sin_ref[mid]
        ).astype(BF16)
        before, after = start, length - start - block

        def placed(part):
            pieces = [part]
            if before:
                pieces.insert(0, jnp.zeros((before, LANES), F32))
            if after:
                pieces.append(jnp.zeros((after, LANES), F32))
            return jnp.concatenate(pieces, 0)

        grad_keys += placed(part_keys)
        grad_values += placed(part_values)
    for index, total in enumerate((grad_keys * HD**-0.5, grad_values)):
        low_ref[0, index] = total[:HALF].astype(BF16)
        mid_ref[0, index] = total[HALF : HALF + length]
        high_ref[0, index] = total[HALF + length :].astype(BF16)


def attention_inputs(joined, query_ids, key_ids):
    window, groups = joined.shape[1], joined.shape[2] // 3 // LANES
    inputs = [
        (joined, (1, window, LANES), lambda s, h, shift=shift: (s, 0, h + shift))
        for shift in (0, groups, 2 * groups)
    ]
    inputs += [
        (ids, (1,) + ids.shape[1:], lambda s, h: (s, 0, 0)) for ids in (query_ids, key_ids)
    ]
    return inputs


def attend(block, joined, query_ids, key_ids):
    streams, window, columns = joined.shape
    length, side = window - 2 * HALF, columns // 3
    return call(
        functools.partial(attend_kernel, block),
        (streams, side // LANES),
        attention_inputs(joined, query_ids, key_ids),
        [((streams, length, side), BF16, (1, length, LANES), lambda s, h: (s, 0, h))],
        limit=24,
    )[0]


def attend_back(block, joined, query_ids, key_ids, grad, cosine, sine):
    streams, length, side = grad.shape

    def pair(rows, kind):
        return (
            (streams, 2, rows, side), kind, (1, 2, rows, LANES), lambda s, h: (s, 0, 0, h)
        )

    return call(
        functools.partial(attend_back_kernel, block),
        (streams, side // LANES),
        attention_inputs(joined, query_ids, key_ids)
        + [(grad, (1, length, LANES), lambda s, h: (s, 0, h)), whole(cosine), whole(sine)],
        [
            ((streams, length, side), BF16, (1, length, LANES), lambda s, h: (s, 0, h)),
            pair(length, F32),
            pair(HALF, BF16),
            pair(HALF, BF16),
        ],
        limit=24,
    )


def join_kernel(dq_ref, mid_ref, low_ref, high_ref, cos_ref, sin_ref, out_ref):
    length, width = dq_ref.shape[1:]
    out_ref[0, :, :width] = dq_ref[0]
    cosine, sine = cos_ref[HALF : HALF + length], sin_ref[HALF : HALF + length]
    for index in range(2):
        for start in range(0, width, LANES):
            lanes = slice(start, start + LANES)
            total = mid_ref[0, index, :, lanes]
            total = total + jnp.concatenate(
                [
                    low_ref[0, index, :, lanes].astype(F32),
                    jnp.zeros((length - 2 * HALF, LANES), F32),
                    high_ref[0, index, :, lanes].astype(F32),
                ],
                0,
            )
            if index == 0:
                total = total * cosine - turned(total) * sine
            to = (1 + index) * width + start
            out_ref[0, :, to : to + LANES] = total.astype(BF16)


def join_grads(grad_query, mid, from_lower, from_upper, cosine, sine):
    streams, length, width = grad_query.shape

    def of_stream(array):
        block = (1,) + array.shape[1:]
        return (array, block, lambda s: (s,) + (0,) * (array.ndim - 1))

    return call(
        join_kernel,
        (streams,),
        [of_stream(array) for array in (grad_query, mid, from_lower, from_upper)]
        + [whole(cosine), whole(sine)],
        [((streams, length, 3 * width), BF16, (1, length, 3 * width), lambda s: (s, 0, 0))],
        limit=24,
    )[0]


def by_rows(array, block):
    return (array, (block, array.shape[1]), lambda i: (i, 0))


def weight_kernel(count, other_ref, own_order_ref, other_order_ref, *refs):
    start = 0
    out_ref = refs[count]
    for piece in refs[:count]:
        span = slice(start, start + piece.shape[0])
        total = matmul(piece[...], own_order_ref[...])
        total = total + matmul(other_ref[span, :], other_order_ref[...])
        out_ref[span, :] = total.astype(BF16)
        start = span.stop


def out_weight(pieces, own, other, own_order, other_order):
    side, width = own_order.shape
    if len(pieces) == 1:
        own_pieces = [(own, own.shape, lambda i: (0, 0))]
    else:
        own_pieces, start = [], 0
        for piece in pieces:
            count = piece.shape[0]
            own_pieces.append(
                (own, (count, side), lambda i, index=start // count: (index, 0))
            )
            start += count
    return call(
        functools.partial(weight_kernel, len(own_pieces)),
        (1,),
        [whole(other), whole(own_order), whole(other_order)] + own_pieces,
        [((width, width), BF16, (width, width), lambda i: (0, 0))],
    )[0]


def out_kernel(
    own_ref, other_ref, own_order_ref, other_order_ref, weight_ref, x_ref, gain_ref,
    att_ref, hidden_ref, norm_ref,
):
    attended = matmul(own_ref[...], own_order_ref[...])
    attended = (attended + matmul(other_ref[...], other_order_ref[...])).astype(BF16)
    att_ref[...] = attended
    hidden = x_ref[...].astype(F32) + matmul(attended, weight_ref[...])
    hidden_ref[...] = hidden
    norm_ref[...] = (normalise(hidden)[0] * gain_ref[1:2, :]).astype(BF16)


def out_project(own, other, own_order, other_order, weight, tokens, gains):
    rows, width = tokens.shape
    block = rows // 2
    return call(
        out_kernel,
        (2,),
        [by_rows(own, block), by_rows(other, block), whole(own_order), whole(other_order)]
        + [whole(weight), by_rows(tokens, block), whole(gains)],
        [
            ((rows, width), kind, (block, width), lambda i: (i, 0))
            for kind in (BF16, F32, BF16)
        ],
    )


def hidden_back_kernel(
    part_ref, other_ref, hidden_ref, g_ref, gain_ref, weight_ref, order_ref,
    grad_ref, side_ref, att_ref,
):
    unit, scale = normalise(hidden_ref[...])
    incoming = part_ref[...] + other_ref[...].astype(F32)
    grad = g_ref[...].astype(F32) + norm_back(unit, scale, gain_ref[1:2, :], incoming)
    low = grad.astype(BF16)
    grad_ref[...] = grad
    side_ref[...] = contract_cols(low, order_ref[...]).astype(BF16)
    attended = contract_cols(low, weight_ref[...]).astype(BF16)
    att_ref[...] = contract_cols(attended, order_ref[...]).astype(BF16)


def hidden_back(part, other, hidden, grad_output, gains, weight, own_order):
    rows, width = hidden.shape
    block, side = rows // 2, own_order.shape[0]
    return call(
        hidden_back_kernel,
        (2,),
        [by_rows(array, block) for array in (part, other, hidden, grad_output)]
        + [whole(gains), whole(weight), whole(own_order)],
        [
            ((rows, size), kind, (block, size), lambda i: (i, 0))
            for size, kind in ((width, F32), (side, BF16), (side, BF16))
        ],
    )


def column_spans(width):
    return [slice(at, min(at + 2 * LANES, width)) for at in range(0, width, 2 * LANES)]


def tile_matmul(left, pieces, columns):
    total, start = None, 0
    for piece in pieces:
        part = matmul(left[:, start : start + piece.shape[0]], piece[:, columns])
        total = part if total is None else total + part
        start += piece.shape[0]
    return total


def feed_kernel(norm_ref, *refs):
    pieces, (mixed_ref, factor_ref, active_ref) = refs[:-3], refs[-3:]
    units = mixed_ref.shape[1]
    for span in column_spans(units):
        gate = tile_matmul(norm_ref, pieces, span)
        up = tile_matmul(norm_ref, pieces, slice(units + span.start, units + span.stop))
        below = 0.5 * (1.0 + lax.erf(gate * 0.5**0.5))
        active = gate * below
        mixed_ref[:, span] = (active * up).astype(BF16)
        active_ref[:, span] = active
        density = jnp.exp(-0.5 * gate * gate) * (2.0 * np.pi) ** -0.5
        factor_ref[:, span] = up * (below + gate * density)


def feed(normed, pieces, units):
    rows = normed.shape[0]
    block = rows // 2
    return call(
        feed_kernel,
        (2,),
        [by_rows(normed, block)] + [whole(piece) for piece in pieces],
        [
            ((rows, units), kind, (block, units), lambda i: (i, 0))
            for kind in (BF16, F32, F32)
        ],
    )


def feed_back_kernel(g_ref, factor_ref, active_ref, *refs):
    pieces, (gate_ref, up_ref) = refs[:-2], refs[-2:]
    for span in column_spans(factor_ref.shape[1]):
        grad = tile_matmul(g_ref, pieces, span)
        gate_ref[:, span] = (grad * factor_ref[:, span]).astype(BF16)
        up_ref[:, span] = (grad * active_ref[:, span]).astype(BF16)


def feed_back(grad_output, factor, active, pieces):
    rows, units = factor.shape
    block = rows // 2
    return call(
        feed_back_kernel,
        (2,),
        [by_rows(array, block) for array in (grad_output, factor, active)]
        + [whole(piece) for piece in pieces],
        [((rows, units), BF16, (block, units), lambda i: (i, 0)) for _ in range(2)],
    )


def shards(tokens, doc_ids, norm_attn, norm_mlp, w_qkv, w_out, w_in, w_down, cotangent):
    streams, block, width = tokens.shape
    shard_rows = w_qkv.shape[0]
    inner, outer = lax.axis_size("inner"), lax.axis_size("outer")
    core = lax.axis_index("core")
    length = 2 * block
    window = length + 2 * HALF
    rows = streams * length
    side = width // 2
    units = w_down.shape[1] // 2
    padded = -(-units // LANES) * LANES
    chips = outer * inner
    onward = [(i, i + 1) for i in range(chips - 1)]
    back = [(i + 1, i) for i in range(chips - 1)]

    def halves(weight, parts, pad):
        size = weight.shape[1] // (2 * parts)
        cut = [weight[:, i * size : (i + 1) * size] for i in range(2 * parts)]
        if pad != size:
            cut = [jnp.pad(piece, ((0, 0), (0, pad - size))) for piece in cut]
        return cut[0::2], cut[1::2]

    def paired(pieces):
        low = jnp.concatenate([piece for one, _ in pieces for piece in one], 1)
        high = jnp.concatenate([piece for _, two in pieces for piece in two], 1)
        mine = jnp.where(core == 0, low, high)
        return ordered(mine, swap(jnp.where(core == 0, high, low)), 0)

    pair_tokens = ordered(tokens, swap(tokens), 1)

    gains = jnp.pad(jnp.stack([norm_attn, norm_mlp], 1), ((0, 0), (0, LANES - 2)))
    cores = core.astype(jnp.int32).reshape(1)
    mine, other = pack_first(cores, w_qkv, gains, w_out)
    pair_one = ordered(mine, swap(other), 0)
    places = tuple(lax.axis_index(name) for name in ("inner", "outer", "dp"))
    later_in, later_down, pair_one, pair_tokens, places = tied(
        w_in, w_down, pair_one, pair_tokens, places
    )
    low = lax.ppermute(pair_tokens[:, length - HALF :], ("outer", "inner"), onward)
    high = lax.ppermute(pair_tokens[:, :HALF], ("outer", "inner"), back)
    one = direct_sends(pair_one)
    pair_two = paired([halves(later_in, 2, padded)])
    pair_three = paired([halves(later_down, 1, padded)])
    three_near = gather_near([pair_three])
    order = arrival_order(*places, width, shard_rows)
    own_order = lax.dynamic_slice_in_dim(order, core * side, side, 0)
    other_order = lax.dynamic_slice_in_dim(order, (1 - core) * side, side, 0)

    def in_order(value):
        return matmul(value.reshape(-1, width), order).astype(BF16)

    own_tokens = in_order(pair_tokens)
    grad_output = in_order(ordered(cotangent, swap(cotangent), 1))

    start = lax.axis_index(("outer", "inner")) * length
    positions = (start - HALF + jnp.arange(window, dtype=jnp.int32)).astype(F32)
    frequency = ROPE_BASE ** (-(jnp.arange(HD // 2, dtype=F32) * 2.0 / HD))
    angles = positions[:, None] * frequency[None, :]
    cosine, sine = jnp.cos(angles), jnp.sin(angles)
    cosine = jnp.tile(cosine, (1, LANES // (HD // 2)))
    sine = jnp.tile(jnp.concatenate([-sine, sine], 1), (1, LANES // HD))
    ids_padded = jnp.pad(doc_ids, ((0, 0), (HALF, HALF)), constant_values=-1)
    key_ids = lax.dynamic_slice_in_dim(ids_padded, start, window, 1)[:, None, :]
    query_ids = lax.dynamic_slice_in_dim(doc_ids, start, length, 1)[:, :, None]

    prepared = (own_tokens, grad_output, order, own_order, other_order)
    prepared += (cosine, sine, key_ids, query_ids)
    prepared, pair_two, three_near, one, low, high = tied(
        prepared, pair_two, three_near, one, low, high
    )
    own_tokens, grad_output, order, own_order, other_order = prepared[:5]
    cosine, sine, key_ids, query_ids = prepared[5:]
    two = direct_sends(pair_two)
    near = gather_near(one)
    low, high = (in_order(end).reshape(end.shape) for end in (low, high))
    three_far = gather_far(*three_near)
    low, high, two, near, three_near, three_far = tied(
        low, high, two, near, three_near, three_far
    )

    far = gather_far(*near)
    two_own = joined_rows(two)
    late = joined_rows([three_near[0], *three_near[1], *three_near[2], *three_far[0], *three_far[1]])
    near, far, two_own, late = tied(near, far, two_own, late)

    three = direct_sends(late)
    two_near = gather_near([two_own])
    first = in_pieces(*near, *far)
    joined, window_norm, gain_rows = project(
        low, own_tokens.reshape(streams, length, width), high, first, cosine, sine, side
    )
    out_half = joined_rows([piece[:, 3 * side + LANES :] for piece in first])
    weight = out_weight(first, out_half, swap(out_half), own_order, other_order)
    three[1], joined, weight, first, two_near = tied(three[1], joined, weight, first, two_near)

    two_far = gather_far(*two_near)
    joined = joined.reshape(streams, window, 3 * side)
    attended = attend(block, joined, query_ids, key_ids).reshape(rows, side)
    attended_low, hidden, normed_mlp_low = out_project(
        attended, swap(attended), own_order, other_order, weight, own_tokens, gain_rows
    )
    hidden, normed_mlp_low, two_near, two_far, three = tied(
        hidden, normed_mlp_low, two_near, two_far, three
    )
    in_half = in_pieces(*two_near, *two_far)
    down_half = [join_late(three, shard_rows)]
    mixed_low, factor, active = feed(normed_mlp_low, in_half, padded)

    grad_gate, grad_up = feed_back(grad_output, factor, active, down_half)
    sum_in = GradSum([normed_mlp_low] * 2, [grad_gate, grad_up], shard_rows)
    sent_in = sum_in.far()
    grad_gate, grad_up, sent_in, mixed_low = tied(grad_gate, grad_up, sent_in, mixed_low)

    in_far = sum_in.send_far(sent_in)
    down_cuts = split_late(grad_output, mixed_low, shard_rows)
    down_arrived = [
        lax.ppermute(cut, "outer", forward("outer", outer - 1)) for cut in down_cuts[1:2]
    ]
    part, part_low = back_project([grad_gate, grad_up], in_half, [F32, BF16])
    part, part_low, in_far, down_arrived[0], down_cuts = tied(
        part, part_low, in_far, down_arrived[0], down_cuts
    )

    in_near = sum_in.send_near(sum_in.near(in_far))
    down_arrived[1:] = [
        lax.ppermute(down_cuts[distance], "outer", forward("outer", outer - distance))
        for distance in range(2, outer)
    ]
    grad_hidden, hidden_side, grad_attended = hidden_back(
        part, swap(part_low), hidden, grad_output, gain_rows, weight, own_order
    )
    grad_query, mid, to_lower, to_upper = attend_back(
        block, joined, query_ids, key_ids, grad_attended.reshape(streams, length, side),
        cosine, sine,
    )
    from_lower = lax.ppermute(to_upper, ("outer", "inner"), onward)
    from_upper = lax.ppermute(to_lower, ("outer", "inner"), back)
    from_lower, from_upper, in_near, down_arrived[:2] = tied(
        from_lower, from_upper, in_near, down_arrived[:2]
    )

    grad_joined = join_grads(grad_query, mid, from_lower, from_upper, cosine, sine)
    grad_joined = grad_joined.reshape(rows, 3 * side)
    normed_low = window_norm.reshape(streams, window, width)[:, HALF : HALF + length]
    sum_attn = GradSum(
        [normed_low.reshape(rows, width), attended_low], [grad_joined, hidden_side], shard_rows
    )
    sent_attn, in_own = sum_attn.far(), sum_in.own(in_near)
    sent_attn, in_own, grad_joined = tied(sent_attn, in_own, grad_joined)

    attn_far = sum_attn.send_far(sent_attn)
    attn_far, down_arrived, grad_joined, mixed_low = tied(
        attn_far, down_arrived, grad_joined, mixed_low
    )

    attn_near = sum_attn.send_near(sum_attn.near(attn_far))
    in_arrived = sum_in.send_direct(in_own)
    sum_down = LateSum([down_cuts[0], *down_arrived], shard_rows)
    down_near = sum_down.send_near(sum_down.near(sum_down.send_far(sum_down.far())))
    out_mine, out_other = back_split(cores, mixed_low, down_half, streams)
    in_mine, in_other = back_split(cores, grad_joined, first, streams)
    attn_near, in_arrived, out_mine, out_other, in_mine, in_other, down_near = tied(
        attn_near, in_arrived, out_mine, out_other, in_mine, in_other, down_near
    )

    attn_own = sum_attn.own(attn_near)
    attn_arrived = sum_attn.send_direct(attn_own)
    output = end_rows(
        output_kernel, cores, [out_mine, swap(out_other)], [hidden], [order], BF16, streams
    ).reshape(tokens.shape)
    grad_tokens = end_rows(
        input_grad_kernel, cores, [in_mine, swap(in_other)], [grad_hidden, own_tokens],
        [gain_rows, order], F32, streams,
    ).reshape(tokens.shape)
    total_mine, total_other = sum_in.total(cores, in_own, in_arrived)
    grad_in, gain_grad_mlp = assemble(
        cores, total_mine, swap(total_other), [(0, 2, padded, units)], w_in, norm_mlp
    )
    total_mine, total_other = sum_down.total(cores, sum_down.own(down_near), [])
    (grad_down,) = assemble(cores, total_mine, swap(total_other), [(0, 1, padded, units)])
    attn_arrived, output, grad_tokens, grad_in, gain_grad_mlp, grad_down = tied(
        attn_arrived, output, grad_tokens, grad_in, gain_grad_mlp, grad_down
    )
    total_mine, total_other = sum_attn.total(cores, attn_own, attn_arrived)
    grad_qkv, grad_out, gain_grad_attn = assemble(
        cores, total_mine, swap(total_other),
        [(0, 3, side, side), (3 * side, 1, side, side)], w_qkv, norm_attn,
    )
    return (
        output,
        grad_tokens,
        gain_grad_attn.reshape(-1),
        gain_grad_mlp.reshape(-1),
        grad_qkv,
        grad_out,
        grad_in,
        grad_down,
    )


def solution(mesh):
    dp, seq = mesh.shape["dp"], mesh.shape["seq"]
    chips = seq // 2
    outer = 4 if chips % 4 == 0 else 1
    fine = Mesh(
        mesh.devices.reshape(dp, outer, chips // outer, 2), ("dp", "outer", "inner", "core")
    )
    line = ("outer", "inner", "core")
    every = ("dp",) + line
    token = P("dp", line, None)
    vector = P(every)
    matrix = P(every, None)
    return jax.shard_map(
        shards,
        mesh=fine,
        in_specs=(token, P("dp", None), vector, vector, matrix, matrix, matrix, matrix, token),
        out_specs=(token, token, vector, vector, matrix, matrix, matrix, matrix),
        check_vma=False,
    )
```

```python
import functools

import jax
import jax.numpy as jnp
import numpy as np
from jax import lax
from jax.experimental import pallas as pl
from jax.experimental.pallas import tpu as pltpu
from jax.sharding import Mesh, PartitionSpec as P

HD = 64
HALF = 64
LANES = 128
NORM_EPSILON = 1e-05
ROPE_BASE = 10000.0
F32 = jnp.float32
BF16 = jnp.bfloat16


def contract_cols(left, right):
    return lax.dot_general(left, right, (((1,), (1,)), ((), ())), preferred_element_type=F32)


def contract_rows(left, right):
    return lax.dot_general(left, right, (((0,), (0,)), ((), ())), preferred_element_type=F32)


def matmul(left, right):
    return jnp.dot(left, right, preferred_element_type=F32)


def tied(*values):
    return lax.optimization_barrier(values)


def call(kernel, grid, ins, outs, scratch=(), limit=40):
    out = pl.pallas_call(
        kernel,
        grid=grid,
        in_specs=[
            pl.BlockSpec(memory_space=pltpu.SMEM) if block is None else pl.BlockSpec(block, index)
            for _, block, index in ins
        ],
        out_specs=[pl.BlockSpec(block, index) for _, _, block, index in outs],
        out_shape=[jax.ShapeDtypeStruct(shape, kind) for shape, kind, _, _ in outs],
        scratch_shapes=list(scratch),
        compiler_params=pltpu.CompilerParams(vmem_limit_bytes=limit * 2**20),
        cost_estimate=pl.CostEstimate(flops=1024, bytes_accessed=1024, transcendentals=0),
    )(*[array for array, _, _ in ins])
    return out


def whole(array):
    return (array, array.shape, lambda *_: (0,) * array.ndim)


def swap(value):
    return lax.ppermute(value, "core", [(0, 1), (1, 0)])


def ordered(mine, other, axis):
    first = lax.axis_index("core") == 0
    return jnp.concatenate(
        [jnp.where(first, mine, other), jnp.where(first, other, mine)], axis=axis
    )


def forward(axis, distance=1):
    count = lax.axis_size(axis)
    return [(i, (i + distance) % count) for i in range(count)]


def ring_gather(axis, piece):
    pieces = [piece]
    for _ in range(1, lax.axis_size(axis)):
        pieces.append(lax.ppermute(pieces[-1], axis, forward(axis)))
    return pieces[1:]


def direct_send(rows, *distances):
    count = lax.axis_size("outer")
    return [
        lax.ppermute(rows, "outer", forward("outer", distance))
        for distance in distances
        if distance < count
    ]


def direct_sends(rows):
    return [rows] + direct_send(rows, *range(1, lax.axis_size("outer")))


def joined_rows(pieces):
    return jnp.concatenate(pieces, 0) if len(pieces) > 1 else pieces[0]


def gather_near(arrived):
    own = joined_rows(arrived)
    return own, ring_gather("inner", own), ring_gather("dp", own)


def copy_kernel(*refs):
    count = len(refs) // 2
    for source, target in zip(refs[:count], refs[count:]):
        target[...] = source[...]


def far_halves(along_x, along_y, half):
    if len(along_x) > 1 or len(along_y) > 1 or half % 32:
        return (
            joined_rows([piece[:half] for piece in along_y]),
            joined_rows([piece[half:] for piece in along_x]),
        )
    columns = along_x[0].shape[1]
    return call(
        copy_kernel,
        (1,),
        [(along_y[0], (half, columns), lambda i: (0, 0))]
        + [(along_x[0], (half, columns), lambda i: (1, 0))],
        [((half, columns), BF16, (half, columns), lambda i: (0, 0)) for _ in range(2)],
    )


def gather_far(own, along_x, along_y):
    one, two = far_halves(along_x, along_y, own.shape[0] // 2)
    return ring_gather("inner", one), ring_gather("dp", two)


def in_pieces(own, along_x, along_y, one, two):
    pieces = [own, *along_x, *along_y, *one, *two]
    if any(piece.shape[0] % LANES for piece in pieces):
        pieces = [joined_rows(pieces)]
    return pieces


def order_blocks(inner, dp):
    blocks = [(0, 0, 0, 2)]
    blocks += [(d, 0, 0, 2) for d in range(1, inner)] + [(0, d, 0, 2) for d in range(1, dp)]
    blocks += [(d, e, 0, 1) for d in range(1, inner) for e in range(1, dp)]
    return blocks + [(d, e, 1, 2) for e in range(1, dp) for d in range(1, inner)]


def late_segments(shard_rows):
    inner, outer, dp = (lax.axis_size(name) for name in ("inner", "outer", "dp"))
    start, at = 0, {}
    for d, e, low, high in order_blocks(inner, dp):
        for part in range(low, high):
            at[d, e, part] = start
            start += shard_rows
    segments = []
    for d, e, low, high in order_blocks(inner, dp):
        for distance in range(low * outer // 2, high * outer // 2):
            first, second = at[d, e, 0], at[d, e, 1]
            if second == first + shard_rows:
                segments.append((distance, first, 2 * shard_rows))
            else:
                segments += [(distance, first, shard_rows), (distance, second, shard_rows)]
    return segments


def join_kernel_rows(segments, *refs):
    pieces, out_ref = refs[:-1], refs[-1]
    at = 0
    for distance, start, count in segments:
        out_ref[at : at + count, :] = pieces[distance][start : start + count, :]
        at += count


def join_late(pieces, shard_rows):
    segments = late_segments(shard_rows)
    columns = pieces[0].shape[1]
    rows = sum(count for _, _, count in segments)
    if shard_rows % 32:
        return jnp.concatenate([pieces[d][at : at + n] for d, at, n in segments], 0)
    return call(
        functools.partial(join_kernel_rows, segments),
        (1,),
        [whole(piece) for piece in pieces],
        [((rows, columns), BF16, (rows, columns), lambda i: (0, 0))],
    )[0]


def split_kernel_rows(segments, left_ref, right_ref, *outs):
    place, at = [], 0
    for distance, start, count in segments:
        place.append((at, distance, start, count))
        at += count
    for top in range(0, at, LANES):
        rows = contract_rows(left_ref[:, top : top + LANES], right_ref[...]).astype(BF16)
        for begin, distance, start, count in place:
            if top <= begin < top + LANES:
                outs[distance][start : start + count, :] = rows[begin - top : begin - top + count]


def split_late(left, right, shard_rows):
    segments = late_segments(shard_rows)
    outer = lax.axis_size("outer")
    rows, columns = left.shape[1] // outer, right.shape[1]
    if shard_rows % 32:
        total, at, cuts = contract_rows(left, right).astype(BF16), 0, {}
        for distance, start, count in segments:
            cuts[distance, start] = total[at : at + count]
            at += count
        return [
            jnp.concatenate([cuts[key] for key in sorted(cuts) if key[0] == distance], 0)
            for distance in range(outer)
        ]
    return call(
        functools.partial(split_kernel_rows, segments),
        (1,),
        [whole(left), whole(right)],
        [((rows, columns), BF16, (rows, columns), lambda i: (0, 0)) for _ in range(outer)],
    )


def arrival_order(x, z, y, width, shard_rows):
    inner, outer, dp = (lax.axis_size(name) for name in ("inner", "outer", "dp"))
    half = outer * shard_rows
    blocks = order_blocks(inner, dp)
    place = np.concatenate([np.arange(low * half, high * half) for _, _, low, high in blocks])
    sizes = [(high - low) * half for _, _, low, high in blocks]
    along_x = np.repeat([block[0] for block in blocks], sizes)
    along_y = np.repeat([block[1] for block in blocks], sizes)
    along_z, row = place // (2 * shard_rows), place % (2 * shard_rows)
    at_x = (x - jnp.asarray(along_x, jnp.int32) + inner) % inner
    at_y = (y - jnp.asarray(along_y, jnp.int32) + dp) % dp
    at_z = (z - jnp.asarray(along_z, jnp.int32) + outer) % outer
    source = ((at_y * outer + at_z) * inner + at_x) * 2 * shard_rows + row
    return (jnp.arange(width, dtype=jnp.int32)[:, None] == source[None, :]).astype(BF16)


def rows_kernel(pairs, layout, *refs):
    rights, refs = refs[:pairs], refs[pairs:]
    inputs, outs = refs[: -len(layout)], refs[-len(layout) :]
    for places, out_ref in zip(layout, outs):
        lefts, adds = inputs[:pairs], inputs[pairs : pairs + len(places)]
        inputs = inputs[pairs + len(places) :]
        start = 0
        for left, right in zip(lefts, rights):
            columns = slice(start, start + right.shape[1])
            start = columns.stop
            total = contract_rows(left[...], right[...])
            for add in adds:
                if add.shape[0] == total.shape[0]:
                    total = total + add[:, columns].astype(F32)
            out_ref[:, columns] = total.astype(BF16)
            for add, at in zip(adds, places):
                if add.shape[0] != total.shape[0]:
                    span = slice(at, at + add.shape[0])
                    part = total[span] + add[:, columns].astype(F32)
                    out_ref[span, columns] = part.astype(BF16)


class GradSum:
    def __init__(self, lefts, rights, shard_rows):
        self.lefts, self.rights = lefts, rights
        self.inner, self.outer, self.dp = (
            lax.axis_size(name) for name in ("inner", "outer", "dp")
        )
        self.shard = 2 * shard_rows
        self.half = self.outer * shard_rows
        self.at_x = 2 * self.half
        self.at_y = self.at_x + (self.inner - 1) * 2 * self.half
        self.at_one = self.at_y + (self.dp - 1) * 2 * self.half
        self.at_two = self.at_one + (self.inner - 1) * (self.dp - 1) * self.half

    def rows(self, *parts):
        depth = self.lefts[0].shape[0]
        columns = sum(right.shape[1] for right in self.rights)
        ins, outs, layout = [whole(right) for right in self.rights], [], []
        for start, count, adds in parts:
            adds = [(rows, place) for rows, place in adds if rows is not None]
            lefts, index = self.lefts, start // count
            if count % LANES or start % count:
                lefts, index = [left[:, start : start + count] for left in lefts], 0
            ins += [
                (left, (depth, count), lambda i, index=index: (0, index)) for left in lefts
            ]
            ins += [whole(rows) for rows, _ in adds]
            outs.append(((count, columns), BF16, (count, columns), lambda i: (0, 0)))
            layout.append([place for _, place in adds])
        return call(
            functools.partial(rows_kernel, len(self.rights), layout), (1,), ins, outs
        )

    def ring(self, axis, part, first):
        arrived = None
        for step in range(1, lax.axis_size(axis)):
            sent = first if step == 1 else self.rows(part(step, arrived))[0]
            arrived = lax.ppermute(sent, axis, forward(axis))
        return arrived

    def one(self, distance, arrived):
        count = (self.dp - 1) * self.half
        return (self.at_one + (distance - 1) * count, count, [(arrived, 0)])

    def two(self, distance, arrived):
        count = (self.inner - 1) * self.half
        return (self.at_two + (distance - 1) * count, count, [(arrived, 0)])

    def far(self):
        return self.rows(self.one(1, None), self.two(1, None))

    def send_far(self, firsts):
        return (
            self.ring("inner", self.one, firsts[0]), self.ring("dp", self.two, firsts[1])
        )

    def along(self, start, distance, arrived, extra, place):
        count = 2 * self.half
        extra = extra[(distance - 1) * self.half : distance * self.half]
        return (start + (distance - 1) * count, count, [(arrived, 0), (extra, place)])

    def along_x(self, distance, arrived):
        return self.along(self.at_x, distance, arrived, self.sums[1], self.half)

    def along_y(self, distance, arrived):
        return self.along(self.at_y, distance, arrived, self.sums[0], 0)

    def near(self, sums):
        self.sums = sums
        return self.rows(self.along_x(1, None), self.along_y(1, None))

    def send_near(self, firsts):
        return (
            self.ring("inner", self.along_x, firsts[0]),
            self.ring("dp", self.along_y, firsts[1]),
        )

    def own(self, nears):
        return self.rows((0, 2 * self.half, [(near, 0) for near in nears]))[0]

    def cut(self, own, distance):
        return own[distance * self.shard : (distance + 1) * self.shard]

    def send_direct(self, own):
        return [
            lax.ppermute(
                self.cut(own, distance), "outer", forward("outer", self.outer - distance)
            )
            for distance in range(1, self.outer)
        ]

    def total(self, core, own, arrived):
        columns = own.shape[1]
        half = self.shard // 2
        return call(
            total_kernel,
            (1,),
            [(core, None, None), (own, (self.shard, columns), lambda i: (0, 0))]
            + [whole(rows) for rows in arrived],
            [((half, columns), F32, (half, columns), lambda i: (0, 0)) for _ in range(2)],
        )


def late_kernel(count, layout, *refs):
    blocks, refs = refs[:count], refs[count:]
    adds, outs = refs[: -len(layout)], refs[-len(layout) :]
    for (start, rows, places), out_ref in zip(layout, outs):
        mine, adds = adds[: len(places)], adds[len(places) :]
        total = None
        for block in blocks:
            part = block[start : start + rows, :].astype(F32)
            total = part if total is None else total + part
        for add in mine:
            if add.shape[0] == rows:
                total = total + add[...].astype(F32)
        out_ref[...] = total.astype(BF16)
        for add, at in zip(mine, places):
            if add.shape[0] != rows:
                span = slice(at, at + add.shape[0])
                out_ref[span, :] = (total[span] + add[...].astype(F32)).astype(BF16)


class LateSum(GradSum):
    def __init__(self, blocks, shard_rows):
        GradSum.__init__(self, [], [], shard_rows)
        self.blocks, self.half = blocks, shard_rows
        self.at_x = 2 * self.half
        self.at_y = self.at_x + (self.inner - 1) * 2 * self.half
        self.at_one = self.at_y + (self.dp - 1) * 2 * self.half
        self.at_two = self.at_one + (self.inner - 1) * (self.dp - 1) * self.half

    def rows(self, *parts):
        columns = self.blocks[0].shape[1]
        parts = [
            (start, count, [add for add in adds if add[0] is not None])
            for start, count, adds in parts
        ]
        if self.half % 32:
            results = []
            for start, count, adds in parts:
                total = sum(block[start : start + count].astype(F32) for block in self.blocks)
                for rows, place in adds:
                    span = slice(place, place + rows.shape[0])
                    total = total.at[span].add(rows.astype(F32))
                results.append(total.astype(BF16))
            return results
        return call(
            functools.partial(
                late_kernel,
                len(self.blocks),
                [(start, count, [at for _, at in adds]) for start, count, adds in parts],
            ),
            (1,),
            [whole(block) for block in self.blocks]
            + [whole(rows) for _, _, adds in parts for rows, _ in adds],
            [
                ((count, columns), BF16, (count, columns), lambda i: (0, 0))
                for _, count, _ in parts
            ],
        )


def own_half(core_ref, value):
    half = value.shape[0] // 2
    return jnp.where(core_ref[0] == 0, value[:half], value[half:])


def total_kernel(core_ref, *refs):
    total = None
    for ref in refs[:-2]:
        rows = ref[...].astype(F32)
        total = rows if total is None else total + rows
    half = total.shape[0] // 2
    first = core_ref[0] == 0
    refs[-2][...] = jnp.where(first, total[:half], total[half:])
    refs[-1][...] = jnp.where(first, total[half:], total[:half])


def assemble_kernel(layout, core_ref, mine_ref, other_ref, *refs):
    first = core_ref[0] == 0
    count = len(layout)
    pair = (
        jnp.where(first, mine_ref[...], other_ref[...]),
        jnp.where(first, other_ref[...], mine_ref[...]),
    )
    outs = refs[-count:] if len(refs) == count else refs[2:-1]
    for out_ref, (start, parts, stride, size) in zip(outs, layout):
        cuts = []
        for i in range(parts):
            at = start + i * stride
            cuts += [half[:, at : at + size] for half in pair]
        out_ref[...] = jnp.concatenate(cuts, 1)
    if len(refs) > count:
        weight_ref, gain_ref = refs[:2]
        product = weight_ref[...].astype(F32) * outs[0][...]
        refs[-1][...] = jnp.sum(product, -1, keepdims=True) / gain_ref[...].astype(F32)


def assemble(core, mine, other, layout, weight=None, gain=None):
    rows = mine.shape[0]
    ins = [(core, None, None), whole(mine), whole(other)]
    sizes = [2 * parts * size for _, parts, _, size in layout]
    if weight is not None:
        ins += [whole(weight), whole(gain.reshape(rows, 1))]
        sizes.append(1)
    return call(
        functools.partial(assemble_kernel, layout),
        (1,),
        ins,
        [((rows, size), F32, (rows, size), lambda i: (0, 0)) for size in sizes],
    )


def pack_kernel(side, core_ref, qkv_ref, gain_ref, out_ref, mine_ref, other_ref):
    def fill(target, half):
        for part in range(3):
            start = (2 * part + half) * side
            target[:, part * side : (part + 1) * side] = qkv_ref[:, start : start + side]
        target[:, 3 * side : 3 * side + LANES] = gain_ref[...]
        target[:, 3 * side + LANES :] = out_ref[:, half * side : (half + 1) * side]

    for half in range(2):

        @pl.when(core_ref[0] == half)
        def _():
            fill(mine_ref, half)
            fill(other_ref, 1 - half)


def pack_first(core, w_qkv, gains, w_out):
    rows, side = w_out.shape[0], w_out.shape[1] // 2
    columns = 4 * side + LANES
    return call(
        functools.partial(pack_kernel, side),
        (1,),
        [(core, None, None), whole(w_qkv), whole(gains), whole(w_out)],
        [((rows, columns), BF16, (rows, columns), lambda i: (0, 0)) for _ in range(2)],
    )


def normalise(values):
    centred = values - jnp.mean(values, -1, keepdims=True)
    scale = lax.rsqrt(jnp.mean(centred * centred, -1, keepdims=True) + NORM_EPSILON)
    return centred * scale, scale


def norm_back(unit, scale, gain, incoming):
    grad = incoming * gain
    return scale * (
        grad
        - jnp.mean(grad, -1, keepdims=True)
        - unit * jnp.mean(grad * unit, -1, keepdims=True)
    )


def piece_matmul(left, pieces):
    total, start = None, 0
    for piece in pieces:
        part = matmul(left[:, start : start + piece.shape[0]], piece[...])
        total = part if total is None else total + part
        start += piece.shape[0]
    return total


def back_kernel(starts, count, *refs):
    grads, pieces, out_refs = refs[: len(starts)], refs[len(starts) : count], refs[count:]
    at = 0
    for piece in pieces:
        total = None
        for grad, start in zip(grads, starts):
            part = contract_cols(grad[...], piece[:, start : start + grad.shape[1]])
            total = part if total is None else total + part
        for out_ref in out_refs:
            out_ref[:, at : at + piece.shape[0]] = total.astype(out_ref.dtype)
        at += piece.shape[0]


def back_project(grads, pieces, kinds):
    rows = grads[0].shape[0]
    block = rows // 2
    starts, end = [], 0
    for grad in grads:
        starts.append(end)
        end += grad.shape[1]
    width = sum(piece.shape[0] for piece in pieces)
    return call(
        functools.partial(back_kernel, starts, len(grads) + len(pieces)),
        (2,),
        [(grad, (block, grad.shape[1]), lambda i: (i, 0)) for grad in grads]
        + [(piece, (piece.shape[0], end), lambda i: (0, 0)) for piece in pieces],
        [((rows, width), kind, (block, width), lambda i: (i, 0)) for kind in kinds],
    )


def split_kernel(core_ref, grad_ref, *refs):
    pieces, (mine_ref, other_ref) = refs[:-2], refs[-2:]
    width = grad_ref.shape[1]
    half = grad_ref.shape[0] // 2
    at = 0
    for piece in pieces:
        total = contract_cols(grad_ref[...], piece[:, :width])
        first = core_ref[0] == 0
        span = slice(at, at + piece.shape[0])
        mine_ref[:, span] = jnp.where(first, total[:half], total[half:])
        other_ref[:, span] = jnp.where(first, total[half:], total[:half]).astype(BF16)
        at = span.stop


def back_split(core, grad, pieces, streams):
    rows, columns = grad.shape
    block = rows // streams
    width = sum(piece.shape[0] for piece in pieces)
    return call(
        split_kernel,
        (streams,),
        [(core, None, None), (grad, (block, columns), lambda i: (i, 0))]
        + [(piece, (piece.shape[0], columns), lambda i: (0, 0)) for piece in pieces],
        [
            ((rows // 2, width), kind, (block // 2, width), lambda i: (i, 0))
            for kind in (F32, BF16)
        ],
    )


def output_kernel(core_ref, mine_ref, other_ref, hidden_ref, order_ref, out_ref):
    total = own_half(core_ref, hidden_ref[...]) + mine_ref[...] + other_ref[...].astype(F32)
    out_ref[...] = contract_cols(total.astype(BF16), order_ref[...]).astype(BF16)


def input_grad_kernel(
    core_ref, mine_ref, other_ref, hidden_ref, x_ref, gain_ref, order_ref, out_ref
):
    unit, scale = normalise(own_half(core_ref, x_ref[...].astype(F32)))
    incoming = mine_ref[...] + other_ref[...].astype(F32)
    total = own_half(core_ref, hidden_ref[...])
    total = total + norm_back(unit, scale, gain_ref[0:1, :], incoming)
    result = None
    for _ in range(3):
        part = total.astype(BF16)
        total = total - part.astype(F32)
        part = contract_cols(part, order_ref[...])
        result = part if result is None else result + part
    out_ref[...] = result


def end_rows(kernel, core, halves, fulls, wholes, kind, streams):
    rows, width = halves[0].shape
    block = rows // streams
    return call(
        kernel,
        (streams,),
        [(core, None, None)]
        + [(array, (block, width), lambda i: (i, 0)) for array in halves]
        + [(array, (2 * block, width), lambda i: (i, 0)) for array in fulls]
        + [whole(array) for array in wholes],
        [((rows, width), kind, (block, width), lambda i: (i, 0))],
    )[0]


def turned(values):
    width = values.shape[-1]
    lane = lax.broadcasted_iota(jnp.int32, values.shape, values.ndim - 1)
    ahead = pltpu.roll(values, width - HD // 2, values.ndim - 1)
    behind = pltpu.roll(values, HD // 2, values.ndim - 1)
    return jnp.where(lane % HD < HD // 2, ahead, behind)


def project_kernel(count, low_ref, x_ref, high_ref, cos_ref, sin_ref, *refs):
    gains, weights = refs[:count], refs[count : 2 * count]
    out_ref, norm_ref, gain_ref = refs[2 * count :]

    @pl.when(pl.program_id(0) == 0)
    def _():
        pick = lax.broadcasted_iota(jnp.int32, (8, LANES), 0) == lax.broadcasted_iota(
            jnp.int32, (8, LANES), 1
        )
        pick = pick.astype(F32).astype(BF16)
        start = 0
        for piece in gains:
            gain_ref[:, start : start + piece.shape[0]] = contract_cols(pick, piece[...])
            start += piece.shape[0]
        for stream in range(x_ref.shape[0]):
            at = stream * cos_ref.shape[0]
            for ref in (low_ref, x_ref, high_ref):
                unit, _ = normalise(ref[stream].astype(F32))
                span = slice(at, at + ref.shape[1])
                norm_ref[span, :] = (unit * gain_ref[0:1, :]).astype(BF16)
                at = span.stop

    values = piece_matmul(norm_ref, weights)
    keep = pl.program_id(0) == 2
    length = cos_ref.shape[0]
    for top in range(0, values.shape[0], length):
        for left in range(0, values.shape[1], LANES):
            part = values[top : top + length, left : left + LANES]
            rotated = part * cos_ref[...] + turned(part) * sin_ref[...]
            out_ref[top : top + length, left : left + LANES] = jnp.where(
                keep, part, rotated
            ).astype(BF16)


def project(low, tokens, high, pieces, cosine, sine, side):
    width = tokens.shape[2]
    rows = tokens.shape[0] * cosine.shape[0]
    gain_block = 3 * side // LANES
    return call(
        functools.partial(project_kernel, len(pieces)),
        (3,),
        [whole(low), whole(tokens), whole(high), whole(cosine), whole(sine)]
        + [(piece, (piece.shape[0], LANES), lambda j: (0, gain_block)) for piece in pieces]
        + [(piece, (piece.shape[0], side), lambda j: (0, j)) for piece in pieces],
        [
            ((rows, 3 * side), BF16, (rows, side), lambda j: (0, j)),
            ((rows, width), BF16, (rows, width), lambda j: (0, 0)),
            ((8, width), F32, (8, width), lambda j: (0, 0)),
        ],
    )


def head_masks():
    lane = lax.broadcasted_iota(jnp.int32, (1, LANES), 1)
    return [(lane // HD == head).astype(F32).astype(BF16) for head in range(LANES // HD)]


def block_mask(query_ids, key_ids):
    rows, width = query_ids.shape[0], key_ids.shape[1]
    offset = lax.broadcasted_iota(jnp.int32, (rows, width), 1) - lax.broadcasted_iota(
        jnp.int32, (rows, width), 0
    )
    return (offset >= 0) & (offset <= 2 * HALF) & (query_ids == key_ids)


def block_probs(query, keys, allowed):
    scores = jnp.where(allowed, contract_cols(query, keys) * HD**-0.5, -1e30)
    grown = jnp.exp(scores - jnp.max(scores, -1, keepdims=True))
    return grown / jnp.sum(grown, -1, keepdims=True)


def attend_kernel(block, q_ref, k_ref, v_ref, qid_ref, kid_ref, out_ref):
    masks = head_masks()
    for start in range(0, out_ref.shape[1], block):
        span = slice(start, start + block + 2 * HALF)
        allowed = block_mask(qid_ref[0, start : start + block], kid_ref[0, :, span])
        query = q_ref[0, HALF + start : HALF + start + block]
        total = None
        for mask in masks:
            probs = block_probs(query * mask, k_ref[0, span], allowed)
            part = matmul(probs.astype(BF16), v_ref[0, span]) * mask.astype(F32)
            total = part if total is None else total + part
        out_ref[0, start : start + block] = total.astype(BF16)


def attend_back_kernel(
    block, q_ref, k_ref, v_ref, qid_ref, kid_ref, grad_ref, cos_ref, sin_ref,
    dq_ref, mid_ref, low_ref, high_ref,
):
    masks = head_masks()
    length = dq_ref.shape[1]
    grad_keys = grad_values = jnp.zeros((length + 2 * HALF, LANES), F32)
    for start in range(0, length, block):
        span = slice(start, start + block + 2 * HALF)
        mid = slice(HALF + start, HALF + start + block)
        rows = slice(start, start + block)
        allowed = block_mask(qid_ref[0, rows], kid_ref[0, :, span])
        query_all, grad_all = q_ref[0, mid], grad_ref[0, rows]
        keys, values = k_ref[0, span], v_ref[0, span]
        grad_query, part_keys, part_values = 0.0, 0.0, 0.0
        for mask in masks:
            query, grad = query_all * mask, grad_all * mask
            probs = block_probs(query, keys, allowed)
            grad_probs = contract_cols(grad, values)
            delta = jnp.sum(probs * grad_probs, -1, keepdims=True)
            grad_scores = (probs * (grad_probs - delta)).astype(BF16)
            grad_query += matmul(grad_scores, keys) * mask.astype(F32)
            part_keys += contract_rows(grad_scores, query)
            part_values += contract_rows(probs.astype(BF16), grad)
        grad_query = grad_query * HD**-0.5
        dq_ref[0, rows] = (
            grad_query * cos_ref[mid] - turned(grad_query) * sin_ref[mid]
        ).astype(BF16)
        before, after = start, length - start - block

        def placed(part):
            pieces = [part]
            if before:
                pieces.insert(0, jnp.zeros((before, LANES), F32))
            if after:
                pieces.append(jnp.zeros((after, LANES), F32))
            return jnp.concatenate(pieces, 0)

        grad_keys += placed(part_keys)
        grad_values += placed(part_values)
    for index, total in enumerate((grad_keys * HD**-0.5, grad_values)):
        low_ref[0, index] = total[:HALF].astype(BF16)
        mid_ref[0, index] = total[HALF : HALF + length]
        high_ref[0, index] = total[HALF + length :].astype(BF16)


def attention_inputs(joined, query_ids, key_ids):
    window, groups = joined.shape[1], joined.shape[2] // 3 // LANES
    inputs = [
        (joined, (1, window, LANES), lambda s, h, shift=shift: (s, 0, h + shift))
        for shift in (0, groups, 2 * groups)
    ]
    inputs += [
        (ids, (1,) + ids.shape[1:], lambda s, h: (s, 0, 0)) for ids in (query_ids, key_ids)
    ]
    return inputs


def attend(block, joined, query_ids, key_ids):
    streams, window, columns = joined.shape
    length, side = window - 2 * HALF, columns // 3
    return call(
        functools.partial(attend_kernel, block),
        (streams, side // LANES),
        attention_inputs(joined, query_ids, key_ids),
        [((streams, length, side), BF16, (1, length, LANES), lambda s, h: (s, 0, h))],
        limit=24,
    )[0]


def attend_back(block, joined, query_ids, key_ids, grad, cosine, sine):
    streams, length, side = grad.shape

    def pair(rows, kind):
        return (
            (streams, 2, rows, side), kind, (1, 2, rows, LANES), lambda s, h: (s, 0, 0, h)
        )

    return call(
        functools.partial(attend_back_kernel, block),
        (streams, side // LANES),
        attention_inputs(joined, query_ids, key_ids)
        + [(grad, (1, length, LANES), lambda s, h: (s, 0, h)), whole(cosine), whole(sine)],
        [
            ((streams, length, side), BF16, (1, length, LANES), lambda s, h: (s, 0, h)),
            pair(length, F32),
            pair(HALF, BF16),
            pair(HALF, BF16),
        ],
        limit=24,
    )


def join_kernel(dq_ref, mid_ref, low_ref, high_ref, cos_ref, sin_ref, out_ref):
    length, width = dq_ref.shape[1:]
    out_ref[0, :, :width] = dq_ref[0]
    cosine, sine = cos_ref[HALF : HALF + length], sin_ref[HALF : HALF + length]
    for index in range(2):
        for start in range(0, width, LANES):
            lanes = slice(start, start + LANES)
            total = mid_ref[0, index, :, lanes]
            total = total + jnp.concatenate(
                [
                    low_ref[0, index, :, lanes].astype(F32),
                    jnp.zeros((length - 2 * HALF, LANES), F32),
                    high_ref[0, index, :, lanes].astype(F32),
                ],
                0,
            )
            if index == 0:
                total = total * cosine - turned(total) * sine
            to = (1 + index) * width + start
            out_ref[0, :, to : to + LANES] = total.astype(BF16)


def join_grads(grad_query, mid, from_lower, from_upper, cosine, sine):
    streams, length, width = grad_query.shape

    def of_stream(array):
        block = (1,) + array.shape[1:]
        return (array, block, lambda s: (s,) + (0,) * (array.ndim - 1))

    return call(
        join_kernel,
        (streams,),
        [of_stream(array) for array in (grad_query, mid, from_lower, from_upper)]
        + [whole(cosine), whole(sine)],
        [((streams, length, 3 * width), BF16, (1, length, 3 * width), lambda s: (s, 0, 0))],
        limit=24,
    )[0]


def by_rows(array, block):
    return (array, (block, array.shape[1]), lambda i: (i, 0))


def weight_kernel(count, other_ref, own_order_ref, other_order_ref, *refs):
    start = 0
    out_ref = refs[count]
    for piece in refs[:count]:
        span = slice(start, start + piece.shape[0])
        total = matmul(piece[...], own_order_ref[...])
        total = total + matmul(other_ref[span, :], other_order_ref[...])
        out_ref[span, :] = total.astype(BF16)
        start = span.stop


def out_weight(pieces, own, other, own_order, other_order):
    side, width = own_order.shape
    if len(pieces) == 1:
        own_pieces = [(own, own.shape, lambda i: (0, 0))]
    else:
        own_pieces, start = [], 0
        for piece in pieces:
            count = piece.shape[0]
            own_pieces.append(
                (own, (count, side), lambda i, index=start // count: (index, 0))
            )
            start += count
    return call(
        functools.partial(weight_kernel, len(own_pieces)),
        (1,),
        [whole(other), whole(own_order), whole(other_order)] + own_pieces,
        [((width, width), BF16, (width, width), lambda i: (0, 0))],
    )[0]


def out_kernel(
    own_ref, other_ref, own_order_ref, other_order_ref, weight_ref, x_ref, gain_ref,
    att_ref, hidden_ref, norm_ref,
):
    attended = matmul(own_ref[...], own_order_ref[...])
    attended = (attended + matmul(other_ref[...], other_order_ref[...])).astype(BF16)
    att_ref[...] = attended
    hidden = x_ref[...].astype(F32) + matmul(attended, weight_ref[...])
    hidden_ref[...] = hidden
    norm_ref[...] = (normalise(hidden)[0] * gain_ref[1:2, :]).astype(BF16)


def out_project(own, other, own_order, other_order, weight, tokens, gains):
    rows, width = tokens.shape
    block = rows // 2
    return call(
        out_kernel,
        (2,),
        [by_rows(own, block), by_rows(other, block), whole(own_order), whole(other_order)]
        + [whole(weight), by_rows(tokens, block), whole(gains)],
        [
            ((rows, width), kind, (block, width), lambda i: (i, 0))
            for kind in (BF16, F32, BF16)
        ],
    )


def hidden_back_kernel(
    part_ref, other_ref, hidden_ref, g_ref, gain_ref, weight_ref, order_ref,
    grad_ref, side_ref, att_ref,
):
    unit, scale = normalise(hidden_ref[...])
    incoming = part_ref[...] + other_ref[...].astype(F32)
    grad = g_ref[...].astype(F32) + norm_back(unit, scale, gain_ref[1:2, :], incoming)
    low = grad.astype(BF16)
    grad_ref[...] = grad
    side_ref[...] = contract_cols(low, order_ref[...]).astype(BF16)
    attended = contract_cols(low, weight_ref[...]).astype(BF16)
    att_ref[...] = contract_cols(attended, order_ref[...]).astype(BF16)


def hidden_back(part, other, hidden, grad_output, gains, weight, own_order):
    rows, width = hidden.shape
    block, side = rows // 2, own_order.shape[0]
    return call(
        hidden_back_kernel,
        (2,),
        [by_rows(array, block) for array in (part, other, hidden, grad_output)]
        + [whole(gains), whole(weight), whole(own_order)],
        [
            ((rows, size), kind, (block, size), lambda i: (i, 0))
            for size, kind in ((width, F32), (side, BF16), (side, BF16))
        ],
    )


def column_spans(width):
    return [slice(at, min(at + 2 * LANES, width)) for at in range(0, width, 2 * LANES)]


def tile_matmul(left, pieces, columns):
    total, start = None, 0
    for piece in pieces:
        part = matmul(left[:, start : start + piece.shape[0]], piece[:, columns])
        total = part if total is None else total + part
        start += piece.shape[0]
    return total


def feed_kernel(norm_ref, *refs):
    pieces, (mixed_ref, factor_ref, active_ref) = refs[:-3], refs[-3:]
    units = mixed_ref.shape[1]
    for span in column_spans(units):
        gate = tile_matmul(norm_ref, pieces, span)
        up = tile_matmul(norm_ref, pieces, slice(units + span.start, units + span.stop))
        below = 0.5 * (1.0 + lax.erf(gate * 0.5**0.5))
        active = gate * below
        mixed_ref[:, span] = (active * up).astype(BF16)
        active_ref[:, span] = active
        density = jnp.exp(-0.5 * gate * gate) * (2.0 * np.pi) ** -0.5
        factor_ref[:, span] = up * (below + gate * density)


def feed(normed, pieces, units):
    rows = normed.shape[0]
    block = rows // 2
    return call(
        feed_kernel,
        (2,),
        [by_rows(normed, block)] + [whole(piece) for piece in pieces],
        [
            ((rows, units), kind, (block, units), lambda i: (i, 0))
            for kind in (BF16, F32, F32)
        ],
    )


def feed_back_kernel(g_ref, factor_ref, active_ref, *refs):
    pieces, (gate_ref, up_ref) = refs[:-2], refs[-2:]
    for span in column_spans(factor_ref.shape[1]):
        grad = tile_matmul(g_ref, pieces, span)
        gate_ref[:, span] = (grad * factor_ref[:, span]).astype(BF16)
        up_ref[:, span] = (grad * active_ref[:, span]).astype(BF16)


def feed_back(grad_output, factor, active, pieces):
    rows, units = factor.shape
    block = rows // 2
    return call(
        feed_back_kernel,
        (2,),
        [by_rows(array, block) for array in (grad_output, factor, active)]
        + [whole(piece) for piece in pieces],
        [((rows, units), BF16, (block, units), lambda i: (i, 0)) for _ in range(2)],
    )


def shards(tokens, doc_ids, norm_attn, norm_mlp, w_qkv, w_out, w_in, w_down, cotangent):
    streams, block, width = tokens.shape
    shard_rows = w_qkv.shape[0]
    inner, outer = lax.axis_size("inner"), lax.axis_size("outer")
    core = lax.axis_index("core")
    length = 2 * block
    window = length + 2 * HALF
    rows = streams * length
    side = width // 2
    units = w_down.shape[1] // 2
    padded = -(-units // LANES) * LANES
    chips = outer * inner
    onward = [(i, i + 1) for i in range(chips - 1)]
    back = [(i + 1, i) for i in range(chips - 1)]

    def halves(weight, parts, pad):
        size = weight.shape[1] // (2 * parts)
        cut = [weight[:, i * size : (i + 1) * size] for i in range(2 * parts)]
        if pad != size:
            cut = [jnp.pad(piece, ((0, 0), (0, pad - size))) for piece in cut]
        return cut[0::2], cut[1::2]

    def paired(pieces):
        low = jnp.concatenate([piece for one, _ in pieces for piece in one], 1)
        high = jnp.concatenate([piece for _, two in pieces for piece in two], 1)
        mine = jnp.where(core == 0, low, high)
        return ordered(mine, swap(jnp.where(core == 0, high, low)), 0)

    pair_tokens = ordered(tokens, swap(tokens), 1)

    gains = jnp.pad(jnp.stack([norm_attn, norm_mlp], 1), ((0, 0), (0, LANES - 2)))
    cores = core.astype(jnp.int32).reshape(1)
    mine, other = pack_first(cores, w_qkv, gains, w_out)
    pair_one = ordered(mine, swap(other), 0)
    places = tuple(lax.axis_index(name) for name in ("inner", "outer", "dp"))
    later_in, later_down, pair_one, pair_tokens, places = tied(
        w_in, w_down, pair_one, pair_tokens, places
    )
    low = lax.ppermute(pair_tokens[:, length - HALF :], ("outer", "inner"), onward)
    high = lax.ppermute(pair_tokens[:, :HALF], ("outer", "inner"), back)
    one = direct_sends(pair_one)
    pair_two = paired([halves(later_in, 2, padded)])
    pair_three = paired([halves(later_down, 1, padded)])
    three_near = gather_near([pair_three])
    order = arrival_order(*places, width, shard_rows)
    own_order = lax.dynamic_slice_in_dim(order, core * side, side, 0)
    other_order = lax.dynamic_slice_in_dim(order, (1 - core) * side, side, 0)

    def in_order(value):
        return matmul(value.reshape(-1, width), order).astype(BF16)

    own_tokens = in_order(pair_tokens)
    grad_output = in_order(ordered(cotangent, swap(cotangent), 1))

    start = lax.axis_index(("outer", "inner")) * length
    positions = (start - HALF + jnp.arange(window, dtype=jnp.int32)).astype(F32)
    frequency = ROPE_BASE ** (-(jnp.arange(HD // 2, dtype=F32) * 2.0 / HD))
    angles = positions[:, None] * frequency[None, :]
    cosine, sine = jnp.cos(angles), jnp.sin(angles)
    cosine = jnp.tile(cosine, (1, LANES // (HD // 2)))
    sine = jnp.tile(jnp.concatenate([-sine, sine], 1), (1, LANES // HD))
    ids_padded = jnp.pad(doc_ids, ((0, 0), (HALF, HALF)), constant_values=-1)
    key_ids = lax.dynamic_slice_in_dim(ids_padded, start, window, 1)[:, None, :]
    query_ids = lax.dynamic_slice_in_dim(doc_ids, start, length, 1)[:, :, None]

    prepared = (own_tokens, grad_output, order, own_order, other_order)
    prepared += (cosine, sine, key_ids, query_ids)
    prepared, pair_two, three_near, one, low, high = tied(
        prepared, pair_two, three_near, one, low, high
    )
    own_tokens, grad_output, order, own_order, other_order = prepared[:5]
    cosine, sine, key_ids, query_ids = prepared[5:]
    two = direct_sends(pair_two)
    three_far = gather_far(*three_near)
    three_near, three_far, one = tied(three_near, three_far, one)

    near = gather_near(one)
    low, high = (in_order(end).reshape(end.shape) for end in (low, high))
    late = joined_rows([three_near[0], *three_near[1], *three_near[2], *three_far[0], *three_far[1]])
    low, high, two, near, late = tied(low, high, two, near, late)

    far = gather_far(*near)
    two_own = joined_rows(two)
    three = [late] + direct_send(late, 1)
    near, far, two_own, three = tied(near, far, two_own, three)

    three += direct_send(late, 2)
    two_near = gather_near([two_own])
    first = in_pieces(*near, *far)
    joined, window_norm, gain_rows = project(
        low, own_tokens.reshape(streams, length, width), high, first, cosine, sine, side
    )
    out_half = joined_rows([piece[:, 3 * side + LANES :] for piece in first])
    weight = out_weight(first, out_half, swap(out_half), own_order, other_order)
    three, joined, weight, first, two_near = tied(three, joined, weight, first, two_near)

    three += direct_send(late, *range(3, outer))
    two_far = gather_far(*two_near)
    joined = joined.reshape(streams, window, 3 * side)
    attended = attend(block, joined, query_ids, key_ids).reshape(rows, side)
    attended_low, hidden, normed_mlp_low = out_project(
        attended, swap(attended), own_order, other_order, weight, own_tokens, gain_rows
    )
    hidden, normed_mlp_low, two_near, two_far, three = tied(
        hidden, normed_mlp_low, two_near, two_far, three
    )
    in_half = in_pieces(*two_near, *two_far)
    down_half = [join_late(three, shard_rows)]
    mixed_low, factor, active = feed(normed_mlp_low, in_half, padded)

    down_cuts = split_late(grad_output, mixed_low, shard_rows)
    down_cuts, factor, active = tied(down_cuts, factor, active)
    grad_gate, grad_up = feed_back(grad_output, factor, active, down_half)
    sum_in = GradSum([normed_mlp_low] * 2, [grad_gate, grad_up], shard_rows)
    sent_in = sum_in.far()
    grad_gate, grad_up, sent_in, mixed_low = tied(grad_gate, grad_up, sent_in, mixed_low)

    in_far = sum_in.send_far(sent_in)
    down_arrived = [
        lax.ppermute(cut, "outer", forward("outer", outer - 1)) for cut in down_cuts[1:2]
    ]
    part, part_low = back_project([grad_gate, grad_up], in_half, [F32, BF16])
    part, part_low, in_far, down_arrived[0], down_cuts = tied(
        part, part_low, in_far, down_arrived[0], down_cuts
    )

    in_near = sum_in.send_near(sum_in.near(in_far))
    down_arrived[1:] = [
        lax.ppermute(down_cuts[distance], "outer", forward("outer", outer - distance))
        for distance in range(2, outer)
    ]
    grad_hidden, hidden_side, grad_attended = hidden_back(
        part, swap(part_low), hidden, grad_output, gain_rows, weight, own_order
    )
    grad_query, mid, to_lower, to_upper = attend_back(
        block, joined, query_ids, key_ids, grad_attended.reshape(streams, length, side),
        cosine, sine,
    )
    from_lower = lax.ppermute(to_upper, ("outer", "inner"), onward)
    from_upper = lax.ppermute(to_lower, ("outer", "inner"), back)
    from_lower, from_upper, in_near, down_arrived[:2] = tied(
        from_lower, from_upper, in_near, down_arrived[:2]
    )

    grad_joined = join_grads(grad_query, mid, from_lower, from_upper, cosine, sine)
    grad_joined = grad_joined.reshape(rows, 3 * side)
    normed_low = window_norm.reshape(streams, window, width)[:, HALF : HALF + length]
    sum_attn = GradSum(
        [normed_low.reshape(rows, width), attended_low], [grad_joined, hidden_side], shard_rows
    )
    sent_attn, in_own = sum_attn.far(), sum_in.own(in_near)
    sent_attn, in_own, grad_joined = tied(sent_attn, in_own, grad_joined)

    attn_far = sum_attn.send_far(sent_attn)
    attn_far, down_arrived, grad_joined, mixed_low = tied(
        attn_far, down_arrived, grad_joined, mixed_low
    )

    attn_near = sum_attn.send_near(sum_attn.near(attn_far))
    in_arrived = sum_in.send_direct(in_own)
    sum_down = LateSum([down_cuts[0], *down_arrived], shard_rows)
    down_far = sum_down.far()
    out_mine, out_other = back_split(cores, mixed_low, down_half, streams)
    in_mine, in_other = back_split(cores, grad_joined, first, streams)
    attn_near, in_arrived, out_mine, out_other, in_mine, in_other, down_far = tied(
        attn_near, in_arrived, out_mine, out_other, in_mine, in_other, down_far
    )

    attn_own = sum_attn.own(attn_near)
    attn_arrived = sum_attn.send_direct(attn_own)
    down_far = sum_down.send_far(down_far)
    attn_arrived[0], down_far, out_mine, in_mine = tied(
        attn_arrived[0], down_far, out_mine, in_mine
    )
    down_near = sum_down.send_near(sum_down.near(down_far))
    output = end_rows(
        output_kernel, cores, [out_mine, swap(out_other)], [hidden], [order], BF16, streams
    ).reshape(tokens.shape)
    grad_tokens = end_rows(
        input_grad_kernel, cores, [in_mine, swap(in_other)], [grad_hidden, own_tokens],
        [gain_rows, order], F32, streams,
    ).reshape(tokens.shape)
    total_mine, total_other = sum_in.total(cores, in_own, in_arrived)
    grad_in, gain_grad_mlp = assemble(
        cores, total_mine, swap(total_other), [(0, 2, padded, units)], w_in, norm_mlp
    )
    total_mine, total_other = sum_down.total(cores, sum_down.own(down_near), [])
    (grad_down,) = assemble(cores, total_mine, swap(total_other), [(0, 1, padded, units)])
    attn_arrived, output, grad_tokens, grad_in, gain_grad_mlp, grad_down = tied(
        attn_arrived, output, grad_tokens, grad_in, gain_grad_mlp, grad_down
    )
    total_mine, total_other = sum_attn.total(cores, attn_own, attn_arrived)
    grad_qkv, grad_out, gain_grad_attn = assemble(
        cores, total_mine, swap(total_other),
        [(0, 3, side, side), (3 * side, 1, side, side)], w_qkv, norm_attn,
    )
    return (
        output,
        grad_tokens,
        gain_grad_attn.reshape(-1),
        gain_grad_mlp.reshape(-1),
        grad_qkv,
        grad_out,
        grad_in,
        grad_down,
    )


def solution(mesh):
    dp, seq = mesh.shape["dp"], mesh.shape["seq"]
    chips = seq // 2
    outer = 4 if chips % 4 == 0 else 1
    fine = Mesh(
        mesh.devices.reshape(dp, outer, chips // outer, 2), ("dp", "outer", "inner", "core")
    )
    line = ("outer", "inner", "core")
    every = ("dp",) + line
    token = P("dp", line, None)
    vector = P(every)
    matrix = P(every, None)
    return jax.shard_map(
        shards,
        mesh=fine,
        in_specs=(token, P("dp", None), vector, vector, matrix, matrix, matrix, matrix, token),
        out_specs=(token, token, vector, vector, matrix, matrix, matrix, matrix),
        check_vma=False,
    )
```

```python
import functools

import jax
import jax.numpy as jnp
import numpy as np
from jax import lax
from jax.experimental import pallas as pl
from jax.experimental.pallas import tpu as pltpu
from jax.sharding import Mesh, PartitionSpec as P

HD = 64
HALF = 64
LANES = 128
NORM_EPSILON = 1e-05
ROPE_BASE = 10000.0
F32 = jnp.float32
BF16 = jnp.bfloat16


def contract_cols(left, right):
    return lax.dot_general(left, right, (((1,), (1,)), ((), ())), preferred_element_type=F32)


def contract_rows(left, right):
    return lax.dot_general(left, right, (((0,), (0,)), ((), ())), preferred_element_type=F32)


def matmul(left, right):
    return jnp.dot(left, right, preferred_element_type=F32)


def tied(*values):
    return lax.optimization_barrier(values)


def call(kernel, grid, ins, outs, scratch=(), limit=40):
    out = pl.pallas_call(
        kernel,
        grid=grid,
        in_specs=[
            pl.BlockSpec(memory_space=pltpu.SMEM) if block is None else pl.BlockSpec(block, index)
            for _, block, index in ins
        ],
        out_specs=[pl.BlockSpec(block, index) for _, _, block, index in outs],
        out_shape=[jax.ShapeDtypeStruct(shape, kind) for shape, kind, _, _ in outs],
        scratch_shapes=list(scratch),
        compiler_params=pltpu.CompilerParams(vmem_limit_bytes=limit * 2**20),
        cost_estimate=pl.CostEstimate(flops=1024, bytes_accessed=1024, transcendentals=0),
    )(*[array for array, _, _ in ins])
    return out


def whole(array):
    return (array, array.shape, lambda *_: (0,) * array.ndim)


def swap(value):
    return lax.ppermute(value, "core", [(0, 1), (1, 0)])


def ordered(mine, other, axis):
    first = lax.axis_index("core") == 0
    return jnp.concatenate(
        [jnp.where(first, mine, other), jnp.where(first, other, mine)], axis=axis
    )


def forward(axis, distance=1):
    count = lax.axis_size(axis)
    return [(i, (i + distance) % count) for i in range(count)]


def ring_gather(axis, piece):
    pieces = [piece]
    for _ in range(1, lax.axis_size(axis)):
        pieces.append(lax.ppermute(pieces[-1], axis, forward(axis)))
    return pieces[1:]


def direct_send(rows, *distances):
    count = lax.axis_size("outer")
    return [
        lax.ppermute(rows, "outer", forward("outer", distance))
        for distance in distances
        if distance < count
    ]


def direct_sends(rows):
    return [rows] + direct_send(rows, *range(1, lax.axis_size("outer")))


def joined_rows(pieces):
    return jnp.concatenate(pieces, 0) if len(pieces) > 1 else pieces[0]


def gather_near(arrived):
    own = joined_rows(arrived)
    return own, ring_gather("inner", own), ring_gather("dp", own)


def copy_kernel(*refs):
    count = len(refs) // 2
    for source, target in zip(refs[:count], refs[count:]):
        target[...] = source[...]


def far_halves(along_x, along_y, half):
    if len(along_x) > 1 or len(along_y) > 1 or half % 32:
        return (
            joined_rows([piece[:half] for piece in along_y]),
            joined_rows([piece[half:] for piece in along_x]),
        )
    columns = along_x[0].shape[1]
    return call(
        copy_kernel,
        (1,),
        [(along_y[0], (half, columns), lambda i: (0, 0))]
        + [(along_x[0], (half, columns), lambda i: (1, 0))],
        [((half, columns), BF16, (half, columns), lambda i: (0, 0)) for _ in range(2)],
    )


def gather_far(own, along_x, along_y):
    one, two = far_halves(along_x, along_y, own.shape[0] // 2)
    return ring_gather("inner", one), ring_gather("dp", two)


def in_pieces(own, along_x, along_y, one, two):
    pieces = [own, *along_x, *along_y, *one, *two]
    if any(piece.shape[0] % LANES for piece in pieces):
        pieces = [joined_rows(pieces)]
    return pieces


def order_blocks(inner, dp):
    blocks = [(0, 0, 0, 2)]
    blocks += [(d, 0, 0, 2) for d in range(1, inner)] + [(0, d, 0, 2) for d in range(1, dp)]
    blocks += [(d, e, 0, 1) for d in range(1, inner) for e in range(1, dp)]
    return blocks + [(d, e, 1, 2) for e in range(1, dp) for d in range(1, inner)]


def late_segments(shard_rows):
    inner, outer, dp = (lax.axis_size(name) for name in ("inner", "outer", "dp"))
    start, at = 0, {}
    for d, e, low, high in order_blocks(inner, dp):
        for part in range(low, high):
            at[d, e, part] = start
            start += shard_rows
    segments = []
    for d, e, low, high in order_blocks(inner, dp):
        for distance in range(low * outer // 2, high * outer // 2):
            first, second = at[d, e, 0], at[d, e, 1]
            if second == first + shard_rows:
                segments.append((distance, first, 2 * shard_rows))
            else:
                segments += [(distance, first, shard_rows), (distance, second, shard_rows)]
    return segments


def join_kernel_rows(segments, *refs):
    pieces, out_ref = refs[:-1], refs[-1]
    at = 0
    for distance, start, count in segments:
        out_ref[at : at + count, :] = pieces[distance][start : start + count, :]
        at += count


def join_late(pieces, shard_rows):
    segments = late_segments(shard_rows)
    columns = pieces[0].shape[1]
    rows = sum(count for _, _, count in segments)
    if shard_rows % 32:
        return jnp.concatenate([pieces[d][at : at + n] for d, at, n in segments], 0)
    return call(
        functools.partial(join_kernel_rows, segments),
        (1,),
        [whole(piece) for piece in pieces],
        [((rows, columns), BF16, (rows, columns), lambda i: (0, 0))],
    )[0]


def split_kernel_rows(segments, left_ref, right_ref, *outs):
    place, at = [], 0
    for distance, start, count in segments:
        place.append((at, distance, start, count))
        at += count
    for top in range(0, at, LANES):
        rows = contract_rows(left_ref[:, top : top + LANES], right_ref[...]).astype(BF16)
        for begin, distance, start, count in place:
            if top <= begin < top + LANES:
                outs[distance][start : start + count, :] = rows[begin - top : begin - top + count]


def split_late(left, right, shard_rows):
    segments = late_segments(shard_rows)
    outer = lax.axis_size("outer")
    rows, columns = left.shape[1] // outer, right.shape[1]
    if shard_rows % 32:
        total, at, cuts = contract_rows(left, right).astype(BF16), 0, {}
        for distance, start, count in segments:
            cuts[distance, start] = total[at : at + count]
            at += count
        return [
            jnp.concatenate([cuts[key] for key in sorted(cuts) if key[0] == distance], 0)
            for distance in range(outer)
        ]
    return call(
        functools.partial(split_kernel_rows, segments),
        (1,),
        [whole(left), whole(right)],
        [((rows, columns), BF16, (rows, columns), lambda i: (0, 0)) for _ in range(outer)],
    )


def arrival_order(x, z, y, width, shard_rows):
    inner, outer, dp = (lax.axis_size(name) for name in ("inner", "outer", "dp"))
    half = outer * shard_rows
    blocks = order_blocks(inner, dp)
    place = np.concatenate([np.arange(low * half, high * half) for _, _, low, high in blocks])
    sizes = [(high - low) * half for _, _, low, high in blocks]
    along_x = np.repeat([block[0] for block in blocks], sizes)
    along_y = np.repeat([block[1] for block in blocks], sizes)
    along_z, row = place // (2 * shard_rows), place % (2 * shard_rows)
    at_x = (x - jnp.asarray(along_x, jnp.int32) + inner) % inner
    at_y = (y - jnp.asarray(along_y, jnp.int32) + dp) % dp
    at_z = (z - jnp.asarray(along_z, jnp.int32) + outer) % outer
    source = ((at_y * outer + at_z) * inner + at_x) * 2 * shard_rows + row
    return (jnp.arange(width, dtype=jnp.int32)[:, None] == source[None, :]).astype(BF16)


def rows_kernel(pairs, layout, *refs):
    rights, refs = refs[:pairs], refs[pairs:]
    inputs, outs = refs[: -len(layout)], refs[-len(layout) :]
    for places, out_ref in zip(layout, outs):
        lefts, adds = inputs[:pairs], inputs[pairs : pairs + len(places)]
        inputs = inputs[pairs + len(places) :]
        start = 0
        for left, right in zip(lefts, rights):
            columns = slice(start, start + right.shape[1])
            start = columns.stop
            total = contract_rows(left[...], right[...])
            for add in adds:
                if add.shape[0] == total.shape[0]:
                    total = total + add[:, columns].astype(F32)
            out_ref[:, columns] = total.astype(BF16)
            for add, at in zip(adds, places):
                if add.shape[0] != total.shape[0]:
                    span = slice(at, at + add.shape[0])
                    part = total[span] + add[:, columns].astype(F32)
                    out_ref[span, columns] = part.astype(BF16)


class GradSum:
    def __init__(self, lefts, rights, shard_rows):
        self.lefts, self.rights = lefts, rights
        self.inner, self.outer, self.dp = (
            lax.axis_size(name) for name in ("inner", "outer", "dp")
        )
        self.shard = 2 * shard_rows
        self.half = self.outer * shard_rows
        self.at_x = 2 * self.half
        self.at_y = self.at_x + (self.inner - 1) * 2 * self.half
        self.at_one = self.at_y + (self.dp - 1) * 2 * self.half
        self.at_two = self.at_one + (self.inner - 1) * (self.dp - 1) * self.half

    def rows(self, *parts):
        depth = self.lefts[0].shape[0]
        columns = sum(right.shape[1] for right in self.rights)
        ins, outs, layout = [whole(right) for right in self.rights], [], []
        for start, count, adds in parts:
            adds = [(rows, place) for rows, place in adds if rows is not None]
            lefts, index = self.lefts, start // count
            if count % LANES or start % count:
                lefts, index = [left[:, start : start + count] for left in lefts], 0
            ins += [
                (left, (depth, count), lambda i, index=index: (0, index)) for left in lefts
            ]
            ins += [whole(rows) for rows, _ in adds]
            outs.append(((count, columns), BF16, (count, columns), lambda i: (0, 0)))
            layout.append([place for _, place in adds])
        return call(
            functools.partial(rows_kernel, len(self.rights), layout), (1,), ins, outs
        )

    def ring(self, axis, part, first):
        arrived = None
        for step in range(1, lax.axis_size(axis)):
            sent = first if step == 1 else self.rows(part(step, arrived))[0]
            arrived = lax.ppermute(sent, axis, forward(axis))
        return arrived

    def one(self, distance, arrived):
        count = (self.dp - 1) * self.half
        return (self.at_one + (distance - 1) * count, count, [(arrived, 0)])

    def two(self, distance, arrived):
        count = (self.inner - 1) * self.half
        return (self.at_two + (distance - 1) * count, count, [(arrived, 0)])

    def far(self):
        return self.rows(self.one(1, None), self.two(1, None))

    def send_far(self, firsts):
        return (
            self.ring("inner", self.one, firsts[0]), self.ring("dp", self.two, firsts[1])
        )

    def along(self, start, distance, arrived, extra, place):
        count = 2 * self.half
        extra = extra[(distance - 1) * self.half : distance * self.half]
        return (start + (distance - 1) * count, count, [(arrived, 0), (extra, place)])

    def along_x(self, distance, arrived):
        return self.along(self.at_x, distance, arrived, self.sums[1], self.half)

    def along_y(self, distance, arrived):
        return self.along(self.at_y, distance, arrived, self.sums[0], 0)

    def near(self, sums):
        self.sums = sums
        return self.rows(self.along_x(1, None), self.along_y(1, None))

    def send_near(self, firsts):
        return (
            self.ring("inner", self.along_x, firsts[0]),
            self.ring("dp", self.along_y, firsts[1]),
        )

    def own(self, nears):
        return self.rows((0, 2 * self.half, [(near, 0) for near in nears]))[0]

    def cut(self, own, distance):
        return own[distance * self.shard : (distance + 1) * self.shard]

    def send_direct(self, own):
        return [
            lax.ppermute(
                self.cut(own, distance), "outer", forward("outer", self.outer - distance)
            )
            for distance in range(1, self.outer)
        ]

    def total(self, core, own, arrived):
        columns = own.shape[1]
        half = self.shard // 2
        return call(
            total_kernel,
            (1,),
            [(core, None, None), (own, (self.shard, columns), lambda i: (0, 0))]
            + [whole(rows) for rows in arrived],
            [((half, columns), F32, (half, columns), lambda i: (0, 0)) for _ in range(2)],
        )


def late_kernel(count, layout, *refs):
    blocks, refs = refs[:count], refs[count:]
    adds, outs = refs[: -len(layout)], refs[-len(layout) :]
    for (start, rows, places), out_ref in zip(layout, outs):
        mine, adds = adds[: len(places)], adds[len(places) :]
        total = None
        for block in blocks:
            part = block[start : start + rows, :].astype(F32)
            total = part if total is None else total + part
        for add in mine:
            if add.shape[0] == rows:
                total = total + add[...].astype(F32)
        out_ref[...] = total.astype(BF16)
        for add, at in zip(mine, places):
            if add.shape[0] != rows:
                span = slice(at, at + add.shape[0])
                out_ref[span, :] = (total[span] + add[...].astype(F32)).astype(BF16)


class LateSum(GradSum):
    def __init__(self, blocks, shard_rows):
        GradSum.__init__(self, [], [], shard_rows)
        self.blocks, self.half = blocks, shard_rows
        self.at_x = 2 * self.half
        self.at_y = self.at_x + (self.inner - 1) * 2 * self.half
        self.at_one = self.at_y + (self.dp - 1) * 2 * self.half
        self.at_two = self.at_one + (self.inner - 1) * (self.dp - 1) * self.half

    def rows(self, *parts):
        columns = self.blocks[0].shape[1]
        parts = [
            (start, count, [add for add in adds if add[0] is not None])
            for start, count, adds in parts
        ]
        if self.half % 32:
            results = []
            for start, count, adds in parts:
                total = sum(block[start : start + count].astype(F32) for block in self.blocks)
                for rows, place in adds:
                    span = slice(place, place + rows.shape[0])
                    total = total.at[span].add(rows.astype(F32))
                results.append(total.astype(BF16))
            return results
        return call(
            functools.partial(
                late_kernel,
                len(self.blocks),
                [(start, count, [at for _, at in adds]) for start, count, adds in parts],
            ),
            (1,),
            [whole(block) for block in self.blocks]
            + [whole(rows) for _, _, adds in parts for rows, _ in adds],
            [
                ((count, columns), BF16, (count, columns), lambda i: (0, 0))
                for _, count, _ in parts
            ],
        )


def own_half(core_ref, value):
    half = value.shape[0] // 2
    return jnp.where(core_ref[0] == 0, value[:half], value[half:])


def total_kernel(core_ref, *refs):
    total = None
    for ref in refs[:-2]:
        rows = ref[...].astype(F32)
        total = rows if total is None else total + rows
    half = total.shape[0] // 2
    first = core_ref[0] == 0
    refs[-2][...] = jnp.where(first, total[:half], total[half:])
    refs[-1][...] = jnp.where(first, total[half:], total[:half])


def assemble_kernel(layout, core_ref, mine_ref, other_ref, *refs):
    first = core_ref[0] == 0
    count = len(layout)
    pair = (
        jnp.where(first, mine_ref[...], other_ref[...]),
        jnp.where(first, other_ref[...], mine_ref[...]),
    )
    outs = refs[-count:] if len(refs) == count else refs[2:-1]
    for out_ref, (start, parts, stride, size) in zip(outs, layout):
        cuts = []
        for i in range(parts):
            at = start + i * stride
            cuts += [half[:, at : at + size] for half in pair]
        out_ref[...] = jnp.concatenate(cuts, 1)
    if len(refs) > count:
        weight_ref, gain_ref = refs[:2]
        product = weight_ref[...].astype(F32) * outs[0][...]
        refs[-1][...] = jnp.sum(product, -1, keepdims=True) / gain_ref[...].astype(F32)


def assemble(core, mine, other, layout, weight=None, gain=None):
    rows = mine.shape[0]
    ins = [(core, None, None), whole(mine), whole(other)]
    sizes = [2 * parts * size for _, parts, _, size in layout]
    if weight is not None:
        ins += [whole(weight), whole(gain.reshape(rows, 1))]
        sizes.append(1)
    return call(
        functools.partial(assemble_kernel, layout),
        (1,),
        ins,
        [((rows, size), F32, (rows, size), lambda i: (0, 0)) for size in sizes],
    )


def pack_kernel(side, core_ref, qkv_ref, gain_ref, out_ref, mine_ref, other_ref):
    def fill(target, half):
        for part in range(3):
            start = (2 * part + half) * side
            target[:, part * side : (part + 1) * side] = qkv_ref[:, start : start + side]
        target[:, 3 * side : 3 * side + LANES] = gain_ref[...]
        target[:, 3 * side + LANES :] = out_ref[:, half * side : (half + 1) * side]

    for half in range(2):

        @pl.when(core_ref[0] == half)
        def _():
            fill(mine_ref, half)
            fill(other_ref, 1 - half)


def pack_first(core, w_qkv, gains, w_out):
    rows, side = w_out.shape[0], w_out.shape[1] // 2
    columns = 4 * side + LANES
    return call(
        functools.partial(pack_kernel, side),
        (1,),
        [(core, None, None), whole(w_qkv), whole(gains), whole(w_out)],
        [((rows, columns), BF16, (rows, columns), lambda i: (0, 0)) for _ in range(2)],
    )


def normalise(values):
    centred = values - jnp.mean(values, -1, keepdims=True)
    scale = lax.rsqrt(jnp.mean(centred * centred, -1, keepdims=True) + NORM_EPSILON)
    return centred * scale, scale


def norm_back(unit, scale, gain, incoming):
    grad = incoming * gain
    return scale * (
        grad
        - jnp.mean(grad, -1, keepdims=True)
        - unit * jnp.mean(grad * unit, -1, keepdims=True)
    )


def piece_matmul(left, pieces):
    total, start = None, 0
    for piece in pieces:
        part = matmul(left[:, start : start + piece.shape[0]], piece[...])
        total = part if total is None else total + part
        start += piece.shape[0]
    return total


def back_kernel(starts, count, *refs):
    grads, pieces, out_refs = refs[: len(starts)], refs[len(starts) : count], refs[count:]
    at = 0
    for piece in pieces:
        total = None
        for grad, start in zip(grads, starts):
            part = contract_cols(grad[...], piece[:, start : start + grad.shape[1]])
            total = part if total is None else total + part
        for out_ref in out_refs:
            out_ref[:, at : at + piece.shape[0]] = total.astype(out_ref.dtype)
        at += piece.shape[0]


def back_project(grads, pieces, kinds):
    rows = grads[0].shape[0]
    block = rows // 2
    starts, end = [], 0
    for grad in grads:
        starts.append(end)
        end += grad.shape[1]
    width = sum(piece.shape[0] for piece in pieces)
    return call(
        functools.partial(back_kernel, starts, len(grads) + len(pieces)),
        (2,),
        [(grad, (block, grad.shape[1]), lambda i: (i, 0)) for grad in grads]
        + [(piece, (piece.shape[0], end), lambda i: (0, 0)) for piece in pieces],
        [((rows, width), kind, (block, width), lambda i: (i, 0)) for kind in kinds],
    )


def split_kernel(core_ref, grad_ref, *refs):
    pieces, (mine_ref, other_ref) = refs[:-2], refs[-2:]
    width = grad_ref.shape[1]
    half = grad_ref.shape[0] // 2
    at = 0
    for piece in pieces:
        total = contract_cols(grad_ref[...], piece[:, :width])
        first = core_ref[0] == 0
        span = slice(at, at + piece.shape[0])
        mine_ref[:, span] = jnp.where(first, total[:half], total[half:])
        other_ref[:, span] = jnp.where(first, total[half:], total[:half]).astype(BF16)
        at = span.stop


def back_split(core, grad, pieces, streams):
    rows, columns = grad.shape
    block = rows // streams
    width = sum(piece.shape[0] for piece in pieces)
    return call(
        split_kernel,
        (streams,),
        [(core, None, None), (grad, (block, columns), lambda i: (i, 0))]
        + [(piece, (piece.shape[0], columns), lambda i: (0, 0)) for piece in pieces],
        [
            ((rows // 2, width), kind, (block // 2, width), lambda i: (i, 0))
            for kind in (F32, BF16)
        ],
    )


def output_kernel(core_ref, mine_ref, other_ref, hidden_ref, order_ref, out_ref):
    total = own_half(core_ref, hidden_ref[...]) + mine_ref[...] + other_ref[...].astype(F32)
    out_ref[...] = contract_cols(total.astype(BF16), order_ref[...]).astype(BF16)


def input_grad_kernel(
    core_ref, mine_ref, other_ref, hidden_ref, x_ref, gain_ref, order_ref, out_ref
):
    unit, scale = normalise(own_half(core_ref, x_ref[...].astype(F32)))
    incoming = mine_ref[...] + other_ref[...].astype(F32)
    total = own_half(core_ref, hidden_ref[...])
    total = total + norm_back(unit, scale, gain_ref[0:1, :], incoming)
    result = None
    for _ in range(3):
        part = total.astype(BF16)
        total = total - part.astype(F32)
        part = contract_cols(part, order_ref[...])
        result = part if result is None else result + part
    out_ref[...] = result


def end_rows(kernel, core, halves, fulls, wholes, kind, streams):
    rows, width = halves[0].shape
    block = rows // streams
    return call(
        kernel,
        (streams,),
        [(core, None, None)]
        + [(array, (block, width), lambda i: (i, 0)) for array in halves]
        + [(array, (2 * block, width), lambda i: (i, 0)) for array in fulls]
        + [whole(array) for array in wholes],
        [((rows, width), kind, (block, width), lambda i: (i, 0))],
    )[0]


def turned(values):
    width = values.shape[-1]
    lane = lax.broadcasted_iota(jnp.int32, values.shape, values.ndim - 1)
    ahead = pltpu.roll(values, width - HD // 2, values.ndim - 1)
    behind = pltpu.roll(values, HD // 2, values.ndim - 1)
    return jnp.where(lane % HD < HD // 2, ahead, behind)


def project_kernel(count, low_ref, x_ref, high_ref, cos_ref, sin_ref, *refs):
    gains, weights = refs[:count], refs[count : 2 * count]
    out_ref, norm_ref, gain_ref = refs[2 * count :]

    @pl.when(pl.program_id(0) == 0)
    def _():
        pick = lax.broadcasted_iota(jnp.int32, (8, LANES), 0) == lax.broadcasted_iota(
            jnp.int32, (8, LANES), 1
        )
        pick = pick.astype(F32).astype(BF16)
        start = 0
        for piece in gains:
            gain_ref[:, start : start + piece.shape[0]] = contract_cols(pick, piece[...])
            start += piece.shape[0]
        for stream in range(x_ref.shape[0]):
            at = stream * cos_ref.shape[0]
            for ref in (low_ref, x_ref, high_ref):
                unit, _ = normalise(ref[stream].astype(F32))
                span = slice(at, at + ref.shape[1])
                norm_ref[span, :] = (unit * gain_ref[0:1, :]).astype(BF16)
                at = span.stop

    values = piece_matmul(norm_ref, weights)
    keep = pl.program_id(0) == 2
    length = cos_ref.shape[0]
    for top in range(0, values.shape[0], length):
        for left in range(0, values.shape[1], LANES):
            part = values[top : top + length, left : left + LANES]
            rotated = part * cos_ref[...] + turned(part) * sin_ref[...]
            out_ref[top : top + length, left : left + LANES] = jnp.where(
                keep, part, rotated
            ).astype(BF16)


def project(low, tokens, high, pieces, cosine, sine, side):
    width = tokens.shape[2]
    rows = tokens.shape[0] * cosine.shape[0]
    gain_block = 3 * side // LANES
    return call(
        functools.partial(project_kernel, len(pieces)),
        (3,),
        [whole(low), whole(tokens), whole(high), whole(cosine), whole(sine)]
        + [(piece, (piece.shape[0], LANES), lambda j: (0, gain_block)) for piece in pieces]
        + [(piece, (piece.shape[0], side), lambda j: (0, j)) for piece in pieces],
        [
            ((rows, 3 * side), BF16, (rows, side), lambda j: (0, j)),
            ((rows, width), BF16, (rows, width), lambda j: (0, 0)),
            ((8, width), F32, (8, width), lambda j: (0, 0)),
        ],
    )


def head_masks():
    lane = lax.broadcasted_iota(jnp.int32, (1, LANES), 1)
    return [(lane // HD == head).astype(F32).astype(BF16) for head in range(LANES // HD)]


def block_mask(query_ids, key_ids):
    rows, width = query_ids.shape[0], key_ids.shape[1]
    offset = lax.broadcasted_iota(jnp.int32, (rows, width), 1) - lax.broadcasted_iota(
        jnp.int32, (rows, width), 0
    )
    return (offset >= 0) & (offset <= 2 * HALF) & (query_ids == key_ids)


def block_probs(query, keys, allowed):
    scores = jnp.where(allowed, contract_cols(query, keys) * HD**-0.5, -1e30)
    grown = jnp.exp(scores - jnp.max(scores, -1, keepdims=True))
    return grown / jnp.sum(grown, -1, keepdims=True)


def attend_kernel(block, q_ref, k_ref, v_ref, qid_ref, kid_ref, out_ref):
    masks = head_masks()
    for start in range(0, out_ref.shape[1], block):
        span = slice(start, start + block + 2 * HALF)
        allowed = block_mask(qid_ref[0, start : start + block], kid_ref[0, :, span])
        query = q_ref[0, HALF + start : HALF + start + block]
        total = None
        for mask in masks:
            probs = block_probs(query * mask, k_ref[0, span], allowed)
            part = matmul(probs.astype(BF16), v_ref[0, span]) * mask.astype(F32)
            total = part if total is None else total + part
        out_ref[0, start : start + block] = total.astype(BF16)


def attend_back_kernel(
    block, q_ref, k_ref, v_ref, qid_ref, kid_ref, grad_ref, cos_ref, sin_ref,
    dq_ref, mid_ref, low_ref, high_ref,
):
    masks = head_masks()
    length = dq_ref.shape[1]
    grad_keys = grad_values = jnp.zeros((length + 2 * HALF, LANES), F32)
    for start in range(0, length, block):
        span = slice(start, start + block + 2 * HALF)
        mid = slice(HALF + start, HALF + start + block)
        rows = slice(start, start + block)
        allowed = block_mask(qid_ref[0, rows], kid_ref[0, :, span])
        query_all, grad_all = q_ref[0, mid], grad_ref[0, rows]
        keys, values = k_ref[0, span], v_ref[0, span]
        grad_query, part_keys, part_values = 0.0, 0.0, 0.0
        for mask in masks:
            query, grad = query_all * mask, grad_all * mask
            probs = block_probs(query, keys, allowed)
            grad_probs = contract_cols(grad, values)
            delta = jnp.sum(probs * grad_probs, -1, keepdims=True)
            grad_scores = (probs * (grad_probs - delta)).astype(BF16)
            grad_query += matmul(grad_scores, keys) * mask.astype(F32)
            part_keys += contract_rows(grad_scores, query)
            part_values += contract_rows(probs.astype(BF16), grad)
        grad_query = grad_query * HD**-0.5
        dq_ref[0, rows] = (
            grad_query * cos_ref[mid] - turned(grad_query) * sin_ref[mid]
        ).astype(BF16)
        before, after = start, length - start - block

        def placed(part):
            pieces = [part]
            if before:
                pieces.insert(0, jnp.zeros((before, LANES), F32))
            if after:
                pieces.append(jnp.zeros((after, LANES), F32))
            return jnp.concatenate(pieces, 0)

        grad_keys += placed(part_keys)
        grad_values += placed(part_values)
    for index, total in enumerate((grad_keys * HD**-0.5, grad_values)):
        low_ref[0, index] = total[:HALF].astype(BF16)
        mid_ref[0, index] = total[HALF : HALF + length]
        high_ref[0, index] = total[HALF + length :].astype(BF16)


def attention_inputs(joined, query_ids, key_ids):
    window, groups = joined.shape[1], joined.shape[2] // 3 // LANES
    inputs = [
        (joined, (1, window, LANES), lambda s, h, shift=shift: (s, 0, h + shift))
        for shift in (0, groups, 2 * groups)
    ]
    inputs += [
        (ids, (1,) + ids.shape[1:], lambda s, h: (s, 0, 0)) for ids in (query_ids, key_ids)
    ]
    return inputs


def attend(block, joined, query_ids, key_ids):
    streams, window, columns = joined.shape
    length, side = window - 2 * HALF, columns // 3
    return call(
        functools.partial(attend_kernel, block),
        (streams, side // LANES),
        attention_inputs(joined, query_ids, key_ids),
        [((streams, length, side), BF16, (1, length, LANES), lambda s, h: (s, 0, h))],
        limit=24,
    )[0]


def attend_back(block, joined, query_ids, key_ids, grad, cosine, sine):
    streams, length, side = grad.shape

    def pair(rows, kind):
        return (
            (streams, 2, rows, side), kind, (1, 2, rows, LANES), lambda s, h: (s, 0, 0, h)
        )

    return call(
        functools.partial(attend_back_kernel, block),
        (streams, side // LANES),
        attention_inputs(joined, query_ids, key_ids)
        + [(grad, (1, length, LANES), lambda s, h: (s, 0, h)), whole(cosine), whole(sine)],
        [
            ((streams, length, side), BF16, (1, length, LANES), lambda s, h: (s, 0, h)),
            pair(length, F32),
            pair(HALF, BF16),
            pair(HALF, BF16),
        ],
        limit=24,
    )


def join_kernel(dq_ref, mid_ref, low_ref, high_ref, cos_ref, sin_ref, out_ref):
    length, width = dq_ref.shape[1:]
    out_ref[0, :, :width] = dq_ref[0]
    cosine, sine = cos_ref[HALF : HALF + length], sin_ref[HALF : HALF + length]
    for index in range(2):
        for start in range(0, width, LANES):
            lanes = slice(start, start + LANES)
            total = mid_ref[0, index, :, lanes]
            total = total + jnp.concatenate(
                [
                    low_ref[0, index, :, lanes].astype(F32),
                    jnp.zeros((length - 2 * HALF, LANES), F32),
                    high_ref[0, index, :, lanes].astype(F32),
                ],
                0,
            )
            if index == 0:
                total = total * cosine - turned(total) * sine
            to = (1 + index) * width + start
            out_ref[0, :, to : to + LANES] = total.astype(BF16)


def join_grads(grad_query, mid, from_lower, from_upper, cosine, sine):
    streams, length, width = grad_query.shape

    def of_stream(array):
        block = (1,) + array.shape[1:]
        return (array, block, lambda s: (s,) + (0,) * (array.ndim - 1))

    return call(
        join_kernel,
        (streams,),
        [of_stream(array) for array in (grad_query, mid, from_lower, from_upper)]
        + [whole(cosine), whole(sine)],
        [((streams, length, 3 * width), BF16, (1, length, 3 * width), lambda s: (s, 0, 0))],
        limit=24,
    )[0]


def by_rows(array, block):
    return (array, (block, array.shape[1]), lambda i: (i, 0))


def weight_kernel(count, other_ref, own_order_ref, other_order_ref, *refs):
    start = 0
    out_ref = refs[count]
    for piece in refs[:count]:
        span = slice(start, start + piece.shape[0])
        total = matmul(piece[...], own_order_ref[...])
        total = total + matmul(other_ref[span, :], other_order_ref[...])
        out_ref[span, :] = total.astype(BF16)
        start = span.stop


def out_weight(pieces, own, other, own_order, other_order):
    side, width = own_order.shape
    if len(pieces) == 1:
        own_pieces = [(own, own.shape, lambda i: (0, 0))]
    else:
        own_pieces, start = [], 0
        for piece in pieces:
            count = piece.shape[0]
            own_pieces.append(
                (own, (count, side), lambda i, index=start // count: (index, 0))
            )
            start += count
    return call(
        functools.partial(weight_kernel, len(own_pieces)),
        (1,),
        [whole(other), whole(own_order), whole(other_order)] + own_pieces,
        [((width, width), BF16, (width, width), lambda i: (0, 0))],
    )[0]


def out_kernel(
    own_ref, other_ref, own_order_ref, other_order_ref, weight_ref, x_ref, gain_ref,
    att_ref, hidden_ref, norm_ref,
):
    attended = matmul(own_ref[...], own_order_ref[...])
    attended = (attended + matmul(other_ref[...], other_order_ref[...])).astype(BF16)
    att_ref[...] = attended
    hidden = x_ref[...].astype(F32) + matmul(attended, weight_ref[...])
    hidden_ref[...] = hidden
    norm_ref[...] = (normalise(hidden)[0] * gain_ref[1:2, :]).astype(BF16)


def out_project(own, other, own_order, other_order, weight, tokens, gains):
    rows, width = tokens.shape
    block = rows // 2
    return call(
        out_kernel,
        (2,),
        [by_rows(own, block), by_rows(other, block), whole(own_order), whole(other_order)]
        + [whole(weight), by_rows(tokens, block), whole(gains)],
        [
            ((rows, width), kind, (block, width), lambda i: (i, 0))
            for kind in (BF16, F32, BF16)
        ],
    )


def hidden_back_kernel(
    part_ref, other_ref, hidden_ref, g_ref, gain_ref, weight_ref, order_ref,
    grad_ref, side_ref, att_ref,
):
    unit, scale = normalise(hidden_ref[...])
    incoming = part_ref[...] + other_ref[...].astype(F32)
    grad = g_ref[...].astype(F32) + norm_back(unit, scale, gain_ref[1:2, :], incoming)
    low = grad.astype(BF16)
    grad_ref[...] = grad
    side_ref[...] = contract_cols(low, order_ref[...]).astype(BF16)
    attended = contract_cols(low, weight_ref[...]).astype(BF16)
    att_ref[...] = contract_cols(attended, order_ref[...]).astype(BF16)


def hidden_back(part, other, hidden, grad_output, gains, weight, own_order):
    rows, width = hidden.shape
    block, side = rows // 2, own_order.shape[0]
    return call(
        hidden_back_kernel,
        (2,),
        [by_rows(array, block) for array in (part, other, hidden, grad_output)]
        + [whole(gains), whole(weight), whole(own_order)],
        [
            ((rows, size), kind, (block, size), lambda i: (i, 0))
            for size, kind in ((width, F32), (side, BF16), (side, BF16))
        ],
    )


def column_spans(width):
    return [slice(at, min(at + 2 * LANES, width)) for at in range(0, width, 2 * LANES)]


def tile_matmul(left, pieces, columns):
    total, start = None, 0
    for piece in pieces:
        part = matmul(left[:, start : start + piece.shape[0]], piece[:, columns])
        total = part if total is None else total + part
        start += piece.shape[0]
    return total


def feed_kernel(norm_ref, *refs):
    pieces, (mixed_ref, factor_ref, active_ref) = refs[:-3], refs[-3:]
    units = mixed_ref.shape[1]
    for span in column_spans(units):
        gate = tile_matmul(norm_ref, pieces, span)
        up = tile_matmul(norm_ref, pieces, slice(units + span.start, units + span.stop))
        below = 0.5 * (1.0 + lax.erf(gate * 0.5**0.5))
        active = gate * below
        mixed_ref[:, span] = (active * up).astype(BF16)
        active_ref[:, span] = active
        density = jnp.exp(-0.5 * gate * gate) * (2.0 * np.pi) ** -0.5
        factor_ref[:, span] = up * (below + gate * density)


def feed(normed, pieces, units):
    rows = normed.shape[0]
    block = rows // 2
    return call(
        feed_kernel,
        (2,),
        [by_rows(normed, block)] + [whole(piece) for piece in pieces],
        [
            ((rows, units), kind, (block, units), lambda i: (i, 0))
            for kind in (BF16, F32, F32)
        ],
    )


def feed_back_kernel(g_ref, factor_ref, active_ref, *refs):
    pieces, (gate_ref, up_ref) = refs[:-2], refs[-2:]
    for span in column_spans(factor_ref.shape[1]):
        grad = tile_matmul(g_ref, pieces, span)
        gate_ref[:, span] = (grad * factor_ref[:, span]).astype(BF16)
        up_ref[:, span] = (grad * active_ref[:, span]).astype(BF16)


def feed_back(grad_output, factor, active, pieces):
    rows, units = factor.shape
    block = rows // 2
    return call(
        feed_back_kernel,
        (2,),
        [by_rows(array, block) for array in (grad_output, factor, active)]
        + [whole(piece) for piece in pieces],
        [((rows, units), BF16, (block, units), lambda i: (i, 0)) for _ in range(2)],
    )


def shards(tokens, doc_ids, norm_attn, norm_mlp, w_qkv, w_out, w_in, w_down, cotangent):
    streams, block, width = tokens.shape
    shard_rows = w_qkv.shape[0]
    inner, outer = lax.axis_size("inner"), lax.axis_size("outer")
    core = lax.axis_index("core")
    length = 2 * block
    window = length + 2 * HALF
    rows = streams * length
    side = width // 2
    units = w_down.shape[1] // 2
    padded = -(-units // LANES) * LANES
    chips = outer * inner
    onward = [(i, i + 1) for i in range(chips - 1)]
    back = [(i + 1, i) for i in range(chips - 1)]

    def halves(weight, parts, pad):
        size = weight.shape[1] // (2 * parts)
        cut = [weight[:, i * size : (i + 1) * size] for i in range(2 * parts)]
        if pad != size:
            cut = [jnp.pad(piece, ((0, 0), (0, pad - size))) for piece in cut]
        return cut[0::2], cut[1::2]

    def paired(pieces):
        low = jnp.concatenate([piece for one, _ in pieces for piece in one], 1)
        high = jnp.concatenate([piece for _, two in pieces for piece in two], 1)
        mine = jnp.where(core == 0, low, high)
        return ordered(mine, swap(jnp.where(core == 0, high, low)), 0)

    pair_tokens = ordered(tokens, swap(tokens), 1)

    gains = jnp.pad(jnp.stack([norm_attn, norm_mlp], 1), ((0, 0), (0, LANES - 2)))
    cores = core.astype(jnp.int32).reshape(1)
    mine, other = pack_first(cores, w_qkv, gains, w_out)
    pair_one = ordered(mine, swap(other), 0)
    places = tuple(lax.axis_index(name) for name in ("inner", "outer", "dp"))
    later_in, later_down, pair_one, pair_tokens, places = tied(
        w_in, w_down, pair_one, pair_tokens, places
    )
    one = direct_sends(pair_one)
    pair_two = paired([halves(later_in, 2, padded)])
    pair_three = paired([halves(later_down, 1, padded)])
    three_near = gather_near([pair_three])
    order = arrival_order(*places, width, shard_rows)
    own_order = lax.dynamic_slice_in_dim(order, core * side, side, 0)
    other_order = lax.dynamic_slice_in_dim(order, (1 - core) * side, side, 0)

    def in_order(value):
        return matmul(value.reshape(-1, width), order).astype(BF16)

    own_tokens = in_order(pair_tokens)
    grad_output = in_order(ordered(cotangent, swap(cotangent), 1))

    start = lax.axis_index(("outer", "inner")) * length
    positions = (start - HALF + jnp.arange(window, dtype=jnp.int32)).astype(F32)
    frequency = ROPE_BASE ** (-(jnp.arange(HD // 2, dtype=F32) * 2.0 / HD))
    angles = positions[:, None] * frequency[None, :]
    cosine, sine = jnp.cos(angles), jnp.sin(angles)
    cosine = jnp.tile(cosine, (1, LANES // (HD // 2)))
    sine = jnp.tile(jnp.concatenate([-sine, sine], 1), (1, LANES // HD))
    ids_padded = jnp.pad(doc_ids, ((0, 0), (HALF, HALF)), constant_values=-1)
    key_ids = lax.dynamic_slice_in_dim(ids_padded, start, window, 1)[:, None, :]
    query_ids = lax.dynamic_slice_in_dim(doc_ids, start, length, 1)[:, :, None]

    prepared = (own_tokens, grad_output, order, own_order, other_order)
    prepared += (cosine, sine, key_ids, query_ids)
    prepared, pair_two, three_near, one, pair_tokens = tied(
        prepared, pair_two, three_near, one, pair_tokens
    )
    own_tokens, grad_output, order, own_order, other_order = prepared[:5]
    cosine, sine, key_ids, query_ids = prepared[5:]
    two = direct_sends(pair_two)
    three_far = gather_far(*three_near)
    low = lax.ppermute(pair_tokens[:, length - HALF :], ("outer", "inner"), onward)
    high = lax.ppermute(pair_tokens[:, :HALF], ("outer", "inner"), back)
    three_near, three_far, one, low, high = tied(three_near, three_far, one, low, high)

    near = gather_near(one)
    low, high = (in_order(end).reshape(end.shape) for end in (low, high))
    late = joined_rows([three_near[0], *three_near[1], *three_near[2], *three_far[0], *three_far[1]])
    low, high, two, near, late = tied(low, high, two, near, late)

    far = gather_far(*near)
    two_own = joined_rows(two)
    three = direct_sends(late)
    near, far, two_own, three[1] = tied(near, far, two_own, three[1])

    two_near = gather_near([two_own])
    first = in_pieces(*near, *far)
    joined, window_norm, gain_rows = project(
        low, own_tokens.reshape(streams, length, width), high, first, cosine, sine, side
    )
    out_half = joined_rows([piece[:, 3 * side + LANES :] for piece in first])
    weight = out_weight(first, out_half, swap(out_half), own_order, other_order)
    three[2:3], joined, weight, first, two_near = tied(
        three[2:3], joined, weight, first, two_near
    )

    two_far = gather_far(*two_near)
    joined = joined.reshape(streams, window, 3 * side)
    attended = attend(block, joined, query_ids, key_ids).reshape(rows, side)
    attended_low, hidden, normed_mlp_low = out_project(
        attended, swap(attended), own_order, other_order, weight, own_tokens, gain_rows
    )
    hidden, normed_mlp_low, two_near, two_far = tied(
        hidden, normed_mlp_low, two_near, two_far
    )
    in_half = in_pieces(*two_near, *two_far)
    mixed_low, factor, active = feed(normed_mlp_low, in_half, padded)

    down_cuts = split_late(grad_output, mixed_low, shard_rows)
    down_cuts, factor, active, three = tied(down_cuts, factor, active, three)
    down_half = [join_late(three, shard_rows)]
    grad_gate, grad_up = feed_back(grad_output, factor, active, down_half)
    sum_in = GradSum([normed_mlp_low] * 2, [grad_gate, grad_up], shard_rows)
    sent_in = sum_in.far()
    grad_gate, grad_up, sent_in, mixed_low = tied(grad_gate, grad_up, sent_in, mixed_low)

    in_far = sum_in.send_far(sent_in)
    down_arrived = [
        lax.ppermute(cut, "outer", forward("outer", outer - 1)) for cut in down_cuts[1:2]
    ]
    part, part_low = back_project([grad_gate, grad_up], in_half, [F32, BF16])
    part, part_low, in_far, down_arrived[0], down_cuts = tied(
        part, part_low, in_far, down_arrived[0], down_cuts
    )

    in_near = sum_in.send_near(sum_in.near(in_far))
    down_arrived[1:] = [
        lax.ppermute(down_cuts[distance], "outer", forward("outer", outer - distance))
        for distance in range(2, outer)
    ]
    grad_hidden, hidden_side, grad_attended = hidden_back(
        part, swap(part_low), hidden, grad_output, gain_rows, weight, own_order
    )
    grad_query, mid, to_lower, to_upper = attend_back(
        block, joined, query_ids, key_ids, grad_attended.reshape(streams, length, side),
        cosine, sine,
    )
    from_lower = lax.ppermute(to_upper, ("outer", "inner"), onward)
    from_upper = lax.ppermute(to_lower, ("outer", "inner"), back)
    from_lower, from_upper, in_near, down_arrived[:2] = tied(
        from_lower, from_upper, in_near, down_arrived[:2]
    )

    grad_joined = join_grads(grad_query, mid, from_lower, from_upper, cosine, sine)
    grad_joined = grad_joined.reshape(rows, 3 * side)
    normed_low = window_norm.reshape(streams, window, width)[:, HALF : HALF + length]
    sum_attn = GradSum(
        [normed_low.reshape(rows, width), attended_low], [grad_joined, hidden_side], shard_rows
    )
    sent_attn, in_own = sum_attn.far(), sum_in.own(in_near)
    sent_attn, in_own, grad_joined = tied(sent_attn, in_own, grad_joined)

    attn_far = sum_attn.send_far(sent_attn)
    attn_far, down_arrived, grad_joined, mixed_low = tied(
        attn_far, down_arrived, grad_joined, mixed_low
    )

    attn_near = sum_attn.send_near(sum_attn.near(attn_far))
    in_arrived = sum_in.send_direct(in_own)
    sum_down = LateSum([down_cuts[0], *down_arrived], shard_rows)
    down_far = sum_down.send_far(sum_down.far())
    out_mine, out_other = back_split(cores, mixed_low, down_half, streams)
    in_mine, in_other = back_split(cores, grad_joined, first, streams)
    attn_near, in_arrived, out_mine, out_other, in_mine, in_other, down_far = tied(
        attn_near, in_arrived, out_mine, out_other, in_mine, in_other, down_far
    )

    attn_own = sum_attn.own(attn_near)
    attn_arrived = sum_attn.send_direct(attn_own)
    output = end_rows(
        output_kernel, cores, [out_mine, swap(out_other)], [hidden], [order], BF16, streams
    ).reshape(tokens.shape)
    grad_tokens = end_rows(
        input_grad_kernel, cores, [in_mine, swap(in_other)], [grad_hidden, own_tokens],
        [gain_rows, order], F32, streams,
    ).reshape(tokens.shape)
    total_mine, total_other = sum_in.total(cores, in_own, in_arrived)
    grad_in, gain_grad_mlp = assemble(
        cores, total_mine, swap(total_other), [(0, 2, padded, units)], w_in, norm_mlp
    )
    down_near = sum_down.send_near(sum_down.near(down_far))
    attn_arrived, output, grad_tokens, grad_in, gain_grad_mlp, down_near = tied(
        attn_arrived, output, grad_tokens, grad_in, gain_grad_mlp, down_near
    )
    down_mine, down_other = sum_down.total(cores, sum_down.own(down_near), [])
    total_mine, total_other = sum_attn.total(cores, attn_own, attn_arrived)
    grad_qkv, grad_out, gain_grad_attn = assemble(
        cores, total_mine, swap(total_other),
        [(0, 3, side, side), (3 * side, 1, side, side)], w_qkv, norm_attn,
    )
    (grad_down,) = assemble(cores, down_mine, swap(down_other), [(0, 1, padded, units)])
    return (
        output,
        grad_tokens,
        gain_grad_attn.reshape(-1),
        gain_grad_mlp.reshape(-1),
        grad_qkv,
        grad_out,
        grad_in,
        grad_down,
    )


def solution(mesh):
    dp, seq = mesh.shape["dp"], mesh.shape["seq"]
    chips = seq // 2
    outer = 4 if chips % 4 == 0 else 1
    fine = Mesh(
        mesh.devices.reshape(dp, outer, chips // outer, 2), ("dp", "outer", "inner", "core")
    )
    line = ("outer", "inner", "core")
    every = ("dp",) + line
    token = P("dp", line, None)
    vector = P(every)
    matrix = P(every, None)
    return jax.shard_map(
        shards,
        mesh=fine,
        in_specs=(token, P("dp", None), vector, vector, matrix, matrix, matrix, matrix, token),
        out_specs=(token, token, vector, vector, matrix, matrix, matrix, matrix),
        check_vma=False,
    )
```

```python
import functools

import jax
import jax.numpy as jnp
import numpy as np
from jax import lax
from jax.experimental import pallas as pl
from jax.experimental.pallas import tpu as pltpu
from jax.sharding import Mesh, PartitionSpec as P

HD = 64
HALF = 64
LANES = 128
NORM_EPSILON = 1e-05
ROPE_BASE = 10000.0
F32 = jnp.float32
BF16 = jnp.bfloat16


def contract_cols(left, right):
    return lax.dot_general(left, right, (((1,), (1,)), ((), ())), preferred_element_type=F32)


def contract_rows(left, right):
    return lax.dot_general(left, right, (((0,), (0,)), ((), ())), preferred_element_type=F32)


def matmul(left, right):
    return jnp.dot(left, right, preferred_element_type=F32)


def tied(*values):
    return lax.optimization_barrier(values)


def call(kernel, grid, ins, outs, scratch=(), limit=40):
    out = pl.pallas_call(
        kernel,
        grid=grid,
        in_specs=[
            pl.BlockSpec(memory_space=pltpu.SMEM) if block is None else pl.BlockSpec(block, index)
            for _, block, index in ins
        ],
        out_specs=[pl.BlockSpec(block, index) for _, _, block, index in outs],
        out_shape=[jax.ShapeDtypeStruct(shape, kind) for shape, kind, _, _ in outs],
        scratch_shapes=list(scratch),
        compiler_params=pltpu.CompilerParams(vmem_limit_bytes=limit * 2**20),
        cost_estimate=pl.CostEstimate(flops=1024, bytes_accessed=1024, transcendentals=0),
    )(*[array for array, _, _ in ins])
    return out


def whole(array):
    return (array, array.shape, lambda *_: (0,) * array.ndim)


def swap(value):
    return lax.ppermute(value, "core", [(0, 1), (1, 0)])


def ordered(mine, other, axis):
    first = lax.axis_index("core") == 0
    return jnp.concatenate(
        [jnp.where(first, mine, other), jnp.where(first, other, mine)], axis=axis
    )


def forward(axis, distance=1):
    count = lax.axis_size(axis)
    return [(i, (i + distance) % count) for i in range(count)]


def ring_gather(axis, piece):
    pieces = [piece]
    for _ in range(1, lax.axis_size(axis)):
        pieces.append(lax.ppermute(pieces[-1], axis, forward(axis)))
    return pieces[1:]


def direct_send(rows, *distances):
    count = lax.axis_size("outer")
    return [
        lax.ppermute(rows, "outer", forward("outer", distance))
        for distance in distances
        if distance < count
    ]


def direct_sends(rows):
    return [rows] + direct_send(rows, *range(1, lax.axis_size("outer")))


def joined_rows(pieces):
    return jnp.concatenate(pieces, 0) if len(pieces) > 1 else pieces[0]


def gather_near(arrived):
    own = joined_rows(arrived)
    return own, ring_gather("inner", own), ring_gather("dp", own)


def copy_kernel(*refs):
    count = len(refs) // 2
    for source, target in zip(refs[:count], refs[count:]):
        target[...] = source[...]


def far_halves(along_x, along_y, half):
    if len(along_x) > 1 or len(along_y) > 1 or half % 32:
        return (
            joined_rows([piece[:half] for piece in along_y]),
            joined_rows([piece[half:] for piece in along_x]),
        )
    columns = along_x[0].shape[1]
    return call(
        copy_kernel,
        (1,),
        [(along_y[0], (half, columns), lambda i: (0, 0))]
        + [(along_x[0], (half, columns), lambda i: (1, 0))],
        [((half, columns), BF16, (half, columns), lambda i: (0, 0)) for _ in range(2)],
    )


def gather_far(own, along_x, along_y):
    one, two = far_halves(along_x, along_y, own.shape[0] // 2)
    return ring_gather("inner", one), ring_gather("dp", two)


def in_pieces(own, along_x, along_y, one, two):
    pieces = [own, *along_x, *along_y, *one, *two]
    if any(piece.shape[0] % LANES for piece in pieces):
        pieces = [joined_rows(pieces)]
    return pieces


def order_blocks(inner, dp):
    blocks = [(0, 0, 0, 2)]
    blocks += [(d, 0, 0, 2) for d in range(1, inner)] + [(0, d, 0, 2) for d in range(1, dp)]
    blocks += [(d, e, 0, 1) for d in range(1, inner) for e in range(1, dp)]
    return blocks + [(d, e, 1, 2) for e in range(1, dp) for d in range(1, inner)]


def late_segments(shard_rows):
    inner, outer, dp = (lax.axis_size(name) for name in ("inner", "outer", "dp"))
    start, at = 0, {}
    for d, e, low, high in order_blocks(inner, dp):
        for part in range(low, high):
            at[d, e, part] = start
            start += shard_rows
    segments = []
    for d, e, low, high in order_blocks(inner, dp):
        for distance in range(low * outer // 2, high * outer // 2):
            first, second = at[d, e, 0], at[d, e, 1]
            if second == first + shard_rows:
                segments.append((distance, first, 2 * shard_rows))
            else:
                segments += [(distance, first, shard_rows), (distance, second, shard_rows)]
    return segments


def join_kernel_rows(segments, *refs):
    pieces, out_ref = refs[:-1], refs[-1]
    at = 0
    for distance, start, count in segments:
        out_ref[at : at + count, :] = pieces[distance][start : start + count, :]
        at += count


def join_late(pieces, shard_rows):
    segments = late_segments(shard_rows)
    columns = pieces[0].shape[1]
    rows = sum(count for _, _, count in segments)
    if shard_rows % 32:
        return jnp.concatenate([pieces[d][at : at + n] for d, at, n in segments], 0)
    return call(
        functools.partial(join_kernel_rows, segments),
        (1,),
        [whole(piece) for piece in pieces],
        [((rows, columns), BF16, (rows, columns), lambda i: (0, 0))],
    )[0]


def split_kernel_rows(segments, left_ref, right_ref, *outs):
    place, at = [], 0
    for distance, start, count in segments:
        place.append((at, distance, start, count))
        at += count
    for top in range(0, at, LANES):
        rows = contract_rows(left_ref[:, top : top + LANES], right_ref[...]).astype(BF16)
        for begin, distance, start, count in place:
            if top <= begin < top + LANES:
                outs[distance][start : start + count, :] = rows[begin - top : begin - top + count]


def split_late(left, right, shard_rows):
    segments = late_segments(shard_rows)
    outer = lax.axis_size("outer")
    rows, columns = left.shape[1] // outer, right.shape[1]
    if shard_rows % 32:
        total, at, cuts = contract_rows(left, right).astype(BF16), 0, {}
        for distance, start, count in segments:
            cuts[distance, start] = total[at : at + count]
            at += count
        return [
            jnp.concatenate([cuts[key] for key in sorted(cuts) if key[0] == distance], 0)
            for distance in range(outer)
        ]
    return call(
        functools.partial(split_kernel_rows, segments),
        (1,),
        [whole(left), whole(right)],
        [((rows, columns), BF16, (rows, columns), lambda i: (0, 0)) for _ in range(outer)],
    )


def arrival_order(x, z, y, width, shard_rows):
    inner, outer, dp = (lax.axis_size(name) for name in ("inner", "outer", "dp"))
    half = outer * shard_rows
    blocks = order_blocks(inner, dp)
    place = np.concatenate([np.arange(low * half, high * half) for _, _, low, high in blocks])
    sizes = [(high - low) * half for _, _, low, high in blocks]
    along_x = np.repeat([block[0] for block in blocks], sizes)
    along_y = np.repeat([block[1] for block in blocks], sizes)
    along_z, row = place // (2 * shard_rows), place % (2 * shard_rows)
    at_x = (x - jnp.asarray(along_x, jnp.int32) + inner) % inner
    at_y = (y - jnp.asarray(along_y, jnp.int32) + dp) % dp
    at_z = (z - jnp.asarray(along_z, jnp.int32) + outer) % outer
    source = ((at_y * outer + at_z) * inner + at_x) * 2 * shard_rows + row
    return (jnp.arange(width, dtype=jnp.int32)[:, None] == source[None, :]).astype(BF16)


def rows_kernel(pairs, layout, *refs):
    rights, refs = refs[:pairs], refs[pairs:]
    inputs, outs = refs[: -len(layout)], refs[-len(layout) :]
    for places, out_ref in zip(layout, outs):
        lefts, adds = inputs[:pairs], inputs[pairs : pairs + len(places)]
        inputs = inputs[pairs + len(places) :]
        start = 0
        for left, right in zip(lefts, rights):
            columns = slice(start, start + right.shape[1])
            start = columns.stop
            total = contract_rows(left[...], right[...])
            for add in adds:
                if add.shape[0] == total.shape[0]:
                    total = total + add[:, columns].astype(F32)
            out_ref[:, columns] = total.astype(BF16)
            for add, at in zip(adds, places):
                if add.shape[0] != total.shape[0]:
                    span = slice(at, at + add.shape[0])
                    part = total[span] + add[:, columns].astype(F32)
                    out_ref[span, columns] = part.astype(BF16)


class GradSum:
    def __init__(self, lefts, rights, shard_rows):
        self.lefts, self.rights = lefts, rights
        self.inner, self.outer, self.dp = (
            lax.axis_size(name) for name in ("inner", "outer", "dp")
        )
        self.shard = 2 * shard_rows
        self.half = self.outer * shard_rows
        self.at_x = 2 * self.half
        self.at_y = self.at_x + (self.inner - 1) * 2 * self.half
        self.at_one = self.at_y + (self.dp - 1) * 2 * self.half
        self.at_two = self.at_one + (self.inner - 1) * (self.dp - 1) * self.half

    def rows(self, *parts):
        depth = self.lefts[0].shape[0]
        columns = sum(right.shape[1] for right in self.rights)
        ins, outs, layout = [whole(right) for right in self.rights], [], []
        for start, count, adds in parts:
            adds = [(rows, place) for rows, place in adds if rows is not None]
            lefts, index = self.lefts, start // count
            if count % LANES or start % count:
                lefts, index = [left[:, start : start + count] for left in lefts], 0
            ins += [
                (left, (depth, count), lambda i, index=index: (0, index)) for left in lefts
            ]
            ins += [whole(rows) for rows, _ in adds]
            outs.append(((count, columns), BF16, (count, columns), lambda i: (0, 0)))
            layout.append([place for _, place in adds])
        return call(
            functools.partial(rows_kernel, len(self.rights), layout), (1,), ins, outs
        )

    def ring(self, axis, part, first):
        arrived = None
        for step in range(1, lax.axis_size(axis)):
            sent = first if step == 1 else self.rows(part(step, arrived))[0]
            arrived = lax.ppermute(sent, axis, forward(axis))
        return arrived

    def one(self, distance, arrived):
        count = (self.dp - 1) * self.half
        return (self.at_one + (distance - 1) * count, count, [(arrived, 0)])

    def two(self, distance, arrived):
        count = (self.inner - 1) * self.half
        return (self.at_two + (distance - 1) * count, count, [(arrived, 0)])

    def far(self):
        return self.rows(self.one(1, None), self.two(1, None))

    def send_far(self, firsts):
        return (
            self.ring("inner", self.one, firsts[0]), self.ring("dp", self.two, firsts[1])
        )

    def along(self, start, distance, arrived, extra, place):
        count = 2 * self.half
        extra = extra[(distance - 1) * self.half : distance * self.half]
        return (start + (distance - 1) * count, count, [(arrived, 0), (extra, place)])

    def along_x(self, distance, arrived):
        return self.along(self.at_x, distance, arrived, self.sums[1], self.half)

    def along_y(self, distance, arrived):
        return self.along(self.at_y, distance, arrived, self.sums[0], 0)

    def near(self, sums):
        self.sums = sums
        return self.rows(self.along_x(1, None), self.along_y(1, None))

    def send_near(self, firsts):
        return (
            self.ring("inner", self.along_x, firsts[0]),
            self.ring("dp", self.along_y, firsts[1]),
        )

    def own(self, nears):
        return self.rows((0, 2 * self.half, [(near, 0) for near in nears]))[0]

    def cut(self, own, distance):
        return own[distance * self.shard : (distance + 1) * self.shard]

    def send_direct(self, own):
        return [
            lax.ppermute(
                self.cut(own, distance), "outer", forward("outer", self.outer - distance)
            )
            for distance in range(1, self.outer)
        ]

    def total(self, core, own, arrived):
        columns = own.shape[1]
        half = self.shard // 2
        return call(
            total_kernel,
            (1,),
            [(core, None, None), (own, (self.shard, columns), lambda i: (0, 0))]
            + [whole(rows) for rows in arrived],
            [((half, columns), F32, (half, columns), lambda i: (0, 0)) for _ in range(2)],
        )


def late_kernel(count, layout, *refs):
    blocks, outs = refs[:count], refs[count:]
    for spans, out_ref in zip(layout, outs):
        at = 0
        for start, rows in spans:
            total = None
            for block in blocks:
                part = block[start : start + rows, :].astype(F32)
                total = part if total is None else total + part
            out_ref[at : at + rows, :] = total.astype(BF16)
            at += rows


def late_rows(blocks, shard_rows):
    inner, dp = lax.axis_size("inner"), lax.axis_size("dp")
    start, spans = 0, {}
    for d, e, low, high in order_blocks(inner, dp):
        rows = (high - low) * shard_rows
        spans.setdefault((d, e), []).append((start, rows))
        start += rows
    columns = blocks[0].shape[1]
    if shard_rows % 32:
        total = sum(block.astype(F32) for block in blocks).astype(BF16)
        return {
            key: joined_rows([total[at : at + rows] for at, rows in cuts])
            for key, cuts in spans.items()
        }
    shape = (2 * shard_rows, columns)
    cuts = call(
        functools.partial(late_kernel, len(blocks), list(spans.values())),
        (1,),
        [whole(block) for block in blocks],
        [(shape, BF16, shape, lambda i: (0, 0)) for _ in spans],
    )
    return dict(zip(spans, cuts))


def late_sends(cuts):
    inner, dp = lax.axis_size("inner"), lax.axis_size("dp")
    return [
        lax.ppermute(
            rows,
            ("dp", "inner"),
            [
                (y * inner + x, (y - e) % dp * inner + (x - d) % inner)
                for y in range(dp)
                for x in range(inner)
            ],
        )
        for (d, e), rows in cuts.items()
        if d or e
    ]


def own_half(core_ref, value):
    half = value.shape[0] // 2
    return jnp.where(core_ref[0] == 0, value[:half], value[half:])


def total_kernel(core_ref, *refs):
    total = None
    for ref in refs[:-2]:
        rows = ref[...].astype(F32)
        total = rows if total is None else total + rows
    half = total.shape[0] // 2
    first = core_ref[0] == 0
    refs[-2][...] = jnp.where(first, total[:half], total[half:])
    refs[-1][...] = jnp.where(first, total[half:], total[:half])


def assemble_kernel(layout, core_ref, mine_ref, other_ref, *refs):
    first = core_ref[0] == 0
    count = len(layout)
    pair = (
        jnp.where(first, mine_ref[...], other_ref[...]),
        jnp.where(first, other_ref[...], mine_ref[...]),
    )
    outs = refs[-count:] if len(refs) == count else refs[2:-1]
    for out_ref, (start, parts, stride, size) in zip(outs, layout):
        cuts = []
        for i in range(parts):
            at = start + i * stride
            cuts += [half[:, at : at + size] for half in pair]
        out_ref[...] = jnp.concatenate(cuts, 1)
    if len(refs) > count:
        weight_ref, gain_ref = refs[:2]
        product = weight_ref[...].astype(F32) * outs[0][...]
        refs[-1][...] = jnp.sum(product, -1, keepdims=True) / gain_ref[...].astype(F32)


def assemble(core, mine, other, layout, weight=None, gain=None):
    rows = mine.shape[0]
    ins = [(core, None, None), whole(mine), whole(other)]
    sizes = [2 * parts * size for _, parts, _, size in layout]
    if weight is not None:
        ins += [whole(weight), whole(gain.reshape(rows, 1))]
        sizes.append(1)
    return call(
        functools.partial(assemble_kernel, layout),
        (1,),
        ins,
        [((rows, size), F32, (rows, size), lambda i: (0, 0)) for size in sizes],
    )


def pack_kernel(side, core_ref, qkv_ref, gain_ref, out_ref, mine_ref, other_ref):
    def fill(target, half):
        for part in range(3):
            start = (2 * part + half) * side
            target[:, part * side : (part + 1) * side] = qkv_ref[:, start : start + side]
        target[:, 3 * side : 3 * side + LANES] = gain_ref[...]
        target[:, 3 * side + LANES :] = out_ref[:, half * side : (half + 1) * side]

    for half in range(2):

        @pl.when(core_ref[0] == half)
        def _():
            fill(mine_ref, half)
            fill(other_ref, 1 - half)


def pack_first(core, w_qkv, gains, w_out):
    rows, side = w_out.shape[0], w_out.shape[1] // 2
    columns = 4 * side + LANES
    return call(
        functools.partial(pack_kernel, side),
        (1,),
        [(core, None, None), whole(w_qkv), whole(gains), whole(w_out)],
        [((rows, columns), BF16, (rows, columns), lambda i: (0, 0)) for _ in range(2)],
    )


def normalise(values):
    centred = values - jnp.mean(values, -1, keepdims=True)
    scale = lax.rsqrt(jnp.mean(centred * centred, -1, keepdims=True) + NORM_EPSILON)
    return centred * scale, scale


def norm_back(unit, scale, gain, incoming):
    grad = incoming * gain
    return scale * (
        grad
        - jnp.mean(grad, -1, keepdims=True)
        - unit * jnp.mean(grad * unit, -1, keepdims=True)
    )


def piece_matmul(left, pieces):
    total, start = None, 0
    for piece in pieces:
        part = matmul(left[:, start : start + piece.shape[0]], piece[...])
        total = part if total is None else total + part
        start += piece.shape[0]
    return total


def back_kernel(starts, count, *refs):
    grads, pieces, out_refs = refs[: len(starts)], refs[len(starts) : count], refs[count:]
    at = 0
    for piece in pieces:
        total = None
        for grad, start in zip(grads, starts):
            part = contract_cols(grad[...], piece[:, start : start + grad.shape[1]])
            total = part if total is None else total + part
        for out_ref in out_refs:
            out_ref[:, at : at + piece.shape[0]] = total.astype(out_ref.dtype)
        at += piece.shape[0]


def back_project(grads, pieces, kinds):
    rows = grads[0].shape[0]
    block = rows // 2
    starts, end = [], 0
    for grad in grads:
        starts.append(end)
        end += grad.shape[1]
    width = sum(piece.shape[0] for piece in pieces)
    return call(
        functools.partial(back_kernel, starts, len(grads) + len(pieces)),
        (2,),
        [(grad, (block, grad.shape[1]), lambda i: (i, 0)) for grad in grads]
        + [(piece, (piece.shape[0], end), lambda i: (0, 0)) for piece in pieces],
        [((rows, width), kind, (block, width), lambda i: (i, 0)) for kind in kinds],
    )


def split_kernel(core_ref, grad_ref, *refs):
    pieces, (mine_ref, other_ref) = refs[:-2], refs[-2:]
    width = grad_ref.shape[1]
    half = grad_ref.shape[0] // 2
    at = 0
    for piece in pieces:
        total = contract_cols(grad_ref[...], piece[:, :width])
        first = core_ref[0] == 0
        span = slice(at, at + piece.shape[0])
        mine_ref[:, span] = jnp.where(first, total[:half], total[half:])
        other_ref[:, span] = jnp.where(first, total[half:], total[:half]).astype(BF16)
        at = span.stop


def back_split(core, grad, pieces, streams):
    rows, columns = grad.shape
    block = rows // streams
    width = sum(piece.shape[0] for piece in pieces)
    return call(
        split_kernel,
        (streams,),
        [(core, None, None), (grad, (block, columns), lambda i: (i, 0))]
        + [(piece, (piece.shape[0], columns), lambda i: (0, 0)) for piece in pieces],
        [
            ((rows // 2, width), kind, (block // 2, width), lambda i: (i, 0))
            for kind in (F32, BF16)
        ],
    )


def output_kernel(core_ref, mine_ref, other_ref, hidden_ref, order_ref, out_ref):
    total = own_half(core_ref, hidden_ref[...]) + mine_ref[...] + other_ref[...].astype(F32)
    out_ref[...] = contract_cols(total.astype(BF16), order_ref[...]).astype(BF16)


def input_grad_kernel(
    core_ref, mine_ref, other_ref, hidden_ref, x_ref, gain_ref, order_ref, out_ref
):
    unit, scale = normalise(own_half(core_ref, x_ref[...].astype(F32)))
    incoming = mine_ref[...] + other_ref[...].astype(F32)
    total = own_half(core_ref, hidden_ref[...])
    total = total + norm_back(unit, scale, gain_ref[0:1, :], incoming)
    result = None
    for _ in range(3):
        part = total.astype(BF16)
        total = total - part.astype(F32)
        part = contract_cols(part, order_ref[...])
        result = part if result is None else result + part
    out_ref[...] = result


def end_rows(kernel, core, halves, fulls, wholes, kind, streams):
    rows, width = halves[0].shape
    block = rows // streams
    return call(
        kernel,
        (streams,),
        [(core, None, None)]
        + [(array, (block, width), lambda i: (i, 0)) for array in halves]
        + [(array, (2 * block, width), lambda i: (i, 0)) for array in fulls]
        + [whole(array) for array in wholes],
        [((rows, width), kind, (block, width), lambda i: (i, 0))],
    )[0]


def turned(values):
    width = values.shape[-1]
    lane = lax.broadcasted_iota(jnp.int32, values.shape, values.ndim - 1)
    ahead = pltpu.roll(values, width - HD // 2, values.ndim - 1)
    behind = pltpu.roll(values, HD // 2, values.ndim - 1)
    return jnp.where(lane % HD < HD // 2, ahead, behind)


def project_kernel(count, low_ref, x_ref, high_ref, cos_ref, sin_ref, *refs):
    gains, weights = refs[:count], refs[count : 2 * count]
    out_ref, norm_ref, gain_ref = refs[2 * count :]

    @pl.when(pl.program_id(0) == 0)
    def _():
        pick = lax.broadcasted_iota(jnp.int32, (8, LANES), 0) == lax.broadcasted_iota(
            jnp.int32, (8, LANES), 1
        )
        pick = pick.astype(F32).astype(BF16)
        start = 0
        for piece in gains:
            gain_ref[:, start : start + piece.shape[0]] = contract_cols(pick, piece[...])
            start += piece.shape[0]
        for stream in range(x_ref.shape[0]):
            at = stream * cos_ref.shape[0]
            for ref in (low_ref, x_ref, high_ref):
                unit, _ = normalise(ref[stream].astype(F32))
                span = slice(at, at + ref.shape[1])
                norm_ref[span, :] = (unit * gain_ref[0:1, :]).astype(BF16)
                at = span.stop

    values = piece_matmul(norm_ref, weights)
    keep = pl.program_id(0) == 2
    length = cos_ref.shape[0]
    for top in range(0, values.shape[0], length):
        for left in range(0, values.shape[1], LANES):
            part = values[top : top + length, left : left + LANES]
            rotated = part * cos_ref[...] + turned(part) * sin_ref[...]
            out_ref[top : top + length, left : left + LANES] = jnp.where(
                keep, part, rotated
            ).astype(BF16)


def project(low, tokens, high, pieces, cosine, sine, side):
    width = tokens.shape[2]
    rows = tokens.shape[0] * cosine.shape[0]
    gain_block = 3 * side // LANES
    return call(
        functools.partial(project_kernel, len(pieces)),
        (3,),
        [whole(low), whole(tokens), whole(high), whole(cosine), whole(sine)]
        + [(piece, (piece.shape[0], LANES), lambda j: (0, gain_block)) for piece in pieces]
        + [(piece, (piece.shape[0], side), lambda j: (0, j)) for piece in pieces],
        [
            ((rows, 3 * side), BF16, (rows, side), lambda j: (0, j)),
            ((rows, width), BF16, (rows, width), lambda j: (0, 0)),
            ((8, width), F32, (8, width), lambda j: (0, 0)),
        ],
    )


def head_masks():
    lane = lax.broadcasted_iota(jnp.int32, (1, LANES), 1)
    return [(lane // HD == head).astype(F32).astype(BF16) for head in range(LANES // HD)]


def block_mask(query_ids, key_ids):
    rows, width = query_ids.shape[0], key_ids.shape[1]
    offset = lax.broadcasted_iota(jnp.int32, (rows, width), 1) - lax.broadcasted_iota(
        jnp.int32, (rows, width), 0
    )
    return (offset >= 0) & (offset <= 2 * HALF) & (query_ids == key_ids)


def block_probs(query, keys, allowed):
    scores = jnp.where(allowed, contract_cols(query, keys) * HD**-0.5, -1e30)
    grown = jnp.exp(scores - jnp.max(scores, -1, keepdims=True))
    return grown / jnp.sum(grown, -1, keepdims=True)


def attend_kernel(block, q_ref, k_ref, v_ref, qid_ref, kid_ref, out_ref):
    masks = head_masks()
    for start in range(0, out_ref.shape[1], block):
        span = slice(start, start + block + 2 * HALF)
        allowed = block_mask(qid_ref[0, start : start + block], kid_ref[0, :, span])
        query = q_ref[0, HALF + start : HALF + start + block]
        total = None
        for mask in masks:
            probs = block_probs(query * mask, k_ref[0, span], allowed)
            part = matmul(probs.astype(BF16), v_ref[0, span]) * mask.astype(F32)
            total = part if total is None else total + part
        out_ref[0, start : start + block] = total.astype(BF16)


def attend_back_kernel(
    block, q_ref, k_ref, v_ref, qid_ref, kid_ref, grad_ref, cos_ref, sin_ref,
    dq_ref, mid_ref, low_ref, high_ref,
):
    masks = head_masks()
    length = dq_ref.shape[1]
    grad_keys = grad_values = jnp.zeros((length + 2 * HALF, LANES), F32)
    for start in range(0, length, block):
        span = slice(start, start + block + 2 * HALF)
        mid = slice(HALF + start, HALF + start + block)
        rows = slice(start, start + block)
        allowed = block_mask(qid_ref[0, rows], kid_ref[0, :, span])
        query_all, grad_all = q_ref[0, mid], grad_ref[0, rows]
        keys, values = k_ref[0, span], v_ref[0, span]
        grad_query, part_keys, part_values = 0.0, 0.0, 0.0
        for mask in masks:
            query, grad = query_all * mask, grad_all * mask
            probs = block_probs(query, keys, allowed)
            grad_probs = contract_cols(grad, values)
            delta = jnp.sum(probs * grad_probs, -1, keepdims=True)
            grad_scores = (probs * (grad_probs - delta)).astype(BF16)
            grad_query += matmul(grad_scores, keys) * mask.astype(F32)
            part_keys += contract_rows(grad_scores, query)
            part_values += contract_rows(probs.astype(BF16), grad)
        grad_query = grad_query * HD**-0.5
        dq_ref[0, rows] = (
            grad_query * cos_ref[mid] - turned(grad_query) * sin_ref[mid]
        ).astype(BF16)
        before, after = start, length - start - block

        def placed(part):
            pieces = [part]
            if before:
                pieces.insert(0, jnp.zeros((before, LANES), F32))
            if after:
                pieces.append(jnp.zeros((after, LANES), F32))
            return jnp.concatenate(pieces, 0)

        grad_keys += placed(part_keys)
        grad_values += placed(part_values)
    for index, total in enumerate((grad_keys * HD**-0.5, grad_values)):
        low_ref[0, index] = total[:HALF].astype(BF16)
        mid_ref[0, index] = total[HALF : HALF + length]
        high_ref[0, index] = total[HALF + length :].astype(BF16)


def attention_inputs(joined, query_ids, key_ids):
    window, groups = joined.shape[1], joined.shape[2] // 3 // LANES
    inputs = [
        (joined, (1, window, LANES), lambda s, h, shift=shift: (s, 0, h + shift))
        for shift in (0, groups, 2 * groups)
    ]
    inputs += [
        (ids, (1,) + ids.shape[1:], lambda s, h: (s, 0, 0)) for ids in (query_ids, key_ids)
    ]
    return inputs


def attend(block, joined, query_ids, key_ids):
    streams, window, columns = joined.shape
    length, side = window - 2 * HALF, columns // 3
    return call(
        functools.partial(attend_kernel, block),
        (streams, side // LANES),
        attention_inputs(joined, query_ids, key_ids),
        [((streams, length, side), BF16, (1, length, LANES), lambda s, h: (s, 0, h))],
        limit=24,
    )[0]


def attend_back(block, joined, query_ids, key_ids, grad, cosine, sine):
    streams, length, side = grad.shape

    def pair(rows, kind):
        return (
            (streams, 2, rows, side), kind, (1, 2, rows, LANES), lambda s, h: (s, 0, 0, h)
        )

    return call(
        functools.partial(attend_back_kernel, block),
        (streams, side // LANES),
        attention_inputs(joined, query_ids, key_ids)
        + [(grad, (1, length, LANES), lambda s, h: (s, 0, h)), whole(cosine), whole(sine)],
        [
            ((streams, length, side), BF16, (1, length, LANES), lambda s, h: (s, 0, h)),
            pair(length, F32),
            pair(HALF, BF16),
            pair(HALF, BF16),
        ],
        limit=24,
    )


def join_kernel(dq_ref, mid_ref, low_ref, high_ref, cos_ref, sin_ref, out_ref):
    length, width = dq_ref.shape[1:]
    out_ref[0, :, :width] = dq_ref[0]
    cosine, sine = cos_ref[HALF : HALF + length], sin_ref[HALF : HALF + length]
    for index in range(2):
        for start in range(0, width, LANES):
            lanes = slice(start, start + LANES)
            total = mid_ref[0, index, :, lanes]
            total = total + jnp.concatenate(
                [
                    low_ref[0, index, :, lanes].astype(F32),
                    jnp.zeros((length - 2 * HALF, LANES), F32),
                    high_ref[0, index, :, lanes].astype(F32),
                ],
                0,
            )
            if index == 0:
                total = total * cosine - turned(total) * sine
            to = (1 + index) * width + start
            out_ref[0, :, to : to + LANES] = total.astype(BF16)


def join_grads(grad_query, mid, from_lower, from_upper, cosine, sine):
    streams, length, width = grad_query.shape

    def of_stream(array):
        block = (1,) + array.shape[1:]
        return (array, block, lambda s: (s,) + (0,) * (array.ndim - 1))

    return call(
        join_kernel,
        (streams,),
        [of_stream(array) for array in (grad_query, mid, from_lower, from_upper)]
        + [whole(cosine), whole(sine)],
        [((streams, length, 3 * width), BF16, (1, length, 3 * width), lambda s: (s, 0, 0))],
        limit=24,
    )[0]


def by_rows(array, block):
    return (array, (block, array.shape[1]), lambda i: (i, 0))


def weight_kernel(count, other_ref, own_order_ref, other_order_ref, *refs):
    start = 0
    out_ref = refs[count]
    for piece in refs[:count]:
        span = slice(start, start + piece.shape[0])
        total = matmul(piece[...], own_order_ref[...])
        total = total + matmul(other_ref[span, :], other_order_ref[...])
        out_ref[span, :] = total.astype(BF16)
        start = span.stop


def out_weight(pieces, own, other, own_order, other_order):
    side, width = own_order.shape
    if len(pieces) == 1:
        own_pieces = [(own, own.shape, lambda i: (0, 0))]
    else:
        own_pieces, start = [], 0
        for piece in pieces:
            count = piece.shape[0]
            own_pieces.append(
                (own, (count, side), lambda i, index=start // count: (index, 0))
            )
            start += count
    return call(
        functools.partial(weight_kernel, len(own_pieces)),
        (1,),
        [whole(other), whole(own_order), whole(other_order)] + own_pieces,
        [((width, width), BF16, (width, width), lambda i: (0, 0))],
    )[0]


def out_kernel(
    own_ref, other_ref, own_order_ref, other_order_ref, weight_ref, x_ref, gain_ref,
    att_ref, hidden_ref, norm_ref,
):
    attended = matmul(own_ref[...], own_order_ref[...])
    attended = (attended + matmul(other_ref[...], other_order_ref[...])).astype(BF16)
    att_ref[...] = attended
    hidden = x_ref[...].astype(F32) + matmul(attended, weight_ref[...])
    hidden_ref[...] = hidden
    norm_ref[...] = (normalise(hidden)[0] * gain_ref[1:2, :]).astype(BF16)


def out_project(own, other, own_order, other_order, weight, tokens, gains):
    rows, width = tokens.shape
    block = rows // 2
    return call(
        out_kernel,
        (2,),
        [by_rows(own, block), by_rows(other, block), whole(own_order), whole(other_order)]
        + [whole(weight), by_rows(tokens, block), whole(gains)],
        [
            ((rows, width), kind, (block, width), lambda i: (i, 0))
            for kind in (BF16, F32, BF16)
        ],
    )


def hidden_back_kernel(
    part_ref, other_ref, hidden_ref, g_ref, gain_ref, weight_ref, order_ref,
    grad_ref, side_ref, att_ref,
):
    unit, scale = normalise(hidden_ref[...])
    incoming = part_ref[...] + other_ref[...].astype(F32)
    grad = g_ref[...].astype(F32) + norm_back(unit, scale, gain_ref[1:2, :], incoming)
    low = grad.astype(BF16)
    grad_ref[...] = grad
    side_ref[...] = contract_cols(low, order_ref[...]).astype(BF16)
    attended = contract_cols(low, weight_ref[...]).astype(BF16)
    att_ref[...] = contract_cols(attended, order_ref[...]).astype(BF16)


def hidden_back(part, other, hidden, grad_output, gains, weight, own_order):
    rows, width = hidden.shape
    block, side = rows // 2, own_order.shape[0]
    return call(
        hidden_back_kernel,
        (2,),
        [by_rows(array, block) for array in (part, other, hidden, grad_output)]
        + [whole(gains), whole(weight), whole(own_order)],
        [
            ((rows, size), kind, (block, size), lambda i: (i, 0))
            for size, kind in ((width, F32), (side, BF16), (side, BF16))
        ],
    )


def column_spans(width):
    return [slice(at, min(at + 2 * LANES, width)) for at in range(0, width, 2 * LANES)]


def tile_matmul(left, pieces, columns):
    total, start = None, 0
    for piece in pieces:
        part = matmul(left[:, start : start + piece.shape[0]], piece[:, columns])
        total = part if total is None else total + part
        start += piece.shape[0]
    return total


def feed_kernel(norm_ref, *refs):
    pieces, (mixed_ref, factor_ref, active_ref) = refs[:-3], refs[-3:]
    units = mixed_ref.shape[1]
    for span in column_spans(units):
        gate = tile_matmul(norm_ref, pieces, span)
        up = tile_matmul(norm_ref, pieces, slice(units + span.start, units + span.stop))
        below = 0.5 * (1.0 + lax.erf(gate * 0.5**0.5))
        active = gate * below
        mixed_ref[:, span] = (active * up).astype(BF16)
        active_ref[:, span] = active
        density = jnp.exp(-0.5 * gate * gate) * (2.0 * np.pi) ** -0.5
        factor_ref[:, span] = up * (below + gate * density)


def feed(normed, pieces, units):
    rows = normed.shape[0]
    block = rows // 2
    return call(
        feed_kernel,
        (2,),
        [by_rows(normed, block)] + [whole(piece) for piece in pieces],
        [
            ((rows, units), kind, (block, units), lambda i: (i, 0))
            for kind in (BF16, F32, F32)
        ],
    )


def feed_back_kernel(g_ref, factor_ref, active_ref, *refs):
    pieces, (gate_ref, up_ref) = refs[:-2], refs[-2:]
    for span in column_spans(factor_ref.shape[1]):
        grad = tile_matmul(g_ref, pieces, span)
        gate_ref[:, span] = (grad * factor_ref[:, span]).astype(BF16)
        up_ref[:, span] = (grad * active_ref[:, span]).astype(BF16)


def feed_back(grad_output, factor, active, pieces):
    rows, units = factor.shape
    block = rows // 2
    return call(
        feed_back_kernel,
        (2,),
        [by_rows(array, block) for array in (grad_output, factor, active)]
        + [whole(piece) for piece in pieces],
        [((rows, units), BF16, (block, units), lambda i: (i, 0)) for _ in range(2)],
    )


def shards(tokens, doc_ids, norm_attn, norm_mlp, w_qkv, w_out, w_in, w_down, cotangent):
    streams, block, width = tokens.shape
    shard_rows = w_qkv.shape[0]
    inner, outer = lax.axis_size("inner"), lax.axis_size("outer")
    core = lax.axis_index("core")
    length = 2 * block
    window = length + 2 * HALF
    rows = streams * length
    side = width // 2
    units = w_down.shape[1] // 2
    padded = -(-units // LANES) * LANES
    chips = outer * inner
    onward = [(i, i + 1) for i in range(chips - 1)]
    back = [(i + 1, i) for i in range(chips - 1)]

    def halves(weight, parts, pad):
        size = weight.shape[1] // (2 * parts)
        cut = [weight[:, i * size : (i + 1) * size] for i in range(2 * parts)]
        if pad != size:
            cut = [jnp.pad(piece, ((0, 0), (0, pad - size))) for piece in cut]
        return cut[0::2], cut[1::2]

    def paired(pieces):
        low = jnp.concatenate([piece for one, _ in pieces for piece in one], 1)
        high = jnp.concatenate([piece for _, two in pieces for piece in two], 1)
        mine = jnp.where(core == 0, low, high)
        return ordered(mine, swap(jnp.where(core == 0, high, low)), 0)

    pair_tokens = ordered(tokens, swap(tokens), 1)

    gains = jnp.pad(jnp.stack([norm_attn, norm_mlp], 1), ((0, 0), (0, LANES - 2)))
    cores = core.astype(jnp.int32).reshape(1)
    mine, other = pack_first(cores, w_qkv, gains, w_out)
    pair_one = ordered(mine, swap(other), 0)
    places = tuple(lax.axis_index(name) for name in ("inner", "outer", "dp"))
    later_in, later_down, pair_one, pair_tokens, places = tied(
        w_in, w_down, pair_one, pair_tokens, places
    )
    one = direct_sends(pair_one)
    pair_two = paired([halves(later_in, 2, padded)])
    pair_three = paired([halves(later_down, 1, padded)])
    three_near = gather_near([pair_three])
    order = arrival_order(*places, width, shard_rows)
    own_order = lax.dynamic_slice_in_dim(order, core * side, side, 0)
    other_order = lax.dynamic_slice_in_dim(order, (1 - core) * side, side, 0)

    def in_order(value):
        return matmul(value.reshape(-1, width), order).astype(BF16)

    own_tokens = in_order(pair_tokens)
    grad_output = in_order(ordered(cotangent, swap(cotangent), 1))

    start = lax.axis_index(("outer", "inner")) * length
    positions = (start - HALF + jnp.arange(window, dtype=jnp.int32)).astype(F32)
    frequency = ROPE_BASE ** (-(jnp.arange(HD // 2, dtype=F32) * 2.0 / HD))
    angles = positions[:, None] * frequency[None, :]
    cosine, sine = jnp.cos(angles), jnp.sin(angles)
    cosine = jnp.tile(cosine, (1, LANES // (HD // 2)))
    sine = jnp.tile(jnp.concatenate([-sine, sine], 1), (1, LANES // HD))
    ids_padded = jnp.pad(doc_ids, ((0, 0), (HALF, HALF)), constant_values=-1)
    key_ids = lax.dynamic_slice_in_dim(ids_padded, start, window, 1)[:, None, :]
    query_ids = lax.dynamic_slice_in_dim(doc_ids, start, length, 1)[:, :, None]

    prepared = (own_tokens, grad_output, order, own_order, other_order)
    prepared += (cosine, sine, key_ids, query_ids)
    prepared, pair_two, three_near, one, pair_tokens = tied(
        prepared, pair_two, three_near, one, pair_tokens
    )
    own_tokens, grad_output, order, own_order, other_order = prepared[:5]
    cosine, sine, key_ids, query_ids = prepared[5:]
    two_one = direct_send(pair_two, 1)
    three_far = gather_far(*three_near)
    low = lax.ppermute(pair_tokens[:, length - HALF :], ("outer", "inner"), onward)
    high = lax.ppermute(pair_tokens[:, :HALF], ("outer", "inner"), back)
    three_near, three_far, one, low, high, two_one, pair_two = tied(
        three_near, three_far, one, low, high, two_one, pair_two
    )
    two = [pair_two] + two_one + direct_send(pair_two, *range(2, outer))

    near = gather_near(one)
    low, high = (in_order(end).reshape(end.shape) for end in (low, high))
    late = joined_rows([three_near[0], *three_near[1], *three_near[2], *three_far[0], *three_far[1]])
    low, high, two, near, late = tied(low, high, two, near, late)

    far = gather_far(*near)
    two_own = joined_rows(two)
    three = direct_sends(late)
    near, far, two_own, three[1] = tied(near, far, two_own, three[1])

    two_near = gather_near([two_own])
    first = in_pieces(*near, *far)
    joined, window_norm, gain_rows = project(
        low, own_tokens.reshape(streams, length, width), high, first, cosine, sine, side
    )
    out_half = joined_rows([piece[:, 3 * side + LANES :] for piece in first])
    weight = out_weight(first, out_half, swap(out_half), own_order, other_order)
    three[3:], joined, weight, first, two_near = tied(
        three[3:], joined, weight, first, two_near
    )

    two_far = gather_far(*two_near)
    joined = joined.reshape(streams, window, 3 * side)
    attended = attend(block, joined, query_ids, key_ids).reshape(rows, side)
    attended_low, hidden, normed_mlp_low = out_project(
        attended, swap(attended), own_order, other_order, weight, own_tokens, gain_rows
    )
    hidden, normed_mlp_low, two_near, two_far = tied(
        hidden, normed_mlp_low, two_near, two_far
    )
    in_half = in_pieces(*two_near, *two_far)
    mixed_low, factor, active = feed(normed_mlp_low, in_half, padded)

    down_cuts = split_late(grad_output, mixed_low, shard_rows)
    down_cuts, factor, active, three = tied(down_cuts, factor, active, three)
    down_half = [join_late(three, shard_rows)]
    grad_gate, grad_up = feed_back(grad_output, factor, active, down_half)
    sum_in = GradSum([normed_mlp_low] * 2, [grad_gate, grad_up], shard_rows)
    sent_in = sum_in.far()
    grad_gate, grad_up, sent_in, mixed_low = tied(grad_gate, grad_up, sent_in, mixed_low)

    in_far = sum_in.send_far(sent_in)
    down_arrived = [
        lax.ppermute(cut, "outer", forward("outer", outer - 1)) for cut in down_cuts[1:2]
    ]
    part, part_low = back_project([grad_gate, grad_up], in_half, [F32, BF16])
    part, part_low, in_far, down_arrived[0], down_cuts = tied(
        part, part_low, in_far, down_arrived[0], down_cuts
    )

    in_near = sum_in.send_near(sum_in.near(in_far))
    down_arrived[1:] = [
        lax.ppermute(down_cuts[distance], "outer", forward("outer", outer - distance))
        for distance in range(2, outer)
    ]
    grad_hidden, hidden_side, grad_attended = hidden_back(
        part, swap(part_low), hidden, grad_output, gain_rows, weight, own_order
    )
    grad_query, mid, to_lower, to_upper = attend_back(
        block, joined, query_ids, key_ids, grad_attended.reshape(streams, length, side),
        cosine, sine,
    )
    from_lower = lax.ppermute(to_upper, ("outer", "inner"), onward)
    from_upper = lax.ppermute(to_lower, ("outer", "inner"), back)
    from_lower, from_upper, in_near, down_arrived[:2] = tied(
        from_lower, from_upper, in_near, down_arrived[:2]
    )

    grad_joined = join_grads(grad_query, mid, from_lower, from_upper, cosine, sine)
    grad_joined = grad_joined.reshape(rows, 3 * side)
    normed_low = window_norm.reshape(streams, window, width)[:, HALF : HALF + length]
    sum_attn = GradSum(
        [normed_low.reshape(rows, width), attended_low], [grad_joined, hidden_side], shard_rows
    )
    sent_attn, in_own = sum_attn.far(), sum_in.own(in_near)
    sent_attn, in_own, grad_joined = tied(sent_attn, in_own, grad_joined)

    attn_far = sum_attn.send_far(sent_attn)
    out_mine, out_other = back_split(cores, mixed_low, down_half, streams)
    in_mine, in_other = back_split(cores, grad_joined, first, streams)
    attn_far, down_arrived, out_mine, out_other, in_mine, in_other = tied(
        attn_far, down_arrived, out_mine, out_other, in_mine, in_other
    )

    attn_near = sum_attn.send_near(sum_attn.near(attn_far))
    in_arrived = sum_in.send_direct(in_own)
    down_rows = late_rows([down_cuts[0], *down_arrived], shard_rows)
    out_other, in_other = swap(out_other), swap(in_other)
    attn_near, in_arrived, out_other, in_other, down_rows = tied(
        attn_near, in_arrived, out_other, in_other, down_rows
    )

    attn_own = sum_attn.own(attn_near)
    attn_arrived = sum_attn.send_direct(attn_own)
    output = end_rows(
        output_kernel, cores, [out_mine, out_other], [hidden], [order], BF16, streams
    ).reshape(tokens.shape)
    grad_tokens = end_rows(
        input_grad_kernel, cores, [in_mine, in_other], [grad_hidden, own_tokens],
        [gain_rows, order], F32, streams,
    ).reshape(tokens.shape)
    total_mine, total_other = sum_in.total(cores, in_own, in_arrived)
    grad_in, gain_grad_mlp = assemble(
        cores, total_mine, swap(total_other), [(0, 2, padded, units)], w_in, norm_mlp
    )
    down_sums = late_sends(down_rows)
    attn_arrived, output, grad_tokens, grad_in, gain_grad_mlp, down_sums = tied(
        attn_arrived, output, grad_tokens, grad_in, gain_grad_mlp, down_sums
    )
    down_mine, down_other = sum_in.total(cores, down_rows[0, 0], down_sums)
    total_mine, total_other = sum_attn.total(cores, attn_own, attn_arrived)
    grad_qkv, grad_out, gain_grad_attn = assemble(
        cores, total_mine, swap(total_other),
        [(0, 3, side, side), (3 * side, 1, side, side)], w_qkv, norm_attn,
    )
    (grad_down,) = assemble(cores, down_mine, swap(down_other), [(0, 1, padded, units)])
    return (
        output,
        grad_tokens,
        gain_grad_attn.reshape(-1),
        gain_grad_mlp.reshape(-1),
        grad_qkv,
        grad_out,
        grad_in,
        grad_down,
    )


def solution(mesh):
    dp, seq = mesh.shape["dp"], mesh.shape["seq"]
    chips = seq // 2
    outer = 4 if chips % 4 == 0 else 1
    fine = Mesh(
        mesh.devices.reshape(dp, outer, chips // outer, 2), ("dp", "outer", "inner", "core")
    )
    line = ("outer", "inner", "core")
    every = ("dp",) + line
    token = P("dp", line, None)
    vector = P(every)
    matrix = P(every, None)
    return jax.shard_map(
        shards,
        mesh=fine,
        in_specs=(token, P("dp", None), vector, vector, matrix, matrix, matrix, matrix, token),
        out_specs=(token, token, vector, vector, matrix, matrix, matrix, matrix),
        check_vma=False,
    )
```

```python
import functools

import jax
import jax.numpy as jnp
import numpy as np
from jax import lax
from jax.experimental import pallas as pl
from jax.experimental.pallas import tpu as pltpu
from jax.sharding import Mesh, PartitionSpec as P

HD = 64
HALF = 64
LANES = 128
NORM_EPSILON = 1e-05
ROPE_BASE = 10000.0
F32 = jnp.float32
BF16 = jnp.bfloat16


def contract_cols(left, right):
    return lax.dot_general(left, right, (((1,), (1,)), ((), ())), preferred_element_type=F32)


def contract_rows(left, right):
    return lax.dot_general(left, right, (((0,), (0,)), ((), ())), preferred_element_type=F32)


def matmul(left, right):
    return jnp.dot(left, right, preferred_element_type=F32)


def tied(*values):
    return lax.optimization_barrier(values)


def call(kernel, grid, ins, outs, scratch=(), limit=40):
    out = pl.pallas_call(
        kernel,
        grid=grid,
        in_specs=[
            pl.BlockSpec(memory_space=pltpu.SMEM) if block is None else pl.BlockSpec(block, index)
            for _, block, index in ins
        ],
        out_specs=[pl.BlockSpec(block, index) for _, _, block, index in outs],
        out_shape=[jax.ShapeDtypeStruct(shape, kind) for shape, kind, _, _ in outs],
        scratch_shapes=list(scratch),
        compiler_params=pltpu.CompilerParams(vmem_limit_bytes=limit * 2**20),
        cost_estimate=pl.CostEstimate(flops=1024, bytes_accessed=1024, transcendentals=0),
    )(*[array for array, _, _ in ins])
    return out


def whole(array):
    return (array, array.shape, lambda *_: (0,) * array.ndim)


def swap(value):
    return lax.ppermute(value, "core", [(0, 1), (1, 0)])


def ordered(mine, other, axis):
    first = lax.axis_index("core") == 0
    return jnp.concatenate(
        [jnp.where(first, mine, other), jnp.where(first, other, mine)], axis=axis
    )


def forward(axis, distance=1):
    count = lax.axis_size(axis)
    return [(i, (i + distance) % count) for i in range(count)]


def ring_gather(axis, piece):
    pieces = [piece]
    for _ in range(1, lax.axis_size(axis)):
        pieces.append(lax.ppermute(pieces[-1], axis, forward(axis)))
    return pieces[1:]


def direct_send(rows, *distances):
    count = lax.axis_size("outer")
    return [
        lax.ppermute(rows, "outer", forward("outer", distance))
        for distance in distances
        if distance < count
    ]


def direct_sends(rows):
    return [rows] + direct_send(rows, *range(1, lax.axis_size("outer")))


def joined_rows(pieces):
    return jnp.concatenate(pieces, 0) if len(pieces) > 1 else pieces[0]


def gather_near(arrived):
    own = joined_rows(arrived)
    return own, ring_gather("inner", own), ring_gather("dp", own)


def copy_kernel(*refs):
    count = len(refs) // 2
    for source, target in zip(refs[:count], refs[count:]):
        target[...] = source[...]


def far_halves(along_x, along_y, half):
    if len(along_x) > 1 or len(along_y) > 1 or half % 32:
        return (
            joined_rows([piece[:half] for piece in along_y]),
            joined_rows([piece[half:] for piece in along_x]),
        )
    columns = along_x[0].shape[1]
    return call(
        copy_kernel,
        (1,),
        [(along_y[0], (half, columns), lambda i: (0, 0))]
        + [(along_x[0], (half, columns), lambda i: (1, 0))],
        [((half, columns), BF16, (half, columns), lambda i: (0, 0)) for _ in range(2)],
    )


def gather_far(own, along_x, along_y):
    one, two = far_halves(along_x, along_y, own.shape[0] // 2)
    return ring_gather("inner", one), ring_gather("dp", two)


def in_pieces(own, along_x, along_y, one, two):
    pieces = [own, *along_x, *along_y, *one, *two]
    if any(piece.shape[0] % LANES for piece in pieces):
        pieces = [joined_rows(pieces)]
    return pieces


def order_blocks(inner, dp):
    blocks = [(0, 0, 0, 2)]
    blocks += [(d, 0, 0, 2) for d in range(1, inner)] + [(0, d, 0, 2) for d in range(1, dp)]
    blocks += [(d, e, 0, 1) for d in range(1, inner) for e in range(1, dp)]
    return blocks + [(d, e, 1, 2) for e in range(1, dp) for d in range(1, inner)]


def late_segments(shard_rows):
    inner, outer, dp = (lax.axis_size(name) for name in ("inner", "outer", "dp"))
    start, at = 0, {}
    for d, e, low, high in order_blocks(inner, dp):
        for part in range(low, high):
            at[d, e, part] = start
            start += shard_rows
    segments = []
    for d, e, low, high in order_blocks(inner, dp):
        for distance in range(low * outer // 2, high * outer // 2):
            first, second = at[d, e, 0], at[d, e, 1]
            if second == first + shard_rows:
                segments.append((distance, first, 2 * shard_rows))
            else:
                segments += [(distance, first, shard_rows), (distance, second, shard_rows)]
    return segments


def join_kernel_rows(segments, *refs):
    pieces, out_ref = refs[:-1], refs[-1]
    at = 0
    for distance, start, count in segments:
        out_ref[at : at + count, :] = pieces[distance][start : start + count, :]
        at += count


def join_late(pieces, shard_rows):
    segments = late_segments(shard_rows)
    columns = pieces[0].shape[1]
    rows = sum(count for _, _, count in segments)
    if shard_rows % 32:
        return jnp.concatenate([pieces[d][at : at + n] for d, at, n in segments], 0)
    return call(
        functools.partial(join_kernel_rows, segments),
        (1,),
        [whole(piece) for piece in pieces],
        [((rows, columns), BF16, (rows, columns), lambda i: (0, 0))],
    )[0]


def split_kernel_rows(segments, left_ref, right_ref, *outs):
    place, at = [], 0
    for distance, start, count in segments:
        place.append((at, distance, start, count))
        at += count
    for top in range(0, at, LANES):
        rows = contract_rows(left_ref[:, top : top + LANES], right_ref[...]).astype(BF16)
        for begin, distance, start, count in place:
            if top <= begin < top + LANES:
                outs[distance][start : start + count, :] = rows[begin - top : begin - top + count]


def split_late(left, right, shard_rows):
    segments = late_segments(shard_rows)
    outer = lax.axis_size("outer")
    rows, columns = left.shape[1] // outer, right.shape[1]
    if shard_rows % 32:
        total, at, cuts = contract_rows(left, right).astype(BF16), 0, {}
        for distance, start, count in segments:
            cuts[distance, start] = total[at : at + count]
            at += count
        return [
            jnp.concatenate([cuts[key] for key in sorted(cuts) if key[0] == distance], 0)
            for distance in range(outer)
        ]
    return call(
        functools.partial(split_kernel_rows, segments),
        (1,),
        [whole(left), whole(right)],
        [((rows, columns), BF16, (rows, columns), lambda i: (0, 0)) for _ in range(outer)],
    )


def arrival_order(x, z, y, width, shard_rows):
    inner, outer, dp = (lax.axis_size(name) for name in ("inner", "outer", "dp"))
    half = outer * shard_rows
    blocks = order_blocks(inner, dp)
    place = np.concatenate([np.arange(low * half, high * half) for _, _, low, high in blocks])
    sizes = [(high - low) * half for _, _, low, high in blocks]
    along_x = np.repeat([block[0] for block in blocks], sizes)
    along_y = np.repeat([block[1] for block in blocks], sizes)
    along_z, row = place // (2 * shard_rows), place % (2 * shard_rows)
    at_x = (x - jnp.asarray(along_x, jnp.int32) + inner) % inner
    at_y = (y - jnp.asarray(along_y, jnp.int32) + dp) % dp
    at_z = (z - jnp.asarray(along_z, jnp.int32) + outer) % outer
    source = ((at_y * outer + at_z) * inner + at_x) * 2 * shard_rows + row
    return (jnp.arange(width, dtype=jnp.int32)[:, None] == source[None, :]).astype(BF16)


def rows_kernel(pairs, layout, *refs):
    rights, refs = refs[:pairs], refs[pairs:]
    inputs, outs = refs[: -len(layout)], refs[-len(layout) :]
    for places, out_ref in zip(layout, outs):
        lefts, adds = inputs[:pairs], inputs[pairs : pairs + len(places)]
        inputs = inputs[pairs + len(places) :]
        start = 0
        for left, right in zip(lefts, rights):
            columns = slice(start, start + right.shape[1])
            start = columns.stop
            total = contract_rows(left[...], right[...])
            for add in adds:
                if add.shape[0] == total.shape[0]:
                    total = total + add[:, columns].astype(F32)
            out_ref[:, columns] = total.astype(BF16)
            for add, at in zip(adds, places):
                if add.shape[0] != total.shape[0]:
                    span = slice(at, at + add.shape[0])
                    part = total[span] + add[:, columns].astype(F32)
                    out_ref[span, columns] = part.astype(BF16)


class GradSum:
    def __init__(self, lefts, rights, shard_rows):
        self.lefts, self.rights = lefts, rights
        self.inner, self.outer, self.dp = (
            lax.axis_size(name) for name in ("inner", "outer", "dp")
        )
        self.shard = 2 * shard_rows
        self.half = self.outer * shard_rows
        self.at_x = 2 * self.half
        self.at_y = self.at_x + (self.inner - 1) * 2 * self.half
        self.at_one = self.at_y + (self.dp - 1) * 2 * self.half
        self.at_two = self.at_one + (self.inner - 1) * (self.dp - 1) * self.half

    def rows(self, *parts):
        depth = self.lefts[0].shape[0]
        columns = sum(right.shape[1] for right in self.rights)
        ins, outs, layout = [whole(right) for right in self.rights], [], []
        for start, count, adds in parts:
            adds = [(rows, place) for rows, place in adds if rows is not None]
            lefts, index = self.lefts, start // count
            if count % LANES or start % count:
                lefts, index = [left[:, start : start + count] for left in lefts], 0
            ins += [
                (left, (depth, count), lambda i, index=index: (0, index)) for left in lefts
            ]
            ins += [whole(rows) for rows, _ in adds]
            outs.append(((count, columns), BF16, (count, columns), lambda i: (0, 0)))
            layout.append([place for _, place in adds])
        return call(
            functools.partial(rows_kernel, len(self.rights), layout), (1,), ins, outs
        )

    def ring(self, axis, part, first):
        arrived = None
        for step in range(1, lax.axis_size(axis)):
            sent = first if step == 1 else self.rows(part(step, arrived))[0]
            arrived = lax.ppermute(sent, axis, forward(axis))
        return arrived

    def one(self, distance, arrived):
        count = (self.dp - 1) * self.half
        return (self.at_one + (distance - 1) * count, count, [(arrived, 0)])

    def two(self, distance, arrived):
        count = (self.inner - 1) * self.half
        return (self.at_two + (distance - 1) * count, count, [(arrived, 0)])

    def far(self):
        return self.rows(self.one(1, None), self.two(1, None))

    def send_far(self, firsts):
        return (
            self.ring("inner", self.one, firsts[0]), self.ring("dp", self.two, firsts[1])
        )

    def along(self, start, distance, arrived, extra, place):
        count = 2 * self.half
        extra = extra[(distance - 1) * self.half : distance * self.half]
        return (start + (distance - 1) * count, count, [(arrived, 0), (extra, place)])

    def along_x(self, distance, arrived):
        return self.along(self.at_x, distance, arrived, self.sums[1], self.half)

    def along_y(self, distance, arrived):
        return self.along(self.at_y, distance, arrived, self.sums[0], 0)

    def near(self, sums):
        self.sums = sums
        return self.rows(self.along_x(1, None), self.along_y(1, None))

    def send_near(self, firsts):
        return (
            self.ring("inner", self.along_x, firsts[0]),
            self.ring("dp", self.along_y, firsts[1]),
        )

    def own(self, nears):
        return self.rows((0, 2 * self.half, [(near, 0) for near in nears]))[0]

    def cut(self, own, distance):
        return own[distance * self.shard : (distance + 1) * self.shard]

    def send_direct(self, own, *distances):
        return [
            lax.ppermute(
                self.cut(own, distance), "outer", forward("outer", self.outer - distance)
            )
            for distance in distances
            if distance < self.outer
        ]

    def total(self, core, own, arrived):
        columns = own.shape[1]
        half = self.shard // 2
        return call(
            total_kernel,
            (1,),
            [(core, None, None), (own, (self.shard, columns), lambda i: (0, 0))]
            + [whole(rows) for rows in arrived],
            [((half, columns), F32, (half, columns), lambda i: (0, 0)) for _ in range(2)],
        )


def late_kernel(count, layout, *refs):
    blocks, outs = refs[:count], refs[count:]
    for spans, out_ref in zip(layout, outs):
        at = 0
        for start, rows in spans:
            total = None
            for block in blocks:
                part = block[start : start + rows, :].astype(F32)
                total = part if total is None else total + part
            out_ref[at : at + rows, :] = total.astype(BF16)
            at += rows


def late_rows(blocks, shard_rows):
    inner, dp = lax.axis_size("inner"), lax.axis_size("dp")
    start, spans = 0, {}
    for d, e, low, high in order_blocks(inner, dp):
        rows = (high - low) * shard_rows
        spans.setdefault((d, e), []).append((start, rows))
        start += rows
    columns = blocks[0].shape[1]
    if shard_rows % 32:
        total = sum(block.astype(F32) for block in blocks).astype(BF16)
        return {
            key: joined_rows([total[at : at + rows] for at, rows in cuts])
            for key, cuts in spans.items()
        }
    shape = (2 * shard_rows, columns)
    cuts = call(
        functools.partial(late_kernel, len(blocks), list(spans.values())),
        (1,),
        [whole(block) for block in blocks],
        [(shape, BF16, shape, lambda i: (0, 0)) for _ in spans],
    )
    return dict(zip(spans, cuts))


def to_owner(d, e):
    inner, dp = lax.axis_size("inner"), lax.axis_size("dp")
    return [
        (y * inner + x, (y - e) % dp * inner + (x - d) % inner)
        for y in range(dp)
        for x in range(inner)
    ]


def late_sends(cuts):
    return [
        lax.ppermute(rows, ("dp", "inner"), to_owner(d, e))
        for (d, e), rows in cuts.items()
        if d or e
    ]


def late_gather(rows):
    inner, dp = lax.axis_size("inner"), lax.axis_size("dp")
    arrived = {(0, 0): rows}
    for d in range(inner):
        for e in range(dp):
            if d or e:
                pairs = [(target, source) for source, target in to_owner(d, e)]
                arrived[d, e] = lax.ppermute(rows, ("dp", "inner"), pairs)
    return arrived


def late_block(arrived, shard_rows):
    blocks, pieces = order_blocks(lax.axis_size("inner"), lax.axis_size("dp")), []
    while blocks:
        d, e, low, high = blocks.pop(0)
        if blocks and blocks[0][:3] == (d, e, high):
            high = blocks.pop(0)[3]
        piece = arrived[d, e]
        if high - low < 2:
            piece = piece[low * shard_rows : high * shard_rows]
        pieces.append(piece)
    return joined_rows(pieces)


def own_half(core_ref, value):
    half = value.shape[0] // 2
    return jnp.where(core_ref[0] == 0, value[:half], value[half:])


def total_kernel(core_ref, *refs):
    total = None
    for ref in refs[:-2]:
        rows = ref[...].astype(F32)
        total = rows if total is None else total + rows
    half = total.shape[0] // 2
    first = core_ref[0] == 0
    refs[-2][...] = jnp.where(first, total[:half], total[half:])
    refs[-1][...] = jnp.where(first, total[half:], total[:half])


def assemble_kernel(layout, core_ref, mine_ref, other_ref, *refs):
    first = core_ref[0] == 0
    count = len(layout)
    pair = (
        jnp.where(first, mine_ref[...], other_ref[...]),
        jnp.where(first, other_ref[...], mine_ref[...]),
    )
    outs = refs[-count:] if len(refs) == count else refs[2:-1]
    for out_ref, (start, parts, stride, size) in zip(outs, layout):
        cuts = []
        for i in range(parts):
            at = start + i * stride
            cuts += [half[:, at : at + size] for half in pair]
        out_ref[...] = jnp.concatenate(cuts, 1)
    if len(refs) > count:
        weight_ref, gain_ref = refs[:2]
        product = weight_ref[...].astype(F32) * outs[0][...]
        refs[-1][...] = jnp.sum(product, -1, keepdims=True) / gain_ref[...].astype(F32)


def assemble(core, mine, other, layout, weight=None, gain=None):
    rows = mine.shape[0]
    ins = [(core, None, None), whole(mine), whole(other)]
    sizes = [2 * parts * size for _, parts, _, size in layout]
    if weight is not None:
        ins += [whole(weight), whole(gain.reshape(rows, 1))]
        sizes.append(1)
    return call(
        functools.partial(assemble_kernel, layout),
        (1,),
        ins,
        [((rows, size), F32, (rows, size), lambda i: (0, 0)) for size in sizes],
    )


def pack_kernel(side, core_ref, qkv_ref, gain_ref, out_ref, mine_ref, other_ref):
    def fill(target, half):
        for part in range(3):
            start = (2 * part + half) * side
            target[:, part * side : (part + 1) * side] = qkv_ref[:, start : start + side]
        target[:, 3 * side : 3 * side + LANES] = gain_ref[...]
        target[:, 3 * side + LANES :] = out_ref[:, half * side : (half + 1) * side]

    for half in range(2):

        @pl.when(core_ref[0] == half)
        def _():
            fill(mine_ref, half)
            fill(other_ref, 1 - half)


def pack_first(core, w_qkv, gains, w_out):
    rows, side = w_out.shape[0], w_out.shape[1] // 2
    columns = 4 * side + LANES
    return call(
        functools.partial(pack_kernel, side),
        (1,),
        [(core, None, None), whole(w_qkv), whole(gains), whole(w_out)],
        [((rows, columns), BF16, (rows, columns), lambda i: (0, 0)) for _ in range(2)],
    )


def normalise(values):
    centred = values - jnp.mean(values, -1, keepdims=True)
    scale = lax.rsqrt(jnp.mean(centred * centred, -1, keepdims=True) + NORM_EPSILON)
    return centred * scale, scale


def norm_back(unit, scale, gain, incoming):
    grad = incoming * gain
    return scale * (
        grad
        - jnp.mean(grad, -1, keepdims=True)
        - unit * jnp.mean(grad * unit, -1, keepdims=True)
    )


def piece_matmul(left, pieces):
    total, start = None, 0
    for piece in pieces:
        part = matmul(left[:, start : start + piece.shape[0]], piece[...])
        total = part if total is None else total + part
        start += piece.shape[0]
    return total


def back_kernel(starts, count, *refs):
    grads, pieces, out_refs = refs[: len(starts)], refs[len(starts) : count], refs[count:]
    at = 0
    for piece in pieces:
        total = None
        for grad, start in zip(grads, starts):
            part = contract_cols(grad[...], piece[:, start : start + grad.shape[1]])
            total = part if total is None else total + part
        for out_ref in out_refs:
            out_ref[:, at : at + piece.shape[0]] = total.astype(out_ref.dtype)
        at += piece.shape[0]


def back_project(grads, pieces, kinds):
    rows = grads[0].shape[0]
    block = rows // 2
    starts, end = [], 0
    for grad in grads:
        starts.append(end)
        end += grad.shape[1]
    width = sum(piece.shape[0] for piece in pieces)
    return call(
        functools.partial(back_kernel, starts, len(grads) + len(pieces)),
        (2,),
        [(grad, (block, grad.shape[1]), lambda i: (i, 0)) for grad in grads]
        + [(piece, (piece.shape[0], end), lambda i: (0, 0)) for piece in pieces],
        [((rows, width), kind, (block, width), lambda i: (i, 0)) for kind in kinds],
    )


def split_kernel(core_ref, grad_ref, *refs):
    pieces, (mine_ref, other_ref) = refs[:-2], refs[-2:]
    width = grad_ref.shape[1]
    half = grad_ref.shape[0] // 2
    at = 0
    for piece in pieces:
        total = contract_cols(grad_ref[...], piece[:, :width])
        first = core_ref[0] == 0
        span = slice(at, at + piece.shape[0])
        mine_ref[:, span] = jnp.where(first, total[:half], total[half:])
        other_ref[:, span] = jnp.where(first, total[half:], total[:half]).astype(BF16)
        at = span.stop


def back_split(core, grad, pieces, streams):
    rows, columns = grad.shape
    block = rows // streams
    width = sum(piece.shape[0] for piece in pieces)
    return call(
        split_kernel,
        (streams,),
        [(core, None, None), (grad, (block, columns), lambda i: (i, 0))]
        + [(piece, (piece.shape[0], columns), lambda i: (0, 0)) for piece in pieces],
        [
            ((rows // 2, width), kind, (block // 2, width), lambda i: (i, 0))
            for kind in (F32, BF16)
        ],
    )


def output_kernel(core_ref, mine_ref, other_ref, hidden_ref, order_ref, out_ref):
    total = own_half(core_ref, hidden_ref[...]) + mine_ref[...] + other_ref[...].astype(F32)
    out_ref[...] = contract_cols(total.astype(BF16), order_ref[...]).astype(BF16)


def input_grad_kernel(
    core_ref, mine_ref, other_ref, hidden_ref, x_ref, gain_ref, order_ref, out_ref
):
    unit, scale = normalise(own_half(core_ref, x_ref[...].astype(F32)))
    incoming = mine_ref[...] + other_ref[...].astype(F32)
    total = own_half(core_ref, hidden_ref[...])
    total = total + norm_back(unit, scale, gain_ref[0:1, :], incoming)
    result = None
    for _ in range(3):
        part = total.astype(BF16)
        total = total - part.astype(F32)
        part = contract_cols(part, order_ref[...])
        result = part if result is None else result + part
    out_ref[...] = result


def end_rows(kernel, core, halves, fulls, wholes, kind, streams):
    rows, width = halves[0].shape
    block = rows // streams
    return call(
        kernel,
        (streams,),
        [(core, None, None)]
        + [(array, (block, width), lambda i: (i, 0)) for array in halves]
        + [(array, (2 * block, width), lambda i: (i, 0)) for array in fulls]
        + [whole(array) for array in wholes],
        [((rows, width), kind, (block, width), lambda i: (i, 0))],
    )[0]


def turned(values):
    width = values.shape[-1]
    lane = lax.broadcasted_iota(jnp.int32, values.shape, values.ndim - 1)
    ahead = pltpu.roll(values, width - HD // 2, values.ndim - 1)
    behind = pltpu.roll(values, HD // 2, values.ndim - 1)
    return jnp.where(lane % HD < HD // 2, ahead, behind)


def project_kernel(count, low_ref, x_ref, high_ref, cos_ref, sin_ref, *refs):
    gains, weights = refs[:count], refs[count : 2 * count]
    out_ref, norm_ref, gain_ref = refs[2 * count :]

    @pl.when(pl.program_id(0) == 0)
    def _():
        pick = lax.broadcasted_iota(jnp.int32, (8, LANES), 0) == lax.broadcasted_iota(
            jnp.int32, (8, LANES), 1
        )
        pick = pick.astype(F32).astype(BF16)
        start = 0
        for piece in gains:
            gain_ref[:, start : start + piece.shape[0]] = contract_cols(pick, piece[...])
            start += piece.shape[0]
        for stream in range(x_ref.shape[0]):
            at = stream * cos_ref.shape[0]
            for ref in (low_ref, x_ref, high_ref):
                unit, _ = normalise(ref[stream].astype(F32))
                span = slice(at, at + ref.shape[1])
                norm_ref[span, :] = (unit * gain_ref[0:1, :]).astype(BF16)
                at = span.stop

    values = piece_matmul(norm_ref, weights)
    keep = pl.program_id(0) == 2
    length = cos_ref.shape[0]
    for top in range(0, values.shape[0], length):
        for left in range(0, values.shape[1], LANES):
            part = values[top : top + length, left : left + LANES]
            rotated = part * cos_ref[...] + turned(part) * sin_ref[...]
            out_ref[top : top + length, left : left + LANES] = jnp.where(
                keep, part, rotated
            ).astype(BF16)


def project(low, tokens, high, pieces, cosine, sine, side):
    width = tokens.shape[2]
    rows = tokens.shape[0] * cosine.shape[0]
    gain_block = 3 * side // LANES
    return call(
        functools.partial(project_kernel, len(pieces)),
        (3,),
        [whole(low), whole(tokens), whole(high), whole(cosine), whole(sine)]
        + [(piece, (piece.shape[0], LANES), lambda j: (0, gain_block)) for piece in pieces]
        + [(piece, (piece.shape[0], side), lambda j: (0, j)) for piece in pieces],
        [
            ((rows, 3 * side), BF16, (rows, side), lambda j: (0, j)),
            ((rows, width), BF16, (rows, width), lambda j: (0, 0)),
            ((8, width), F32, (8, width), lambda j: (0, 0)),
        ],
    )


def head_masks():
    lane = lax.broadcasted_iota(jnp.int32, (1, LANES), 1)
    return [(lane // HD == head).astype(F32).astype(BF16) for head in range(LANES // HD)]


def block_mask(query_ids, key_ids):
    rows, width = query_ids.shape[0], key_ids.shape[1]
    offset = lax.broadcasted_iota(jnp.int32, (rows, width), 1) - lax.broadcasted_iota(
        jnp.int32, (rows, width), 0
    )
    return (offset >= 0) & (offset <= 2 * HALF) & (query_ids == key_ids)


def block_probs(query, keys, allowed):
    scores = jnp.where(allowed, contract_cols(query, keys) * HD**-0.5, -1e30)
    grown = jnp.exp(scores - jnp.max(scores, -1, keepdims=True))
    return grown / jnp.sum(grown, -1, keepdims=True)


def attend_kernel(block, q_ref, k_ref, v_ref, qid_ref, kid_ref, out_ref):
    masks = head_masks()
    for start in range(0, out_ref.shape[1], block):
        span = slice(start, start + block + 2 * HALF)
        allowed = block_mask(qid_ref[0, start : start + block], kid_ref[0, :, span])
        query = q_ref[0, HALF + start : HALF + start + block]
        total = None
        for mask in masks:
            probs = block_probs(query * mask, k_ref[0, span], allowed)
            part = matmul(probs.astype(BF16), v_ref[0, span]) * mask.astype(F32)
            total = part if total is None else total + part
        out_ref[0, start : start + block] = total.astype(BF16)


def attend_back_kernel(
    block, q_ref, k_ref, v_ref, qid_ref, kid_ref, grad_ref, cos_ref, sin_ref,
    dq_ref, mid_ref, low_ref, high_ref,
):
    masks = head_masks()
    length = dq_ref.shape[1]
    grad_keys = grad_values = jnp.zeros((length + 2 * HALF, LANES), F32)
    for start in range(0, length, block):
        span = slice(start, start + block + 2 * HALF)
        mid = slice(HALF + start, HALF + start + block)
        rows = slice(start, start + block)
        allowed = block_mask(qid_ref[0, rows], kid_ref[0, :, span])
        query_all, grad_all = q_ref[0, mid], grad_ref[0, rows]
        keys, values = k_ref[0, span], v_ref[0, span]
        grad_query, part_keys, part_values = 0.0, 0.0, 0.0
        for mask in masks:
            query, grad = query_all * mask, grad_all * mask
            probs = block_probs(query, keys, allowed)
            grad_probs = contract_cols(grad, values)
            delta = jnp.sum(probs * grad_probs, -1, keepdims=True)
            grad_scores = (probs * (grad_probs - delta)).astype(BF16)
            grad_query += matmul(grad_scores, keys) * mask.astype(F32)
            part_keys += contract_rows(grad_scores, query)
            part_values += contract_rows(probs.astype(BF16), grad)
        grad_query = grad_query * HD**-0.5
        dq_ref[0, rows] = (
            grad_query * cos_ref[mid] - turned(grad_query) * sin_ref[mid]
        ).astype(BF16)
        before, after = start, length - start - block

        def placed(part):
            pieces = [part]
            if before:
                pieces.insert(0, jnp.zeros((before, LANES), F32))
            if after:
                pieces.append(jnp.zeros((after, LANES), F32))
            return jnp.concatenate(pieces, 0)

        grad_keys += placed(part_keys)
        grad_values += placed(part_values)
    for index, total in enumerate((grad_keys * HD**-0.5, grad_values)):
        low_ref[0, index] = total[:HALF].astype(BF16)
        mid_ref[0, index] = total[HALF : HALF + length]
        high_ref[0, index] = total[HALF + length :].astype(BF16)


def attention_inputs(joined, query_ids, key_ids):
    window, groups = joined.shape[1], joined.shape[2] // 3 // LANES
    inputs = [
        (joined, (1, window, LANES), lambda s, h, shift=shift: (s, 0, h + shift))
        for shift in (0, groups, 2 * groups)
    ]
    inputs += [
        (ids, (1,) + ids.shape[1:], lambda s, h: (s, 0, 0)) for ids in (query_ids, key_ids)
    ]
    return inputs


def attend(block, joined, query_ids, key_ids):
    streams, window, columns = joined.shape
    length, side = window - 2 * HALF, columns // 3
    return call(
        functools.partial(attend_kernel, block),
        (streams, side // LANES),
        attention_inputs(joined, query_ids, key_ids),
        [((streams, length, side), BF16, (1, length, LANES), lambda s, h: (s, 0, h))],
        limit=24,
    )[0]


def attend_back(block, joined, query_ids, key_ids, grad, cosine, sine):
    streams, length, side = grad.shape

    def pair(rows, kind):
        return (
            (streams, 2, rows, side), kind, (1, 2, rows, LANES), lambda s, h: (s, 0, 0, h)
        )

    return call(
        functools.partial(attend_back_kernel, block),
        (streams, side // LANES),
        attention_inputs(joined, query_ids, key_ids)
        + [(grad, (1, length, LANES), lambda s, h: (s, 0, h)), whole(cosine), whole(sine)],
        [
            ((streams, length, side), BF16, (1, length, LANES), lambda s, h: (s, 0, h)),
            pair(length, F32),
            pair(HALF, BF16),
            pair(HALF, BF16),
        ],
        limit=24,
    )


def join_kernel(dq_ref, mid_ref, low_ref, high_ref, cos_ref, sin_ref, out_ref):
    length, width = dq_ref.shape[1:]
    out_ref[0, :, :width] = dq_ref[0]
    cosine, sine = cos_ref[HALF : HALF + length], sin_ref[HALF : HALF + length]
    for index in range(2):
        for start in range(0, width, LANES):
            lanes = slice(start, start + LANES)
            total = mid_ref[0, index, :, lanes]
            total = total + jnp.concatenate(
                [
                    low_ref[0, index, :, lanes].astype(F32),
                    jnp.zeros((length - 2 * HALF, LANES), F32),
                    high_ref[0, index, :, lanes].astype(F32),
                ],
                0,
            )
            if index == 0:
                total = total * cosine - turned(total) * sine
            to = (1 + index) * width + start
            out_ref[0, :, to : to + LANES] = total.astype(BF16)


def join_grads(grad_query, mid, from_lower, from_upper, cosine, sine):
    streams, length, width = grad_query.shape

    def of_stream(array):
        block = (1,) + array.shape[1:]
        return (array, block, lambda s: (s,) + (0,) * (array.ndim - 1))

    return call(
        join_kernel,
        (streams,),
        [of_stream(array) for array in (grad_query, mid, from_lower, from_upper)]
        + [whole(cosine), whole(sine)],
        [((streams, length, 3 * width), BF16, (1, length, 3 * width), lambda s: (s, 0, 0))],
        limit=24,
    )[0]


def by_rows(array, block):
    return (array, (block, array.shape[1]), lambda i: (i, 0))


def weight_kernel(count, other_ref, own_order_ref, other_order_ref, *refs):
    start = 0
    out_ref = refs[count]
    for piece in refs[:count]:
        span = slice(start, start + piece.shape[0])
        total = matmul(piece[...], own_order_ref[...])
        total = total + matmul(other_ref[span, :], other_order_ref[...])
        out_ref[span, :] = total.astype(BF16)
        start = span.stop


def out_weight(pieces, own, other, own_order, other_order):
    side, width = own_order.shape
    if len(pieces) == 1:
        own_pieces = [(own, own.shape, lambda i: (0, 0))]
    else:
        own_pieces, start = [], 0
        for piece in pieces:
            count = piece.shape[0]
            own_pieces.append(
                (own, (count, side), lambda i, index=start // count: (index, 0))
            )
            start += count
    return call(
        functools.partial(weight_kernel, len(own_pieces)),
        (1,),
        [whole(other), whole(own_order), whole(other_order)] + own_pieces,
        [((width, width), BF16, (width, width), lambda i: (0, 0))],
    )[0]


def out_kernel(
    own_ref, other_ref, own_order_ref, other_order_ref, weight_ref, x_ref, gain_ref,
    att_ref, hidden_ref, norm_ref,
):
    attended = matmul(own_ref[...], own_order_ref[...])
    attended = (attended + matmul(other_ref[...], other_order_ref[...])).astype(BF16)
    att_ref[...] = attended
    hidden = x_ref[...].astype(F32) + matmul(attended, weight_ref[...])
    hidden_ref[...] = hidden
    norm_ref[...] = (normalise(hidden)[0] * gain_ref[1:2, :]).astype(BF16)


def out_project(own, other, own_order, other_order, weight, tokens, gains):
    rows, width = tokens.shape
    block = rows // 2
    return call(
        out_kernel,
        (2,),
        [by_rows(own, block), by_rows(other, block), whole(own_order), whole(other_order)]
        + [whole(weight), by_rows(tokens, block), whole(gains)],
        [
            ((rows, width), kind, (block, width), lambda i: (i, 0))
            for kind in (BF16, F32, BF16)
        ],
    )


def hidden_back_kernel(
    part_ref, other_ref, hidden_ref, g_ref, gain_ref, weight_ref, order_ref,
    grad_ref, side_ref, att_ref,
):
    unit, scale = normalise(hidden_ref[...])
    incoming = part_ref[...] + other_ref[...].astype(F32)
    grad = g_ref[...].astype(F32) + norm_back(unit, scale, gain_ref[1:2, :], incoming)
    low = grad.astype(BF16)
    grad_ref[...] = grad
    side_ref[...] = contract_cols(low, order_ref[...]).astype(BF16)
    attended = contract_cols(low, weight_ref[...]).astype(BF16)
    att_ref[...] = contract_cols(attended, order_ref[...]).astype(BF16)


def hidden_back(part, other, hidden, grad_output, gains, weight, own_order):
    rows, width = hidden.shape
    block, side = rows // 2, own_order.shape[0]
    return call(
        hidden_back_kernel,
        (2,),
        [by_rows(array, block) for array in (part, other, hidden, grad_output)]
        + [whole(gains), whole(weight), whole(own_order)],
        [
            ((rows, size), kind, (block, size), lambda i: (i, 0))
            for size, kind in ((width, F32), (side, BF16), (side, BF16))
        ],
    )


def column_spans(width):
    return [slice(at, min(at + 2 * LANES, width)) for at in range(0, width, 2 * LANES)]


def tile_matmul(left, pieces, columns):
    total, start = None, 0
    for piece in pieces:
        part = matmul(left[:, start : start + piece.shape[0]], piece[:, columns])
        total = part if total is None else total + part
        start += piece.shape[0]
    return total


def feed_kernel(norm_ref, *refs):
    pieces, (mixed_ref, factor_ref, active_ref) = refs[:-3], refs[-3:]
    units = mixed_ref.shape[1]
    for span in column_spans(units):
        gate = tile_matmul(norm_ref, pieces, span)
        up = tile_matmul(norm_ref, pieces, slice(units + span.start, units + span.stop))
        below = 0.5 * (1.0 + lax.erf(gate * 0.5**0.5))
        active = gate * below
        mixed_ref[:, span] = (active * up).astype(BF16)
        active_ref[:, span] = active
        density = jnp.exp(-0.5 * gate * gate) * (2.0 * np.pi) ** -0.5
        factor_ref[:, span] = up * (below + gate * density)


def feed(normed, pieces, units):
    rows = normed.shape[0]
    block = rows // 2
    return call(
        feed_kernel,
        (2,),
        [by_rows(normed, block)] + [whole(piece) for piece in pieces],
        [
            ((rows, units), kind, (block, units), lambda i: (i, 0))
            for kind in (BF16, F32, F32)
        ],
    )


def feed_back_kernel(g_ref, factor_ref, active_ref, *refs):
    pieces, (gate_ref, up_ref) = refs[:-2], refs[-2:]
    for span in column_spans(factor_ref.shape[1]):
        grad = tile_matmul(g_ref, pieces, span)
        gate_ref[:, span] = (grad * factor_ref[:, span]).astype(BF16)
        up_ref[:, span] = (grad * active_ref[:, span]).astype(BF16)


def feed_back(grad_output, factor, active, pieces):
    rows, units = factor.shape
    block = rows // 2
    return call(
        feed_back_kernel,
        (2,),
        [by_rows(array, block) for array in (grad_output, factor, active)]
        + [whole(piece) for piece in pieces],
        [((rows, units), BF16, (block, units), lambda i: (i, 0)) for _ in range(2)],
    )


def shards(tokens, doc_ids, norm_attn, norm_mlp, w_qkv, w_out, w_in, w_down, cotangent):
    streams, block, width = tokens.shape
    shard_rows = w_qkv.shape[0]
    inner, outer = lax.axis_size("inner"), lax.axis_size("outer")
    core = lax.axis_index("core")
    length = 2 * block
    window = length + 2 * HALF
    rows = streams * length
    side = width // 2
    units = w_down.shape[1] // 2
    padded = -(-units // LANES) * LANES
    chips = outer * inner
    onward = [(i, i + 1) for i in range(chips - 1)]
    back = [(i + 1, i) for i in range(chips - 1)]

    def halves(weight, parts, pad):
        size = weight.shape[1] // (2 * parts)
        cut = [weight[:, i * size : (i + 1) * size] for i in range(2 * parts)]
        if pad != size:
            cut = [jnp.pad(piece, ((0, 0), (0, pad - size))) for piece in cut]
        return cut[0::2], cut[1::2]

    def paired(pieces):
        low = jnp.concatenate([piece for one, _ in pieces for piece in one], 1)
        high = jnp.concatenate([piece for _, two in pieces for piece in two], 1)
        mine = jnp.where(core == 0, low, high)
        return ordered(mine, swap(jnp.where(core == 0, high, low)), 0)

    pair_tokens = ordered(tokens, swap(tokens), 1)

    gains = jnp.pad(jnp.stack([norm_attn, norm_mlp], 1), ((0, 0), (0, LANES - 2)))
    cores = core.astype(jnp.int32).reshape(1)
    mine, other = pack_first(cores, w_qkv, gains, w_out)
    pair_one = ordered(mine, swap(other), 0)
    places = tuple(lax.axis_index(name) for name in ("inner", "outer", "dp"))
    later_in, later_down, pair_one, pair_tokens, places = tied(
        w_in, w_down, pair_one, pair_tokens, places
    )
    one = direct_sends(pair_one)
    pair_two = paired([halves(later_in, 2, padded)])
    pair_three = paired([halves(later_down, 1, padded)])
    low = lax.ppermute(pair_tokens[:, length - HALF :], ("outer", "inner"), onward)
    high = lax.ppermute(pair_tokens[:, :HALF], ("outer", "inner"), back)
    pair_three, low, high = tied(pair_three, low, high)
    late = late_gather(pair_three)
    order = arrival_order(*places, width, shard_rows)
    own_order = lax.dynamic_slice_in_dim(order, core * side, side, 0)
    other_order = lax.dynamic_slice_in_dim(order, (1 - core) * side, side, 0)

    def in_order(value):
        return matmul(value.reshape(-1, width), order).astype(BF16)

    own_tokens = in_order(pair_tokens)
    grad_output = in_order(ordered(cotangent, swap(cotangent), 1))

    start = lax.axis_index(("outer", "inner")) * length
    positions = (start - HALF + jnp.arange(window, dtype=jnp.int32)).astype(F32)
    frequency = ROPE_BASE ** (-(jnp.arange(HD // 2, dtype=F32) * 2.0 / HD))
    angles = positions[:, None] * frequency[None, :]
    cosine, sine = jnp.cos(angles), jnp.sin(angles)
    cosine = jnp.tile(cosine, (1, LANES // (HD // 2)))
    sine = jnp.tile(jnp.concatenate([-sine, sine], 1), (1, LANES // HD))
    ids_padded = jnp.pad(doc_ids, ((0, 0), (HALF, HALF)), constant_values=-1)
    key_ids = lax.dynamic_slice_in_dim(ids_padded, start, window, 1)[:, None, :]
    query_ids = lax.dynamic_slice_in_dim(doc_ids, start, length, 1)[:, :, None]

    prepared = (own_tokens, grad_output, order, own_order, other_order)
    prepared += (cosine, sine, key_ids, query_ids)
    prepared, pair_two, late, one = tied(prepared, pair_two, late, one)
    own_tokens, grad_output, order, own_order, other_order = prepared[:5]
    cosine, sine, key_ids, query_ids = prepared[5:]
    two = direct_sends(pair_two)
    near = gather_near(one)
    low, high = (in_order(end).reshape(end.shape) for end in (low, high))
    late = late_block(late, shard_rows)
    low, high, two, near, late = tied(low, high, two, near, late)

    far = gather_far(*near)
    two_own = joined_rows(two)
    three = direct_sends(late)
    near, far, two_own, three[1] = tied(near, far, two_own, three[1])

    two_near = gather_near([two_own])
    first = in_pieces(*near, *far)
    joined, window_norm, gain_rows = project(
        low, own_tokens.reshape(streams, length, width), high, first, cosine, sine, side
    )
    out_half = joined_rows([piece[:, 3 * side + LANES :] for piece in first])
    weight = out_weight(first, out_half, swap(out_half), own_order, other_order)
    three[3:], joined, weight, first, two_near = tied(
        three[3:], joined, weight, first, two_near
    )

    two_far = gather_far(*two_near)
    joined = joined.reshape(streams, window, 3 * side)
    attended = attend(block, joined, query_ids, key_ids).reshape(rows, side)
    attended_low, hidden, normed_mlp_low = out_project(
        attended, swap(attended), own_order, other_order, weight, own_tokens, gain_rows
    )
    hidden, normed_mlp_low, two_near, two_far = tied(
        hidden, normed_mlp_low, two_near, two_far
    )
    in_half = in_pieces(*two_near, *two_far)
    mixed_low, factor, active = feed(normed_mlp_low, in_half, padded)

    down_cuts = split_late(grad_output, mixed_low, shard_rows)
    down_cuts, factor, active, three = tied(down_cuts, factor, active, three)
    down_half = [join_late(three, shard_rows)]
    grad_gate, grad_up = feed_back(grad_output, factor, active, down_half)
    sum_in = GradSum([normed_mlp_low] * 2, [grad_gate, grad_up], shard_rows)
    sent_in = sum_in.far()
    grad_gate, grad_up, sent_in, mixed_low = tied(grad_gate, grad_up, sent_in, mixed_low)

    in_far = sum_in.send_far(sent_in)
    down_arrived = [
        lax.ppermute(cut, "outer", forward("outer", outer - 1)) for cut in down_cuts[1:2]
    ]
    part, part_low = back_project([grad_gate, grad_up], in_half, [F32, BF16])
    part, part_low, in_far, down_arrived[0], down_cuts = tied(
        part, part_low, in_far, down_arrived[0], down_cuts
    )

    in_near = sum_in.send_near(sum_in.near(in_far))
    down_arrived[1:] = [
        lax.ppermute(down_cuts[distance], "outer", forward("outer", outer - distance))
        for distance in range(2, outer)
    ]
    grad_hidden, hidden_side, grad_attended = hidden_back(
        part, swap(part_low), hidden, grad_output, gain_rows, weight, own_order
    )
    grad_query, mid, to_lower, to_upper = attend_back(
        block, joined, query_ids, key_ids, grad_attended.reshape(streams, length, side),
        cosine, sine,
    )
    from_lower = lax.ppermute(to_upper, ("outer", "inner"), onward)
    from_upper = lax.ppermute(to_lower, ("outer", "inner"), back)
    from_lower, from_upper, in_near, down_arrived[:2] = tied(
        from_lower, from_upper, in_near, down_arrived[:2]
    )

    grad_joined = join_grads(grad_query, mid, from_lower, from_upper, cosine, sine)
    grad_joined = grad_joined.reshape(rows, 3 * side)
    normed_low = window_norm.reshape(streams, window, width)[:, HALF : HALF + length]
    sum_attn = GradSum(
        [normed_low.reshape(rows, width), attended_low], [grad_joined, hidden_side], shard_rows
    )
    sent_attn, in_own = sum_attn.far(), sum_in.own(in_near)
    sent_attn, in_own, grad_joined = tied(sent_attn, in_own, grad_joined)

    attn_far = sum_attn.send_far(sent_attn)
    in_arrived = sum_in.send_direct(in_own, 1)
    out_mine, out_other = back_split(cores, mixed_low, down_half, streams)
    in_mine, in_other = back_split(cores, grad_joined, first, streams)
    attn_far, in_arrived, in_own, down_arrived, out_mine, out_other, in_mine, in_other = tied(
        attn_far, in_arrived, in_own, down_arrived, out_mine, out_other, in_mine, in_other
    )

    attn_near = sum_attn.send_near(sum_attn.near(attn_far))
    in_arrived = in_arrived + sum_in.send_direct(in_own, *range(2, outer))
    down_rows = late_rows([down_cuts[0], *down_arrived], shard_rows)
    attn_near, in_arrived, out_other, in_other, down_rows = tied(
        attn_near, in_arrived, out_other, in_other, down_rows
    )

    attn_own = sum_attn.own(attn_near)
    attn_arrived = sum_attn.send_direct(attn_own, *range(1, outer))
    output = end_rows(
        output_kernel, cores, [out_mine, swap(out_other)], [hidden], [order], BF16, streams
    ).reshape(tokens.shape)
    grad_tokens = end_rows(
        input_grad_kernel, cores, [in_mine, swap(in_other)], [grad_hidden, own_tokens],
        [gain_rows, order], F32, streams,
    ).reshape(tokens.shape)
    total_mine, total_other = sum_in.total(cores, in_own, in_arrived)
    grad_in, gain_grad_mlp = assemble(
        cores, total_mine, swap(total_other), [(0, 2, padded, units)], w_in, norm_mlp
    )
    down_sums = late_sends(down_rows)
    attn_arrived, output, grad_tokens, grad_in, gain_grad_mlp, down_sums = tied(
        attn_arrived, output, grad_tokens, grad_in, gain_grad_mlp, down_sums
    )
    down_mine, down_other = sum_in.total(cores, down_rows[0, 0], down_sums)
    total_mine, total_other = sum_attn.total(cores, attn_own, attn_arrived)
    grad_qkv, grad_out, gain_grad_attn = assemble(
        cores, total_mine, swap(total_other),
        [(0, 3, side, side), (3 * side, 1, side, side)], w_qkv, norm_attn,
    )
    (grad_down,) = assemble(cores, down_mine, swap(down_other), [(0, 1, padded, units)])
    return (
        output,
        grad_tokens,
        gain_grad_attn.reshape(-1),
        gain_grad_mlp.reshape(-1),
        grad_qkv,
        grad_out,
        grad_in,
        grad_down,
    )


def solution(mesh):
    dp, seq = mesh.shape["dp"], mesh.shape["seq"]
    chips = seq // 2
    outer = 4 if chips % 4 == 0 else 1
    fine = Mesh(
        mesh.devices.reshape(dp, outer, chips // outer, 2), ("dp", "outer", "inner", "core")
    )
    line = ("outer", "inner", "core")
    every = ("dp",) + line
    token = P("dp", line, None)
    vector = P(every)
    matrix = P(every, None)
    return jax.shard_map(
        shards,
        mesh=fine,
        in_specs=(token, P("dp", None), vector, vector, matrix, matrix, matrix, matrix, token),
        out_specs=(token, token, vector, vector, matrix, matrix, matrix, matrix),
        check_vma=False,
    )
```

```python
import functools

import jax
import jax.numpy as jnp
import numpy as np
from jax import lax
from jax.experimental import pallas as pl
from jax.experimental.pallas import tpu as pltpu
from jax.sharding import Mesh, PartitionSpec as P

HD = 64
HALF = 64
LANES = 128
NORM_EPSILON = 1e-05
ROPE_BASE = 10000.0
F32 = jnp.float32
BF16 = jnp.bfloat16


def contract_cols(left, right):
    return lax.dot_general(left, right, (((1,), (1,)), ((), ())), preferred_element_type=F32)


def contract_rows(left, right):
    return lax.dot_general(left, right, (((0,), (0,)), ((), ())), preferred_element_type=F32)


def matmul(left, right):
    return jnp.dot(left, right, preferred_element_type=F32)


def tied(*values):
    return lax.optimization_barrier(values)


def call(kernel, grid, ins, outs, scratch=(), limit=40):
    out = pl.pallas_call(
        kernel,
        grid=grid,
        in_specs=[
            pl.BlockSpec(memory_space=pltpu.SMEM) if block is None else pl.BlockSpec(block, index)
            for _, block, index in ins
        ],
        out_specs=[pl.BlockSpec(block, index) for _, _, block, index in outs],
        out_shape=[jax.ShapeDtypeStruct(shape, kind) for shape, kind, _, _ in outs],
        scratch_shapes=list(scratch),
        compiler_params=pltpu.CompilerParams(vmem_limit_bytes=limit * 2**20),
        cost_estimate=pl.CostEstimate(flops=1024, bytes_accessed=1024, transcendentals=0),
    )(*[array for array, _, _ in ins])
    return out


def whole(array):
    return (array, array.shape, lambda *_: (0,) * array.ndim)


def swap(value):
    return lax.ppermute(value, "core", [(0, 1), (1, 0)])


def ordered(mine, other, axis):
    first = lax.axis_index("core") == 0
    return jnp.concatenate(
        [jnp.where(first, mine, other), jnp.where(first, other, mine)], axis=axis
    )


def forward(axis, distance=1):
    count = lax.axis_size(axis)
    return [(i, (i + distance) % count) for i in range(count)]


def ring_gather(axis, piece):
    pieces = [piece]
    for _ in range(1, lax.axis_size(axis)):
        pieces.append(lax.ppermute(pieces[-1], axis, forward(axis)))
    return pieces[1:]


def direct_send(rows, *distances):
    count = lax.axis_size("outer")
    return [
        lax.ppermute(rows, "outer", forward("outer", distance))
        for distance in distances
        if distance < count
    ]


def direct_sends(rows):
    return [rows] + direct_send(rows, *range(1, lax.axis_size("outer")))


def joined_rows(pieces):
    return jnp.concatenate(pieces, 0) if len(pieces) > 1 else pieces[0]


def gather_near(arrived):
    own = joined_rows(arrived)
    return own, ring_gather("inner", own), ring_gather("dp", own)


def copy_kernel(*refs):
    count = len(refs) // 2
    for source, target in zip(refs[:count], refs[count:]):
        target[...] = source[...]


def far_halves(along_x, along_y, half):
    if len(along_x) > 1 or len(along_y) > 1 or half % 32:
        return (
            joined_rows([piece[:half] for piece in along_y]),
            joined_rows([piece[half:] for piece in along_x]),
        )
    columns = along_x[0].shape[1]
    return call(
        copy_kernel,
        (1,),
        [(along_y[0], (half, columns), lambda i: (0, 0))]
        + [(along_x[0], (half, columns), lambda i: (1, 0))],
        [((half, columns), BF16, (half, columns), lambda i: (0, 0)) for _ in range(2)],
    )


def gather_far(own, along_x, along_y):
    one, two = far_halves(along_x, along_y, own.shape[0] // 2)
    return ring_gather("inner", one), ring_gather("dp", two)


def in_pieces(own, along_x, along_y, one, two):
    pieces = [own, *along_x, *along_y, *one, *two]
    if any(piece.shape[0] % LANES for piece in pieces):
        pieces = [joined_rows(pieces)]
    return pieces


def order_blocks(inner, dp):
    blocks = [(0, 0, 0, 2)]
    blocks += [(d, 0, 0, 2) for d in range(1, inner)] + [(0, d, 0, 2) for d in range(1, dp)]
    blocks += [(d, e, 0, 1) for d in range(1, inner) for e in range(1, dp)]
    return blocks + [(d, e, 1, 2) for e in range(1, dp) for d in range(1, inner)]


def late_segments(shard_rows):
    inner, outer, dp = (lax.axis_size(name) for name in ("inner", "outer", "dp"))
    start, at = 0, {}
    for d, e, low, high in order_blocks(inner, dp):
        for part in range(low, high):
            at[d, e, part] = start
            start += shard_rows
    segments = []
    for d, e, low, high in order_blocks(inner, dp):
        for distance in range(low * outer // 2, high * outer // 2):
            first, second = at[d, e, 0], at[d, e, 1]
            if second == first + shard_rows:
                segments.append((distance, first, 2 * shard_rows))
            else:
                segments += [(distance, first, shard_rows), (distance, second, shard_rows)]
    return segments


def join_kernel_rows(segments, *refs):
    pieces, out_ref = refs[:-1], refs[-1]
    at = 0
    for distance, start, count in segments:
        out_ref[at : at + count, :] = pieces[distance][start : start + count, :]
        at += count


def join_late(pieces, shard_rows):
    segments = late_segments(shard_rows)
    columns = pieces[0].shape[1]
    rows = sum(count for _, _, count in segments)
    if shard_rows % 32:
        return jnp.concatenate([pieces[d][at : at + n] for d, at, n in segments], 0)
    return call(
        functools.partial(join_kernel_rows, segments),
        (1,),
        [whole(piece) for piece in pieces],
        [((rows, columns), BF16, (rows, columns), lambda i: (0, 0))],
    )[0]


def split_kernel_rows(segments, left_ref, right_ref, *outs):
    place, at = [], 0
    for distance, start, count in segments:
        place.append((at, distance, start, count))
        at += count
    for top in range(0, at, LANES):
        rows = contract_rows(left_ref[:, top : top + LANES], right_ref[...]).astype(BF16)
        for begin, distance, start, count in place:
            if top <= begin < top + LANES:
                outs[distance][start : start + count, :] = rows[begin - top : begin - top + count]


def split_late(left, right, shard_rows):
    segments = late_segments(shard_rows)
    outer = lax.axis_size("outer")
    rows, columns = left.shape[1] // outer, right.shape[1]
    if shard_rows % 32:
        total, at, cuts = contract_rows(left, right).astype(BF16), 0, {}
        for distance, start, count in segments:
            cuts[distance, start] = total[at : at + count]
            at += count
        return [
            jnp.concatenate([cuts[key] for key in sorted(cuts) if key[0] == distance], 0)
            for distance in range(outer)
        ]
    return call(
        functools.partial(split_kernel_rows, segments),
        (1,),
        [whole(left), whole(right)],
        [((rows, columns), BF16, (rows, columns), lambda i: (0, 0)) for _ in range(outer)],
    )


def arrival_order(x, z, y, width, shard_rows):
    inner, outer, dp = (lax.axis_size(name) for name in ("inner", "outer", "dp"))
    half = outer * shard_rows
    blocks = order_blocks(inner, dp)
    place = np.concatenate([np.arange(low * half, high * half) for _, _, low, high in blocks])
    sizes = [(high - low) * half for _, _, low, high in blocks]
    along_x = np.repeat([block[0] for block in blocks], sizes)
    along_y = np.repeat([block[1] for block in blocks], sizes)
    along_z, row = place // (2 * shard_rows), place % (2 * shard_rows)
    at_x = (x - jnp.asarray(along_x, jnp.int32) + inner) % inner
    at_y = (y - jnp.asarray(along_y, jnp.int32) + dp) % dp
    at_z = (z - jnp.asarray(along_z, jnp.int32) + outer) % outer
    source = ((at_y * outer + at_z) * inner + at_x) * 2 * shard_rows + row
    return (jnp.arange(width, dtype=jnp.int32)[:, None] == source[None, :]).astype(BF16)


def rows_kernel(pairs, layout, *refs):
    rights, refs = refs[:pairs], refs[pairs:]
    inputs, outs = refs[: -len(layout)], refs[-len(layout) :]
    for places, out_ref in zip(layout, outs):
        lefts, adds = inputs[:pairs], inputs[pairs : pairs + len(places)]
        inputs = inputs[pairs + len(places) :]
        start = 0
        for left, right in zip(lefts, rights):
            columns = slice(start, start + right.shape[1])
            start = columns.stop
            total = contract_rows(left[...], right[...])
            for add in adds:
                if add.shape[0] == total.shape[0]:
                    total = total + add[:, columns].astype(F32)
            out_ref[:, columns] = total.astype(BF16)
            for add, at in zip(adds, places):
                if add.shape[0] != total.shape[0]:
                    span = slice(at, at + add.shape[0])
                    part = total[span] + add[:, columns].astype(F32)
                    out_ref[span, columns] = part.astype(BF16)


class GradSum:
    def __init__(self, lefts, rights, shard_rows):
        self.lefts, self.rights = lefts, rights
        self.inner, self.outer, self.dp = (
            lax.axis_size(name) for name in ("inner", "outer", "dp")
        )
        self.shard = 2 * shard_rows
        self.half = self.outer * shard_rows
        self.at_x = 2 * self.half
        self.at_y = self.at_x + (self.inner - 1) * 2 * self.half
        self.at_one = self.at_y + (self.dp - 1) * 2 * self.half
        self.at_two = self.at_one + (self.inner - 1) * (self.dp - 1) * self.half

    def rows(self, *parts):
        depth = self.lefts[0].shape[0]
        columns = sum(right.shape[1] for right in self.rights)
        ins, outs, layout = [whole(right) for right in self.rights], [], []
        for start, count, adds in parts:
            adds = [(rows, place) for rows, place in adds if rows is not None]
            lefts, index = self.lefts, start // count
            if count % LANES or start % count:
                lefts, index = [left[:, start : start + count] for left in lefts], 0
            ins += [
                (left, (depth, count), lambda i, index=index: (0, index)) for left in lefts
            ]
            ins += [whole(rows) for rows, _ in adds]
            outs.append(((count, columns), BF16, (count, columns), lambda i: (0, 0)))
            layout.append([place for _, place in adds])
        return call(
            functools.partial(rows_kernel, len(self.rights), layout), (1,), ins, outs
        )

    def ring(self, axis, part, first):
        arrived = None
        for step in range(1, lax.axis_size(axis)):
            sent = first if step == 1 else self.rows(part(step, arrived))[0]
            arrived = lax.ppermute(sent, axis, forward(axis))
        return arrived

    def one(self, distance, arrived):
        count = (self.dp - 1) * self.half
        return (self.at_one + (distance - 1) * count, count, [(arrived, 0)])

    def two(self, distance, arrived):
        count = (self.inner - 1) * self.half
        return (self.at_two + (distance - 1) * count, count, [(arrived, 0)])

    def far(self):
        return self.rows(self.one(1, None), self.two(1, None))

    def send_far(self, firsts):
        return (
            self.ring("inner", self.one, firsts[0]), self.ring("dp", self.two, firsts[1])
        )

    def along(self, start, distance, arrived, extra, place):
        count = 2 * self.half
        extra = extra[(distance - 1) * self.half : distance * self.half]
        return (start + (distance - 1) * count, count, [(arrived, 0), (extra, place)])

    def along_x(self, distance, arrived):
        return self.along(self.at_x, distance, arrived, self.sums[1], self.half)

    def along_y(self, distance, arrived):
        return self.along(self.at_y, distance, arrived, self.sums[0], 0)

    def near(self, sums):
        self.sums = sums
        return self.rows(self.along_x(1, None), self.along_y(1, None))

    def send_near(self, firsts):
        return (
            self.ring("inner", self.along_x, firsts[0]),
            self.ring("dp", self.along_y, firsts[1]),
        )

    def own(self, nears):
        return self.rows((0, 2 * self.half, [(near, 0) for near in nears]))[0]

    def cut(self, own, distance):
        return own[distance * self.shard : (distance + 1) * self.shard]

    def send_direct(self, own, *distances):
        return [
            lax.ppermute(
                self.cut(own, distance), "outer", forward("outer", self.outer - distance)
            )
            for distance in distances
            if distance < self.outer
        ]

    def total(self, core, own, arrived):
        columns = own.shape[1]
        half = self.shard // 2
        return call(
            total_kernel,
            (1,),
            [(core, None, None), (own, (self.shard, columns), lambda i: (0, 0))]
            + [whole(rows) for rows in arrived],
            [((half, columns), F32, (half, columns), lambda i: (0, 0)) for _ in range(2)],
        )


def late_kernel(count, layout, *refs):
    blocks, outs = refs[:count], refs[count:]
    for spans, out_ref in zip(layout, outs):
        at = 0
        for start, rows in spans:
            total = None
            for block in blocks:
                part = block[start : start + rows, :].astype(F32)
                total = part if total is None else total + part
            out_ref[at : at + rows, :] = total.astype(BF16)
            at += rows


def late_rows(blocks, shard_rows):
    inner, dp = lax.axis_size("inner"), lax.axis_size("dp")
    start, spans = 0, {}
    for d, e, low, high in order_blocks(inner, dp):
        rows = (high - low) * shard_rows
        spans.setdefault((d, e), []).append((start, rows))
        start += rows
    columns = blocks[0].shape[1]
    if shard_rows % 32:
        total = sum(block.astype(F32) for block in blocks).astype(BF16)
        return {
            key: joined_rows([total[at : at + rows] for at, rows in cuts])
            for key, cuts in spans.items()
        }
    shape = (2 * shard_rows, columns)
    cuts = call(
        functools.partial(late_kernel, len(blocks), list(spans.values())),
        (1,),
        [whole(block) for block in blocks],
        [(shape, BF16, shape, lambda i: (0, 0)) for _ in spans],
    )
    return dict(zip(spans, cuts))


def late_sends(cuts):
    inner, dp = lax.axis_size("inner"), lax.axis_size("dp")
    return [
        lax.ppermute(
            rows,
            ("dp", "inner"),
            [
                (y * inner + x, (y - e) % dp * inner + (x - d) % inner)
                for y in range(dp)
                for x in range(inner)
            ],
        )
        for (d, e), rows in cuts.items()
        if d or e
    ]


def own_half(core_ref, value):
    half = value.shape[0] // 2
    return jnp.where(core_ref[0] == 0, value[:half], value[half:])


def total_kernel(core_ref, *refs):
    total = None
    for ref in refs[:-2]:
        rows = ref[...].astype(F32)
        total = rows if total is None else total + rows
    half = total.shape[0] // 2
    first = core_ref[0] == 0
    refs[-2][...] = jnp.where(first, total[:half], total[half:])
    refs[-1][...] = jnp.where(first, total[half:], total[:half])


def assemble_kernel(layout, core_ref, mine_ref, other_ref, *refs):
    first = core_ref[0] == 0
    count = len(layout)
    pair = (
        jnp.where(first, mine_ref[...], other_ref[...]),
        jnp.where(first, other_ref[...], mine_ref[...]),
    )
    outs = refs[-count:] if len(refs) == count else refs[2:-1]
    for out_ref, (start, parts, stride, size) in zip(outs, layout):
        cuts = []
        for i in range(parts):
            at = start + i * stride
            cuts += [half[:, at : at + size] for half in pair]
        out_ref[...] = jnp.concatenate(cuts, 1)
    if len(refs) > count:
        weight_ref, gain_ref = refs[:2]
        product = weight_ref[...].astype(F32) * outs[0][...]
        refs[-1][...] = jnp.sum(product, -1, keepdims=True) / gain_ref[...].astype(F32)


def assemble(core, mine, other, layout, weight=None, gain=None):
    rows = mine.shape[0]
    ins = [(core, None, None), whole(mine), whole(other)]
    sizes = [2 * parts * size for _, parts, _, size in layout]
    if weight is not None:
        ins += [whole(weight), whole(gain.reshape(rows, 1))]
        sizes.append(1)
    return call(
        functools.partial(assemble_kernel, layout),
        (1,),
        ins,
        [((rows, size), F32, (rows, size), lambda i: (0, 0)) for size in sizes],
    )


def pack_kernel(side, core_ref, qkv_ref, gain_ref, out_ref, mine_ref, other_ref):
    def fill(target, half):
        for part in range(3):
            start = (2 * part + half) * side
            target[:, part * side : (part + 1) * side] = qkv_ref[:, start : start + side]
        target[:, 3 * side : 3 * side + LANES] = gain_ref[...]
        target[:, 3 * side + LANES :] = out_ref[:, half * side : (half + 1) * side]

    for half in range(2):

        @pl.when(core_ref[0] == half)
        def _():
            fill(mine_ref, half)
            fill(other_ref, 1 - half)


def pack_first(core, w_qkv, gains, w_out):
    rows, side = w_out.shape[0], w_out.shape[1] // 2
    columns = 4 * side + LANES
    return call(
        functools.partial(pack_kernel, side),
        (1,),
        [(core, None, None), whole(w_qkv), whole(gains), whole(w_out)],
        [((rows, columns), BF16, (rows, columns), lambda i: (0, 0)) for _ in range(2)],
    )


def normalise(values):
    centred = values - jnp.mean(values, -1, keepdims=True)
    scale = lax.rsqrt(jnp.mean(centred * centred, -1, keepdims=True) + NORM_EPSILON)
    return centred * scale, scale


def norm_back(unit, scale, gain, incoming):
    grad = incoming * gain
    return scale * (
        grad
        - jnp.mean(grad, -1, keepdims=True)
        - unit * jnp.mean(grad * unit, -1, keepdims=True)
    )


def piece_matmul(left, pieces):
    total, start = None, 0
    for piece in pieces:
        part = matmul(left[:, start : start + piece.shape[0]], piece[...])
        total = part if total is None else total + part
        start += piece.shape[0]
    return total


def back_kernel(starts, count, *refs):
    grads, pieces, out_refs = refs[: len(starts)], refs[len(starts) : count], refs[count:]
    at = 0
    for piece in pieces:
        total = None
        for grad, start in zip(grads, starts):
            part = contract_cols(grad[...], piece[:, start : start + grad.shape[1]])
            total = part if total is None else total + part
        for out_ref in out_refs:
            out_ref[:, at : at + piece.shape[0]] = total.astype(out_ref.dtype)
        at += piece.shape[0]


def back_project(grads, pieces, kinds):
    rows = grads[0].shape[0]
    block = rows // 2
    starts, end = [], 0
    for grad in grads:
        starts.append(end)
        end += grad.shape[1]
    width = sum(piece.shape[0] for piece in pieces)
    return call(
        functools.partial(back_kernel, starts, len(grads) + len(pieces)),
        (2,),
        [(grad, (block, grad.shape[1]), lambda i: (i, 0)) for grad in grads]
        + [(piece, (piece.shape[0], end), lambda i: (0, 0)) for piece in pieces],
        [((rows, width), kind, (block, width), lambda i: (i, 0)) for kind in kinds],
    )


def split_kernel(core_ref, grad_ref, *refs):
    pieces, (mine_ref, other_ref) = refs[:-2], refs[-2:]
    width = grad_ref.shape[1]
    half = grad_ref.shape[0] // 2
    at = 0
    for piece in pieces:
        total = contract_cols(grad_ref[...], piece[:, :width])
        first = core_ref[0] == 0
        span = slice(at, at + piece.shape[0])
        mine_ref[:, span] = jnp.where(first, total[:half], total[half:])
        other_ref[:, span] = jnp.where(first, total[half:], total[:half]).astype(BF16)
        at = span.stop


def back_split(core, grad, pieces, streams):
    rows, columns = grad.shape
    block = rows // streams
    width = sum(piece.shape[0] for piece in pieces)
    return call(
        split_kernel,
        (streams,),
        [(core, None, None), (grad, (block, columns), lambda i: (i, 0))]
        + [(piece, (piece.shape[0], columns), lambda i: (0, 0)) for piece in pieces],
        [
            ((rows // 2, width), kind, (block // 2, width), lambda i: (i, 0))
            for kind in (F32, BF16)
        ],
    )


def output_kernel(core_ref, mine_ref, other_ref, hidden_ref, order_ref, out_ref):
    total = own_half(core_ref, hidden_ref[...]) + mine_ref[...] + other_ref[...].astype(F32)
    out_ref[...] = contract_cols(total.astype(BF16), order_ref[...]).astype(BF16)


def input_grad_kernel(
    core_ref, mine_ref, other_ref, hidden_ref, x_ref, gain_ref, order_ref, out_ref
):
    unit, scale = normalise(own_half(core_ref, x_ref[...].astype(F32)))
    incoming = mine_ref[...] + other_ref[...].astype(F32)
    total = own_half(core_ref, hidden_ref[...])
    total = total + norm_back(unit, scale, gain_ref[0:1, :], incoming)
    result = None
    for _ in range(3):
        part = total.astype(BF16)
        total = total - part.astype(F32)
        part = contract_cols(part, order_ref[...])
        result = part if result is None else result + part
    out_ref[...] = result


def end_rows(kernel, core, halves, fulls, wholes, kind, streams):
    rows, width = halves[0].shape
    block = rows // streams
    return call(
        kernel,
        (streams,),
        [(core, None, None)]
        + [(array, (block, width), lambda i: (i, 0)) for array in halves]
        + [(array, (2 * block, width), lambda i: (i, 0)) for array in fulls]
        + [whole(array) for array in wholes],
        [((rows, width), kind, (block, width), lambda i: (i, 0))],
    )[0]


def turned(values):
    width = values.shape[-1]
    lane = lax.broadcasted_iota(jnp.int32, values.shape, values.ndim - 1)
    ahead = pltpu.roll(values, width - HD // 2, values.ndim - 1)
    behind = pltpu.roll(values, HD // 2, values.ndim - 1)
    return jnp.where(lane % HD < HD // 2, ahead, behind)


def project_kernel(count, low_ref, x_ref, high_ref, cos_ref, sin_ref, *refs):
    gains, weights = refs[:count], refs[count : 2 * count]
    out_ref, norm_ref, gain_ref = refs[2 * count :]

    @pl.when(pl.program_id(0) == 0)
    def _():
        pick = lax.broadcasted_iota(jnp.int32, (8, LANES), 0) == lax.broadcasted_iota(
            jnp.int32, (8, LANES), 1
        )
        pick = pick.astype(F32).astype(BF16)
        start = 0
        for piece in gains:
            gain_ref[:, start : start + piece.shape[0]] = contract_cols(pick, piece[...])
            start += piece.shape[0]
        for stream in range(x_ref.shape[0]):
            at = stream * cos_ref.shape[0]
            for ref in (low_ref, x_ref, high_ref):
                unit, _ = normalise(ref[stream].astype(F32))
                span = slice(at, at + ref.shape[1])
                norm_ref[span, :] = (unit * gain_ref[0:1, :]).astype(BF16)
                at = span.stop

    values = piece_matmul(norm_ref, weights)
    keep = pl.program_id(0) == 2
    length = cos_ref.shape[0]
    for top in range(0, values.shape[0], length):
        for left in range(0, values.shape[1], LANES):
            part = values[top : top + length, left : left + LANES]
            rotated = part * cos_ref[...] + turned(part) * sin_ref[...]
            out_ref[top : top + length, left : left + LANES] = jnp.where(
                keep, part, rotated
            ).astype(BF16)


def project(low, tokens, high, pieces, cosine, sine, side):
    width = tokens.shape[2]
    rows = tokens.shape[0] * cosine.shape[0]
    gain_block = 3 * side // LANES
    return call(
        functools.partial(project_kernel, len(pieces)),
        (3,),
        [whole(low), whole(tokens), whole(high), whole(cosine), whole(sine)]
        + [(piece, (piece.shape[0], LANES), lambda j: (0, gain_block)) for piece in pieces]
        + [(piece, (piece.shape[0], side), lambda j: (0, j)) for piece in pieces],
        [
            ((rows, 3 * side), BF16, (rows, side), lambda j: (0, j)),
            ((rows, width), BF16, (rows, width), lambda j: (0, 0)),
            ((8, width), F32, (8, width), lambda j: (0, 0)),
        ],
    )


def head_masks():
    lane = lax.broadcasted_iota(jnp.int32, (1, LANES), 1)
    return [(lane // HD == head).astype(F32).astype(BF16) for head in range(LANES // HD)]


def block_mask(query_ids, key_ids):
    rows, width = query_ids.shape[0], key_ids.shape[1]
    offset = lax.broadcasted_iota(jnp.int32, (rows, width), 1) - lax.broadcasted_iota(
        jnp.int32, (rows, width), 0
    )
    return (offset >= 0) & (offset <= 2 * HALF) & (query_ids == key_ids)


def block_probs(query, keys, allowed):
    scores = jnp.where(allowed, contract_cols(query, keys) * HD**-0.5, -1e30)
    grown = jnp.exp(scores - jnp.max(scores, -1, keepdims=True))
    return grown / jnp.sum(grown, -1, keepdims=True)


def attend_kernel(block, q_ref, k_ref, v_ref, qid_ref, kid_ref, out_ref):
    masks = head_masks()
    for start in range(0, out_ref.shape[1], block):
        span = slice(start, start + block + 2 * HALF)
        allowed = block_mask(qid_ref[0, start : start + block], kid_ref[0, :, span])
        query = q_ref[0, HALF + start : HALF + start + block]
        total = None
        for mask in masks:
            probs = block_probs(query * mask, k_ref[0, span], allowed)
            part = matmul(probs.astype(BF16), v_ref[0, span]) * mask.astype(F32)
            total = part if total is None else total + part
        out_ref[0, start : start + block] = total.astype(BF16)


def attend_back_kernel(
    block, q_ref, k_ref, v_ref, qid_ref, kid_ref, grad_ref, cos_ref, sin_ref,
    dq_ref, mid_ref, low_ref, high_ref,
):
    masks = head_masks()
    length = dq_ref.shape[1]
    grad_keys = grad_values = jnp.zeros((length + 2 * HALF, LANES), F32)
    for start in range(0, length, block):
        span = slice(start, start + block + 2 * HALF)
        mid = slice(HALF + start, HALF + start + block)
        rows = slice(start, start + block)
        allowed = block_mask(qid_ref[0, rows], kid_ref[0, :, span])
        query_all, grad_all = q_ref[0, mid], grad_ref[0, rows]
        keys, values = k_ref[0, span], v_ref[0, span]
        grad_query, part_keys, part_values = 0.0, 0.0, 0.0
        for mask in masks:
            query, grad = query_all * mask, grad_all * mask
            probs = block_probs(query, keys, allowed)
            grad_probs = contract_cols(grad, values)
            delta = jnp.sum(probs * grad_probs, -1, keepdims=True)
            grad_scores = (probs * (grad_probs - delta)).astype(BF16)
            grad_query += matmul(grad_scores, keys) * mask.astype(F32)
            part_keys += contract_rows(grad_scores, query)
            part_values += contract_rows(probs.astype(BF16), grad)
        grad_query = grad_query * HD**-0.5
        dq_ref[0, rows] = (
            grad_query * cos_ref[mid] - turned(grad_query) * sin_ref[mid]
        ).astype(BF16)
        before, after = start, length - start - block

        def placed(part):
            pieces = [part]
            if before:
                pieces.insert(0, jnp.zeros((before, LANES), F32))
            if after:
                pieces.append(jnp.zeros((after, LANES), F32))
            return jnp.concatenate(pieces, 0)

        grad_keys += placed(part_keys)
        grad_values += placed(part_values)
    for index, total in enumerate((grad_keys * HD**-0.5, grad_values)):
        low_ref[0, index] = total[:HALF].astype(BF16)
        mid_ref[0, index] = total[HALF : HALF + length]
        high_ref[0, index] = total[HALF + length :].astype(BF16)


def attention_inputs(joined, query_ids, key_ids):
    window, groups = joined.shape[1], joined.shape[2] // 3 // LANES
    inputs = [
        (joined, (1, window, LANES), lambda s, h, shift=shift: (s, 0, h + shift))
        for shift in (0, groups, 2 * groups)
    ]
    inputs += [
        (ids, (1,) + ids.shape[1:], lambda s, h: (s, 0, 0)) for ids in (query_ids, key_ids)
    ]
    return inputs


def attend(block, joined, query_ids, key_ids):
    streams, window, columns = joined.shape
    length, side = window - 2 * HALF, columns // 3
    return call(
        functools.partial(attend_kernel, block),
        (streams, side // LANES),
        attention_inputs(joined, query_ids, key_ids),
        [((streams, length, side), BF16, (1, length, LANES), lambda s, h: (s, 0, h))],
        limit=24,
    )[0]


def attend_back(block, joined, query_ids, key_ids, grad, cosine, sine):
    streams, length, side = grad.shape

    def pair(rows, kind):
        return (
            (streams, 2, rows, side), kind, (1, 2, rows, LANES), lambda s, h: (s, 0, 0, h)
        )

    return call(
        functools.partial(attend_back_kernel, block),
        (streams, side // LANES),
        attention_inputs(joined, query_ids, key_ids)
        + [(grad, (1, length, LANES), lambda s, h: (s, 0, h)), whole(cosine), whole(sine)],
        [
            ((streams, length, side), BF16, (1, length, LANES), lambda s, h: (s, 0, h)),
            pair(length, F32),
            pair(HALF, BF16),
            pair(HALF, BF16),
        ],
        limit=24,
    )


def join_kernel(dq_ref, mid_ref, low_ref, high_ref, cos_ref, sin_ref, out_ref):
    length, width = dq_ref.shape[1:]
    out_ref[0, :, :width] = dq_ref[0]
    cosine, sine = cos_ref[HALF : HALF + length], sin_ref[HALF : HALF + length]
    for index in range(2):
        for start in range(0, width, LANES):
            lanes = slice(start, start + LANES)
            total = mid_ref[0, index, :, lanes]
            total = total + jnp.concatenate(
                [
                    low_ref[0, index, :, lanes].astype(F32),
                    jnp.zeros((length - 2 * HALF, LANES), F32),
                    high_ref[0, index, :, lanes].astype(F32),
                ],
                0,
            )
            if index == 0:
                total = total * cosine - turned(total) * sine
            to = (1 + index) * width + start
            out_ref[0, :, to : to + LANES] = total.astype(BF16)


def join_grads(grad_query, mid, from_lower, from_upper, cosine, sine):
    streams, length, width = grad_query.shape

    def of_stream(array):
        block = (1,) + array.shape[1:]
        return (array, block, lambda s: (s,) + (0,) * (array.ndim - 1))

    return call(
        join_kernel,
        (streams,),
        [of_stream(array) for array in (grad_query, mid, from_lower, from_upper)]
        + [whole(cosine), whole(sine)],
        [((streams, length, 3 * width), BF16, (1, length, 3 * width), lambda s: (s, 0, 0))],
        limit=24,
    )[0]


def by_rows(array, block):
    return (array, (block, array.shape[1]), lambda i: (i, 0))


def weight_kernel(count, other_ref, own_order_ref, other_order_ref, *refs):
    start = 0
    out_ref = refs[count]
    for piece in refs[:count]:
        span = slice(start, start + piece.shape[0])
        total = matmul(piece[...], own_order_ref[...])
        total = total + matmul(other_ref[span, :], other_order_ref[...])
        out_ref[span, :] = total.astype(BF16)
        start = span.stop


def out_weight(pieces, own, other, own_order, other_order):
    side, width = own_order.shape
    if len(pieces) == 1:
        own_pieces = [(own, own.shape, lambda i: (0, 0))]
    else:
        own_pieces, start = [], 0
        for piece in pieces:
            count = piece.shape[0]
            own_pieces.append(
                (own, (count, side), lambda i, index=start // count: (index, 0))
            )
            start += count
    return call(
        functools.partial(weight_kernel, len(own_pieces)),
        (1,),
        [whole(other), whole(own_order), whole(other_order)] + own_pieces,
        [((width, width), BF16, (width, width), lambda i: (0, 0))],
    )[0]


def out_kernel(
    own_ref, other_ref, own_order_ref, other_order_ref, weight_ref, x_ref, gain_ref,
    att_ref, hidden_ref, norm_ref,
):
    attended = matmul(own_ref[...], own_order_ref[...])
    attended = (attended + matmul(other_ref[...], other_order_ref[...])).astype(BF16)
    att_ref[...] = attended
    hidden = x_ref[...].astype(F32) + matmul(attended, weight_ref[...])
    hidden_ref[...] = hidden
    norm_ref[...] = (normalise(hidden)[0] * gain_ref[1:2, :]).astype(BF16)


def out_project(own, other, own_order, other_order, weight, tokens, gains):
    rows, width = tokens.shape
    block = rows // 2
    return call(
        out_kernel,
        (2,),
        [by_rows(own, block), by_rows(other, block), whole(own_order), whole(other_order)]
        + [whole(weight), by_rows(tokens, block), whole(gains)],
        [
            ((rows, width), kind, (block, width), lambda i: (i, 0))
            for kind in (BF16, F32, BF16)
        ],
    )


def hidden_back_kernel(
    part_ref, other_ref, hidden_ref, g_ref, gain_ref, weight_ref, order_ref,
    grad_ref, side_ref, att_ref,
):
    unit, scale = normalise(hidden_ref[...])
    incoming = part_ref[...] + other_ref[...].astype(F32)
    grad = g_ref[...].astype(F32) + norm_back(unit, scale, gain_ref[1:2, :], incoming)
    low = grad.astype(BF16)
    grad_ref[...] = grad
    side_ref[...] = contract_cols(low, order_ref[...]).astype(BF16)
    attended = contract_cols(low, weight_ref[...]).astype(BF16)
    att_ref[...] = contract_cols(attended, order_ref[...]).astype(BF16)


def hidden_back(part, other, hidden, grad_output, gains, weight, own_order):
    rows, width = hidden.shape
    block, side = rows // 2, own_order.shape[0]
    return call(
        hidden_back_kernel,
        (2,),
        [by_rows(array, block) for array in (part, other, hidden, grad_output)]
        + [whole(gains), whole(weight), whole(own_order)],
        [
            ((rows, size), kind, (block, size), lambda i: (i, 0))
            for size, kind in ((width, F32), (side, BF16), (side, BF16))
        ],
    )


def column_spans(width):
    return [slice(at, min(at + 2 * LANES, width)) for at in range(0, width, 2 * LANES)]


def tile_matmul(left, pieces, columns):
    total, start = None, 0
    for piece in pieces:
        part = matmul(left[:, start : start + piece.shape[0]], piece[:, columns])
        total = part if total is None else total + part
        start += piece.shape[0]
    return total


def feed_kernel(norm_ref, *refs):
    pieces, (mixed_ref, factor_ref, active_ref) = refs[:-3], refs[-3:]
    units = mixed_ref.shape[1]
    for span in column_spans(units):
        gate = tile_matmul(norm_ref, pieces, span)
        up = tile_matmul(norm_ref, pieces, slice(units + span.start, units + span.stop))
        below = 0.5 * (1.0 + lax.erf(gate * 0.5**0.5))
        active = gate * below
        mixed_ref[:, span] = (active * up).astype(BF16)
        active_ref[:, span] = active
        density = jnp.exp(-0.5 * gate * gate) * (2.0 * np.pi) ** -0.5
        factor_ref[:, span] = up * (below + gate * density)


def feed(normed, pieces, units):
    rows = normed.shape[0]
    block = rows // 2
    return call(
        feed_kernel,
        (2,),
        [by_rows(normed, block)] + [whole(piece) for piece in pieces],
        [
            ((rows, units), kind, (block, units), lambda i: (i, 0))
            for kind in (BF16, F32, F32)
        ],
    )


def feed_back_kernel(g_ref, factor_ref, active_ref, *refs):
    pieces, (gate_ref, up_ref) = refs[:-2], refs[-2:]
    for span in column_spans(factor_ref.shape[1]):
        grad = tile_matmul(g_ref, pieces, span)
        gate_ref[:, span] = (grad * factor_ref[:, span]).astype(BF16)
        up_ref[:, span] = (grad * active_ref[:, span]).astype(BF16)


def feed_back(grad_output, factor, active, pieces):
    rows, units = factor.shape
    block = rows // 2
    return call(
        feed_back_kernel,
        (2,),
        [by_rows(array, block) for array in (grad_output, factor, active)]
        + [whole(piece) for piece in pieces],
        [((rows, units), BF16, (block, units), lambda i: (i, 0)) for _ in range(2)],
    )


def shards(tokens, doc_ids, norm_attn, norm_mlp, w_qkv, w_out, w_in, w_down, cotangent):
    streams, block, width = tokens.shape
    shard_rows = w_qkv.shape[0]
    inner, outer = lax.axis_size("inner"), lax.axis_size("outer")
    core = lax.axis_index("core")
    length = 2 * block
    window = length + 2 * HALF
    rows = streams * length
    side = width // 2
    units = w_down.shape[1] // 2
    padded = -(-units // LANES) * LANES
    chips = outer * inner
    onward = [(i, i + 1) for i in range(chips - 1)]
    back = [(i + 1, i) for i in range(chips - 1)]

    def halves(weight, parts, pad):
        size = weight.shape[1] // (2 * parts)
        cut = [weight[:, i * size : (i + 1) * size] for i in range(2 * parts)]
        if pad != size:
            cut = [jnp.pad(piece, ((0, 0), (0, pad - size))) for piece in cut]
        return cut[0::2], cut[1::2]

    def paired(pieces):
        low = jnp.concatenate([piece for one, _ in pieces for piece in one], 1)
        high = jnp.concatenate([piece for _, two in pieces for piece in two], 1)
        mine = jnp.where(core == 0, low, high)
        return ordered(mine, swap(jnp.where(core == 0, high, low)), 0)

    pair_tokens = ordered(tokens, swap(tokens), 1)

    gains = jnp.pad(jnp.stack([norm_attn, norm_mlp], 1), ((0, 0), (0, LANES - 2)))
    cores = core.astype(jnp.int32).reshape(1)
    mine, other = pack_first(cores, w_qkv, gains, w_out)
    pair_one = ordered(mine, swap(other), 0)
    places = tuple(lax.axis_index(name) for name in ("inner", "outer", "dp"))
    later_in, later_down, pair_one, pair_tokens, places = tied(
        w_in, w_down, pair_one, pair_tokens, places
    )
    one = direct_sends(pair_one)
    pair_two = paired([halves(later_in, 2, padded)])
    pair_three = paired([halves(later_down, 1, padded)])
    three_near = gather_near([pair_three])
    order = arrival_order(*places, width, shard_rows)
    own_order = lax.dynamic_slice_in_dim(order, core * side, side, 0)
    other_order = lax.dynamic_slice_in_dim(order, (1 - core) * side, side, 0)

    def in_order(value):
        return matmul(value.reshape(-1, width), order).astype(BF16)

    own_tokens = in_order(pair_tokens)
    grad_output = in_order(ordered(cotangent, swap(cotangent), 1))

    start = lax.axis_index(("outer", "inner")) * length
    positions = (start - HALF + jnp.arange(window, dtype=jnp.int32)).astype(F32)
    frequency = ROPE_BASE ** (-(jnp.arange(HD // 2, dtype=F32) * 2.0 / HD))
    angles = positions[:, None] * frequency[None, :]
    cosine, sine = jnp.cos(angles), jnp.sin(angles)
    cosine = jnp.tile(cosine, (1, LANES // (HD // 2)))
    sine = jnp.tile(jnp.concatenate([-sine, sine], 1), (1, LANES // HD))
    ids_padded = jnp.pad(doc_ids, ((0, 0), (HALF, HALF)), constant_values=-1)
    key_ids = lax.dynamic_slice_in_dim(ids_padded, start, window, 1)[:, None, :]
    query_ids = lax.dynamic_slice_in_dim(doc_ids, start, length, 1)[:, :, None]

    prepared = (own_tokens, grad_output, order, own_order, other_order)
    prepared += (cosine, sine, key_ids, query_ids)
    prepared, pair_two, three_near, one, pair_tokens = tied(
        prepared, pair_two, three_near, one, pair_tokens
    )
    own_tokens, grad_output, order, own_order, other_order = prepared[:5]
    cosine, sine, key_ids, query_ids = prepared[5:]
    two_one = direct_send(pair_two, 1)
    three_far = gather_far(*three_near)
    low = lax.ppermute(pair_tokens[:, length - HALF :], ("outer", "inner"), onward)
    high = lax.ppermute(pair_tokens[:, :HALF], ("outer", "inner"), back)
    three_near, three_far, one, low, high, two_one, pair_two = tied(
        three_near, three_far, one, low, high, two_one, pair_two
    )
    two = [pair_two] + two_one + direct_send(pair_two, *range(2, outer))

    near = gather_near(one)
    low, high = (in_order(end).reshape(end.shape) for end in (low, high))
    late = joined_rows([three_near[0], *three_near[1], *three_near[2], *three_far[0], *three_far[1]])
    low, high, two, near, late = tied(low, high, two, near, late)

    far = gather_far(*near)
    two_own = joined_rows(two)
    three = direct_sends(late)
    near, far, two_own, three[1] = tied(near, far, two_own, three[1])

    two_near = gather_near([two_own])
    first = in_pieces(*near, *far)
    joined, window_norm, gain_rows = project(
        low, own_tokens.reshape(streams, length, width), high, first, cosine, sine, side
    )
    out_half = joined_rows([piece[:, 3 * side + LANES :] for piece in first])
    weight = out_weight(first, out_half, swap(out_half), own_order, other_order)
    three[3:], joined, weight, first, two_near = tied(
        three[3:], joined, weight, first, two_near
    )

    two_far = gather_far(*two_near)
    joined = joined.reshape(streams, window, 3 * side)
    attended = attend(block, joined, query_ids, key_ids).reshape(rows, side)
    attended_low, hidden, normed_mlp_low = out_project(
        attended, swap(attended), own_order, other_order, weight, own_tokens, gain_rows
    )
    hidden, normed_mlp_low, two_near, two_far = tied(
        hidden, normed_mlp_low, two_near, two_far
    )
    in_half = in_pieces(*two_near, *two_far)
    mixed_low, factor, active = feed(normed_mlp_low, in_half, padded)

    down_cuts = split_late(grad_output, mixed_low, shard_rows)
    down_cuts, factor, active, three = tied(down_cuts, factor, active, three)
    down_half = [join_late(three, shard_rows)]
    grad_gate, grad_up = feed_back(grad_output, factor, active, down_half)
    sum_in = GradSum([normed_mlp_low] * 2, [grad_gate, grad_up], shard_rows)
    sent_in = sum_in.far()
    grad_gate, grad_up, sent_in, mixed_low = tied(grad_gate, grad_up, sent_in, mixed_low)

    in_far = sum_in.send_far(sent_in)
    down_arrived = [
        lax.ppermute(cut, "outer", forward("outer", outer - 1)) for cut in down_cuts[1:2]
    ]
    part, part_low = back_project([grad_gate, grad_up], in_half, [F32, BF16])
    part, part_low, in_far, down_arrived[0], down_cuts = tied(
        part, part_low, in_far, down_arrived[0], down_cuts
    )

    in_near = sum_in.send_near(sum_in.near(in_far))
    down_arrived[1:] = [
        lax.ppermute(down_cuts[distance], "outer", forward("outer", outer - distance))
        for distance in range(2, outer)
    ]
    grad_hidden, hidden_side, grad_attended = hidden_back(
        part, swap(part_low), hidden, grad_output, gain_rows, weight, own_order
    )
    grad_query, mid, to_lower, to_upper = attend_back(
        block, joined, query_ids, key_ids, grad_attended.reshape(streams, length, side),
        cosine, sine,
    )
    from_lower = lax.ppermute(to_upper, ("outer", "inner"), onward)
    from_upper = lax.ppermute(to_lower, ("outer", "inner"), back)
    from_lower, from_upper, in_near, down_arrived[:2] = tied(
        from_lower, from_upper, in_near, down_arrived[:2]
    )

    grad_joined = join_grads(grad_query, mid, from_lower, from_upper, cosine, sine)
    grad_joined = grad_joined.reshape(rows, 3 * side)
    normed_low = window_norm.reshape(streams, window, width)[:, HALF : HALF + length]
    sum_attn = GradSum(
        [normed_low.reshape(rows, width), attended_low], [grad_joined, hidden_side], shard_rows
    )
    sent_attn, in_own = sum_attn.far(), sum_in.own(in_near)
    sent_attn, in_own, grad_joined = tied(sent_attn, in_own, grad_joined)

    attn_far = sum_attn.send_far(sent_attn)
    in_arrived = sum_in.send_direct(in_own, 1)
    out_mine, out_other = back_split(cores, mixed_low, down_half, streams)
    in_mine, in_other = back_split(cores, grad_joined, first, streams)
    attn_far, in_arrived, in_own, down_arrived, out_mine, out_other, in_mine, in_other = tied(
        attn_far, in_arrived, in_own, down_arrived, out_mine, out_other, in_mine, in_other
    )

    attn_near = sum_attn.send_near(sum_attn.near(attn_far))
    in_arrived = in_arrived + sum_in.send_direct(in_own, *range(2, outer))
    down_rows = late_rows([down_cuts[0], *down_arrived], shard_rows)
    attn_near, in_arrived, out_other, in_other, down_rows = tied(
        attn_near, in_arrived, out_other, in_other, down_rows
    )

    attn_own = sum_attn.own(attn_near)
    attn_arrived = sum_attn.send_direct(attn_own, *range(1, outer))
    output = end_rows(
        output_kernel, cores, [out_mine, swap(out_other)], [hidden], [order], BF16, streams
    ).reshape(tokens.shape)
    grad_tokens = end_rows(
        input_grad_kernel, cores, [in_mine, swap(in_other)], [grad_hidden, own_tokens],
        [gain_rows, order], F32, streams,
    ).reshape(tokens.shape)
    total_mine, total_other = sum_in.total(cores, in_own, in_arrived)
    grad_in, gain_grad_mlp = assemble(
        cores, total_mine, swap(total_other), [(0, 2, padded, units)], w_in, norm_mlp
    )
    down_sums = late_sends(down_rows)
    attn_arrived, output, grad_tokens, grad_in, gain_grad_mlp, down_sums = tied(
        attn_arrived, output, grad_tokens, grad_in, gain_grad_mlp, down_sums
    )
    down_mine, down_other = sum_in.total(cores, down_rows[0, 0], down_sums)
    total_mine, total_other = sum_attn.total(cores, attn_own, attn_arrived)
    grad_qkv, grad_out, gain_grad_attn = assemble(
        cores, total_mine, swap(total_other),
        [(0, 3, side, side), (3 * side, 1, side, side)], w_qkv, norm_attn,
    )
    (grad_down,) = assemble(cores, down_mine, swap(down_other), [(0, 1, padded, units)])
    return (
        output,
        grad_tokens,
        gain_grad_attn.reshape(-1),
        gain_grad_mlp.reshape(-1),
        grad_qkv,
        grad_out,
        grad_in,
        grad_down,
    )


def solution(mesh):
    dp, seq = mesh.shape["dp"], mesh.shape["seq"]
    chips = seq // 2
    outer = 4 if chips % 4 == 0 else 1
    fine = Mesh(
        mesh.devices.reshape(dp, outer, chips // outer, 2), ("dp", "outer", "inner", "core")
    )
    line = ("outer", "inner", "core")
    every = ("dp",) + line
    token = P("dp", line, None)
    vector = P(every)
    matrix = P(every, None)
    return jax.shard_map(
        shards,
        mesh=fine,
        in_specs=(token, P("dp", None), vector, vector, matrix, matrix, matrix, matrix, token),
        out_specs=(token, token, vector, vector, matrix, matrix, matrix, matrix),
        check_vma=False,
    )
```

```python
import functools

import jax
import jax.numpy as jnp
import numpy as np
from jax import lax
from jax.experimental import pallas as pl
from jax.experimental.pallas import tpu as pltpu
from jax.sharding import Mesh, PartitionSpec as P

HD = 64
HALF = 64
LANES = 128
NORM_EPSILON = 1e-05
ROPE_BASE = 10000.0
F32 = jnp.float32
BF16 = jnp.bfloat16


def contract_cols(left, right):
    return lax.dot_general(left, right, (((1,), (1,)), ((), ())), preferred_element_type=F32)


def contract_rows(left, right):
    return lax.dot_general(left, right, (((0,), (0,)), ((), ())), preferred_element_type=F32)


def matmul(left, right):
    return jnp.dot(left, right, preferred_element_type=F32)


def tied(*values):
    return lax.optimization_barrier(values)


def call(kernel, grid, ins, outs, scratch=(), limit=40):
    out = pl.pallas_call(
        kernel,
        grid=grid,
        in_specs=[
            pl.BlockSpec(memory_space=pltpu.SMEM) if block is None else pl.BlockSpec(block, index)
            for _, block, index in ins
        ],
        out_specs=[pl.BlockSpec(block, index) for _, _, block, index in outs],
        out_shape=[jax.ShapeDtypeStruct(shape, kind) for shape, kind, _, _ in outs],
        scratch_shapes=list(scratch),
        compiler_params=pltpu.CompilerParams(vmem_limit_bytes=limit * 2**20),
        cost_estimate=pl.CostEstimate(flops=1024, bytes_accessed=1024, transcendentals=0),
    )(*[array for array, _, _ in ins])
    return out


def whole(array):
    return (array, array.shape, lambda *_: (0,) * array.ndim)


def swap(value):
    return lax.ppermute(value, "core", [(0, 1), (1, 0)])


def ordered(mine, other, axis):
    first = lax.axis_index("core") == 0
    return jnp.concatenate(
        [jnp.where(first, mine, other), jnp.where(first, other, mine)], axis=axis
    )


def forward(axis, distance=1):
    count = lax.axis_size(axis)
    return [(i, (i + distance) % count) for i in range(count)]


def ring_gather(axis, piece):
    pieces = [piece]
    for _ in range(1, lax.axis_size(axis)):
        pieces.append(lax.ppermute(pieces[-1], axis, forward(axis)))
    return pieces[1:]


def direct_send(rows, *distances):
    count = lax.axis_size("outer")
    return [
        lax.ppermute(rows, "outer", forward("outer", distance))
        for distance in distances
        if distance < count
    ]


def direct_sends(rows):
    return [rows] + direct_send(rows, *range(1, lax.axis_size("outer")))


def joined_rows(pieces):
    return jnp.concatenate(pieces, 0) if len(pieces) > 1 else pieces[0]


def gather_near(arrived):
    own = joined_rows(arrived)
    return own, ring_gather("inner", own), ring_gather("dp", own)


def copy_kernel(*refs):
    count = len(refs) // 2
    for source, target in zip(refs[:count], refs[count:]):
        target[...] = source[...]


def far_halves(along_x, along_y, half):
    if len(along_x) > 1 or len(along_y) > 1 or half % 32:
        return (
            joined_rows([piece[:half] for piece in along_y]),
            joined_rows([piece[half:] for piece in along_x]),
        )
    columns = along_x[0].shape[1]
    return call(
        copy_kernel,
        (1,),
        [(along_y[0], (half, columns), lambda i: (0, 0))]
        + [(along_x[0], (half, columns), lambda i: (1, 0))],
        [((half, columns), BF16, (half, columns), lambda i: (0, 0)) for _ in range(2)],
    )


def gather_far(own, along_x, along_y):
    one, two = far_halves(along_x, along_y, own.shape[0] // 2)
    return ring_gather("inner", one), ring_gather("dp", two)


def in_pieces(own, along_x, along_y, one, two):
    pieces = [own, *along_x, *along_y, *one, *two]
    if any(piece.shape[0] % LANES for piece in pieces):
        pieces = [joined_rows(pieces)]
    return pieces


def order_blocks(inner, dp):
    blocks = [(0, 0, 0, 2)]
    blocks += [(d, 0, 0, 2) for d in range(1, inner)] + [(0, d, 0, 2) for d in range(1, dp)]
    blocks += [(d, e, 0, 1) for d in range(1, inner) for e in range(1, dp)]
    return blocks + [(d, e, 1, 2) for e in range(1, dp) for d in range(1, inner)]


def late_segments(shard_rows):
    inner, outer, dp = (lax.axis_size(name) for name in ("inner", "outer", "dp"))
    start, at = 0, {}
    for d, e, low, high in order_blocks(inner, dp):
        for part in range(low, high):
            at[d, e, part] = start
            start += shard_rows
    segments = []
    for d, e, low, high in order_blocks(inner, dp):
        for distance in range(low * outer // 2, high * outer // 2):
            first, second = at[d, e, 0], at[d, e, 1]
            if second == first + shard_rows:
                segments.append((distance, first, 2 * shard_rows))
            else:
                segments += [(distance, first, shard_rows), (distance, second, shard_rows)]
    return segments


def join_kernel_rows(segments, *refs):
    pieces, out_ref = refs[:-1], refs[-1]
    at = 0
    for distance, start, count in segments:
        out_ref[at : at + count, :] = pieces[distance][start : start + count, :]
        at += count


def join_late(pieces, shard_rows):
    segments = late_segments(shard_rows)
    columns = pieces[0].shape[1]
    rows = sum(count for _, _, count in segments)
    if shard_rows % 32:
        return jnp.concatenate([pieces[d][at : at + n] for d, at, n in segments], 0)
    return call(
        functools.partial(join_kernel_rows, segments),
        (1,),
        [whole(piece) for piece in pieces],
        [((rows, columns), BF16, (rows, columns), lambda i: (0, 0))],
    )[0]


def split_kernel_rows(segments, left_ref, right_ref, *outs):
    place, at = [], 0
    for distance, start, count in segments:
        place.append((at, distance, start, count))
        at += count
    for top in range(0, at, LANES):
        rows = contract_rows(left_ref[:, top : top + LANES], right_ref[...]).astype(BF16)
        for begin, distance, start, count in place:
            if top <= begin < top + LANES:
                outs[distance][start : start + count, :] = rows[begin - top : begin - top + count]


def split_late(left, right, shard_rows):
    segments = late_segments(shard_rows)
    outer = lax.axis_size("outer")
    rows, columns = left.shape[1] // outer, right.shape[1]
    if shard_rows % 32:
        total, at, cuts = contract_rows(left, right).astype(BF16), 0, {}
        for distance, start, count in segments:
            cuts[distance, start] = total[at : at + count]
            at += count
        return [
            jnp.concatenate([cuts[key] for key in sorted(cuts) if key[0] == distance], 0)
            for distance in range(outer)
        ]
    return call(
        functools.partial(split_kernel_rows, segments),
        (1,),
        [whole(left), whole(right)],
        [((rows, columns), BF16, (rows, columns), lambda i: (0, 0)) for _ in range(outer)],
    )


def arrival_order(x, z, y, width, shard_rows):
    inner, outer, dp = (lax.axis_size(name) for name in ("inner", "outer", "dp"))
    half = outer * shard_rows
    blocks = order_blocks(inner, dp)
    place = np.concatenate([np.arange(low * half, high * half) for _, _, low, high in blocks])
    sizes = [(high - low) * half for _, _, low, high in blocks]
    along_x = np.repeat([block[0] for block in blocks], sizes)
    along_y = np.repeat([block[1] for block in blocks], sizes)
    along_z, row = place // (2 * shard_rows), place % (2 * shard_rows)
    at_x = (x - jnp.asarray(along_x, jnp.int32) + inner) % inner
    at_y = (y - jnp.asarray(along_y, jnp.int32) + dp) % dp
    at_z = (z - jnp.asarray(along_z, jnp.int32) + outer) % outer
    source = ((at_y * outer + at_z) * inner + at_x) * 2 * shard_rows + row
    return (jnp.arange(width, dtype=jnp.int32)[:, None] == source[None, :]).astype(BF16)


def rows_kernel(pairs, layout, *refs):
    rights, refs = refs[:pairs], refs[pairs:]
    inputs, outs = refs[: -len(layout)], refs[-len(layout) :]
    for places, out_ref in zip(layout, outs):
        lefts, adds = inputs[:pairs], inputs[pairs : pairs + len(places)]
        inputs = inputs[pairs + len(places) :]
        start = 0
        for left, right in zip(lefts, rights):
            columns = slice(start, start + right.shape[1])
            start = columns.stop
            total = contract_rows(left[...], right[...])
            for add in adds:
                if add.shape[0] == total.shape[0]:
                    total = total + add[:, columns].astype(F32)
            out_ref[:, columns] = total.astype(BF16)
            for add, at in zip(adds, places):
                if add.shape[0] != total.shape[0]:
                    span = slice(at, at + add.shape[0])
                    part = total[span] + add[:, columns].astype(F32)
                    out_ref[span, columns] = part.astype(BF16)


class GradSum:
    def __init__(self, lefts, rights, shard_rows):
        self.lefts, self.rights = lefts, rights
        self.inner, self.outer, self.dp = (
            lax.axis_size(name) for name in ("inner", "outer", "dp")
        )
        self.shard = 2 * shard_rows
        self.half = self.outer * shard_rows
        self.at_x = 2 * self.half
        self.at_y = self.at_x + (self.inner - 1) * 2 * self.half
        self.at_one = self.at_y + (self.dp - 1) * 2 * self.half
        self.at_two = self.at_one + (self.inner - 1) * (self.dp - 1) * self.half

    def rows(self, *parts):
        depth = self.lefts[0].shape[0]
        columns = sum(right.shape[1] for right in self.rights)
        ins, outs, layout = [whole(right) for right in self.rights], [], []
        for start, count, adds in parts:
            adds = [(rows, place) for rows, place in adds if rows is not None]
            lefts, index = self.lefts, start // count
            if count % LANES or start % count:
                lefts, index = [left[:, start : start + count] for left in lefts], 0
            ins += [
                (left, (depth, count), lambda i, index=index: (0, index)) for left in lefts
            ]
            ins += [whole(rows) for rows, _ in adds]
            outs.append(((count, columns), BF16, (count, columns), lambda i: (0, 0)))
            layout.append([place for _, place in adds])
        return call(
            functools.partial(rows_kernel, len(self.rights), layout), (1,), ins, outs
        )

    def ring(self, axis, part, first):
        arrived = None
        for step in range(1, lax.axis_size(axis)):
            sent = first if step == 1 else self.rows(part(step, arrived))[0]
            arrived = lax.ppermute(sent, axis, forward(axis))
        return arrived

    def one(self, distance, arrived):
        count = (self.dp - 1) * self.half
        return (self.at_one + (distance - 1) * count, count, [(arrived, 0)])

    def two(self, distance, arrived):
        count = (self.inner - 1) * self.half
        return (self.at_two + (distance - 1) * count, count, [(arrived, 0)])

    def far(self):
        return self.rows(self.one(1, None), self.two(1, None))

    def send_far(self, firsts):
        return (
            self.ring("inner", self.one, firsts[0]), self.ring("dp", self.two, firsts[1])
        )

    def along(self, start, distance, arrived, extra, place):
        count = 2 * self.half
        extra = extra[(distance - 1) * self.half : distance * self.half]
        return (start + (distance - 1) * count, count, [(arrived, 0), (extra, place)])

    def along_x(self, distance, arrived):
        return self.along(self.at_x, distance, arrived, self.sums[1], self.half)

    def along_y(self, distance, arrived):
        return self.along(self.at_y, distance, arrived, self.sums[0], 0)

    def near(self, sums):
        self.sums = sums
        return self.rows(self.along_x(1, None), self.along_y(1, None))

    def send_near(self, firsts):
        return (
            self.ring("inner", self.along_x, firsts[0]),
            self.ring("dp", self.along_y, firsts[1]),
        )

    def own(self, nears):
        return self.rows((0, 2 * self.half, [(near, 0) for near in nears]))[0]

    def cut(self, own, distance):
        return own[distance * self.shard : (distance + 1) * self.shard]

    def send_direct(self, own, *distances):
        return [
            lax.ppermute(
                self.cut(own, distance), "outer", forward("outer", self.outer - distance)
            )
            for distance in distances
            if distance < self.outer
        ]

    def total(self, core, own, arrived):
        columns = own.shape[1]
        half = self.shard // 2
        return call(
            total_kernel,
            (1,),
            [(core, None, None), (own, (self.shard, columns), lambda i: (0, 0))]
            + [whole(rows) for rows in arrived],
            [((half, columns), F32, (half, columns), lambda i: (0, 0)) for _ in range(2)],
        )


def late_kernel(count, layout, *refs):
    blocks, outs = refs[:count], refs[count:]
    for spans, out_ref in zip(layout, outs):
        at = 0
        for start, rows in spans:
            total = None
            for block in blocks:
                part = block[start : start + rows, :].astype(F32)
                total = part if total is None else total + part
            out_ref[at : at + rows, :] = total.astype(BF16)
            at += rows


def late_rows(blocks, shard_rows):
    inner, dp = lax.axis_size("inner"), lax.axis_size("dp")
    start, spans = 0, {}
    for d, e, low, high in order_blocks(inner, dp):
        rows = (high - low) * shard_rows
        spans.setdefault((d, e), []).append((start, rows))
        start += rows
    columns = blocks[0].shape[1]
    if shard_rows % 32:
        total = sum(block.astype(F32) for block in blocks).astype(BF16)
        return {
            key: joined_rows([total[at : at + rows] for at, rows in cuts])
            for key, cuts in spans.items()
        }
    shape = (2 * shard_rows, columns)
    cuts = call(
        functools.partial(late_kernel, len(blocks), list(spans.values())),
        (1,),
        [whole(block) for block in blocks],
        [(shape, BF16, shape, lambda i: (0, 0)) for _ in spans],
    )
    return dict(zip(spans, cuts))


def late_sends(cuts):
    inner, dp = lax.axis_size("inner"), lax.axis_size("dp")
    return [
        lax.ppermute(
            rows,
            ("dp", "inner"),
            [
                (y * inner + x, (y - e) % dp * inner + (x - d) % inner)
                for y in range(dp)
                for x in range(inner)
            ],
        )
        for (d, e), rows in cuts.items()
        if d or e
    ]


def own_half(core_ref, value):
    half = value.shape[0] // 2
    return jnp.where(core_ref[0] == 0, value[:half], value[half:])


def total_kernel(core_ref, *refs):
    total = None
    for ref in refs[:-2]:
        rows = ref[...].astype(F32)
        total = rows if total is None else total + rows
    half = total.shape[0] // 2
    first = core_ref[0] == 0
    refs[-2][...] = jnp.where(first, total[:half], total[half:])
    refs[-1][...] = jnp.where(first, total[half:], total[:half])


def assemble_kernel(layout, core_ref, mine_ref, other_ref, *refs):
    first = core_ref[0] == 0
    count = len(layout)
    pair = (
        jnp.where(first, mine_ref[...], other_ref[...]),
        jnp.where(first, other_ref[...], mine_ref[...]),
    )
    outs = refs[-count:] if len(refs) == count else refs[2:-1]
    for out_ref, (start, parts, stride, size) in zip(outs, layout):
        cuts = []
        for i in range(parts):
            at = start + i * stride
            cuts += [half[:, at : at + size] for half in pair]
        out_ref[...] = jnp.concatenate(cuts, 1)
    if len(refs) > count:
        weight_ref, gain_ref = refs[:2]
        product = weight_ref[...].astype(F32) * outs[0][...]
        refs[-1][...] = jnp.sum(product, -1, keepdims=True) / gain_ref[...].astype(F32)


def assemble(core, mine, other, layout, weight=None, gain=None):
    rows = mine.shape[0]
    ins = [(core, None, None), whole(mine), whole(other)]
    sizes = [2 * parts * size for _, parts, _, size in layout]
    if weight is not None:
        ins += [whole(weight), whole(gain.reshape(rows, 1))]
        sizes.append(1)
    return call(
        functools.partial(assemble_kernel, layout),
        (1,),
        ins,
        [((rows, size), F32, (rows, size), lambda i: (0, 0)) for size in sizes],
    )


def pack_kernel(side, core_ref, qkv_ref, gain_ref, out_ref, mine_ref, other_ref):
    def fill(target, half):
        for part in range(3):
            start = (2 * part + half) * side
            target[:, part * side : (part + 1) * side] = qkv_ref[:, start : start + side]
        target[:, 3 * side : 3 * side + LANES] = gain_ref[...]
        target[:, 3 * side + LANES :] = out_ref[:, half * side : (half + 1) * side]

    for half in range(2):

        @pl.when(core_ref[0] == half)
        def _():
            fill(mine_ref, half)
            fill(other_ref, 1 - half)


def pack_first(core, w_qkv, gains, w_out):
    rows, side = w_out.shape[0], w_out.shape[1] // 2
    columns = 4 * side + LANES
    return call(
        functools.partial(pack_kernel, side),
        (1,),
        [(core, None, None), whole(w_qkv), whole(gains), whole(w_out)],
        [((rows, columns), BF16, (rows, columns), lambda i: (0, 0)) for _ in range(2)],
    )


def normalise(values):
    centred = values - jnp.mean(values, -1, keepdims=True)
    scale = lax.rsqrt(jnp.mean(centred * centred, -1, keepdims=True) + NORM_EPSILON)
    return centred * scale, scale


def norm_back(unit, scale, gain, incoming):
    grad = incoming * gain
    return scale * (
        grad
        - jnp.mean(grad, -1, keepdims=True)
        - unit * jnp.mean(grad * unit, -1, keepdims=True)
    )


def piece_matmul(left, pieces):
    total, start = None, 0
    for piece in pieces:
        part = matmul(left[:, start : start + piece.shape[0]], piece[...])
        total = part if total is None else total + part
        start += piece.shape[0]
    return total


def back_kernel(starts, count, *refs):
    grads, pieces, out_refs = refs[: len(starts)], refs[len(starts) : count], refs[count:]
    at = 0
    for piece in pieces:
        total = None
        for grad, start in zip(grads, starts):
            part = contract_cols(grad[...], piece[:, start : start + grad.shape[1]])
            total = part if total is None else total + part
        for out_ref in out_refs:
            out_ref[:, at : at + piece.shape[0]] = total.astype(out_ref.dtype)
        at += piece.shape[0]


def back_project(grads, pieces, kinds):
    rows = grads[0].shape[0]
    block = rows // 2
    starts, end = [], 0
    for grad in grads:
        starts.append(end)
        end += grad.shape[1]
    width = sum(piece.shape[0] for piece in pieces)
    return call(
        functools.partial(back_kernel, starts, len(grads) + len(pieces)),
        (2,),
        [(grad, (block, grad.shape[1]), lambda i: (i, 0)) for grad in grads]
        + [(piece, (piece.shape[0], end), lambda i: (0, 0)) for piece in pieces],
        [((rows, width), kind, (block, width), lambda i: (i, 0)) for kind in kinds],
    )


def split_kernel(core_ref, grad_ref, *refs):
    pieces, (mine_ref, other_ref) = refs[:-2], refs[-2:]
    width = grad_ref.shape[1]
    half = grad_ref.shape[0] // 2
    at = 0
    for piece in pieces:
        total = contract_cols(grad_ref[...], piece[:, :width])
        first = core_ref[0] == 0
        span = slice(at, at + piece.shape[0])
        mine_ref[:, span] = jnp.where(first, total[:half], total[half:])
        other_ref[:, span] = jnp.where(first, total[half:], total[:half]).astype(BF16)
        at = span.stop


def back_split(core, grad, pieces, streams):
    rows, columns = grad.shape
    block = rows // streams
    width = sum(piece.shape[0] for piece in pieces)
    return call(
        split_kernel,
        (streams,),
        [(core, None, None), (grad, (block, columns), lambda i: (i, 0))]
        + [(piece, (piece.shape[0], columns), lambda i: (0, 0)) for piece in pieces],
        [
            ((rows // 2, width), kind, (block // 2, width), lambda i: (i, 0))
            for kind in (F32, BF16)
        ],
    )


def output_kernel(core_ref, mine_ref, other_ref, hidden_ref, order_ref, out_ref):
    total = own_half(core_ref, hidden_ref[...]) + mine_ref[...] + other_ref[...].astype(F32)
    out_ref[...] = contract_cols(total.astype(BF16), order_ref[...]).astype(BF16)


def input_grad_kernel(
    core_ref, mine_ref, other_ref, hidden_ref, x_ref, gain_ref, order_ref, out_ref
):
    unit, scale = normalise(own_half(core_ref, x_ref[...].astype(F32)))
    incoming = mine_ref[...] + other_ref[...].astype(F32)
    total = own_half(core_ref, hidden_ref[...])
    total = total + norm_back(unit, scale, gain_ref[0:1, :], incoming)
    result = None
    for _ in range(3):
        part = total.astype(BF16)
        total = total - part.astype(F32)
        part = contract_cols(part, order_ref[...])
        result = part if result is None else result + part
    out_ref[...] = result


def end_rows(kernel, core, halves, fulls, wholes, kind, streams):
    rows, width = halves[0].shape
    block = rows // streams
    return call(
        kernel,
        (streams,),
        [(core, None, None)]
        + [(array, (block, width), lambda i: (i, 0)) for array in halves]
        + [(array, (2 * block, width), lambda i: (i, 0)) for array in fulls]
        + [whole(array) for array in wholes],
        [((rows, width), kind, (block, width), lambda i: (i, 0))],
    )[0]


def turned(values):
    width = values.shape[-1]
    lane = lax.broadcasted_iota(jnp.int32, values.shape, values.ndim - 1)
    ahead = pltpu.roll(values, width - HD // 2, values.ndim - 1)
    behind = pltpu.roll(values, HD // 2, values.ndim - 1)
    return jnp.where(lane % HD < HD // 2, ahead, behind)


def project_kernel(count, low_ref, x_ref, high_ref, cos_ref, sin_ref, *refs):
    gains, weights = refs[:count], refs[count : 2 * count]
    out_ref, norm_ref, gain_ref = refs[2 * count :]

    @pl.when(pl.program_id(0) == 0)
    def _():
        pick = lax.broadcasted_iota(jnp.int32, (8, LANES), 0) == lax.broadcasted_iota(
            jnp.int32, (8, LANES), 1
        )
        pick = pick.astype(F32).astype(BF16)
        start = 0
        for piece in gains:
            gain_ref[:, start : start + piece.shape[0]] = contract_cols(pick, piece[...])
            start += piece.shape[0]
        for stream in range(x_ref.shape[0]):
            at = stream * cos_ref.shape[0]
            for ref in (low_ref, x_ref, high_ref):
                unit, _ = normalise(ref[stream].astype(F32))
                span = slice(at, at + ref.shape[1])
                norm_ref[span, :] = (unit * gain_ref[0:1, :]).astype(BF16)
                at = span.stop

    values = piece_matmul(norm_ref, weights)
    keep = pl.program_id(0) == 2
    length = cos_ref.shape[0]
    for top in range(0, values.shape[0], length):
        for left in range(0, values.shape[1], LANES):
            part = values[top : top + length, left : left + LANES]
            rotated = part * cos_ref[...] + turned(part) * sin_ref[...]
            out_ref[top : top + length, left : left + LANES] = jnp.where(
                keep, part, rotated
            ).astype(BF16)


def project(low, tokens, high, pieces, cosine, sine, side):
    width = tokens.shape[2]
    rows = tokens.shape[0] * cosine.shape[0]
    gain_block = 3 * side // LANES
    return call(
        functools.partial(project_kernel, len(pieces)),
        (3,),
        [whole(low), whole(tokens), whole(high), whole(cosine), whole(sine)]
        + [(piece, (piece.shape[0], LANES), lambda j: (0, gain_block)) for piece in pieces]
        + [(piece, (piece.shape[0], side), lambda j: (0, j)) for piece in pieces],
        [
            ((rows, 3 * side), BF16, (rows, side), lambda j: (0, j)),
            ((rows, width), BF16, (rows, width), lambda j: (0, 0)),
            ((8, width), F32, (8, width), lambda j: (0, 0)),
        ],
    )


def head_masks():
    lane = lax.broadcasted_iota(jnp.int32, (1, LANES), 1)
    return [(lane // HD == head).astype(F32).astype(BF16) for head in range(LANES // HD)]


def block_mask(query_ids, key_ids):
    rows, width = query_ids.shape[0], key_ids.shape[1]
    offset = lax.broadcasted_iota(jnp.int32, (rows, width), 1) - lax.broadcasted_iota(
        jnp.int32, (rows, width), 0
    )
    return (offset >= 0) & (offset <= 2 * HALF) & (query_ids == key_ids)


def block_probs(query, keys, allowed):
    scores = jnp.where(allowed, contract_cols(query, keys) * HD**-0.5, -1e30)
    grown = jnp.exp(scores - jnp.max(scores, -1, keepdims=True))
    return grown / jnp.sum(grown, -1, keepdims=True)


def attend_kernel(block, q_ref, k_ref, v_ref, qid_ref, kid_ref, out_ref):
    masks = head_masks()
    for start in range(0, out_ref.shape[1], block):
        span = slice(start, start + block + 2 * HALF)
        allowed = block_mask(qid_ref[0, start : start + block], kid_ref[0, :, span])
        query = q_ref[0, HALF + start : HALF + start + block]
        total = None
        for mask in masks:
            probs = block_probs(query * mask, k_ref[0, span], allowed)
            part = matmul(probs.astype(BF16), v_ref[0, span]) * mask.astype(F32)
            total = part if total is None else total + part
        out_ref[0, start : start + block] = total.astype(BF16)


def attend_back_kernel(
    block, q_ref, k_ref, v_ref, qid_ref, kid_ref, grad_ref, cos_ref, sin_ref,
    dq_ref, mid_ref, low_ref, high_ref,
):
    masks = head_masks()
    length = dq_ref.shape[1]
    grad_keys = grad_values = jnp.zeros((length + 2 * HALF, LANES), F32)
    for start in range(0, length, block):
        span = slice(start, start + block + 2 * HALF)
        mid = slice(HALF + start, HALF + start + block)
        rows = slice(start, start + block)
        allowed = block_mask(qid_ref[0, rows], kid_ref[0, :, span])
        query_all, grad_all = q_ref[0, mid], grad_ref[0, rows]
        keys, values = k_ref[0, span], v_ref[0, span]
        grad_query, part_keys, part_values = 0.0, 0.0, 0.0
        for mask in masks:
            query, grad = query_all * mask, grad_all * mask
            probs = block_probs(query, keys, allowed)
            grad_probs = contract_cols(grad, values)
            delta = jnp.sum(probs * grad_probs, -1, keepdims=True)
            grad_scores = (probs * (grad_probs - delta)).astype(BF16)
            grad_query += matmul(grad_scores, keys) * mask.astype(F32)
            part_keys += contract_rows(grad_scores, query)
            part_values += contract_rows(probs.astype(BF16), grad)
        grad_query = grad_query * HD**-0.5
        dq_ref[0, rows] = (
            grad_query * cos_ref[mid] - turned(grad_query) * sin_ref[mid]
        ).astype(BF16)
        before, after = start, length - start - block

        def placed(part):
            pieces = [part]
            if before:
                pieces.insert(0, jnp.zeros((before, LANES), F32))
            if after:
                pieces.append(jnp.zeros((after, LANES), F32))
            return jnp.concatenate(pieces, 0)

        grad_keys += placed(part_keys)
        grad_values += placed(part_values)
    for index, total in enumerate((grad_keys * HD**-0.5, grad_values)):
        low_ref[0, index] = total[:HALF].astype(BF16)
        mid_ref[0, index] = total[HALF : HALF + length]
        high_ref[0, index] = total[HALF + length :].astype(BF16)


def attention_inputs(joined, query_ids, key_ids):
    window, groups = joined.shape[1], joined.shape[2] // 3 // LANES
    inputs = [
        (joined, (1, window, LANES), lambda s, h, shift=shift: (s, 0, h + shift))
        for shift in (0, groups, 2 * groups)
    ]
    inputs += [
        (ids, (1,) + ids.shape[1:], lambda s, h: (s, 0, 0)) for ids in (query_ids, key_ids)
    ]
    return inputs


def attend(block, joined, query_ids, key_ids):
    streams, window, columns = joined.shape
    length, side = window - 2 * HALF, columns // 3
    return call(
        functools.partial(attend_kernel, block),
        (streams, side // LANES),
        attention_inputs(joined, query_ids, key_ids),
        [((streams, length, side), BF16, (1, length, LANES), lambda s, h: (s, 0, h))],
        limit=24,
    )[0]


def attend_back(block, joined, query_ids, key_ids, grad, cosine, sine):
    streams, length, side = grad.shape

    def pair(rows, kind):
        return (
            (streams, 2, rows, side), kind, (1, 2, rows, LANES), lambda s, h: (s, 0, 0, h)
        )

    return call(
        functools.partial(attend_back_kernel, block),
        (streams, side // LANES),
        attention_inputs(joined, query_ids, key_ids)
        + [(grad, (1, length, LANES), lambda s, h: (s, 0, h)), whole(cosine), whole(sine)],
        [
            ((streams, length, side), BF16, (1, length, LANES), lambda s, h: (s, 0, h)),
            pair(length, F32),
            pair(HALF, BF16),
            pair(HALF, BF16),
        ],
        limit=24,
    )


def join_kernel(dq_ref, mid_ref, low_ref, high_ref, cos_ref, sin_ref, out_ref):
    length, width = dq_ref.shape[1:]
    out_ref[0, :, :width] = dq_ref[0]
    cosine, sine = cos_ref[HALF : HALF + length], sin_ref[HALF : HALF + length]
    for index in range(2):
        for start in range(0, width, LANES):
            lanes = slice(start, start + LANES)
            total = mid_ref[0, index, :, lanes]
            total = total + jnp.concatenate(
                [
                    low_ref[0, index, :, lanes].astype(F32),
                    jnp.zeros((length - 2 * HALF, LANES), F32),
                    high_ref[0, index, :, lanes].astype(F32),
                ],
                0,
            )
            if index == 0:
                total = total * cosine - turned(total) * sine
            to = (1 + index) * width + start
            out_ref[0, :, to : to + LANES] = total.astype(BF16)


def join_grads(grad_query, mid, from_lower, from_upper, cosine, sine):
    streams, length, width = grad_query.shape

    def of_stream(array):
        block = (1,) + array.shape[1:]
        return (array, block, lambda s: (s,) + (0,) * (array.ndim - 1))

    return call(
        join_kernel,
        (streams,),
        [of_stream(array) for array in (grad_query, mid, from_lower, from_upper)]
        + [whole(cosine), whole(sine)],
        [((streams, length, 3 * width), BF16, (1, length, 3 * width), lambda s: (s, 0, 0))],
        limit=24,
    )[0]


def by_rows(array, block):
    return (array, (block, array.shape[1]), lambda i: (i, 0))


def weight_kernel(count, other_ref, own_order_ref, other_order_ref, *refs):
    start = 0
    out_ref = refs[count]
    for piece in refs[:count]:
        span = slice(start, start + piece.shape[0])
        total = matmul(piece[...], own_order_ref[...])
        total = total + matmul(other_ref[span, :], other_order_ref[...])
        out_ref[span, :] = total.astype(BF16)
        start = span.stop


def out_weight(pieces, own, other, own_order, other_order):
    side, width = own_order.shape
    if len(pieces) == 1:
        own_pieces = [(own, own.shape, lambda i: (0, 0))]
    else:
        own_pieces, start = [], 0
        for piece in pieces:
            count = piece.shape[0]
            own_pieces.append(
                (own, (count, side), lambda i, index=start // count: (index, 0))
            )
            start += count
    return call(
        functools.partial(weight_kernel, len(own_pieces)),
        (1,),
        [whole(other), whole(own_order), whole(other_order)] + own_pieces,
        [((width, width), BF16, (width, width), lambda i: (0, 0))],
    )[0]


def out_kernel(
    own_ref, other_ref, own_order_ref, other_order_ref, weight_ref, x_ref, gain_ref,
    att_ref, hidden_ref, norm_ref,
):
    attended = matmul(own_ref[...], own_order_ref[...])
    attended = (attended + matmul(other_ref[...], other_order_ref[...])).astype(BF16)
    att_ref[...] = attended
    hidden = x_ref[...].astype(F32) + matmul(attended, weight_ref[...])
    hidden_ref[...] = hidden
    norm_ref[...] = (normalise(hidden)[0] * gain_ref[1:2, :]).astype(BF16)


def out_project(own, other, own_order, other_order, weight, tokens, gains):
    rows, width = tokens.shape
    block = rows // 2
    return call(
        out_kernel,
        (2,),
        [by_rows(own, block), by_rows(other, block), whole(own_order), whole(other_order)]
        + [whole(weight), by_rows(tokens, block), whole(gains)],
        [
            ((rows, width), kind, (block, width), lambda i: (i, 0))
            for kind in (BF16, F32, BF16)
        ],
    )


def hidden_back_kernel(
    part_ref, other_ref, hidden_ref, g_ref, gain_ref, weight_ref, order_ref,
    grad_ref, side_ref, att_ref,
):
    unit, scale = normalise(hidden_ref[...])
    incoming = part_ref[...] + other_ref[...].astype(F32)
    grad = g_ref[...].astype(F32) + norm_back(unit, scale, gain_ref[1:2, :], incoming)
    low = grad.astype(BF16)
    grad_ref[...] = grad
    side_ref[...] = contract_cols(low, order_ref[...]).astype(BF16)
    attended = contract_cols(low, weight_ref[...]).astype(BF16)
    att_ref[...] = contract_cols(attended, order_ref[...]).astype(BF16)


def hidden_back(part, other, hidden, grad_output, gains, weight, own_order):
    rows, width = hidden.shape
    block, side = rows // 2, own_order.shape[0]
    return call(
        hidden_back_kernel,
        (2,),
        [by_rows(array, block) for array in (part, other, hidden, grad_output)]
        + [whole(gains), whole(weight), whole(own_order)],
        [
            ((rows, size), kind, (block, size), lambda i: (i, 0))
            for size, kind in ((width, F32), (side, BF16), (side, BF16))
        ],
    )


def column_spans(width):
    return [slice(at, min(at + 2 * LANES, width)) for at in range(0, width, 2 * LANES)]


def tile_matmul(left, pieces, columns):
    total, start = None, 0
    for piece in pieces:
        part = matmul(left[:, start : start + piece.shape[0]], piece[:, columns])
        total = part if total is None else total + part
        start += piece.shape[0]
    return total


def feed_kernel(norm_ref, *refs):
    pieces, (mixed_ref, factor_ref, active_ref) = refs[:-3], refs[-3:]
    units = mixed_ref.shape[1]
    for span in column_spans(units):
        gate = tile_matmul(norm_ref, pieces, span)
        up = tile_matmul(norm_ref, pieces, slice(units + span.start, units + span.stop))
        below = 0.5 * (1.0 + lax.erf(gate * 0.5**0.5))
        active = gate * below
        mixed_ref[:, span] = (active * up).astype(BF16)
        active_ref[:, span] = active
        density = jnp.exp(-0.5 * gate * gate) * (2.0 * np.pi) ** -0.5
        factor_ref[:, span] = up * (below + gate * density)


def feed(normed, pieces, units):
    rows = normed.shape[0]
    block = rows // 2
    return call(
        feed_kernel,
        (2,),
        [by_rows(normed, block)] + [whole(piece) for piece in pieces],
        [
            ((rows, units), kind, (block, units), lambda i: (i, 0))
            for kind in (BF16, F32, F32)
        ],
    )


def feed_back_kernel(g_ref, factor_ref, active_ref, *refs):
    pieces, (gate_ref, up_ref) = refs[:-2], refs[-2:]
    for span in column_spans(factor_ref.shape[1]):
        grad = tile_matmul(g_ref, pieces, span)
        gate_ref[:, span] = (grad * factor_ref[:, span]).astype(BF16)
        up_ref[:, span] = (grad * active_ref[:, span]).astype(BF16)


def feed_back(grad_output, factor, active, pieces):
    rows, units = factor.shape
    block = rows // 2
    return call(
        feed_back_kernel,
        (2,),
        [by_rows(array, block) for array in (grad_output, factor, active)]
        + [whole(piece) for piece in pieces],
        [((rows, units), BF16, (block, units), lambda i: (i, 0)) for _ in range(2)],
    )


def shards(tokens, doc_ids, norm_attn, norm_mlp, w_qkv, w_out, w_in, w_down, cotangent):
    streams, block, width = tokens.shape
    shard_rows = w_qkv.shape[0]
    inner, outer = lax.axis_size("inner"), lax.axis_size("outer")
    core = lax.axis_index("core")
    length = 2 * block
    window = length + 2 * HALF
    rows = streams * length
    side = width // 2
    units = w_down.shape[1] // 2
    padded = -(-units // LANES) * LANES
    chips = outer * inner
    onward = [(i, i + 1) for i in range(chips - 1)]
    back = [(i + 1, i) for i in range(chips - 1)]

    def halves(weight, parts, pad):
        size = weight.shape[1] // (2 * parts)
        cut = [weight[:, i * size : (i + 1) * size] for i in range(2 * parts)]
        if pad != size:
            cut = [jnp.pad(piece, ((0, 0), (0, pad - size))) for piece in cut]
        return cut[0::2], cut[1::2]

    def paired(pieces):
        low = jnp.concatenate([piece for one, _ in pieces for piece in one], 1)
        high = jnp.concatenate([piece for _, two in pieces for piece in two], 1)
        mine = jnp.where(core == 0, low, high)
        return ordered(mine, swap(jnp.where(core == 0, high, low)), 0)

    pair_tokens = ordered(tokens, swap(tokens), 1)

    gains = jnp.pad(jnp.stack([norm_attn, norm_mlp], 1), ((0, 0), (0, LANES - 2)))
    cores = core.astype(jnp.int32).reshape(1)
    mine, other = pack_first(cores, w_qkv, gains, w_out)
    pair_one = ordered(mine, swap(other), 0)
    places = tuple(lax.axis_index(name) for name in ("inner", "outer", "dp"))
    later_in, later_down, pair_one, pair_tokens, places = tied(
        w_in, w_down, pair_one, pair_tokens, places
    )
    one = direct_sends(pair_one)
    pair_two = paired([halves(later_in, 2, padded)])
    pair_three = paired([halves(later_down, 1, padded)])
    three_near = gather_near([pair_three])
    order = arrival_order(*places, width, shard_rows)
    own_order = lax.dynamic_slice_in_dim(order, core * side, side, 0)
    other_order = lax.dynamic_slice_in_dim(order, (1 - core) * side, side, 0)

    def in_order(value):
        return matmul(value.reshape(-1, width), order).astype(BF16)

    own_tokens = in_order(pair_tokens)
    grad_output = in_order(ordered(cotangent, swap(cotangent), 1))

    start = lax.axis_index(("outer", "inner")) * length
    positions = (start - HALF + jnp.arange(window, dtype=jnp.int32)).astype(F32)
    frequency = ROPE_BASE ** (-(jnp.arange(HD // 2, dtype=F32) * 2.0 / HD))
    angles = positions[:, None] * frequency[None, :]
    cosine, sine = jnp.cos(angles), jnp.sin(angles)
    cosine = jnp.tile(cosine, (1, LANES // (HD // 2)))
    sine = jnp.tile(jnp.concatenate([-sine, sine], 1), (1, LANES // HD))
    ids_padded = jnp.pad(doc_ids, ((0, 0), (HALF, HALF)), constant_values=-1)
    key_ids = lax.dynamic_slice_in_dim(ids_padded, start, window, 1)[:, None, :]
    query_ids = lax.dynamic_slice_in_dim(doc_ids, start, length, 1)[:, :, None]

    prepared = (own_tokens, grad_output, order, own_order, other_order)
    prepared += (cosine, sine, key_ids, query_ids)
    prepared, pair_two, three_near, one, pair_tokens = tied(
        prepared, pair_two, three_near, one, pair_tokens
    )
    own_tokens, grad_output, order, own_order, other_order = prepared[:5]
    cosine, sine, key_ids, query_ids = prepared[5:]
    two_one = direct_send(pair_two, 1)
    three_far = gather_far(*three_near)
    low = lax.ppermute(pair_tokens[:, length - HALF :], ("outer", "inner"), onward)
    high = lax.ppermute(pair_tokens[:, :HALF], ("outer", "inner"), back)
    three_near, three_far, one, low, high, two_one, pair_two = tied(
        three_near, three_far, one, low, high, two_one, pair_two
    )
    two = [pair_two] + two_one + direct_send(pair_two, *range(2, outer))

    near = gather_near(one)
    low, high = (in_order(end).reshape(end.shape) for end in (low, high))
    late = joined_rows([three_near[0], *three_near[1], *three_near[2], *three_far[0], *three_far[1]])
    low, high, two, near, late = tied(low, high, two, near, late)

    far = gather_far(*near)
    two_own = joined_rows(two)
    three = direct_sends(late)
    near, far, two_own, three[1] = tied(near, far, two_own, three[1])

    two_near = gather_near([two_own])
    first = in_pieces(*near, *far)
    joined, window_norm, gain_rows = project(
        low, own_tokens.reshape(streams, length, width), high, first, cosine, sine, side
    )
    out_half = joined_rows([piece[:, 3 * side + LANES :] for piece in first])
    weight = out_weight(first, out_half, swap(out_half), own_order, other_order)
    three[3:], joined, weight, first, two_near = tied(
        three[3:], joined, weight, first, two_near
    )

    two_far = gather_far(*two_near)
    joined = joined.reshape(streams, window, 3 * side)
    attended = attend(block, joined, query_ids, key_ids).reshape(rows, side)
    attended_low, hidden, normed_mlp_low = out_project(
        attended, swap(attended), own_order, other_order, weight, own_tokens, gain_rows
    )
    hidden, normed_mlp_low, two_near, two_far = tied(
        hidden, normed_mlp_low, two_near, two_far
    )
    in_half = in_pieces(*two_near, *two_far)
    mixed_low, factor, active = feed(normed_mlp_low, in_half, padded)

    factor, active, three = tied(factor, active, three)
    down_half = [join_late(three, shard_rows)]
    grad_gate, grad_up = feed_back(grad_output, factor, active, down_half)
    sum_in = GradSum([normed_mlp_low] * 2, [grad_gate, grad_up], shard_rows)
    sent_in = sum_in.far()
    grad_gate, grad_up, sent_in, mixed_low = tied(grad_gate, grad_up, sent_in, mixed_low)

    in_far = sum_in.send_far(sent_in)
    down_cuts = split_late(grad_output, mixed_low, shard_rows)
    down_arrived = [
        lax.ppermute(cut, "outer", forward("outer", outer - 1)) for cut in down_cuts[1:2]
    ]
    part, part_low = back_project([grad_gate, grad_up], in_half, [F32, BF16])
    part, part_low, in_far, down_arrived[0], down_cuts = tied(
        part, part_low, in_far, down_arrived[0], down_cuts
    )

    in_near = sum_in.send_near(sum_in.near(in_far))
    down_arrived[1:] = [
        lax.ppermute(down_cuts[distance], "outer", forward("outer", outer - distance))
        for distance in range(2, outer)
    ]
    grad_hidden, hidden_side, grad_attended = hidden_back(
        part, swap(part_low), hidden, grad_output, gain_rows, weight, own_order
    )
    grad_query, mid, to_lower, to_upper = attend_back(
        block, joined, query_ids, key_ids, grad_attended.reshape(streams, length, side),
        cosine, sine,
    )
    from_lower = lax.ppermute(to_upper, ("outer", "inner"), onward)
    from_upper = lax.ppermute(to_lower, ("outer", "inner"), back)
    from_lower, from_upper, in_near, down_arrived[:2] = tied(
        from_lower, from_upper, in_near, down_arrived[:2]
    )

    grad_joined = join_grads(grad_query, mid, from_lower, from_upper, cosine, sine)
    grad_joined = grad_joined.reshape(rows, 3 * side)
    normed_low = window_norm.reshape(streams, window, width)[:, HALF : HALF + length]
    sum_attn = GradSum(
        [normed_low.reshape(rows, width), attended_low], [grad_joined, hidden_side], shard_rows
    )
    sent_attn, in_own = sum_attn.far(), sum_in.own(in_near)
    sent_attn, in_own, grad_joined = tied(sent_attn, in_own, grad_joined)

    attn_far = sum_attn.send_far(sent_attn)
    in_arrived = sum_in.send_direct(in_own, 1)
    out_mine, out_other = back_split(cores, mixed_low, down_half, streams)
    in_mine, in_other = back_split(cores, grad_joined, first, streams)
    attn_far, in_arrived, in_own, down_arrived, out_mine, out_other, in_mine, in_other = tied(
        attn_far, in_arrived, in_own, down_arrived, out_mine, out_other, in_mine, in_other
    )

    attn_near = sum_attn.send_near(sum_attn.near(attn_far))
    in_arrived = in_arrived + sum_in.send_direct(in_own, *range(2, outer))
    down_rows = late_rows([down_cuts[0], *down_arrived], shard_rows)
    attn_near, in_arrived, out_other, in_other, down_rows = tied(
        attn_near, in_arrived, out_other, in_other, down_rows
    )

    attn_own = sum_attn.own(attn_near)
    attn_arrived = sum_attn.send_direct(attn_own, *range(1, outer))
    output = end_rows(
        output_kernel, cores, [out_mine, swap(out_other)], [hidden], [order], BF16, streams
    ).reshape(tokens.shape)
    grad_tokens = end_rows(
        input_grad_kernel, cores, [in_mine, swap(in_other)], [grad_hidden, own_tokens],
        [gain_rows, order], F32, streams,
    ).reshape(tokens.shape)
    total_mine, total_other = sum_in.total(cores, in_own, in_arrived)
    grad_in, gain_grad_mlp = assemble(
        cores, total_mine, swap(total_other), [(0, 2, padded, units)], w_in, norm_mlp
    )
    output, grad_tokens, down_rows = tied(output, grad_tokens, down_rows)
    down_sums = late_sends(down_rows)
    attn_arrived, output, grad_tokens, grad_in, gain_grad_mlp, down_sums = tied(
        attn_arrived, output, grad_tokens, grad_in, gain_grad_mlp, down_sums
    )
    down_mine, down_other = sum_in.total(cores, down_rows[0, 0], down_sums)
    total_mine, total_other = sum_attn.total(cores, attn_own, attn_arrived)
    grad_qkv, grad_out, gain_grad_attn = assemble(
        cores, total_mine, swap(total_other),
        [(0, 3, side, side), (3 * side, 1, side, side)], w_qkv, norm_attn,
    )
    (grad_down,) = assemble(cores, down_mine, swap(down_other), [(0, 1, padded, units)])
    return (
        output,
        grad_tokens,
        gain_grad_attn.reshape(-1),
        gain_grad_mlp.reshape(-1),
        grad_qkv,
        grad_out,
        grad_in,
        grad_down,
    )


def solution(mesh):
    dp, seq = mesh.shape["dp"], mesh.shape["seq"]
    chips = seq // 2
    outer = 4 if chips % 4 == 0 else 1
    fine = Mesh(
        mesh.devices.reshape(dp, outer, chips // outer, 2), ("dp", "outer", "inner", "core")
    )
    line = ("outer", "inner", "core")
    every = ("dp",) + line
    token = P("dp", line, None)
    vector = P(every)
    matrix = P(every, None)
    return jax.shard_map(
        shards,
        mesh=fine,
        in_specs=(token, P("dp", None), vector, vector, matrix, matrix, matrix, matrix, token),
        out_specs=(token, token, vector, vector, matrix, matrix, matrix, matrix),
        check_vma=False,
    )
```

```python
import functools

import jax
import jax.numpy as jnp
import numpy as np
from jax import lax
from jax.experimental import pallas as pl
from jax.experimental.pallas import tpu as pltpu
from jax.sharding import Mesh, PartitionSpec as P

HD = 64
HALF = 64
LANES = 128
NORM_EPSILON = 1e-05
ROPE_BASE = 10000.0
F32 = jnp.float32
BF16 = jnp.bfloat16


def contract_cols(left, right):
    return lax.dot_general(left, right, (((1,), (1,)), ((), ())), preferred_element_type=F32)


def contract_rows(left, right):
    return lax.dot_general(left, right, (((0,), (0,)), ((), ())), preferred_element_type=F32)


def matmul(left, right):
    return jnp.dot(left, right, preferred_element_type=F32)


def tied(*values):
    return lax.optimization_barrier(values)


def call(kernel, grid, ins, outs, scratch=(), limit=40):
    out = pl.pallas_call(
        kernel,
        grid=grid,
        in_specs=[
            pl.BlockSpec(memory_space=pltpu.SMEM) if block is None else pl.BlockSpec(block, index)
            for _, block, index in ins
        ],
        out_specs=[pl.BlockSpec(block, index) for _, _, block, index in outs],
        out_shape=[jax.ShapeDtypeStruct(shape, kind) for shape, kind, _, _ in outs],
        scratch_shapes=list(scratch),
        compiler_params=pltpu.CompilerParams(vmem_limit_bytes=limit * 2**20),
        cost_estimate=pl.CostEstimate(flops=1024, bytes_accessed=1024, transcendentals=0),
    )(*[array for array, _, _ in ins])
    return out


def whole(array):
    return (array, array.shape, lambda *_: (0,) * array.ndim)


def swap(value):
    return lax.ppermute(value, "core", [(0, 1), (1, 0)])


def ordered(mine, other, axis):
    first = lax.axis_index("core") == 0
    return jnp.concatenate(
        [jnp.where(first, mine, other), jnp.where(first, other, mine)], axis=axis
    )


def forward(axis, distance=1):
    count = lax.axis_size(axis)
    return [(i, (i + distance) % count) for i in range(count)]


def ring_gather(axis, piece):
    pieces = [piece]
    for _ in range(1, lax.axis_size(axis)):
        pieces.append(lax.ppermute(pieces[-1], axis, forward(axis)))
    return pieces[1:]


def direct_send(rows, *distances):
    count = lax.axis_size("outer")
    return [
        lax.ppermute(rows, "outer", forward("outer", distance))
        for distance in distances
        if distance < count
    ]


def direct_sends(rows):
    return [rows] + direct_send(rows, *range(1, lax.axis_size("outer")))


def joined_rows(pieces):
    return jnp.concatenate(pieces, 0) if len(pieces) > 1 else pieces[0]


def gather_near(arrived):
    own = joined_rows(arrived)
    return own, ring_gather("inner", own), ring_gather("dp", own)


def copy_kernel(*refs):
    count = len(refs) // 2
    for source, target in zip(refs[:count], refs[count:]):
        target[...] = source[...]


def far_halves(along_x, along_y, half):
    if len(along_x) > 1 or len(along_y) > 1 or half % 32:
        return (
            joined_rows([piece[:half] for piece in along_y]),
            joined_rows([piece[half:] for piece in along_x]),
        )
    columns = along_x[0].shape[1]
    return call(
        copy_kernel,
        (1,),
        [(along_y[0], (half, columns), lambda i: (0, 0))]
        + [(along_x[0], (half, columns), lambda i: (1, 0))],
        [((half, columns), BF16, (half, columns), lambda i: (0, 0)) for _ in range(2)],
    )


def gather_far(own, along_x, along_y):
    one, two = far_halves(along_x, along_y, own.shape[0] // 2)
    return ring_gather("inner", one), ring_gather("dp", two)


def in_pieces(own, along_x, along_y, one, two):
    pieces = [own, *along_x, *along_y, *one, *two]
    if any(piece.shape[0] % LANES for piece in pieces):
        pieces = [joined_rows(pieces)]
    return pieces


def order_blocks(inner, dp):
    blocks = [(0, 0, 0, 2)]
    blocks += [(d, 0, 0, 2) for d in range(1, inner)] + [(0, d, 0, 2) for d in range(1, dp)]
    blocks += [(d, e, 0, 1) for d in range(1, inner) for e in range(1, dp)]
    return blocks + [(d, e, 1, 2) for e in range(1, dp) for d in range(1, inner)]


def late_segments(shard_rows):
    inner, outer, dp = (lax.axis_size(name) for name in ("inner", "outer", "dp"))
    start, at = 0, {}
    for d, e, low, high in order_blocks(inner, dp):
        for part in range(low, high):
            at[d, e, part] = start
            start += shard_rows
    segments = []
    for d, e, low, high in order_blocks(inner, dp):
        for distance in range(low * outer // 2, high * outer // 2):
            first, second = at[d, e, 0], at[d, e, 1]
            if second == first + shard_rows:
                segments.append((distance, first, 2 * shard_rows))
            else:
                segments += [(distance, first, shard_rows), (distance, second, shard_rows)]
    return segments


def join_kernel_rows(segments, *refs):
    pieces, out_ref = refs[:-1], refs[-1]
    at = 0
    for distance, start, count in segments:
        out_ref[at : at + count, :] = pieces[distance][start : start + count, :]
        at += count


def join_late(pieces, shard_rows):
    segments = late_segments(shard_rows)
    columns = pieces[0].shape[1]
    rows = sum(count for _, _, count in segments)
    if shard_rows % 32:
        return jnp.concatenate([pieces[d][at : at + n] for d, at, n in segments], 0)
    return call(
        functools.partial(join_kernel_rows, segments),
        (1,),
        [whole(piece) for piece in pieces],
        [((rows, columns), BF16, (rows, columns), lambda i: (0, 0))],
    )[0]


def split_kernel_rows(segments, left_ref, right_ref, *outs):
    place, at = [], 0
    for distance, start, count in segments:
        place.append((at, distance, start, count))
        at += count
    for top in range(0, at, LANES):
        rows = contract_rows(left_ref[:, top : top + LANES], right_ref[...]).astype(BF16)
        for begin, distance, start, count in place:
            if top <= begin < top + LANES:
                outs[distance][start : start + count, :] = rows[begin - top : begin - top + count]


def split_late(left, right, shard_rows):
    segments = late_segments(shard_rows)
    outer = lax.axis_size("outer")
    rows, columns = left.shape[1] // outer, right.shape[1]
    if shard_rows % 32:
        total, at, cuts = contract_rows(left, right).astype(BF16), 0, {}
        for distance, start, count in segments:
            cuts[distance, start] = total[at : at + count]
            at += count
        return [
            jnp.concatenate([cuts[key] for key in sorted(cuts) if key[0] == distance], 0)
            for distance in range(outer)
        ]
    return call(
        functools.partial(split_kernel_rows, segments),
        (1,),
        [whole(left), whole(right)],
        [((rows, columns), BF16, (rows, columns), lambda i: (0, 0)) for _ in range(outer)],
    )


def arrival_order(x, z, y, width, shard_rows):
    inner, outer, dp = (lax.axis_size(name) for name in ("inner", "outer", "dp"))
    half = outer * shard_rows
    blocks = order_blocks(inner, dp)
    place = np.concatenate([np.arange(low * half, high * half) for _, _, low, high in blocks])
    sizes = [(high - low) * half for _, _, low, high in blocks]
    along_x = np.repeat([block[0] for block in blocks], sizes)
    along_y = np.repeat([block[1] for block in blocks], sizes)
    along_z, row = place // (2 * shard_rows), place % (2 * shard_rows)
    at_x = (x - jnp.asarray(along_x, jnp.int32) + inner) % inner
    at_y = (y - jnp.asarray(along_y, jnp.int32) + dp) % dp
    at_z = (z - jnp.asarray(along_z, jnp.int32) + outer) % outer
    source = ((at_y * outer + at_z) * inner + at_x) * 2 * shard_rows + row
    return (jnp.arange(width, dtype=jnp.int32)[:, None] == source[None, :]).astype(BF16)


def rows_kernel(pairs, layout, *refs):
    rights, refs = refs[:pairs], refs[pairs:]
    inputs, outs = refs[: -len(layout)], refs[-len(layout) :]
    for places, out_ref in zip(layout, outs):
        lefts, adds = inputs[:pairs], inputs[pairs : pairs + len(places)]
        inputs = inputs[pairs + len(places) :]
        start = 0
        for left, right in zip(lefts, rights):
            columns = slice(start, start + right.shape[1])
            start = columns.stop
            total = contract_rows(left[...], right[...])
            for add in adds:
                if add.shape[0] == total.shape[0]:
                    total = total + add[:, columns].astype(F32)
            out_ref[:, columns] = total.astype(BF16)
            for add, at in zip(adds, places):
                if add.shape[0] != total.shape[0]:
                    span = slice(at, at + add.shape[0])
                    part = total[span] + add[:, columns].astype(F32)
                    out_ref[span, columns] = part.astype(BF16)


class GradSum:
    def __init__(self, lefts, rights, shard_rows):
        self.lefts, self.rights = lefts, rights
        self.inner, self.outer, self.dp = (
            lax.axis_size(name) for name in ("inner", "outer", "dp")
        )
        self.shard = 2 * shard_rows
        self.half = self.outer * shard_rows
        self.at_x = 2 * self.half
        self.at_y = self.at_x + (self.inner - 1) * 2 * self.half
        self.at_one = self.at_y + (self.dp - 1) * 2 * self.half
        self.at_two = self.at_one + (self.inner - 1) * (self.dp - 1) * self.half

    def rows(self, *parts):
        depth = self.lefts[0].shape[0]
        columns = sum(right.shape[1] for right in self.rights)
        ins, outs, layout = [whole(right) for right in self.rights], [], []
        for start, count, adds in parts:
            adds = [(rows, place) for rows, place in adds if rows is not None]
            lefts, index = self.lefts, start // count
            if count % LANES or start % count:
                lefts, index = [left[:, start : start + count] for left in lefts], 0
            ins += [
                (left, (depth, count), lambda i, index=index: (0, index)) for left in lefts
            ]
            ins += [whole(rows) for rows, _ in adds]
            outs.append(((count, columns), BF16, (count, columns), lambda i: (0, 0)))
            layout.append([place for _, place in adds])
        return call(
            functools.partial(rows_kernel, len(self.rights), layout), (1,), ins, outs
        )

    def ring(self, axis, part, first):
        arrived = None
        for step in range(1, lax.axis_size(axis)):
            sent = first if step == 1 else self.rows(part(step, arrived))[0]
            arrived = lax.ppermute(sent, axis, forward(axis))
        return arrived

    def one(self, distance, arrived):
        count = (self.dp - 1) * self.half
        return (self.at_one + (distance - 1) * count, count, [(arrived, 0)])

    def two(self, distance, arrived):
        count = (self.inner - 1) * self.half
        return (self.at_two + (distance - 1) * count, count, [(arrived, 0)])

    def far(self):
        return self.rows(self.one(1, None), self.two(1, None))

    def send_far(self, firsts):
        return (
            self.ring("inner", self.one, firsts[0]), self.ring("dp", self.two, firsts[1])
        )

    def along(self, start, distance, arrived, extra, place):
        count = 2 * self.half
        extra = extra[(distance - 1) * self.half : distance * self.half]
        return (start + (distance - 1) * count, count, [(arrived, 0), (extra, place)])

    def along_x(self, distance, arrived):
        return self.along(self.at_x, distance, arrived, self.sums[1], self.half)

    def along_y(self, distance, arrived):
        return self.along(self.at_y, distance, arrived, self.sums[0], 0)

    def near(self, sums):
        self.sums = sums
        return self.rows(self.along_x(1, None), self.along_y(1, None))

    def send_near(self, firsts):
        return (
            self.ring("inner", self.along_x, firsts[0]),
            self.ring("dp", self.along_y, firsts[1]),
        )

    def own(self, nears):
        return self.rows((0, 2 * self.half, [(near, 0) for near in nears]))[0]

    def cut(self, own, distance):
        return own[distance * self.shard : (distance + 1) * self.shard]

    def send_direct(self, own, *distances):
        return [
            lax.ppermute(
                self.cut(own, distance), "outer", forward("outer", self.outer - distance)
            )
            for distance in distances
            if distance < self.outer
        ]

    def total(self, core, own, arrived):
        columns = own.shape[1]
        half = self.shard // 2
        return call(
            total_kernel,
            (1,),
            [(core, None, None), (own, (self.shard, columns), lambda i: (0, 0))]
            + [whole(rows) for rows in arrived],
            [((half, columns), F32, (half, columns), lambda i: (0, 0)) for _ in range(2)],
        )


def late_kernel(count, layout, *refs):
    blocks, outs = refs[:count], refs[count:]
    for spans, out_ref in zip(layout, outs):
        at = 0
        for start, rows in spans:
            total = None
            for block in blocks:
                part = block[start : start + rows, :].astype(F32)
                total = part if total is None else total + part
            out_ref[at : at + rows, :] = total.astype(BF16)
            at += rows


def late_rows(blocks, shard_rows):
    inner, dp = lax.axis_size("inner"), lax.axis_size("dp")
    start, spans = 0, {}
    for d, e, low, high in order_blocks(inner, dp):
        rows = (high - low) * shard_rows
        spans.setdefault((d, e), []).append((start, rows))
        start += rows
    columns = blocks[0].shape[1]
    if shard_rows % 32:
        total = sum(block.astype(F32) for block in blocks).astype(BF16)
        return {
            key: joined_rows([total[at : at + rows] for at, rows in cuts])
            for key, cuts in spans.items()
        }
    shape = (2 * shard_rows, columns)
    cuts = call(
        functools.partial(late_kernel, len(blocks), list(spans.values())),
        (1,),
        [whole(block) for block in blocks],
        [(shape, BF16, shape, lambda i: (0, 0)) for _ in spans],
    )
    return dict(zip(spans, cuts))


def late_sends(cuts):
    inner, dp = lax.axis_size("inner"), lax.axis_size("dp")
    return [
        lax.ppermute(
            rows,
            ("dp", "inner"),
            [
                (y * inner + x, (y - e) % dp * inner + (x - d) % inner)
                for y in range(dp)
                for x in range(inner)
            ],
        )
        for (d, e), rows in cuts.items()
        if d or e
    ]


def own_half(core_ref, value):
    half = value.shape[0] // 2
    return jnp.where(core_ref[0] == 0, value[:half], value[half:])


def total_kernel(core_ref, *refs):
    total = None
    for ref in refs[:-2]:
        rows = ref[...].astype(F32)
        total = rows if total is None else total + rows
    half = total.shape[0] // 2
    first = core_ref[0] == 0
    refs[-2][...] = jnp.where(first, total[:half], total[half:])
    refs[-1][...] = jnp.where(first, total[half:], total[:half])


def assemble_kernel(layout, core_ref, mine_ref, other_ref, *refs):
    first = core_ref[0] == 0
    count = len(layout)
    pair = (
        jnp.where(first, mine_ref[...], other_ref[...]),
        jnp.where(first, other_ref[...], mine_ref[...]),
    )
    outs = refs[-count:] if len(refs) == count else refs[2:-1]
    for out_ref, (start, parts, stride, size) in zip(outs, layout):
        cuts = []
        for i in range(parts):
            at = start + i * stride
            cuts += [half[:, at : at + size] for half in pair]
        out_ref[...] = jnp.concatenate(cuts, 1)
    if len(refs) > count:
        weight_ref, gain_ref = refs[:2]
        product = weight_ref[...].astype(F32) * outs[0][...]
        refs[-1][...] = jnp.sum(product, -1, keepdims=True) / gain_ref[...].astype(F32)


def assemble(core, mine, other, layout, weight=None, gain=None):
    rows = mine.shape[0]
    ins = [(core, None, None), whole(mine), whole(other)]
    sizes = [2 * parts * size for _, parts, _, size in layout]
    if weight is not None:
        ins += [whole(weight), whole(gain.reshape(rows, 1))]
        sizes.append(1)
    return call(
        functools.partial(assemble_kernel, layout),
        (1,),
        ins,
        [((rows, size), F32, (rows, size), lambda i: (0, 0)) for size in sizes],
    )


def pack_kernel(side, core_ref, qkv_ref, gain_ref, out_ref, mine_ref, other_ref):
    def fill(target, half):
        for part in range(3):
            start = (2 * part + half) * side
            target[:, part * side : (part + 1) * side] = qkv_ref[:, start : start + side]
        target[:, 3 * side : 3 * side + LANES] = gain_ref[...]
        target[:, 3 * side + LANES :] = out_ref[:, half * side : (half + 1) * side]

    for half in range(2):

        @pl.when(core_ref[0] == half)
        def _():
            fill(mine_ref, half)
            fill(other_ref, 1 - half)


def pack_first(core, w_qkv, gains, w_out):
    rows, side = w_out.shape[0], w_out.shape[1] // 2
    columns = 4 * side + LANES
    return call(
        functools.partial(pack_kernel, side),
        (1,),
        [(core, None, None), whole(w_qkv), whole(gains), whole(w_out)],
        [((rows, columns), BF16, (rows, columns), lambda i: (0, 0)) for _ in range(2)],
    )


def normalise(values):
    centred = values - jnp.mean(values, -1, keepdims=True)
    scale = lax.rsqrt(jnp.mean(centred * centred, -1, keepdims=True) + NORM_EPSILON)
    return centred * scale, scale


def norm_back(unit, scale, gain, incoming):
    grad = incoming * gain
    return scale * (
        grad
        - jnp.mean(grad, -1, keepdims=True)
        - unit * jnp.mean(grad * unit, -1, keepdims=True)
    )


def piece_matmul(left, pieces):
    total, start = None, 0
    for piece in pieces:
        part = matmul(left[:, start : start + piece.shape[0]], piece[...])
        total = part if total is None else total + part
        start += piece.shape[0]
    return total


def back_kernel(starts, count, *refs):
    grads, pieces, out_refs = refs[: len(starts)], refs[len(starts) : count], refs[count:]
    at = 0
    for piece in pieces:
        total = None
        for grad, start in zip(grads, starts):
            part = contract_cols(grad[...], piece[:, start : start + grad.shape[1]])
            total = part if total is None else total + part
        for out_ref in out_refs:
            out_ref[:, at : at + piece.shape[0]] = total.astype(out_ref.dtype)
        at += piece.shape[0]


def back_project(grads, pieces, kinds):
    rows = grads[0].shape[0]
    block = rows // 2
    starts, end = [], 0
    for grad in grads:
        starts.append(end)
        end += grad.shape[1]
    width = sum(piece.shape[0] for piece in pieces)
    return call(
        functools.partial(back_kernel, starts, len(grads) + len(pieces)),
        (2,),
        [(grad, (block, grad.shape[1]), lambda i: (i, 0)) for grad in grads]
        + [(piece, (piece.shape[0], end), lambda i: (0, 0)) for piece in pieces],
        [((rows, width), kind, (block, width), lambda i: (i, 0)) for kind in kinds],
    )


def split_kernel(core_ref, grad_ref, *refs):
    pieces, (mine_ref, other_ref) = refs[:-2], refs[-2:]
    width = grad_ref.shape[1]
    half = grad_ref.shape[0] // 2
    at = 0
    for piece in pieces:
        total = contract_cols(grad_ref[...], piece[:, :width])
        first = core_ref[0] == 0
        span = slice(at, at + piece.shape[0])
        mine_ref[:, span] = jnp.where(first, total[:half], total[half:])
        other_ref[:, span] = jnp.where(first, total[half:], total[:half]).astype(BF16)
        at = span.stop


def back_split(core, grad, pieces, streams):
    rows, columns = grad.shape
    block = rows // streams
    width = sum(piece.shape[0] for piece in pieces)
    return call(
        split_kernel,
        (streams,),
        [(core, None, None), (grad, (block, columns), lambda i: (i, 0))]
        + [(piece, (piece.shape[0], columns), lambda i: (0, 0)) for piece in pieces],
        [
            ((rows // 2, width), kind, (block // 2, width), lambda i: (i, 0))
            for kind in (F32, BF16)
        ],
    )


def output_kernel(core_ref, mine_ref, other_ref, hidden_ref, order_ref, out_ref):
    total = own_half(core_ref, hidden_ref[...]) + mine_ref[...] + other_ref[...].astype(F32)
    out_ref[...] = contract_cols(total.astype(BF16), order_ref[...]).astype(BF16)


def input_grad_kernel(
    core_ref, mine_ref, other_ref, hidden_ref, x_ref, gain_ref, order_ref, out_ref
):
    unit, scale = normalise(own_half(core_ref, x_ref[...].astype(F32)))
    incoming = mine_ref[...] + other_ref[...].astype(F32)
    total = own_half(core_ref, hidden_ref[...])
    total = total + norm_back(unit, scale, gain_ref[0:1, :], incoming)
    result = None
    for _ in range(3):
        part = total.astype(BF16)
        total = total - part.astype(F32)
        part = contract_cols(part, order_ref[...])
        result = part if result is None else result + part
    out_ref[...] = result


def end_rows(kernel, core, halves, fulls, wholes, kind, streams):
    rows, width = halves[0].shape
    block = rows // streams
    return call(
        kernel,
        (streams,),
        [(core, None, None)]
        + [(array, (block, width), lambda i: (i, 0)) for array in halves]
        + [(array, (2 * block, width), lambda i: (i, 0)) for array in fulls]
        + [whole(array) for array in wholes],
        [((rows, width), kind, (block, width), lambda i: (i, 0))],
    )[0]


def turned(values):
    width = values.shape[-1]
    lane = lax.broadcasted_iota(jnp.int32, values.shape, values.ndim - 1)
    ahead = pltpu.roll(values, width - HD // 2, values.ndim - 1)
    behind = pltpu.roll(values, HD // 2, values.ndim - 1)
    return jnp.where(lane % HD < HD // 2, ahead, behind)


def project_kernel(count, low_ref, x_ref, high_ref, cos_ref, sin_ref, *refs):
    gains, weights = refs[:count], refs[count : 2 * count]
    out_ref, norm_ref, gain_ref = refs[2 * count :]

    @pl.when(pl.program_id(0) == 0)
    def _():
        pick = lax.broadcasted_iota(jnp.int32, (8, LANES), 0) == lax.broadcasted_iota(
            jnp.int32, (8, LANES), 1
        )
        pick = pick.astype(F32).astype(BF16)
        start = 0
        for piece in gains:
            gain_ref[:, start : start + piece.shape[0]] = contract_cols(pick, piece[...])
            start += piece.shape[0]
        for stream in range(x_ref.shape[0]):
            at = stream * cos_ref.shape[0]
            for ref in (low_ref, x_ref, high_ref):
                unit, _ = normalise(ref[stream].astype(F32))
                span = slice(at, at + ref.shape[1])
                norm_ref[span, :] = (unit * gain_ref[0:1, :]).astype(BF16)
                at = span.stop

    values = piece_matmul(norm_ref, weights)
    keep = pl.program_id(0) == 2
    length = cos_ref.shape[0]
    for top in range(0, values.shape[0], length):
        for left in range(0, values.shape[1], LANES):
            part = values[top : top + length, left : left + LANES]
            rotated = part * cos_ref[...] + turned(part) * sin_ref[...]
            out_ref[top : top + length, left : left + LANES] = jnp.where(
                keep, part, rotated
            ).astype(BF16)


def project(low, tokens, high, pieces, cosine, sine, side):
    width = tokens.shape[2]
    rows = tokens.shape[0] * cosine.shape[0]
    gain_block = 3 * side // LANES
    return call(
        functools.partial(project_kernel, len(pieces)),
        (3,),
        [whole(low), whole(tokens), whole(high), whole(cosine), whole(sine)]
        + [(piece, (piece.shape[0], LANES), lambda j: (0, gain_block)) for piece in pieces]
        + [(piece, (piece.shape[0], side), lambda j: (0, j)) for piece in pieces],
        [
            ((rows, 3 * side), BF16, (rows, side), lambda j: (0, j)),
            ((rows, width), BF16, (rows, width), lambda j: (0, 0)),
            ((8, width), F32, (8, width), lambda j: (0, 0)),
        ],
    )


def head_masks():
    lane = lax.broadcasted_iota(jnp.int32, (1, LANES), 1)
    return [(lane // HD == head).astype(F32).astype(BF16) for head in range(LANES // HD)]


def block_mask(query_ids, key_ids):
    rows, width = query_ids.shape[0], key_ids.shape[1]
    offset = lax.broadcasted_iota(jnp.int32, (rows, width), 1) - lax.broadcasted_iota(
        jnp.int32, (rows, width), 0
    )
    return (offset >= 0) & (offset <= 2 * HALF) & (query_ids == key_ids)


def block_probs(query, keys, allowed):
    scores = jnp.where(allowed, contract_cols(query, keys) * HD**-0.5, -1e30)
    grown = jnp.exp(scores - jnp.max(scores, -1, keepdims=True))
    return grown / jnp.sum(grown, -1, keepdims=True)


def attend_kernel(block, q_ref, k_ref, v_ref, qid_ref, kid_ref, out_ref):
    masks = head_masks()
    for start in range(0, out_ref.shape[1], block):
        span = slice(start, start + block + 2 * HALF)
        allowed = block_mask(qid_ref[0, start : start + block], kid_ref[0, :, span])
        query = q_ref[0, HALF + start : HALF + start + block]
        total = None
        for mask in masks:
            probs = block_probs(query * mask, k_ref[0, span], allowed)
            part = matmul(probs.astype(BF16), v_ref[0, span]) * mask.astype(F32)
            total = part if total is None else total + part
        out_ref[0, start : start + block] = total.astype(BF16)


def attend_back_kernel(
    block, q_ref, k_ref, v_ref, qid_ref, kid_ref, grad_ref, cos_ref, sin_ref,
    dq_ref, mid_ref, low_ref, high_ref,
):
    masks = head_masks()
    length = dq_ref.shape[1]
    grad_keys = grad_values = jnp.zeros((length + 2 * HALF, LANES), F32)
    for start in range(0, length, block):
        span = slice(start, start + block + 2 * HALF)
        mid = slice(HALF + start, HALF + start + block)
        rows = slice(start, start + block)
        allowed = block_mask(qid_ref[0, rows], kid_ref[0, :, span])
        query_all, grad_all = q_ref[0, mid], grad_ref[0, rows]
        keys, values = k_ref[0, span], v_ref[0, span]
        grad_query, part_keys, part_values = 0.0, 0.0, 0.0
        for mask in masks:
            query, grad = query_all * mask, grad_all * mask
            probs = block_probs(query, keys, allowed)
            grad_probs = contract_cols(grad, values)
            delta = jnp.sum(probs * grad_probs, -1, keepdims=True)
            grad_scores = (probs * (grad_probs - delta)).astype(BF16)
            grad_query += matmul(grad_scores, keys) * mask.astype(F32)
            part_keys += contract_rows(grad_scores, query)
            part_values += contract_rows(probs.astype(BF16), grad)
        grad_query = grad_query * HD**-0.5
        dq_ref[0, rows] = (
            grad_query * cos_ref[mid] - turned(grad_query) * sin_ref[mid]
        ).astype(BF16)
        before, after = start, length - start - block

        def placed(part):
            pieces = [part]
            if before:
                pieces.insert(0, jnp.zeros((before, LANES), F32))
            if after:
                pieces.append(jnp.zeros((after, LANES), F32))
            return jnp.concatenate(pieces, 0)

        grad_keys += placed(part_keys)
        grad_values += placed(part_values)
    for index, total in enumerate((grad_keys * HD**-0.5, grad_values)):
        low_ref[0, index] = total[:HALF].astype(BF16)
        mid_ref[0, index] = total[HALF : HALF + length]
        high_ref[0, index] = total[HALF + length :].astype(BF16)


def attention_inputs(joined, query_ids, key_ids):
    window, groups = joined.shape[1], joined.shape[2] // 3 // LANES
    inputs = [
        (joined, (1, window, LANES), lambda s, h, shift=shift: (s, 0, h + shift))
        for shift in (0, groups, 2 * groups)
    ]
    inputs += [
        (ids, (1,) + ids.shape[1:], lambda s, h: (s, 0, 0)) for ids in (query_ids, key_ids)
    ]
    return inputs


def attend(block, joined, query_ids, key_ids):
    streams, window, columns = joined.shape
    length, side = window - 2 * HALF, columns // 3
    return call(
        functools.partial(attend_kernel, block),
        (streams, side // LANES),
        attention_inputs(joined, query_ids, key_ids),
        [((streams, length, side), BF16, (1, length, LANES), lambda s, h: (s, 0, h))],
        limit=24,
    )[0]


def attend_back(block, joined, query_ids, key_ids, grad, cosine, sine):
    streams, length, side = grad.shape

    def pair(rows, kind):
        return (
            (streams, 2, rows, side), kind, (1, 2, rows, LANES), lambda s, h: (s, 0, 0, h)
        )

    return call(
        functools.partial(attend_back_kernel, block),
        (streams, side // LANES),
        attention_inputs(joined, query_ids, key_ids)
        + [(grad, (1, length, LANES), lambda s, h: (s, 0, h)), whole(cosine), whole(sine)],
        [
            ((streams, length, side), BF16, (1, length, LANES), lambda s, h: (s, 0, h)),
            pair(length, F32),
            pair(HALF, BF16),
            pair(HALF, BF16),
        ],
        limit=24,
    )


def join_kernel(dq_ref, mid_ref, low_ref, high_ref, cos_ref, sin_ref, out_ref):
    length, width = dq_ref.shape[1:]
    out_ref[0, :, :width] = dq_ref[0]
    cosine, sine = cos_ref[HALF : HALF + length], sin_ref[HALF : HALF + length]
    for index in range(2):
        for start in range(0, width, LANES):
            lanes = slice(start, start + LANES)
            total = mid_ref[0, index, :, lanes]
            total = total + jnp.concatenate(
                [
                    low_ref[0, index, :, lanes].astype(F32),
                    jnp.zeros((length - 2 * HALF, LANES), F32),
                    high_ref[0, index, :, lanes].astype(F32),
                ],
                0,
            )
            if index == 0:
                total = total * cosine - turned(total) * sine
            to = (1 + index) * width + start
            out_ref[0, :, to : to + LANES] = total.astype(BF16)


def join_grads(grad_query, mid, from_lower, from_upper, cosine, sine):
    streams, length, width = grad_query.shape

    def of_stream(array):
        block = (1,) + array.shape[1:]
        return (array, block, lambda s: (s,) + (0,) * (array.ndim - 1))

    return call(
        join_kernel,
        (streams,),
        [of_stream(array) for array in (grad_query, mid, from_lower, from_upper)]
        + [whole(cosine), whole(sine)],
        [((streams, length, 3 * width), BF16, (1, length, 3 * width), lambda s: (s, 0, 0))],
        limit=24,
    )[0]


def by_rows(array, block):
    return (array, (block, array.shape[1]), lambda i: (i, 0))


def weight_kernel(count, other_ref, own_order_ref, other_order_ref, *refs):
    start = 0
    out_ref = refs[count]
    for piece in refs[:count]:
        span = slice(start, start + piece.shape[0])
        total = matmul(piece[...], own_order_ref[...])
        total = total + matmul(other_ref[span, :], other_order_ref[...])
        out_ref[span, :] = total.astype(BF16)
        start = span.stop


def out_weight(pieces, own, other, own_order, other_order):
    side, width = own_order.shape
    if len(pieces) == 1:
        own_pieces = [(own, own.shape, lambda i: (0, 0))]
    else:
        own_pieces, start = [], 0
        for piece in pieces:
            count = piece.shape[0]
            own_pieces.append(
                (own, (count, side), lambda i, index=start // count: (index, 0))
            )
            start += count
    return call(
        functools.partial(weight_kernel, len(own_pieces)),
        (1,),
        [whole(other), whole(own_order), whole(other_order)] + own_pieces,
        [((width, width), BF16, (width, width), lambda i: (0, 0))],
    )[0]


def out_kernel(
    own_ref, other_ref, own_order_ref, other_order_ref, weight_ref, x_ref, gain_ref,
    att_ref, hidden_ref, norm_ref,
):
    attended = matmul(own_ref[...], own_order_ref[...])
    attended = (attended + matmul(other_ref[...], other_order_ref[...])).astype(BF16)
    att_ref[...] = attended
    hidden = x_ref[...].astype(F32) + matmul(attended, weight_ref[...])
    hidden_ref[...] = hidden
    norm_ref[...] = (normalise(hidden)[0] * gain_ref[1:2, :]).astype(BF16)


def out_project(own, other, own_order, other_order, weight, tokens, gains):
    rows, width = tokens.shape
    block = rows // 2
    return call(
        out_kernel,
        (2,),
        [by_rows(own, block), by_rows(other, block), whole(own_order), whole(other_order)]
        + [whole(weight), by_rows(tokens, block), whole(gains)],
        [
            ((rows, width), kind, (block, width), lambda i: (i, 0))
            for kind in (BF16, F32, BF16)
        ],
    )


def hidden_back_kernel(
    part_ref, other_ref, hidden_ref, g_ref, gain_ref, weight_ref, order_ref,
    grad_ref, side_ref, att_ref,
):
    unit, scale = normalise(hidden_ref[...])
    incoming = part_ref[...] + other_ref[...].astype(F32)
    grad = g_ref[...].astype(F32) + norm_back(unit, scale, gain_ref[1:2, :], incoming)
    low = grad.astype(BF16)
    grad_ref[...] = grad
    side_ref[...] = contract_cols(low, order_ref[...]).astype(BF16)
    attended = contract_cols(low, weight_ref[...]).astype(BF16)
    att_ref[...] = contract_cols(attended, order_ref[...]).astype(BF16)


def hidden_back(part, other, hidden, grad_output, gains, weight, own_order):
    rows, width = hidden.shape
    block, side = rows // 2, own_order.shape[0]
    return call(
        hidden_back_kernel,
        (2,),
        [by_rows(array, block) for array in (part, other, hidden, grad_output)]
        + [whole(gains), whole(weight), whole(own_order)],
        [
            ((rows, size), kind, (block, size), lambda i: (i, 0))
            for size, kind in ((width, F32), (side, BF16), (side, BF16))
        ],
    )


def column_spans(width):
    return [slice(at, min(at + 2 * LANES, width)) for at in range(0, width, 2 * LANES)]


def tile_matmul(left, pieces, columns):
    total, start = None, 0
    for piece in pieces:
        part = matmul(left[:, start : start + piece.shape[0]], piece[:, columns])
        total = part if total is None else total + part
        start += piece.shape[0]
    return total


def feed_kernel(norm_ref, *refs):
    pieces, (mixed_ref, factor_ref, active_ref) = refs[:-3], refs[-3:]
    units = mixed_ref.shape[1]
    for span in column_spans(units):
        gate = tile_matmul(norm_ref, pieces, span)
        up = tile_matmul(norm_ref, pieces, slice(units + span.start, units + span.stop))
        below = 0.5 * (1.0 + lax.erf(gate * 0.5**0.5))
        active = gate * below
        mixed_ref[:, span] = (active * up).astype(BF16)
        active_ref[:, span] = active
        density = jnp.exp(-0.5 * gate * gate) * (2.0 * np.pi) ** -0.5
        factor_ref[:, span] = up * (below + gate * density)


def feed(normed, pieces, units):
    rows = normed.shape[0]
    block = rows // 2
    return call(
        feed_kernel,
        (2,),
        [by_rows(normed, block)] + [whole(piece) for piece in pieces],
        [
            ((rows, units), kind, (block, units), lambda i: (i, 0))
            for kind in (BF16, F32, F32)
        ],
    )


def feed_back_kernel(g_ref, factor_ref, active_ref, *refs):
    pieces, (gate_ref, up_ref) = refs[:-2], refs[-2:]
    for span in column_spans(factor_ref.shape[1]):
        grad = tile_matmul(g_ref, pieces, span)
        gate_ref[:, span] = (grad * factor_ref[:, span]).astype(BF16)
        up_ref[:, span] = (grad * active_ref[:, span]).astype(BF16)


def feed_back(grad_output, factor, active, pieces):
    rows, units = factor.shape
    block = rows // 2
    return call(
        feed_back_kernel,
        (2,),
        [by_rows(array, block) for array in (grad_output, factor, active)]
        + [whole(piece) for piece in pieces],
        [((rows, units), BF16, (block, units), lambda i: (i, 0)) for _ in range(2)],
    )


def shards(tokens, doc_ids, norm_attn, norm_mlp, w_qkv, w_out, w_in, w_down, cotangent):
    streams, block, width = tokens.shape
    shard_rows = w_qkv.shape[0]
    inner, outer = lax.axis_size("inner"), lax.axis_size("outer")
    core = lax.axis_index("core")
    length = 2 * block
    window = length + 2 * HALF
    rows = streams * length
    side = width // 2
    units = w_down.shape[1] // 2
    padded = -(-units // LANES) * LANES
    chips = outer * inner
    onward = [(i, i + 1) for i in range(chips - 1)]
    back = [(i + 1, i) for i in range(chips - 1)]

    def halves(weight, parts, pad):
        size = weight.shape[1] // (2 * parts)
        cut = [weight[:, i * size : (i + 1) * size] for i in range(2 * parts)]
        if pad != size:
            cut = [jnp.pad(piece, ((0, 0), (0, pad - size))) for piece in cut]
        return cut[0::2], cut[1::2]

    def paired(pieces):
        low = jnp.concatenate([piece for one, _ in pieces for piece in one], 1)
        high = jnp.concatenate([piece for _, two in pieces for piece in two], 1)
        mine = jnp.where(core == 0, low, high)
        return ordered(mine, swap(jnp.where(core == 0, high, low)), 0)

    pair_tokens = ordered(tokens, swap(tokens), 1)

    gains = jnp.pad(jnp.stack([norm_attn, norm_mlp], 1), ((0, 0), (0, LANES - 2)))
    cores = core.astype(jnp.int32).reshape(1)
    mine, other = pack_first(cores, w_qkv, gains, w_out)
    pair_one = ordered(mine, swap(other), 0)
    places = tuple(lax.axis_index(name) for name in ("inner", "outer", "dp"))
    later_in, later_down, pair_one, pair_tokens, places = tied(
        w_in, w_down, pair_one, pair_tokens, places
    )
    one = direct_sends(pair_one)
    pair_two = paired([halves(later_in, 2, padded)])
    pair_three = paired([halves(later_down, 1, padded)])
    three_near = gather_near([pair_three])
    order = arrival_order(*places, width, shard_rows)
    own_order = lax.dynamic_slice_in_dim(order, core * side, side, 0)
    other_order = lax.dynamic_slice_in_dim(order, (1 - core) * side, side, 0)

    def in_order(value):
        return matmul(value.reshape(-1, width), order).astype(BF16)

    own_tokens = in_order(pair_tokens)
    grad_output = in_order(ordered(cotangent, swap(cotangent), 1))

    start = lax.axis_index(("outer", "inner")) * length
    positions = (start - HALF + jnp.arange(window, dtype=jnp.int32)).astype(F32)
    frequency = ROPE_BASE ** (-(jnp.arange(HD // 2, dtype=F32) * 2.0 / HD))
    angles = positions[:, None] * frequency[None, :]
    cosine, sine = jnp.cos(angles), jnp.sin(angles)
    cosine = jnp.tile(cosine, (1, LANES // (HD // 2)))
    sine = jnp.tile(jnp.concatenate([-sine, sine], 1), (1, LANES // HD))
    ids_padded = jnp.pad(doc_ids, ((0, 0), (HALF, HALF)), constant_values=-1)
    key_ids = lax.dynamic_slice_in_dim(ids_padded, start, window, 1)[:, None, :]
    query_ids = lax.dynamic_slice_in_dim(doc_ids, start, length, 1)[:, :, None]

    prepared = (own_tokens, grad_output, order, own_order, other_order)
    prepared += (cosine, sine, key_ids, query_ids)
    prepared, pair_two, three_near, one, pair_tokens = tied(
        prepared, pair_two, three_near, one, pair_tokens
    )
    own_tokens, grad_output, order, own_order, other_order = prepared[:5]
    cosine, sine, key_ids, query_ids = prepared[5:]
    two_one = direct_send(pair_two, 1)
    three_far = gather_far(*three_near)
    low = lax.ppermute(pair_tokens[:, length - HALF :], ("outer", "inner"), onward)
    high = lax.ppermute(pair_tokens[:, :HALF], ("outer", "inner"), back)
    three_near, three_far, one, low, high, two_one, pair_two = tied(
        three_near, three_far, one, low, high, two_one, pair_two
    )
    two = [pair_two] + two_one + direct_send(pair_two, *range(2, outer))

    near = gather_near(one)
    low, high = (in_order(end).reshape(end.shape) for end in (low, high))
    late = joined_rows([three_near[0], *three_near[1], *three_near[2], *three_far[0], *three_far[1]])
    low, high, two, near, late = tied(low, high, two, near, late)

    far = gather_far(*near)
    two_own = joined_rows(two)
    three = direct_sends(late)
    near, far, two_own, three[1] = tied(near, far, two_own, three[1])

    two_near = gather_near([two_own])
    first = in_pieces(*near, *far)
    joined, window_norm, gain_rows = project(
        low, own_tokens.reshape(streams, length, width), high, first, cosine, sine, side
    )
    out_half = joined_rows([piece[:, 3 * side + LANES :] for piece in first])
    weight = out_weight(first, out_half, swap(out_half), own_order, other_order)
    three[3:], joined, weight, first, two_near = tied(
        three[3:], joined, weight, first, two_near
    )

    two_far = gather_far(*two_near)
    joined = joined.reshape(streams, window, 3 * side)
    attended = attend(block, joined, query_ids, key_ids).reshape(rows, side)
    attended_low, hidden, normed_mlp_low = out_project(
        attended, swap(attended), own_order, other_order, weight, own_tokens, gain_rows
    )
    hidden, normed_mlp_low, two_near, two_far = tied(
        hidden, normed_mlp_low, two_near, two_far
    )
    in_half = in_pieces(*two_near, *two_far)
    mixed_low, factor, active = feed(normed_mlp_low, in_half, padded)

    down_cuts = split_late(grad_output, mixed_low, shard_rows)
    down_cuts, factor, active, three = tied(down_cuts, factor, active, three)
    down_half = [join_late(three, shard_rows)]
    grad_gate, grad_up = feed_back(grad_output, factor, active, down_half)
    sum_in = GradSum([normed_mlp_low] * 2, [grad_gate, grad_up], shard_rows)
    sent_in = sum_in.far()
    grad_gate, grad_up, sent_in, mixed_low = tied(grad_gate, grad_up, sent_in, mixed_low)

    in_far = sum_in.send_far(sent_in)
    down_arrived = [
        lax.ppermute(cut, "outer", forward("outer", outer - 1)) for cut in down_cuts[1:2]
    ]
    part, part_low = back_project([grad_gate, grad_up], in_half, [F32, BF16])
    part, part_low, in_far, down_arrived[0], down_cuts = tied(
        part, part_low, in_far, down_arrived[0], down_cuts
    )

    in_near = sum_in.send_near(sum_in.near(in_far))
    down_arrived[1:] = [
        lax.ppermute(down_cuts[distance], "outer", forward("outer", outer - distance))
        for distance in range(2, outer)
    ]
    grad_hidden, hidden_side, grad_attended = hidden_back(
        part, swap(part_low), hidden, grad_output, gain_rows, weight, own_order
    )
    grad_query, mid, to_lower, to_upper = attend_back(
        block, joined, query_ids, key_ids, grad_attended.reshape(streams, length, side),
        cosine, sine,
    )
    from_lower = lax.ppermute(to_upper, ("outer", "inner"), onward)
    from_upper = lax.ppermute(to_lower, ("outer", "inner"), back)
    from_lower, from_upper, in_near, down_arrived[:2] = tied(
        from_lower, from_upper, in_near, down_arrived[:2]
    )

    grad_joined = join_grads(grad_query, mid, from_lower, from_upper, cosine, sine)
    grad_joined = grad_joined.reshape(rows, 3 * side)
    normed_low = window_norm.reshape(streams, window, width)[:, HALF : HALF + length]
    sum_attn = GradSum(
        [normed_low.reshape(rows, width), attended_low], [grad_joined, hidden_side], shard_rows
    )
    sent_attn, in_own = sum_attn.far(), sum_in.own(in_near)
    sent_attn, in_own, grad_joined = tied(sent_attn, in_own, grad_joined)

    attn_far = sum_attn.send_far(sent_attn)
    in_arrived = sum_in.send_direct(in_own, 1)
    out_mine, out_other = back_split(cores, mixed_low, down_half, streams)
    in_mine, in_other = back_split(cores, grad_joined, first, streams)
    attn_far, in_arrived, in_own, down_arrived, out_mine, out_other, in_mine, in_other = tied(
        attn_far, in_arrived, in_own, down_arrived, out_mine, out_other, in_mine, in_other
    )

    attn_near = sum_attn.send_near(sum_attn.near(attn_far))
    in_arrived = in_arrived + sum_in.send_direct(in_own, *range(2, outer))
    down_rows = late_rows([down_cuts[0], *down_arrived], shard_rows)
    attn_near, in_arrived, out_other, in_other, down_rows = tied(
        attn_near, in_arrived, out_other, in_other, down_rows
    )

    attn_own = sum_attn.own(attn_near)
    attn_arrived = sum_attn.send_direct(attn_own, *range(1, outer))
    output = end_rows(
        output_kernel, cores, [out_mine, swap(out_other)], [hidden], [order], BF16, streams
    ).reshape(tokens.shape)
    grad_tokens = end_rows(
        input_grad_kernel, cores, [in_mine, swap(in_other)], [grad_hidden, own_tokens],
        [gain_rows, order], F32, streams,
    ).reshape(tokens.shape)
    total_mine, total_other = sum_in.total(cores, in_own, in_arrived)
    grad_in, gain_grad_mlp = assemble(
        cores, total_mine, swap(total_other), [(0, 2, padded, units)], w_in, norm_mlp
    )
    output, grad_tokens, down_rows = tied(output, grad_tokens, down_rows)
    down_sums = late_sends(down_rows)
    attn_arrived, output, grad_tokens, grad_in, gain_grad_mlp, down_sums = tied(
        attn_arrived, output, grad_tokens, grad_in, gain_grad_mlp, down_sums
    )
    down_mine, down_other = sum_in.total(cores, down_rows[0, 0], down_sums)
    total_mine, total_other = sum_attn.total(cores, attn_own, attn_arrived)
    grad_qkv, grad_out, gain_grad_attn = assemble(
        cores, total_mine, swap(total_other),
        [(0, 3, side, side), (3 * side, 1, side, side)], w_qkv, norm_attn,
    )
    (grad_down,) = assemble(cores, down_mine, swap(down_other), [(0, 1, padded, units)])
    return (
        output,
        grad_tokens,
        gain_grad_attn.reshape(-1),
        gain_grad_mlp.reshape(-1),
        grad_qkv,
        grad_out,
        grad_in,
        grad_down,
    )


def solution(mesh):
    dp, seq = mesh.shape["dp"], mesh.shape["seq"]
    chips = seq // 2
    outer = 4 if chips % 4 == 0 else 1
    fine = Mesh(
        mesh.devices.reshape(dp, outer, chips // outer, 2), ("dp", "outer", "inner", "core")
    )
    line = ("outer", "inner", "core")
    every = ("dp",) + line
    token = P("dp", line, None)
    vector = P(every)
    matrix = P(every, None)
    return jax.shard_map(
        shards,
        mesh=fine,
        in_specs=(token, P("dp", None), vector, vector, matrix, matrix, matrix, matrix, token),
        out_specs=(token, token, vector, vector, matrix, matrix, matrix, matrix),
        check_vma=False,
    )
```
